32 devices in a mesh: dp: 4 (over z), seq: 4 (over y, x), tensor: 2 (over core).
Axes of the slice: x: 2, y: 2, z: 4, core: 2. Of those that a mesh axis runs over, the one named last changes fastest.
Arguments:
- hidden_in: bfloat16 [4, 1536, 2048], P('dp', 'seq'), may hold values from -6 to 6
- teacher: bfloat16 [4, 1536, 2048], P('dp', 'seq'), may hold values from -6 to 6
- segment_ids: int32 [4, 1536], P('dp'), may hold values from 0 to 2, as said below
- valid_mask: int32 [4, 1536], replicated, may hold values from 0 to 1, as said below
- norm1_gain: bfloat16 [2048], P(('dp', 'seq')), may hold values from 0.5 to 1.5
- w_z: bfloat16 [2048, 3072], P(('dp', 'seq'), 'tensor'), may hold values from -0.125 to 0.125
- w_x: bfloat16 [2048, 3072], P(('dp', 'seq'), 'tensor'), may hold values from -0.125 to 0.125
- w_bc: bfloat16 [2048, 512], replicated, may hold values from -0.125 to 0.125
- w_dt: bfloat16 [2048, 48], P(('dp', 'seq'), 'tensor'), may hold values from -0.125 to 0.125
- conv_weight: float32 [3584, 4], replicated, may hold values from -3 to 3
- conv_bias: float32 [3584], replicated, may hold values from -3 to 3
- dt_bias: float32 [48], replicated, may hold values from -3 to 0
- a_log: float32 [48], replicated, may hold values from -11 to -2
- d_skip: float32 [48], replicated, may hold values from 0.5 to 1.5
- group_gain: float32 [48, 64], replicated, may hold values from 0.5 to 1.5
- w_mamba_out: bfloat16 [3072, 2048], P('tensor', ('dp', 'seq')), may hold values from -0.109375 to 0.109375
- w_query: bfloat16 [2048, 1024], P(('dp', 'seq'), 'tensor'), may hold values from -0.125 to 0.125
- w_key: bfloat16 [2048, 256], P(('dp', 'seq'), 'tensor'), may hold values from -0.125 to 0.125
- w_value: bfloat16 [2048, 256], P(('dp', 'seq'), 'tensor'), may hold values from -0.125 to 0.125
- w_attn_out: bfloat16 [1024, 2048], P('tensor', ('dp', 'seq')), may hold values from -0.75 to 0.75
- norm2_gain: bfloat16 [2048], P(('dp', 'seq')), may hold values from 0.5 to 1.5
- w_gate: bfloat16 [2048, 4096], P(('dp', 'seq'), 'tensor'), may hold values from -0.125 to 0.125
- w_up: bfloat16 [2048, 4096], P(('dp', 'seq'), 'tensor'), may hold values from -0.125 to 0.125
- w_down: bfloat16 [4096, 2048], P('tensor', ('dp', 'seq')), may hold values from -0.09375 to 0.09375
Outputs:
- block_output: bfloat16 [4, 1536, 2048], P('dp', 'seq')
- grad_input: float32 [4, 1536, 2048], P('dp', 'seq')
- grad_norm1_gain: float32 [2048], P(('dp', 'seq'))
- grad_w_z: float32 [2048, 3072], P(('dp', 'seq'), 'tensor')
- grad_w_x: float32 [2048, 3072], P(('dp', 'seq'), 'tensor')
- grad_w_bc: float32 [2048, 512], replicated
- grad_w_dt: float32 [2048, 48], P(('dp', 'seq'), 'tensor')
- grad_conv_weight: float32 [3584, 4], replicated
- grad_conv_bias: float32 [3584], replicated
- grad_dt_bias: float32 [48], replicated
- grad_a_log: float32 [48], replicated
- grad_d_skip: float32 [48], replicated
- grad_group_gain: float32 [48, 64], replicated
- grad_w_mamba_out: float32 [3072, 2048], P('tensor', ('dp', 'seq'))
- grad_w_query: float32 [2048, 1024], P(('dp', 'seq'), 'tensor')
- grad_w_key: float32 [2048, 256], P(('dp', 'seq'), 'tensor')
- grad_w_value: float32 [2048, 256], P(('dp', 'seq'), 'tensor')
- grad_w_attn_out: float32 [1024, 2048], P('tensor', ('dp', 'seq'))
- grad_norm2_gain: float32 [2048], P(('dp', 'seq'))
- grad_w_gate: float32 [2048, 4096], P(('dp', 'seq'), 'tensor')
- grad_w_up: float32 [2048, 4096], P(('dp', 'seq'), 'tensor')
- grad_w_down: float32 [4096, 2048], P('tensor', ('dp', 'seq'))
The draws below stay inside these ranges and needn't reach their ends.
Inputs may be any that keep to these rules, and one draw needn't show every extreme that they name: `segment_ids`: ids never fall along a row and start at 0; segment 1 begins within the first 192 positions of the row and segment 2 within its last 192. `valid_mask`: the last position of every row is valid.
All inputs are finite; a program needn't handle non-finite values.
Results may differ from the reference program's by a relative error of at most 0.012.
The reference program's roundings to bfloat16 on the way count: a program that leaves them out, or rounds other values in their place, can miss the bound.
Values may be sent and summed in bfloat16 or wider, within the bound.
A program may use at most 256 MiB of HBM per device.

```python
from functools import partial
import jax
import jax.numpy as jnp
from jax import lax

D = 2048
MH = 48
HP = 64
NS = 256
KC = 4
HQ = 8
HK = 2
HD = 128
FF = 4096
TOK_DEV = 384
DI = 3072
LENGTH = 1536
BATCH = 4
TOKENS = 6144


def draw_segment_ids(key, part):
    key = jax.random.fold_in(key, 11)
    first_key, last_key = jax.random.split(key)
    first_cut = jax.random.randint(first_key, (BATCH, 1), 1, TOK_DEV // 2 + 1)
    last_cut = LENGTH - jax.random.randint(last_key, (BATCH, 1), 1, TOK_DEV // 2 + 1)
    positions = jnp.arange(LENGTH)[None, :]
    return (positions >= first_cut).astype(jnp.int32) + (positions >= last_cut).astype(jnp.int32)


def draw_valid_mask(key, part):
    key = jax.random.fold_in(key, 23)
    levels = jax.random.randint(key, (BATCH, LENGTH), 0, 1000)
    threshold = 300 + 600 * jnp.arange(LENGTH) // LENGTH
    drawn = (levels < threshold[None, :]).astype(jnp.int32)
    return drawn.at[:, LENGTH - 1].set(1)


def shard_levels(rng, shape, cuts, least, high):
    factor_of, own = 1.0, jax.random.fold_in(rng, 6)
    for dim, parts in cuts:
        heights = jnp.exp(jax.random.uniform(jax.random.fold_in(own, dim), (parts,), jnp.float32, least / len(cuts), high / len(cuts)))
        factor_of = factor_of * jnp.repeat(heights, shape[dim] // parts).reshape([-1 if axis == dim else 1 for axis in range(len(shape))])
    return factor_of


def bell_draw(key, extent, deviation, reach, pieces=(), held_as=jnp.bfloat16):
    factor_of = shard_levels(key, extent, pieces, -0.22, 0.18) if pieces else 1.0
    array = jax.random.normal(key, extent, jnp.float32) * deviation * factor_of
    return jnp.minimum(jnp.maximum(array, -reach), reach).astype(held_as)


def setup_inputs(seed: int = 0) -> dict:
    arg_keys = jax.random.split(jax.random.key(seed), 25)
    hidden_in = bell_draw(arg_keys[0], (BATCH, LENGTH, D), 1.0, 6.0, ((0, 4), (1, 4)))
    teacher = bell_draw(arg_keys[1], (BATCH, LENGTH, D), 1.0, 6.0, ((0, 4), (1, 4)))
    segment_ids = draw_segment_ids(jax.random.fold_in(arg_keys[24], 71), 0)
    valid_mask = draw_valid_mask(jax.random.fold_in(arg_keys[24], 71), 0)
    norm1_gain = jnp.clip(1.0 + 0.1 * jax.random.normal(arg_keys[4], (D,), jnp.float32), 0.5, 1.5).astype(jnp.bfloat16)
    w_z = bell_draw(arg_keys[5], (D, DI), D ** -0.5, 0.125, ((0, 16), (1, 2)))
    w_x = bell_draw(arg_keys[6], (D, DI), D ** -0.5, 0.125, ((0, 16), (1, 2)))
    w_bc = bell_draw(arg_keys[7], (D, 2 * NS), D ** -0.5, 0.125)
    w_dt = bell_draw(arg_keys[8], (D, MH), D ** -0.5, 0.125, ((0, 16), (1, 2)))
    conv_weight = bell_draw(arg_keys[9], (DI + 2 * NS, KC), 0.5, 3.0, (), jnp.float32)
    conv_bias = bell_draw(arg_keys[10], (DI + 2 * NS,), 0.5, 3.0, (), jnp.float32)
    dt_bias = jnp.clip(jax.random.uniform(arg_keys[11], (MH,), jnp.float32, -3.0, 0.0), -3.0, 0.0)
    a_log = jnp.clip(jax.random.uniform(arg_keys[12], (MH,), jnp.float32, -11.0, -2.0), -11.0, -2.0)
    d_skip = jnp.clip(jax.random.uniform(arg_keys[13], (MH,), jnp.float32, 0.5, 1.5), 0.5, 1.5)
    group_gain = jnp.clip(1.0 + 0.1 * jax.random.normal(arg_keys[14], (MH, HP), jnp.float32), 0.5, 1.5)
    w_mamba_out = bell_draw(arg_keys[15], (DI, D), DI ** -0.5, 0.109375, ((0, 2), (1, 16)))
    w_query = bell_draw(arg_keys[16], (D, HQ * HD), D ** -0.5, 0.125, ((0, 16), (1, 2)))
    w_key = bell_draw(arg_keys[17], (D, HK * HD), D ** -0.5, 0.125, ((0, 16), (1, 2)))
    w_value = bell_draw(arg_keys[18], (D, HK * HD), D ** -0.5, 0.125, ((0, 16), (1, 2)))
    w_attn_out = bell_draw(arg_keys[19], (HQ * HD, D), (HQ * HD // 16) ** -0.5, 0.75, ((0, 2), (1, 16)))
    norm2_gain = jnp.clip(1.0 + 0.1 * jax.random.normal(arg_keys[20], (D,), jnp.float32), 0.5, 1.5).astype(jnp.bfloat16)
    w_gate = bell_draw(arg_keys[21], (D, FF), D ** -0.5, 0.125, ((0, 16), (1, 2)))
    w_up = bell_draw(arg_keys[22], (D, FF), D ** -0.5, 0.125, ((0, 16), (1, 2)))
    w_down = bell_draw(arg_keys[23], (FF, D), FF ** -0.5, 0.09375, ((0, 2), (1, 16)))
    return {"hidden_in": hidden_in, "teacher": teacher, "segment_ids": segment_ids, "valid_mask": valid_mask, "norm1_gain": norm1_gain, "w_z": w_z, "w_x": w_x, "w_bc": w_bc, "w_dt": w_dt, "conv_weight": conv_weight, "conv_bias": conv_bias, "dt_bias": dt_bias, "a_log": a_log, "d_skip": d_skip, "group_gain": group_gain, "w_mamba_out": w_mamba_out, "w_query": w_query, "w_key": w_key, "w_value": w_value, "w_attn_out": w_attn_out, "norm2_gain": norm2_gain, "w_gate": w_gate, "w_up": w_up, "w_down": w_down}


EPSILON = 1e-06
GROUP_EPSILON = 1e-05
ROPE_BASE = 10000.0
HIGHEST = lax.Precision.HIGHEST

@jax.custom_vjp
def low(v):
    return lax.optimization_barrier(v.astype(jnp.bfloat16)).astype(jnp.float32)

@jax.custom_vjp
def low_back(v):
    return v

def low_keep(v):
    return (low(v), None)

def low_pass(kept, grad):
    return (grad,)

def back_keep(v):
    return (v, None)

def back_low(kept, grad):
    return (low(grad),)
low.defvjp(low_keep, low_pass)
low_back.defvjp(back_keep, back_low)

def precise_dot(left_side, right_side):
    return jnp.dot(left_side, right_side, precision=HIGHEST, preferred_element_type=jnp.float32)

def rms_norm(values, gain_row):
    scale_row = lax.rsqrt(lax.optimization_barrier(jnp.mean(values * values, axis=-1, keepdims=True)) + EPSILON)
    return values * scale_row * gain_row

def rotate(values, positions):
    half_dim = values.shape[-1] // 2
    frequency = ROPE_BASE ** (-2.0 * jnp.arange(half_dim).astype(jnp.float32) / values.shape[-1])
    angles = positions.astype(jnp.float32)[:, None] * frequency[None, :]
    cosine = jnp.cos(angles)[:, None, :]
    sine_part = jnp.sin(angles)[:, None, :]
    first_half = values[..., :half_dim]
    second = values[..., half_dim:]
    return jnp.concatenate([first_half * cosine - second * sine_part, second * cosine + first_half * sine_part], axis=-1)

def conv_silu(extended, seg_ext, seg_rows, weights, bias_row):
    size_rows = seg_rows.shape[0]
    summed = jnp.zeros((size_rows, weights.shape[0]), jnp.float32) + bias_row[None, :]
    for tap_index in range(weights.shape[1]):
        window = lax.slice_in_dim(extended, tap_index, tap_index + size_rows, axis=0)
        keep_mask = (lax.slice_in_dim(seg_ext, tap_index, tap_index + size_rows) == seg_rows).astype(jnp.float32)
        summed = summed + window * weights[:, tap_index][None, :] * keep_mask[:, None]
    return jax.nn.silu(summed)

def group_gate(ssm_out, gate_z, group_gain):
    mixed_val = ssm_out * jax.nn.silu(gate_z)
    return mixed_val * lax.rsqrt(lax.optimization_barrier(jnp.mean(mixed_val * mixed_val, axis=-1, keepdims=True)) + GROUP_EPSILON) * group_gain[None]

def ssd_block(rate, d_skip_row, state_in, block_inputs):
    heads_x, b_rows, c_rows, dt_rows, seg_rows, seg_before = block_inputs
    size_rows = seg_rows.shape[0]
    cumul = jnp.cumsum(-rate[None, :] * dt_rows, axis=0)
    order_pos = jnp.arange(size_rows)
    allowed = (seg_rows[:, None] == seg_rows[None, :]) & (order_pos[:, None] >= order_pos[None, :])
    differ = cumul[:, None, :] - cumul[None, :, :]
    decay = jnp.exp(jnp.where(allowed[:, :, None], differ, -jnp.inf))
    gram = precise_dot(c_rows, b_rows.T)
    mixing = gram[:, :, None] * decay * dt_rows[None, :, :]
    outputs = jnp.einsum('tsh,shp->thp', mixing, heads_x, precision=HIGHEST)
    entry_keep = (seg_rows == seg_before).astype(jnp.float32)
    entry_part = jnp.einsum('tn,hpn->thp', c_rows, state_in, precision=HIGHEST)
    outputs = outputs + jnp.exp(cumul)[:, :, None] * entry_keep[:, None, None] * entry_part
    outputs = outputs + d_skip_row[None, :, None] * heads_x
    tail_keep = (seg_rows == seg_rows[-1]).astype(jnp.float32)
    tail_weight = jnp.exp(cumul[-1][None, :] - cumul) * tail_keep[:, None] * dt_rows
    local_state = jnp.einsum('sh,shp,sn->hpn', tail_weight, heads_x, b_rows, precision=HIGHEST)
    carry_factor = jnp.exp(cumul[-1]) * (seg_rows[-1] == seg_before).astype(jnp.float32)
    state_out = carry_factor[:, None, None] * state_in + local_state
    return (state_out, outputs)

def ssd_row(heads_x, b_rows, c_rows, dt_rows, seg_row, rate, d_skip_row):
    length_rows = seg_row.shape[0]
    blocks = length_rows // TOK_DEV
    seg_blocks = seg_row.reshape(blocks, TOK_DEV)
    seg_before = jnp.concatenate([jnp.full((1,), -1, jnp.int32), seg_blocks[:-1, -1]])
    state_zero = jnp.zeros((MH, HP, NS), jnp.float32)
    block_fn = jax.checkpoint(partial(ssd_block, rate, d_skip_row))
    block_inputs = (heads_x.reshape(blocks, TOK_DEV, MH, HP), b_rows.reshape(blocks, TOK_DEV, NS), c_rows.reshape(blocks, TOK_DEV, NS), dt_rows.reshape(blocks, TOK_DEV, MH), seg_blocks, seg_before)
    final_state, outputs = lax.scan(block_fn, state_zero, block_inputs)
    return outputs.reshape(length_rows, MH, HP)

def attention_row(queries, keys, values, seg_row):
    length_rows = queries.shape[0]
    groups = HQ // HK
    grouped = queries.reshape(length_rows, HK, groups, HD)
    key_pos = jnp.arange(length_rows)

    def one_block(block_index):
        start_row = (block_index * TOK_DEV).astype(jnp.int32)
        query_blk = lax.dynamic_slice_in_dim(grouped, start_row, TOK_DEV, 0)
        query_pos = start_row + jnp.arange(TOK_DEV)
        query_seg = lax.dynamic_slice_in_dim(seg_row, start_row, TOK_DEV)
        scores = jnp.einsum('tkgd,skd->kgts', query_blk, keys, precision=HIGHEST) * HD ** (-0.5)
        scores = low_back(scores)
        allowed = (query_pos[:, None] >= key_pos[None, :]) & (query_seg[:, None] == seg_row[None, :])
        scores = jnp.where(allowed[None, None], scores, -jnp.inf)
        probs = low(jax.nn.softmax(scores, axis=-1))
        return jnp.einsum('kgts,skd->tkgd', probs, values, precision=HIGHEST).reshape(TOK_DEV, HQ * HD)
    outputs = lax.map(jax.checkpoint(one_block), jnp.arange(length_rows // TOK_DEV))
    return outputs.reshape(length_rows, HQ * HD)

def layer_row(params, hidden_row, teacher_row, seg_row, mask_row, token_count):
    gain_one, w_z, w_x, w_bc, w_dt, conv_weight, conv_bias, dt_bias, a_log, d_skip, group_gain, w_mamba_out, w_query, w_key, w_value, w_attn_out, gain_two, w_gate, w_up, w_down = params
    length_rows = hidden_row.shape[0]
    normed = low(rms_norm(hidden_row, gain_one))
    gate_z = low_back(precise_dot(normed, w_z))
    pre_x = low(low_back(precise_dot(normed, w_x)))
    pre_bc = low(precise_dot(normed, w_bc))
    dt_raw = low_back(precise_dot(normed, w_dt))
    pre_all = jnp.concatenate([pre_x, pre_bc], axis=1)
    seg_ext = jnp.concatenate([jnp.full((KC - 1,), -1, jnp.int32), seg_row])
    extended = jnp.concatenate([jnp.zeros((KC - 1, pre_all.shape[1]), jnp.float32), pre_all], axis=0)
    mixed = low(conv_silu(extended, seg_ext, seg_row, conv_weight, conv_bias))
    heads_x = mixed[:, :DI].reshape(length_rows, MH, HP)
    b_rows = mixed[:, DI:DI + NS]
    c_rows = mixed[:, DI + NS:]
    dt_rows = jax.nn.softplus(dt_raw + dt_bias[None, :])
    ssm_out = ssd_row(heads_x, b_rows, c_rows, dt_rows, seg_row, jnp.exp(a_log), d_skip)
    gated = low(group_gate(ssm_out, gate_z.reshape(length_rows, MH, HP), group_gain).reshape(length_rows, DI))
    positions = jnp.arange(length_rows)
    queries = low(rotate(low_back(precise_dot(normed, w_query)).reshape(length_rows, HQ, HD), positions))
    keys = low(rotate(low_back(precise_dot(normed, w_key)).reshape(length_rows, HK, HD), positions))
    values = low(low_back(precise_dot(normed, w_value))).reshape(length_rows, HK, HD)
    attended = low(low_back(attention_row(queries, keys, values, seg_row)))
    branch = low_back(precise_dot(gated, w_mamba_out) + precise_dot(attended, w_attn_out))
    middle = hidden_row + branch
    normed_two = low(rms_norm(middle, gain_two))
    gate_pre = low_back(precise_dot(normed_two, w_gate))
    up_pre = low_back(precise_dot(normed_two, w_up))
    activated = low(jax.nn.silu(gate_pre) * up_pre)
    output = middle + low_back(precise_dot(activated, w_down))
    error = output - teacher_row
    loss_term = TOKENS * jnp.sum(mask_row[:, None] * error * error) / token_count
    return (loss_term, output)

def reference(hidden_in, teacher, segment_ids, valid_mask, norm1_gain, w_z, w_x, w_bc, w_dt, conv_weight, conv_bias, dt_bias, a_log, d_skip, group_gain, w_mamba_out, w_query, w_key, w_value, w_attn_out, norm2_gain, w_gate, w_up, w_down):
    params = (norm1_gain.astype(jnp.float32), w_z.astype(jnp.float32), w_x.astype(jnp.float32), w_bc.astype(jnp.float32), w_dt.astype(jnp.float32), conv_weight.astype(jnp.float32), conv_bias.astype(jnp.float32), dt_bias.astype(jnp.float32), a_log.astype(jnp.float32), d_skip.astype(jnp.float32), group_gain.astype(jnp.float32), w_mamba_out.astype(jnp.float32), w_query.astype(jnp.float32), w_key.astype(jnp.float32), w_value.astype(jnp.float32), w_attn_out.astype(jnp.float32), norm2_gain.astype(jnp.float32), w_gate.astype(jnp.float32), w_up.astype(jnp.float32), w_down.astype(jnp.float32))
    token_count = jnp.sum(valid_mask).astype(jnp.float32)

    def per_row(totals, row_inputs):
        hidden_row, teacher_row, seg_row, mask_row = row_inputs

        def forward(param_set, inputs_row):
            return layer_row(param_set, inputs_row, teacher_row.astype(jnp.float32), seg_row, mask_row.astype(jnp.float32), token_count)
        (loss_term, output), pull_back = jax.vjp(forward, params, hidden_row.astype(jnp.float32))
        grads, grad_row = pull_back((jnp.ones((), jnp.float32), jnp.zeros_like(output)))
        totals = jax.tree.map(jnp.add, totals, grads)
        return (totals, (output.astype(jnp.bfloat16), grad_row))
    zero_tree = jax.tree.map(jnp.zeros_like, params)
    totals, (outputs, grad_input) = lax.scan(per_row, zero_tree, (hidden_in, teacher, segment_ids, valid_mask))
    g_norm_one, g_w_z, g_w_x, g_w_bc, g_w_dt, g_conv_w, g_conv_b, g_dt_bias, g_a_log, g_d_skip, g_group, g_w_mo, g_w_q, g_w_k, g_w_v, g_w_ao, g_norm_two, g_w_gate, g_w_up, g_w_down = totals
    return (outputs, grad_input, g_norm_one, g_w_z, g_w_x, g_w_bc, g_w_dt, g_conv_w, g_conv_b, g_dt_bias, g_a_log, g_d_skip, g_group, g_w_mo, g_w_q, g_w_k, g_w_v, g_w_ao, g_norm_two, g_w_gate, g_w_up, g_w_down)
```

```python
from functools import partial

import jax
import jax.numpy as jnp
from jax import lax
from jax.experimental import pallas as pl
from jax.experimental.pallas import tpu as pltpu
from jax.sharding import PartitionSpec as P

MH = 48
HP = 64
NS = 256
KC = 4
HD = 128


EPSILON = 1e-06
GROUP_EPSILON = 1e-05
ROPE_BASE = 10000.0
HIGHEST = lax.Precision.HIGHEST


def shifted(block, axis, distance):
    devices = range(lax.axis_size(axis))
    route = [(i - distance, i) for i in devices if i - distance in devices]
    return lax.ppermute(block, axis, route)


def carried_in(part, axis, combine, identity, reverse):
    count = lax.axis_size(axis)
    place = lax.axis_index(axis)
    ahead = count - 1 - place if reverse else place
    gathered = jax.tree.map(lambda a: lax.all_gather(a, axis), part)
    state = jax.tree.map(lambda a, e: jnp.zeros_like(a) + jnp.asarray(e, a.dtype), part, identity)

    def one(lap, state):
        source = count - 1 - lap if reverse else lap
        return combine(
            state, jax.tree.map(lambda a: lax.dynamic_index_in_dim(a, source, 0, False), gathered)
        )

    return lax.fori_loop(0, ahead, one, state)


def mat_dot(left_side, right_side):
    return jnp.dot(left_side, right_side, preferred_element_type=jnp.float32)


def dot_left_t(left_side, right_side):
    return lax.dot_general(
        left_side, right_side, (((0,), (0,)), ((), ())), preferred_element_type=jnp.float32
    )


def dot_right_t(left_side, right_side):
    return lax.dot_general(
        left_side, right_side, (((1,), (1,)), ((), ())), preferred_element_type=jnp.float32
    )


def rms_norm(values, gain_row):
    scale_row = lax.rsqrt(jnp.mean(values * values, axis=-1, keepdims=True) + EPSILON)
    return values * scale_row * gain_row


def rotate(positions, values):
    half_dim = values.shape[-1] // 2
    frequency = ROPE_BASE ** (-2.0 * jnp.arange(half_dim).astype(jnp.float32) / values.shape[-1])
    angles = positions.astype(jnp.float32)[:, None] * frequency[None, :]
    cosine = jnp.cos(angles)[:, None, :]
    sine_part = jnp.sin(angles)[:, None, :]
    first_half = values[..., :half_dim]
    second = values[..., half_dim:]
    return jnp.concatenate(
        [first_half * cosine - second * sine_part, second * cosine + first_half * sine_part],
        axis=-1,
    )


def conv_silu(seg_ext, seg_rows, extended, weights, bias_row):
    size_rows = seg_rows.shape[0]
    summed = jnp.zeros((size_rows, weights.shape[0]), jnp.float32) + bias_row[None, :]
    for tap_index in range(weights.shape[1]):
        window = lax.slice_in_dim(extended, tap_index, tap_index + size_rows, axis=0)
        keep_mask = (
            lax.slice_in_dim(seg_ext, tap_index, tap_index + size_rows) == seg_rows
        ).astype(jnp.float32)
        summed = summed + window * weights[:, tap_index][None, :] * keep_mask[:, None]
    return jax.nn.silu(summed)


def group_gate(ssm_out, gate_z, group_gain):
    mixed_val = ssm_out * jax.nn.silu(gate_z)
    return (
        mixed_val
        * lax.rsqrt(jnp.mean(mixed_val * mixed_val, axis=-1, keepdims=True) + GROUP_EPSILON)
        * group_gain[None]
    )


def swiglu(gate_pre, up_pre):
    return jax.nn.silu(gate_pre) * up_pre


def split_mixed(mixed_in, heads_local):
    size_rows = mixed_in.shape[0]
    width_x = heads_local * HP
    heads_x = mixed_in[:, :width_x].reshape(size_rows, heads_local, HP)
    return (heads_x, mixed_in[:, width_x : width_x + NS], mixed_in[:, width_x + NS :])


def ssd_main(seg_rows, seg_before, mixed_in, dt_raw, dt_bias_row, a_log_row, d_skip_row):
    size_rows = seg_rows.shape[0]
    heads_x, b_rows, c_rows = split_mixed(mixed_in, dt_raw.shape[1])
    dt_rows = jax.nn.softplus(dt_raw + dt_bias_row[None, :])
    cumul = jnp.cumsum(-jnp.exp(a_log_row)[None, :] * dt_rows, axis=0)
    order_pos = jnp.arange(size_rows)
    allowed = (seg_rows[:, None] == seg_rows[None, :]) & (order_pos[:, None] >= order_pos[None, :])
    differ = cumul[:, None, :] - cumul[None, :, :]
    decay = jnp.exp(jnp.where(allowed[:, :, None], differ, -jnp.inf))
    gram = jnp.dot(c_rows, b_rows.T, precision=HIGHEST, preferred_element_type=jnp.float32)
    mixing = gram[:, :, None] * decay * dt_rows[None, :, :]
    outputs = jnp.einsum("tsh,shp->thp", mixing, heads_x, precision=HIGHEST)
    outputs = outputs + d_skip_row[None, :, None] * heads_x
    tail_keep = (seg_rows == seg_rows[-1]).astype(jnp.float32)
    tail_weight = jnp.exp(cumul[-1][None, :] - cumul) * tail_keep[:, None] * dt_rows
    local_state = jnp.einsum("sh,shp,sn->hpn", tail_weight, heads_x, b_rows, precision=HIGHEST)
    carry_factor = jnp.exp(cumul[-1]) * (seg_rows[-1] == seg_before).astype(jnp.float32)
    return (outputs, carry_factor, local_state)


def ssd_state(seg_rows, seg_before, mixed_in, dt_raw, dt_bias_row, a_log_row, entry_state):
    heads_x, b_rows, c_rows = split_mixed(mixed_in, dt_raw.shape[1])
    dt_rows = jax.nn.softplus(dt_raw + dt_bias_row[None, :])
    cumul = jnp.cumsum(-jnp.exp(a_log_row)[None, :] * dt_rows, axis=0)
    entry_keep = (seg_rows == seg_before).astype(jnp.float32)
    entry_part = jnp.einsum("tn,hpn->thp", c_rows, entry_state, precision=HIGHEST)
    return jnp.exp(cumul)[:, :, None] * entry_keep[:, None, None] * entry_part


def chain_states(earlier, later):
    return (earlier[0] * later[0], later[0][:, None, None] * earlier[1] + later[1])


def block_scores(queries, keys_all, vals_all, seg_full, query_pos, seg_query, block_index, key_len):
    key_blk = keys_all[block_index * key_len : (block_index + 1) * key_len]
    val_blk = vals_all[block_index * key_len : (block_index + 1) * key_len]
    seg_key = seg_full[block_index * key_len : (block_index + 1) * key_len]
    key_pos = block_index * key_len + jnp.arange(key_len)
    scores = jnp.einsum(
        "tkgd,skd->kgts", queries, key_blk, preferred_element_type=jnp.float32
    ) * HD ** (-0.5)
    allowed = (query_pos[:, None] >= key_pos[None, :]) & (seg_query[:, None] == seg_key[None, :])
    return (key_blk, val_blk, jnp.where(allowed[None, None], scores, -jnp.inf))


def attend_forward(queries, keys_all, vals_all, seg_full, query_pos, seg_query, block_count):
    key_len = keys_all.shape[0] // block_count
    stat_shape = (queries.shape[1], queries.shape[2], queries.shape[0])
    running_max = jnp.full(stat_shape, -1e30, jnp.float32)
    running_sum = jnp.zeros(stat_shape, jnp.float32)
    for block_index in range(block_count):
        needed = block_index * key_len <= query_pos[-1]

        def stat_step(stats, block_index=block_index):
            old_max, old_sum = stats
            key_blk, val_blk, scores = block_scores(
                queries, keys_all, vals_all, seg_full, query_pos, seg_query, block_index, key_len
            )
            new_max = jnp.maximum(old_max, jnp.max(scores, axis=-1))
            new_sum = old_sum * jnp.exp(old_max - new_max) + jnp.sum(
                jnp.exp(scores - new_max[..., None]), axis=-1
            )
            return (new_max, new_sum)

        running_max, running_sum = lax.cond(
            needed, stat_step, lambda stats: stats, (running_max, running_sum)
        )
    log_total = running_max + jnp.log(running_sum)
    attended = jnp.zeros(queries.shape, jnp.float32)
    for block_index in range(block_count):
        needed = block_index * key_len <= query_pos[-1]

        def value_step(total, block_index=block_index):
            key_blk, val_blk, scores = block_scores(
                queries, keys_all, vals_all, seg_full, query_pos, seg_query, block_index, key_len
            )
            probs = jnp.exp(scores - log_total[..., None]).astype(jnp.bfloat16)
            return total + jnp.einsum(
                "kgts,skd->tkgd", probs, val_blk, preferred_element_type=jnp.float32
            )

        attended = lax.cond(needed, value_step, lambda total: total, attended)
    return (log_total, attended)


def attend_backward(
    queries, keys_all, vals_all, seg_full, query_pos, seg_query, block_count, grad_out, log_total
):
    key_len = keys_all.shape[0] // block_count
    delta = jnp.zeros(log_total.shape, jnp.float32)
    for block_index in range(block_count):
        needed = block_index * key_len <= query_pos[-1]

        def delta_step(total, block_index=block_index):
            key_blk, val_blk, scores = block_scores(
                queries, keys_all, vals_all, seg_full, query_pos, seg_query, block_index, key_len
            )
            probs = jnp.exp(scores - log_total[..., None])
            grad_probs = jnp.einsum(
                "tkgd,skd->kgts", grad_out, val_blk, preferred_element_type=jnp.float32
            )
            return total + jnp.sum(probs * grad_probs, axis=-1)

        delta = lax.cond(needed, delta_step, lambda total: total, delta)
    grad_query = jnp.zeros(queries.shape, jnp.float32)
    empty_part = jnp.zeros((key_len, keys_all.shape[1], keys_all.shape[2]), jnp.float32)
    key_parts = []
    val_parts = []
    for block_index in range(block_count):
        needed = block_index * key_len <= query_pos[-1]

        def grad_step(total, block_index=block_index):
            key_blk, val_blk, scores = block_scores(
                queries, keys_all, vals_all, seg_full, query_pos, seg_query, block_index, key_len
            )
            probs = jnp.exp(scores - log_total[..., None])
            grad_probs = jnp.einsum(
                "tkgd,skd->kgts", grad_out, val_blk, preferred_element_type=jnp.float32
            )
            grad_scores = (probs * (grad_probs - delta[..., None])).astype(jnp.bfloat16)
            new_total = total + jnp.einsum(
                "kgts,skd->tkgd", grad_scores, key_blk, preferred_element_type=jnp.float32
            ) * HD ** (-0.5)
            key_part = jnp.einsum(
                "kgts,tkgd->skd", grad_scores, queries, preferred_element_type=jnp.float32
            ) * HD ** (-0.5)
            val_part = jnp.einsum(
                "kgts,tkgd->skd",
                probs.astype(jnp.bfloat16),
                grad_out,
                preferred_element_type=jnp.float32,
            )
            return (new_total, key_part, val_part)

        grad_query, key_part, val_part = lax.cond(
            needed, grad_step, lambda total: (total, empty_part, empty_part), grad_query
        )
        key_parts.append(key_part)
        val_parts.append(val_part)
    return (grad_query, jnp.concatenate(key_parts, axis=0), jnp.concatenate(val_parts, axis=0))


def local(
    hidden_in,
    teacher,
    segment_ids,
    valid_mask,
    norm1_gain,
    w_z,
    w_x,
    w_bc,
    w_dt,
    conv_weight,
    conv_bias,
    dt_bias,
    a_log,
    d_skip,
    group_gain,
    w_mamba_out,
    w_query,
    w_key,
    w_value,
    w_attn_out,
    norm2_gain,
    w_gate,
    w_up,
    w_down,
):
    tensor_rank = lax.axis_index("tensor")
    seq_rank = lax.axis_index("seq")
    data_rank = lax.axis_index("dp")
    seq_count = lax.axis_size("seq")
    tensor_count = lax.axis_size("tensor")
    size_rows = hidden_in.shape[1]
    full_length = segment_ids.shape[1]
    row_start = seq_rank * size_rows
    seg_full = segment_ids[0]
    seg_local = lax.dynamic_slice_in_dim(seg_full, row_start, size_rows)
    seg_padded = jnp.concatenate([jnp.full((KC - 1,), -1, jnp.int32), seg_full])
    seg_ext = lax.dynamic_slice_in_dim(seg_padded, row_start, size_rows + KC - 1)
    seg_prev = lax.dynamic_index_in_dim(seg_padded, row_start + KC - 2, keepdims=False)
    token_count = jnp.sum(valid_mask).astype(jnp.float32)
    mask_rows = lax.dynamic_slice(valid_mask, (data_rank, row_start), (1, size_rows))[0].astype(
        jnp.float32
    )
    total_tokens = float(valid_mask.shape[0] * valid_mask.shape[1])
    (
        gain_one,
        full_z,
        full_x,
        full_dt,
        full_mo,
        full_q,
        full_k,
        full_v,
        full_ao,
        gain_two,
        full_gate,
        full_up,
        full_down,
    ) = (
        lax.all_gather(norm1_gain, ("dp", "seq"), axis=0, tiled=True),
        lax.all_gather(w_z, ("dp", "seq"), axis=0, tiled=True),
        lax.all_gather(w_x, ("dp", "seq"), axis=0, tiled=True),
        lax.all_gather(w_dt, ("dp", "seq"), axis=0, tiled=True),
        lax.all_gather(w_mamba_out, ("dp", "seq"), axis=1, tiled=True),
        lax.all_gather(w_query, ("dp", "seq"), axis=0, tiled=True),
        lax.all_gather(w_key, ("dp", "seq"), axis=0, tiled=True),
        lax.all_gather(w_value, ("dp", "seq"), axis=0, tiled=True),
        lax.all_gather(w_attn_out, ("dp", "seq"), axis=1, tiled=True),
        lax.all_gather(norm2_gain, ("dp", "seq"), axis=0, tiled=True),
        lax.all_gather(w_gate, ("dp", "seq"), axis=0, tiled=True),
        lax.all_gather(w_up, ("dp", "seq"), axis=0, tiled=True),
        lax.all_gather(w_down, ("dp", "seq"), axis=1, tiled=True),
    )
    heads_local = MH // tensor_count
    width_x = heads_local * HP
    head_start = tensor_rank * heads_local
    hidden = hidden_in[0].astype(jnp.float32)
    normed_f, norm_one_pull = jax.vjp(rms_norm, hidden, gain_one.astype(jnp.float32))
    normed = normed_f.astype(jnp.bfloat16)
    gate_z = mat_dot(normed, full_z)
    pre_x = mat_dot(normed, full_x).astype(jnp.bfloat16)
    pre_bc = mat_dot(normed, w_bc).astype(jnp.bfloat16)
    dt_raw = mat_dot(normed, full_dt)
    pre_all = jnp.concatenate([pre_x, pre_bc], axis=1)
    rim_rows = shifted(pre_all[size_rows - (KC - 1) :], "seq", 1)
    extended = jnp.concatenate([rim_rows, pre_all], axis=0).astype(jnp.float32)
    conv_local = jnp.concatenate(
        [
            lax.dynamic_slice_in_dim(conv_weight, head_start * HP, width_x, 0),
            conv_weight[MH * HP :],
        ],
        axis=0,
    )
    bias_local = jnp.concatenate(
        [lax.dynamic_slice_in_dim(conv_bias, head_start * HP, width_x, 0), conv_bias[MH * HP :]],
        axis=0,
    )
    mixed_f, conv_pull = jax.vjp(
        partial(conv_silu, seg_ext, seg_local), extended, conv_local, bias_local
    )
    mixed_in = lax.optimization_barrier(mixed_f.astype(jnp.bfloat16)).astype(jnp.float32)
    dt_bias_loc = lax.dynamic_slice_in_dim(dt_bias, head_start, heads_local)
    a_log_loc = lax.dynamic_slice_in_dim(a_log, head_start, heads_local)
    d_skip_loc = lax.dynamic_slice_in_dim(d_skip, head_start, heads_local)
    group_loc = lax.dynamic_slice_in_dim(group_gain, head_start, heads_local, 0)
    (ssm_local, carry_dev, state_dev), main_pull = jax.vjp(
        partial(ssd_main, seg_local, seg_prev), mixed_in, dt_raw, dt_bias_loc, a_log_loc, d_skip_loc
    )
    identity = (jnp.ones_like(carry_dev), jnp.zeros_like(state_dev))
    entry_state = carried_in((carry_dev, state_dev), "seq", chain_states, identity, False)[1]
    ssm_entry, state_pull = jax.vjp(
        partial(ssd_state, seg_local, seg_prev),
        mixed_in,
        dt_raw,
        dt_bias_loc,
        a_log_loc,
        entry_state,
    )
    ssm_out = ssm_local + ssm_entry
    gated_f, gate_pull = jax.vjp(
        group_gate, ssm_out, gate_z.reshape(size_rows, heads_local, HP), group_loc
    )
    gated = gated_f.reshape(size_rows, width_x).astype(jnp.bfloat16)
    mamba_part = mat_dot(gated, full_mo)
    positions = row_start + jnp.arange(size_rows)
    heads_q = full_q.shape[1] // HD
    heads_kv = full_k.shape[1] // HD
    groups = heads_q // heads_kv
    query_rot, query_pull = jax.vjp(
        partial(rotate, positions), mat_dot(normed, full_q).reshape(size_rows, heads_q, HD)
    )
    queries = query_rot.astype(jnp.bfloat16).reshape(size_rows, heads_kv, groups, HD)
    key_rot, key_pull = jax.vjp(
        partial(rotate, positions), mat_dot(normed, full_k).reshape(size_rows, heads_kv, HD)
    )
    keys_local = key_rot.astype(jnp.bfloat16).reshape(size_rows, heads_kv * HD)
    vals_local = mat_dot(normed, full_v).astype(jnp.bfloat16)
    keys_all, vals_all = (
        lax.all_gather(keys_local, "seq", axis=0, tiled=True),
        lax.all_gather(vals_local, "seq", axis=0, tiled=True),
    )
    keys_all = keys_all.reshape(full_length, heads_kv, HD)
    vals_all = vals_all.reshape(full_length, heads_kv, HD)
    block_count = seq_count // 4
    log_total, attended_f = attend_forward(
        queries, keys_all, vals_all, seg_full, positions, seg_local, block_count
    )
    attended = attended_f.reshape(size_rows, heads_q * HD).astype(jnp.bfloat16)
    branch = lax.psum(mamba_part + mat_dot(attended, full_ao), "tensor")
    middle = hidden + branch
    normed_two_f, norm_two_pull = jax.vjp(rms_norm, middle, gain_two.astype(jnp.float32))
    normed_two = normed_two_f.astype(jnp.bfloat16)
    act_f, glu_pull = jax.vjp(swiglu, mat_dot(normed_two, full_gate), mat_dot(normed_two, full_up))
    activated = act_f.astype(jnp.bfloat16)
    block_out = middle + lax.psum(mat_dot(activated, full_down), "tensor")
    (
        back_z,
        back_x,
        back_dt,
        back_mo,
        back_q,
        back_k,
        back_v,
        back_ao,
        back_gate,
        back_up,
        back_down,
    ) = (
        lax.all_gather(w_z, ("dp", "seq"), axis=0, tiled=True),
        lax.all_gather(w_x, ("dp", "seq"), axis=0, tiled=True),
        lax.all_gather(w_dt, ("dp", "seq"), axis=0, tiled=True),
        lax.all_gather(w_mamba_out, ("dp", "seq"), axis=1, tiled=True),
        lax.all_gather(w_query, ("dp", "seq"), axis=0, tiled=True),
        lax.all_gather(w_key, ("dp", "seq"), axis=0, tiled=True),
        lax.all_gather(w_value, ("dp", "seq"), axis=0, tiled=True),
        lax.all_gather(w_attn_out, ("dp", "seq"), axis=1, tiled=True),
        lax.all_gather(w_gate, ("dp", "seq"), axis=0, tiled=True),
        lax.all_gather(w_up, ("dp", "seq"), axis=0, tiled=True),
        lax.all_gather(w_down, ("dp", "seq"), axis=1, tiled=True),
    )
    d_out = (
        2.0
        * total_tokens
        / token_count
        * mask_rows[:, None]
        * (block_out - teacher[0].astype(jnp.float32))
    )
    d_mlp = d_out.astype(jnp.bfloat16)
    grad_down = dot_left_t(activated, d_mlp)
    d_gate_f, d_up_f = glu_pull(dot_right_t(d_mlp, back_down))
    d_gate = d_gate_f.astype(jnp.bfloat16)
    d_up = d_up_f.astype(jnp.bfloat16)
    grad_gate = dot_left_t(normed_two, d_gate)
    grad_up = dot_left_t(normed_two, d_up)
    d_normed_two = lax.psum(dot_right_t(d_gate, back_gate) + dot_right_t(d_up, back_up), "tensor")
    d_middle_n, grad_gain_two = norm_two_pull(d_normed_two)
    d_middle = d_out + d_middle_n
    d_branch = d_middle.astype(jnp.bfloat16)
    grad_ao = dot_left_t(attended, d_branch)
    grad_mo = dot_left_t(gated, d_branch)
    d_attended = (
        dot_right_t(d_branch, back_ao).astype(jnp.bfloat16).reshape(size_rows, heads_kv, groups, HD)
    )
    d_gated = dot_right_t(d_branch, back_mo).reshape(size_rows, heads_local, HP)
    d_ssm, d_gate_z_f, grad_group = gate_pull(d_gated)
    d_gate_z = d_gate_z_f.reshape(size_rows, width_x).astype(jnp.bfloat16)
    d_mixed_s, d_dt_s, d_dtb_s, d_alog_s, d_entry = state_pull(d_ssm)
    state_grad = carried_in((carry_dev, d_entry), "seq", chain_states, identity, True)[1]
    d_carry = jnp.sum(state_grad * entry_state, axis=(1, 2))
    d_mixed_m, d_dt_m, d_dtb_m, d_alog_m, grad_skip = main_pull((d_ssm, d_carry, state_grad))
    d_dt_raw = (d_dt_s + d_dt_m).astype(jnp.bfloat16)
    d_ext, grad_conv_loc, grad_bias_loc = conv_pull(d_mixed_s + d_mixed_m)
    rim_grad = shifted(d_ext[: KC - 1], "seq", -1)
    d_pre = d_ext[KC - 1 :] + jnp.pad(rim_grad, ((size_rows - (KC - 1), 0), (0, 0)))
    d_pre_x = d_pre[:, :width_x].astype(jnp.bfloat16)
    d_pre_bc = d_pre[:, width_x:]
    grad_query_rot, key_grads_all, val_grads_all = attend_backward(
        queries,
        keys_all,
        vals_all,
        seg_full,
        positions,
        seg_local,
        block_count,
        d_attended,
        log_total,
    )
    key_grad, val_grad = (
        lax.psum_scatter(
            key_grads_all.reshape(full_length, heads_kv * HD).astype(jnp.bfloat16),
            "seq",
            scatter_dimension=0,
            tiled=True,
        ).astype(jnp.float32),
        lax.psum_scatter(
            val_grads_all.reshape(full_length, heads_kv * HD).astype(jnp.bfloat16),
            "seq",
            scatter_dimension=0,
            tiled=True,
        ).astype(jnp.float32),
    )
    d_query = (
        query_pull(grad_query_rot.reshape(size_rows, heads_q, HD))[0]
        .reshape(size_rows, heads_q * HD)
        .astype(jnp.bfloat16)
    )
    d_key = (
        key_pull(key_grad.reshape(size_rows, heads_kv, HD))[0]
        .reshape(size_rows, heads_kv * HD)
        .astype(jnp.bfloat16)
    )
    d_value = val_grad.astype(jnp.bfloat16)
    grad_z = dot_left_t(normed, d_gate_z)
    grad_x = dot_left_t(normed, d_pre_x)
    grad_dt = dot_left_t(normed, d_dt_raw)
    grad_q = dot_left_t(normed, d_query)
    grad_k = dot_left_t(normed, d_key)
    grad_v = dot_left_t(normed, d_value)
    normed_wide = normed.astype(jnp.float32)
    bc_weight = w_bc.astype(jnp.float32)
    grad_bc = jnp.dot(
        normed_wide.T, d_pre_bc, precision=HIGHEST, preferred_element_type=jnp.float32
    )
    d_normed_part = (
        dot_right_t(d_gate_z, back_z)
        + dot_right_t(d_pre_x, back_x)
        + dot_right_t(d_dt_raw, back_dt)
        + dot_right_t(d_query, back_q)
        + dot_right_t(d_key, back_k)
        + dot_right_t(d_value, back_v)
        + jnp.dot(d_pre_bc, bc_weight.T, precision=HIGHEST, preferred_element_type=jnp.float32)
    )
    d_normed = lax.psum(d_normed_part.astype(jnp.bfloat16), "tensor").astype(jnp.float32)
    d_hidden_n, grad_gain_one = norm_one_pull(d_normed)
    grad_input = d_middle + d_hidden_n
    conv_x_full = lax.dynamic_update_slice_in_dim(
        jnp.zeros((MH * HP, KC), jnp.float32), grad_conv_loc[:width_x], head_start * HP, 0
    )
    grad_conv_full = jnp.concatenate([conv_x_full, grad_conv_loc[width_x:]], axis=0)
    bias_x_full = lax.dynamic_update_slice_in_dim(
        jnp.zeros((MH * HP,), jnp.float32), grad_bias_loc[:width_x], head_start * HP, 0
    )
    grad_bias_full = jnp.concatenate([bias_x_full, grad_bias_loc[width_x:]], axis=0)
    grad_dtb_full = lax.dynamic_update_slice_in_dim(
        jnp.zeros((MH,), jnp.float32), d_dtb_s + d_dtb_m, head_start, 0
    )
    grad_alog_full = lax.dynamic_update_slice_in_dim(
        jnp.zeros((MH,), jnp.float32), d_alog_s + d_alog_m, head_start, 0
    )
    grad_skip_full = lax.dynamic_update_slice_in_dim(
        jnp.zeros((MH,), jnp.float32), grad_skip, head_start, 0
    )
    grad_group_full = lax.dynamic_update_slice_in_dim(
        jnp.zeros((MH, HP), jnp.float32), grad_group, head_start, 0
    )
    sum_bc, sum_conv, sum_bias, sum_dtb, sum_alog, sum_skip, sum_group = lax.psum(
        (
            grad_bc,
            grad_conv_full,
            grad_bias_full,
            grad_dtb_full,
            grad_alog_full,
            grad_skip_full,
            grad_group_full,
        ),
        ("dp", "seq", "tensor"),
    )
    (
        out_gain_one,
        out_z,
        out_x,
        out_dt,
        out_mo,
        out_q,
        out_k,
        out_v,
        out_ao,
        out_gain_two,
        out_gate,
        out_up,
        out_down,
    ) = (
        lax.psum_scatter(grad_gain_one, ("dp", "seq"), scatter_dimension=0, tiled=True),
        lax.psum_scatter(grad_z, ("dp", "seq"), scatter_dimension=0, tiled=True),
        lax.psum_scatter(grad_x, ("dp", "seq"), scatter_dimension=0, tiled=True),
        lax.psum_scatter(grad_dt, ("dp", "seq"), scatter_dimension=0, tiled=True),
        lax.psum_scatter(grad_mo, ("dp", "seq"), scatter_dimension=1, tiled=True),
        lax.psum_scatter(grad_q, ("dp", "seq"), scatter_dimension=0, tiled=True),
        lax.psum_scatter(grad_k, ("dp", "seq"), scatter_dimension=0, tiled=True),
        lax.psum_scatter(grad_v, ("dp", "seq"), scatter_dimension=0, tiled=True),
        lax.psum_scatter(grad_ao, ("dp", "seq"), scatter_dimension=1, tiled=True),
        lax.psum_scatter(grad_gain_two, ("dp", "seq"), scatter_dimension=0, tiled=True),
        lax.psum_scatter(grad_gate, ("dp", "seq"), scatter_dimension=0, tiled=True),
        lax.psum_scatter(grad_up, ("dp", "seq"), scatter_dimension=0, tiled=True),
        lax.psum_scatter(grad_down, ("dp", "seq"), scatter_dimension=1, tiled=True),
    )
    return (
        block_out.astype(jnp.bfloat16)[None],
        grad_input[None],
        out_gain_one,
        out_z,
        out_x,
        sum_bc,
        out_dt,
        sum_conv,
        sum_bias,
        sum_dtb,
        sum_alog,
        sum_skip,
        sum_group,
        out_mo,
        out_q,
        out_k,
        out_v,
        out_ao,
        out_gain_two,
        out_gate,
        out_up,
        out_down,
    )


GROUP = 4
CHUNK = 128
HEADS = 6
MESH_ID = pl.DeviceIdType.MESH
VMEM_BYTES = 56 * 1024 * 1024


def dot_f32(left_side, right_side, left_dim, right_dim):
    return lax.dot_general(
        left_side,
        right_side,
        (((left_dim,), (right_dim,)), ((), ())),
        preferred_element_type=jnp.float32,
    )


def halves(values):
    high = values.astype(jnp.bfloat16)
    return (high, (values - high.astype(jnp.float32)).astype(jnp.bfloat16))


def dot_split(exact, parts, left_dim, right_dim):
    high, low = parts
    return dot_f32(exact, high, left_dim, right_dim) + dot_f32(exact, low, left_dim, right_dim)


def dot_split_left(parts, exact, left_dim, right_dim):
    high, low = parts
    return dot_f32(high, exact, left_dim, right_dim) + dot_f32(low, exact, left_dim, right_dim)


def dot_splits(left_parts, right_parts, left_dim, right_dim):
    left_high, left_low = left_parts
    right_high, right_low = right_parts
    return dot_f32(left_high, right_high, left_dim, right_dim) + (
        dot_f32(left_high, right_low, left_dim, right_dim)
        + dot_f32(left_low, right_high, left_dim, right_dim)
    )


def plane_place():
    data, place, core = lax.axis_index("dp"), lax.axis_index("seq"), lax.axis_index("tensor")
    along_x = place + 1 - 2 * lax.rem(place, 2)
    along_y = lax.rem(place + 2, GROUP)
    across = GROUP - 1 - place
    return (data, place, core, along_x, along_y, across)


def meet(devices):
    barrier = pltpu.get_barrier_semaphore()
    for device in devices:
        pl.semaphore_signal(barrier, inc=1, device_id=device, device_id_type=MESH_ID)
    pl.semaphore_wait(barrier, len(devices))


def remote(source, target, send_sem, recv_sem, device):
    return pltpu.make_async_remote_copy(
        src_ref=source,
        dst_ref=target,
        send_sem=send_sem,
        recv_sem=recv_sem,
        device_id=device,
        device_id_type=MESH_ID,
    )


def any_specs(count):
    return [pl.BlockSpec(memory_space=pl.ANY)] * count


def vmem_specs(count):
    return [pl.BlockSpec(memory_space=pltpu.VMEM)] * count


def gather_kernel(own_ref, all_ref, local_sem, send_sems, recv_sems):
    data, place, core, along_x, along_y, across = plane_place()
    half = own_ref.shape[0] // 2
    to_x, to_y, partner = (data, along_x, core), (data, along_y, core), (data, place, 1 - core)

    def block(chip, part):
        return all_ref.at[2 * chip + core, pl.ds(part * half, half)]

    meet((to_x, to_y, partner))
    own = pltpu.make_async_copy(own_ref, all_ref.at[2 * place + core], local_sem)
    own.start()

    def push(index, source, target, device):
        copy = remote(source, target, send_sems.at[index], recv_sems.at[index], device)
        copy.start()
        return copy

    first, second = own_ref.at[pl.ds(0, half)], own_ref.at[pl.ds(half, half)]
    x_first = push(0, first, block(place, 0), to_x)
    y_second = push(1, second, block(place, 1), to_y)
    x_second = push(2, second, block(place, 1), to_x)
    y_first = push(3, first, block(place, 0), to_y)
    pair_own = push(4, own_ref, all_ref.at[2 * place + core], partner)
    x_first.wait_recv()
    over_y = push(5, block(along_x, 0), block(along_x, 0), to_y)
    y_second.wait_recv()
    over_x = push(6, block(along_y, 1), block(along_y, 1), to_x)
    x_second.wait_recv()
    mine_x = all_ref.at[2 * along_x + core]
    pair_x = push(7, mine_x, mine_x, partner)
    y_first.wait_recv()
    mine_y = all_ref.at[2 * along_y + core]
    pair_y = push(8, mine_y, mine_y, partner)
    over_y.wait_recv()
    pair_a = push(9, block(across, 0), block(across, 0), partner)
    over_x.wait_recv()
    pair_b = push(10, block(across, 1), block(across, 1), partner)
    own.wait()
    for copy in (pair_own, pair_x, pair_y, pair_a, pair_b):
        copy.wait_recv()
    for copy in (
        x_first,
        y_second,
        x_second,
        y_first,
        pair_own,
        over_y,
        over_x,
        pair_x,
        pair_y,
        pair_a,
        pair_b,
    ):
        copy.wait_send()


def gather_plane(own):
    rows, width = own.shape
    gathered = pl.pallas_call(
        gather_kernel,
        out_shape=jax.ShapeDtypeStruct((2 * GROUP, rows, width), own.dtype),
        in_specs=any_specs(1),
        out_specs=any_specs(1)[0],
        scratch_shapes=[
            pltpu.SemaphoreType.DMA,
            pltpu.SemaphoreType.DMA((11,)),
            pltpu.SemaphoreType.DMA((11,)),
        ],
        compiler_params=pltpu.CompilerParams(collective_id=1, has_side_effects=True),
    )(own)
    return gathered.reshape(2 * GROUP * rows, width)


def scatter_kernel(part_ref, sum_ref, pair_in, outgoing, arrived, pair_s, pair_r, send_s, recv_s):
    data, place, core, along_x, along_y, across = plane_place()
    partner = (data, place, 1 - core)
    others = (across, along_x, along_y)
    step = 16
    laps = part_ref.shape[1] // step
    meet([partner] + [(data, chip, core) for chip in others])
    pair = []
    for index, chip in enumerate(others + (place,)):
        copy = remote(
            part_ref.at[2 * chip + 1 - core],
            pair_in.at[index],
            pair_s.at[index],
            pair_r.at[index],
            partner,
        )
        copy.start()
        pair.append(copy)
    sends = []
    for index, chip in enumerate(others):
        pair[index].wait_recv()

        def add_pair(lap, carry, index=index, chip=chip):
            rows = pl.ds(lap * step, step)
            outgoing[index, rows] = (
                part_ref[2 * chip + core, rows].astype(jnp.float32)
                + pair_in[index, rows].astype(jnp.float32)
            ).astype(jnp.bfloat16)
            return carry

        lax.fori_loop(0, laps, add_pair, 0)
        copy = remote(
            outgoing.at[index],
            arrived.at[index],
            send_s.at[index],
            recv_s.at[index],
            (data, chip, core),
        )
        copy.start()
        sends.append(copy)
    pair[3].wait_recv()
    for copy in sends:
        copy.wait_recv()

    def add_all(lap, carry):
        rows = pl.ds(lap * step, step)
        total = part_ref[2 * place + core, rows].astype(jnp.float32)
        total = total + pair_in[3, rows].astype(jnp.float32)
        for index in range(3):
            total = total + arrived[index, rows].astype(jnp.float32)
        sum_ref[rows] = total
        return carry

    lax.fori_loop(0, laps, add_all, 0)
    for copy in pair + sends:
        copy.wait_send()


def scatter_plane(part):
    rows, width = part.shape[0] // (2 * GROUP), part.shape[1]
    return pl.pallas_call(
        scatter_kernel,
        out_shape=jax.ShapeDtypeStruct((rows, width), jnp.float32),
        in_specs=vmem_specs(1),
        out_specs=vmem_specs(1)[0],
        scratch_shapes=[
            pltpu.VMEM((4, rows, width), jnp.bfloat16),
            pltpu.VMEM((3, rows, width), jnp.bfloat16),
            pltpu.VMEM((3, rows, width), jnp.bfloat16),
            pltpu.SemaphoreType.DMA((4,)),
            pltpu.SemaphoreType.DMA((4,)),
            pltpu.SemaphoreType.DMA((3,)),
            pltpu.SemaphoreType.DMA((3,)),
        ],
        compiler_params=pltpu.CompilerParams(
            collective_id=2, has_side_effects=True, vmem_limit_bytes=VMEM_BYTES
        ),
    )(part.reshape(2 * GROUP, rows, width))


def exchange_kernel(moves, count_in, *refs):
    data, place, core, along_x, along_y, across = plane_place()
    sources, targets = refs[:count_in], refs[count_in:-3]
    local_sems, send_sems, recv_sems = refs[-3:]
    others = (across, along_x, along_y)
    meet([(data, chip, core) for chip in others])
    copies = []
    for index, chip in enumerate(others):
        for at, move in enumerate(moves):
            source, target = move(sources, targets, place, chip)
            copy = remote(
                source,
                target,
                send_sems.at[index, at],
                recv_sems.at[index, at],
                (data, chip, core),
            )
            copy.start()
            copies.append(copy)
    own = []
    for at, move in enumerate(moves):
        source, target = move(sources, targets, place, place)
        copy = pltpu.make_async_copy(source, target, local_sems.at[at])
        copy.start()
        own.append(copy)
    for copy in own:
        copy.wait()
    for copy in copies:
        copy.wait()


def exchange_plane(moves, arrays, out_shapes, identity):
    shapes = tuple(jax.ShapeDtypeStruct(shape, jnp.bfloat16) for shape in out_shapes)
    return pl.pallas_call(
        partial(exchange_kernel, moves, len(arrays)),
        out_shape=shapes,
        in_specs=any_specs(len(arrays)),
        out_specs=any_specs(len(shapes)),
        scratch_shapes=[
            pltpu.SemaphoreType.DMA((len(moves),)),
            pltpu.SemaphoreType.DMA((3, len(moves))),
            pltpu.SemaphoreType.DMA((3, len(moves))),
        ],
        compiler_params=pltpu.CompilerParams(collective_id=identity, has_side_effects=True),
    )(*arrays)


def column_move(source, target, start, width):
    def move(sources, targets, place, chip):
        columns = pl.ds(pl.multiple_of(chip * width, 128), width)
        return (
            sources[source].at[:, columns],
            targets[target].at[place, :, pl.ds(start, width)],
        )

    return move


def row_move(source, target, start, height):
    def move(sources, targets, place, chip):
        rows = pl.ds(pl.multiple_of(chip * height, 16), height)
        return (
            sources[source].at[rows],
            targets[target].at[place, pl.ds(start, height)],
        )

    return move


def block_move(source, target):
    def move(sources, targets, place, chip):
        return (sources[source].at[chip], targets[target].at[place])

    return move


def misc_move(source, target, start):
    def move(sources, targets, place, chip):
        return (
            sources[source].at[chip],
            targets[target].at[place, :, pl.ds(start, 128)],
        )

    return move


def lane_masks():
    lane = lax.broadcasted_iota(jnp.int32, (1, 2 * HP), 1)
    return (lane < HP, lane >= HP)


def pair_columns(ref, pair):
    low, high = lane_masks()
    return jnp.where(low, ref[:, 2 * pair : 2 * pair + 1], ref[:, 2 * pair + 1 : 2 * pair + 2])


def head_sums(values):
    low, high = lane_masks()
    first = jnp.sum(jnp.where(low, values, 0.0), axis=1, keepdims=True)
    second = jnp.sum(jnp.where(high, values, 0.0), axis=1, keepdims=True)
    return (first, second)


def head_means(values):
    low, high = lane_masks()
    first, second = head_sums(values)
    return jnp.where(low, first, second) * (1.0 / HP)


def stack_heads(values):
    low, high = lane_masks()
    zero = jnp.zeros_like(values)
    return jnp.concatenate([jnp.where(low, values, zero), jnp.where(high, values, zero)], axis=0)


def allowed_in(segc_ref, segr_ref):
    size = segc_ref.shape[0]
    row = lax.broadcasted_iota(jnp.int32, (size, size), 0)
    column = lax.broadcasted_iota(jnp.int32, (size, size), 1)
    return (segc_ref[...] == segr_ref[0]) & (row >= column)


def head_decay(allowed, cumc_ref, cumr_ref, head):
    differ = cumc_ref[:, head : head + 1] - cumr_ref[0, head : head + 1, :]
    return jnp.exp(jnp.where(allowed, differ, -jnp.inf))


def ssd_forward_kernel(
    x_ref,
    b_ref,
    c_ref,
    z_ref,
    dtr_ref,
    cumc_ref,
    cumr_ref,
    enter_ref,
    leave_ref,
    segc_ref,
    segr_ref,
    skip_ref,
    gain_ref,
    gated_ref,
    ssm_ref,
    states_ref,
    state,
):
    @pl.when(pl.program_id(0) == 0)
    def _():
        state[...] = jnp.zeros_like(state)

    size = x_ref.shape[0]
    entry = state[...]
    states_ref[0] = entry
    b_rows, c_rows = b_ref[...], c_ref[...]
    gram = dot_f32(c_rows, b_rows, 1, 1)
    allowed = allowed_in(segc_ref, segr_ref)
    entered = dot_split(c_rows, halves(entry), 1, 0)
    for pair in range(HEADS // 2):
        lanes = slice(2 * HP * pair, 2 * HP * (pair + 1))
        heads_x = x_ref[:, lanes]
        mixing = [
            gram * head_decay(allowed, cumc_ref, cumr_ref, head) * dtr_ref[0, head : head + 1, :]
            for head in (2 * pair, 2 * pair + 1)
        ]
        out = dot_split_left(
            halves(jnp.concatenate(mixing, axis=1)), stack_heads(heads_x), 1, 0
        )
        wide_x = heads_x.astype(jnp.float32)
        enter = pair_columns(enter_ref, pair)
        out = out + enter * entered[:, lanes] + skip_ref[:, lanes] * wide_x
        ssm_ref[:, lanes] = out
        gate = z_ref[:, lanes]
        value = out * (gate * jax.nn.sigmoid(gate))
        scale = lax.rsqrt(head_means(value * value) + GROUP_EPSILON)
        gated_ref[:, lanes] = (value * scale * gain_ref[:, lanes]).astype(jnp.bfloat16)
        weighted = halves(pair_columns(leave_ref, pair) * wide_x)
        state[:, lanes] = enter[size - 1 :, :] * entry[:, lanes] + dot_split(
            b_rows, weighted, 0, 0
        )


def ssd_backward_kernel(
    x_ref,
    b_ref,
    c_ref,
    z_ref,
    dtr_ref,
    cumc_ref,
    cumr_ref,
    enter_ref,
    leave_ref,
    segc_ref,
    segr_ref,
    skip_ref,
    gain_ref,
    ssm_ref,
    states_ref,
    dgated_ref,
    dx_ref,
    db_ref,
    dc_ref,
    dz_ref,
    rowsum_ref,
    dleave_ref,
    denter_ref,
    colsum_ref,
    carry_ref,
    dskip_ref,
    dgain_ref,
    state,
):
    @pl.when(pl.program_id(0) == 0)
    def _():
        state[...] = jnp.zeros_like(state)
        dskip_ref[...] = jnp.zeros_like(dskip_ref)
        dgain_ref[...] = jnp.zeros_like(dgain_ref)

    size = x_ref.shape[0]
    later = state[...]
    later_parts = halves(later)
    entry = states_ref[0]
    entry_parts = halves(entry)
    carry_ref[0] = jnp.sum(later * entry, axis=0, keepdims=True)
    b_rows, c_rows = b_ref[...], c_ref[...]
    gram = dot_f32(c_rows, b_rows, 1, 1)
    allowed = allowed_in(segc_ref, segr_ref)
    entered = dot_split(c_rows, entry_parts, 1, 0)
    d_weighted = dot_split(b_rows, later_parts, 1, 0)
    d_gram = jnp.zeros((size, size), jnp.float32)
    d_c = jnp.zeros(c_rows.shape, jnp.float32)
    d_b = jnp.zeros(b_rows.shape, jnp.float32)
    low, high = lane_masks()
    rowsum_ref[...] = jnp.zeros_like(rowsum_ref)
    dleave_ref[...] = jnp.zeros_like(dleave_ref)
    denter_ref[...] = jnp.zeros_like(denter_ref)
    colsum_ref[...] = jnp.zeros_like(colsum_ref)
    for pair in range(HEADS // 2):
        lanes = slice(2 * HP * pair, 2 * HP * (pair + 1))
        heads_x = x_ref[:, lanes]
        wide_x = heads_x.astype(jnp.float32)
        ssm, gate, gain = ssm_ref[:, lanes], z_ref[:, lanes], gain_ref[:, lanes]
        d_gated = dgated_ref[:, lanes]
        sigmoid = jax.nn.sigmoid(gate)
        silu = gate * sigmoid
        value = ssm * silu
        scale = lax.rsqrt(head_means(value * value) + GROUP_EPSILON)
        dgain_ref[:, lanes] += jnp.sum(d_gated * value * scale, axis=0, keepdims=True)
        d_scaled = d_gated * gain
        d_value = scale * d_scaled - value * (scale * scale * scale) * head_means(d_scaled * value)
        d_out = d_value * silu
        dz_ref[:, lanes] = (d_value * ssm * (sigmoid * (1.0 + gate * (1.0 - sigmoid)))).astype(
            jnp.bfloat16
        )
        dskip_ref[:, lanes] += jnp.sum(d_out * wide_x, axis=0, keepdims=True)
        enter, leave = pair_columns(enter_ref, pair), pair_columns(leave_ref, pair)
        d_out_parts = [stack_heads(half) for half in halves(d_out)]
        mixing = []
        for side in range(2):
            head = 2 * pair + side
            d_mixing = dot_split_left(
                [half[size * side : size * (side + 1)] for half in d_out_parts], heads_x, 1, 1
            )
            decay = head_decay(allowed, cumc_ref, cumr_ref, head)
            dt_row = dtr_ref[0, head : head + 1, :]
            weighted_gram = gram * decay
            mixing.append(weighted_gram * dt_row)
            d_gram = d_gram + d_mixing * (decay * dt_row)
            product = d_mixing * weighted_gram
            colsum_ref[0, head : head + 1, :] = jnp.sum(product, axis=0, keepdims=True)
            rowsum_ref[:, head : head + 1] = jnp.sum(product * dt_row, axis=1, keepdims=True)
        d_x = dot_splits(halves(jnp.concatenate(mixing, axis=0)), d_out_parts, 0, 0)
        first, second = head_sums(d_out * entered[:, lanes])
        denter_ref[:, 2 * pair : 2 * pair + 1] = first
        denter_ref[:, 2 * pair + 1 : 2 * pair + 2] = second
        first, second = head_sums(d_weighted[:, lanes] * wide_x)
        dleave_ref[:, 2 * pair : 2 * pair + 1] = first
        dleave_ref[:, 2 * pair + 1 : 2 * pair + 2] = second
        dx_ref[:, lanes] = d_x + skip_ref[:, lanes] * d_out + leave * d_weighted[:, lanes]
        d_entered = halves(enter * d_out)
        weighted = halves(leave * wide_x)
        d_c = d_c + dot_splits(d_entered, [half[:, lanes] for half in entry_parts], 1, 1)
        d_b = d_b + dot_splits(weighted, [half[:, lanes] for half in later_parts], 1, 1)
        state[:, lanes] = enter[size - 1 :, :] * later[:, lanes] + dot_split(
            c_rows, d_entered, 0, 0
        )
    d_gram_parts = halves(d_gram)
    dc_ref[...] = d_c + dot_split_left(d_gram_parts, b_rows, 1, 0)
    db_ref[...] = d_b + dot_split_left(d_gram_parts, c_rows, 0, 0)


def ssd_specs(length, reverse):
    laps = length // CHUNK

    def at(lap):
        return laps - 1 - lap if reverse else lap

    def tall(width):
        return pl.BlockSpec((CHUNK, width), lambda lap: (at(lap), 0))

    def flat(height):
        return pl.BlockSpec((1, height, CHUNK), lambda lap: (at(lap), 0, 0))

    def whole(width):
        return pl.BlockSpec((1, width), lambda lap: (0, 0))

    def slab(height, width):
        return pl.BlockSpec((1, height, width), lambda lap: (at(lap), 0, 0))

    return (laps, tall, flat, whole, slab)


def ssd_forward(arrays):
    length, width = arrays[0].shape
    laps, tall, flat, whole, slab = ssd_specs(length, False)
    return pl.pallas_call(
        ssd_forward_kernel,
        grid=(laps,),
        in_specs=[
            tall(width),
            tall(NS),
            tall(NS),
            tall(width),
            flat(8),
            tall(8),
            flat(8),
            tall(8),
            tall(8),
            tall(1),
            flat(1),
            whole(width),
            whole(width),
        ],
        out_specs=[tall(width), tall(width), slab(NS, width)],
        out_shape=[
            jax.ShapeDtypeStruct((length, width), jnp.bfloat16),
            jax.ShapeDtypeStruct((length, width), jnp.float32),
            jax.ShapeDtypeStruct((laps, NS, width), jnp.float32),
        ],
        scratch_shapes=[pltpu.VMEM((NS, width), jnp.float32)],
        compiler_params=pltpu.CompilerParams(vmem_limit_bytes=VMEM_BYTES),
    )(*arrays)


def ssd_backward(arrays, ssm, states, d_gated):
    length, width = arrays[0].shape
    laps, tall, flat, whole, slab = ssd_specs(length, True)
    shaped = jax.ShapeDtypeStruct
    return pl.pallas_call(
        ssd_backward_kernel,
        grid=(laps,),
        in_specs=[
            tall(width),
            tall(NS),
            tall(NS),
            tall(width),
            flat(8),
            tall(8),
            flat(8),
            tall(8),
            tall(8),
            tall(1),
            flat(1),
            whole(width),
            whole(width),
            tall(width),
            slab(NS, width),
            tall(width),
        ],
        out_specs=[
            tall(width),
            tall(NS),
            tall(NS),
            tall(width),
            tall(8),
            tall(8),
            tall(8),
            flat(8),
            slab(1, width),
            whole(width),
            whole(width),
        ],
        out_shape=[
            shaped((length, width), jnp.float32),
            shaped((length, NS), jnp.float32),
            shaped((length, NS), jnp.float32),
            shaped((length, width), jnp.bfloat16),
            shaped((length, 8), jnp.float32),
            shaped((length, 8), jnp.float32),
            shaped((length, 8), jnp.float32),
            shaped((laps, 8, CHUNK), jnp.float32),
            shaped((laps, 1, width), jnp.float32),
            shaped((1, width), jnp.float32),
            shaped((1, width), jnp.float32),
        ],
        scratch_shapes=[pltpu.VMEM((NS, width), jnp.float32)],
        compiler_params=pltpu.CompilerParams(vmem_limit_bytes=VMEM_BYTES),
    )(*arrays, ssm, states, d_gated)


QUERY_ROWS = 256


def masked_scores(q_rows, k_ref, segc_ref, segr_ref, start, reach):
    rows = q_rows.shape[0]
    scores = dot_f32(q_rows, k_ref[:reach], 1, 1) * HD ** (-0.5)
    row = lax.broadcasted_iota(jnp.int32, (rows, reach), 0) + start
    column = lax.broadcasted_iota(jnp.int32, (rows, reach), 1)
    allowed = (segc_ref[start : start + rows] == segr_ref[:, :reach]) & (row >= column)
    return jnp.where(allowed, scores, -jnp.inf)


def attend_forward_kernel(q_ref, k_ref, v_ref, segc_ref, segr_ref, out_ref, total_ref):
    for start in range(0, q_ref.shape[0], QUERY_ROWS):
        reach = start + QUERY_ROWS
        rows = slice(start, reach)
        scores = masked_scores(q_ref[rows], k_ref, segc_ref, segr_ref, start, reach)
        top = jnp.max(scores, axis=1, keepdims=True)
        powers = jnp.exp(scores - top)
        total = jnp.sum(powers, axis=1, keepdims=True)
        probs = (powers * (1.0 / total)).astype(jnp.bfloat16)
        out_ref[rows] = dot_f32(probs, v_ref[:reach], 1, 0).astype(jnp.bfloat16)
        total_ref[rows] = top + jnp.log(total)


def attend_backward_kernel(
    q_ref, k_ref, v_ref, segc_ref, segr_ref, total_ref, dout_ref, dq_ref, dk_ref, dv_ref
):
    dk_ref[...] = jnp.zeros_like(dk_ref)
    dv_ref[...] = jnp.zeros_like(dv_ref)
    for start in range(0, q_ref.shape[0], QUERY_ROWS):
        reach = start + QUERY_ROWS
        rows = slice(start, reach)
        q_rows, d_out = q_ref[rows], dout_ref[rows]
        scores = masked_scores(q_rows, k_ref, segc_ref, segr_ref, start, reach)
        probs = jnp.exp(scores - total_ref[rows])
        d_probs = dot_f32(d_out, v_ref[:reach], 1, 1)
        delta = jnp.sum(probs * d_probs, axis=1, keepdims=True)
        d_scores = (probs * (d_probs - delta)).astype(jnp.bfloat16)
        dq_ref[rows] = dot_f32(d_scores, k_ref[:reach], 1, 0) * HD ** (-0.5)
        dk_ref[:reach] += dot_f32(d_scores, q_rows, 0, 0) * HD ** (-0.5)
        dv_ref[:reach] += dot_f32(probs.astype(jnp.bfloat16), d_out, 0, 0)


def attend(kernel, arrays, out_shapes):
    return pl.pallas_call(
        kernel,
        in_specs=vmem_specs(len(arrays)),
        out_specs=vmem_specs(len(out_shapes)),
        out_shape=[jax.ShapeDtypeStruct(shape, dtype) for shape, dtype in out_shapes],
        compiler_params=pltpu.CompilerParams(vmem_limit_bytes=VMEM_BYTES),
    )(*arrays)


def turn(cosine, sine_part, first_half, second):
    return (
        first_half * cosine - second * sine_part,
        second * cosine + first_half * sine_part,
    )


def over_chips(block):
    place = lax.axis_index("seq")
    count = lax.axis_size("seq")
    stacked = jnp.zeros((count,) + block.shape, block.dtype)
    stacked = lax.dynamic_update_index_in_dim(stacked, block, place, 0)
    for mask in range(1, count):
        moved = lax.ppermute(block, "seq", [(i, i ^ mask) for i in range(count)])
        stacked = lax.dynamic_update_index_in_dim(stacked, moved, place ^ mask, 0)
    return stacked


def sum_from_chips(blocks):
    place = lax.axis_index("seq")
    count = lax.axis_size("seq")
    total = lax.dynamic_index_in_dim(blocks, place, 0, False).astype(jnp.float32)
    for mask in range(1, count):
        block = lax.dynamic_index_in_dim(blocks, place ^ mask, 0, False)
        moved = lax.ppermute(block, "seq", [(i, i ^ mask) for i in range(count)])
        total = total + moved.astype(jnp.float32)
    return total


def both_cores(block):
    core = lax.axis_index("tensor")
    other = lax.ppermute(block, "tensor", [(0, 1), (1, 0)])
    return jnp.where(
        core == 0,
        jnp.concatenate([block, other], axis=0),
        jnp.concatenate([other, block], axis=0),
    )


def heads_local_plan(
    hidden_in,
    teacher,
    segment_ids,
    valid_mask,
    norm1_gain,
    w_z,
    w_x,
    w_bc,
    w_dt,
    conv_weight,
    conv_bias,
    dt_bias,
    a_log,
    d_skip,
    group_gain,
    w_mamba_out,
    w_query,
    w_key,
    w_value,
    w_attn_out,
    norm2_gain,
    w_gate,
    w_up,
    w_down,
):
    place, core, data_rank = (
        lax.axis_index("seq"),
        lax.axis_index("tensor"),
        lax.axis_index("dp"),
    )
    data_count = lax.axis_size("dp")
    chip_rows, width = hidden_in.shape[1:]
    own_rows = chip_rows // 2
    length = segment_ids.shape[1]
    slice_rows = w_z.shape[0]
    width_x = HEADS * HP
    hidden_units = w_gate.shape[1] // GROUP
    segment = segment_ids[0]
    seg_column, seg_row = segment[:, None], segment[None, :]
    own_start = place * chip_rows + core * own_rows
    token_count = jnp.sum(valid_mask).astype(jnp.float32)
    mask_rows = lax.dynamic_slice(valid_mask, (data_rank, own_start), (1, own_rows))[0]
    total_tokens = float(valid_mask.shape[0] * valid_mask.shape[1])
    bf16 = jnp.bfloat16

    quarter = HD // (2 * GROUP)
    misc = jnp.stack(
        [
            jnp.concatenate(
                [
                    w_key[:, quarter * chip : quarter * (chip + 1)],
                    w_key[:, HD // 2 + quarter * chip : HD // 2 + quarter * (chip + 1)],
                    w_value[:, 2 * quarter * chip : 2 * quarter * (chip + 1)],
                    w_dt[:, HEADS * chip : HEADS * (chip + 1)],
                    norm1_gain[:, None],
                    norm2_gain[:, None],
                    jnp.zeros((slice_rows, 128 - 4 * quarter - HEADS - 2), bf16),
                ],
                axis=1,
            )
            for chip in range(GROUP)
        ]
    )
    width_in = 2 * width_x + HD + 128
    (in_slices,) = exchange_plane(
        (
            column_move(0, 0, 0, width_x),
            column_move(1, 0, width_x, width_x),
            column_move(2, 0, 2 * width_x, HD),
            misc_move(3, 0, 2 * width_x + HD),
        ),
        (w_z, w_x, w_query, misc),
        [(GROUP, slice_rows, width_in)],
        3,
    )
    full_in = lax.all_gather(in_slices, "dp", axis=0, tiled=True).reshape(width, width_in)
    hidden_own = lax.dynamic_slice(hidden_in[0], (core * own_rows, 0), (own_rows, width))
    hidden = gather_plane(hidden_own).astype(jnp.float32)
    hidden_own = hidden_own.astype(jnp.float32)
    out_rows = width_x + HD
    out_slices, gu_slices, down_slices = exchange_plane(
        (
            row_move(0, 0, 0, width_x),
            row_move(1, 0, width_x, HD),
            column_move(2, 1, 0, hidden_units),
            column_move(3, 1, hidden_units, hidden_units),
            row_move(4, 2, 0, hidden_units),
        ),
        (w_mamba_out, w_attn_out, w_gate, w_up, w_down),
        [
            (GROUP, out_rows, slice_rows),
            (GROUP, slice_rows, 2 * hidden_units),
            (GROUP, hidden_units, slice_rows),
        ],
        4,
    )
    full_out = (
        lax.all_gather(out_slices, "dp", axis=0, tiled=True)
        .transpose(1, 0, 2)
        .reshape(out_rows, width)
    )
    full_gu = lax.all_gather(gu_slices, "dp", axis=0, tiled=True).reshape(width, 2 * hidden_units)
    full_down = (
        lax.all_gather(down_slices, "dp", axis=0, tiled=True)
        .transpose(1, 0, 2)
        .reshape(hidden_units, width)
    )
    gain_column = 2 * width_x + HD + 4 * quarter + HEADS
    gain_one = full_in[:, gain_column].astype(jnp.float32)
    gain_two = full_in[:, gain_column + 1].astype(jnp.float32)

    scale_one = lax.rsqrt(jnp.mean(hidden * hidden, axis=-1, keepdims=True) + EPSILON)
    normed = (hidden * scale_one * gain_one).astype(bf16)
    projected = mat_dot(normed, full_in)
    gate_z = projected[:, :width_x]
    pre_all = jnp.concatenate(
        [projected[:, width_x : 2 * width_x].astype(bf16), mat_dot(normed, w_bc).astype(bf16)],
        axis=1,
    )
    dt_raw = projected[:, 2 * width_x + HD + 4 * quarter :][:, :HEADS]
    head_start = core * (MH // 2) + place * HEADS
    positions = jnp.arange(length)
    frequency = ROPE_BASE ** (-2.0 * jnp.arange(HD // 2).astype(jnp.float32) / HD)
    angles = positions.astype(jnp.float32)[:, None] * frequency[None, :]
    cosine, sine_part = jnp.cos(angles), jnp.sin(angles)
    cos_part = lax.dynamic_slice_in_dim(cosine, quarter * place, quarter, 1)
    sin_part = lax.dynamic_slice_in_dim(sine_part, quarter * place, quarter, 1)
    query_raw = projected[:, 2 * width_x : 2 * width_x + HD]
    queries = jnp.concatenate(
        turn(cosine, sine_part, query_raw[:, : HD // 2], query_raw[:, HD // 2 :]), axis=1
    ).astype(bf16)
    kv_raw = projected[:, 2 * width_x + HD :][:, : 4 * quarter]
    key_first, key_second = turn(
        cos_part, sin_part, kv_raw[:, :quarter], kv_raw[:, quarter : 2 * quarter]
    )
    kv_all = over_chips(
        jnp.concatenate([key_first, key_second, kv_raw[:, 2 * quarter :]], axis=1).astype(bf16)
    )
    keys = jnp.concatenate(
        [kv_all[chip, :, :quarter] for chip in range(GROUP)]
        + [kv_all[chip, :, quarter : 2 * quarter] for chip in range(GROUP)],
        axis=1,
    )
    vals = jnp.concatenate([kv_all[chip, :, 2 * quarter :] for chip in range(GROUP)], axis=1)

    seg_ext = jnp.concatenate([jnp.full((KC - 1,), -1, jnp.int32), segment])
    extended = jnp.concatenate(
        [jnp.zeros((KC - 1, pre_all.shape[1]), bf16), pre_all], axis=0
    ).astype(jnp.float32)
    conv_local = jnp.concatenate(
        [
            lax.dynamic_slice_in_dim(conv_weight, head_start * HP, width_x, 0),
            conv_weight[MH * HP :],
        ],
        axis=0,
    )
    bias_local = jnp.concatenate(
        [lax.dynamic_slice_in_dim(conv_bias, head_start * HP, width_x, 0), conv_bias[MH * HP :]],
        axis=0,
    )
    mixed_f, conv_pull = jax.vjp(
        partial(conv_silu, seg_ext, segment), extended, conv_local, bias_local
    )
    mixed = mixed_f.astype(bf16)
    heads_x, b_rows, c_rows = (
        mixed[:, :width_x],
        mixed[:, width_x : width_x + NS],
        mixed[:, width_x + NS :],
    )
    dt_bias_loc = lax.dynamic_slice_in_dim(dt_bias, head_start, HEADS)
    rate = jnp.exp(lax.dynamic_slice_in_dim(a_log, head_start, HEADS))
    skip_loc = lax.dynamic_slice_in_dim(d_skip, head_start, HEADS)
    gain_loc = lax.dynamic_slice_in_dim(group_gain, head_start, HEADS, 0).reshape(1, width_x)
    laps = length // CHUNK
    dt_rows = jax.nn.softplus(dt_raw + dt_bias_loc[None, :])
    dt_laps = dt_rows.reshape(laps, CHUNK, HEADS)
    seg_laps = segment.reshape(laps, CHUNK)
    seg_last = seg_laps[:, -1]
    seg_before = jnp.concatenate([jnp.full((1,), -1, jnp.int32), seg_last[:-1]])
    cumul = jnp.cumsum(-rate * dt_laps, axis=1)
    keep_enter = (seg_laps == seg_before[:, None]).astype(jnp.float32)[:, :, None]
    keep_leave = (seg_laps == seg_last[:, None]).astype(jnp.float32)[:, :, None]
    enter = jnp.exp(cumul) * keep_enter
    leave_bare = jnp.exp(cumul[:, -1:] - cumul) * keep_leave
    leave = leave_bare * dt_laps

    def tall(values):
        return jnp.pad(values, ((0, 0), (0, 0), (0, 8 - HEADS))).reshape(length, 8)

    def flat(values):
        return jnp.pad(values, ((0, 0), (0, 0), (0, 8 - HEADS))).transpose(0, 2, 1)

    ssd_arrays = (
        heads_x,
        b_rows,
        c_rows,
        gate_z,
        flat(dt_laps),
        tall(cumul),
        flat(cumul),
        tall(enter),
        tall(leave),
        seg_column,
        seg_laps[:, None, :],
        jnp.repeat(skip_loc, HP)[None, :],
        gain_loc,
    )
    gated, ssm, states = ssd_forward(ssd_arrays)
    attended, log_total = attend(
        attend_forward_kernel,
        (queries, keys, vals, seg_column, seg_row),
        (((length, HD), bf16), ((length, 1), jnp.float32)),
    )
    outs = jnp.concatenate([gated, attended], axis=1)
    middle = hidden_own + scatter_plane(mat_dot(outs, full_out).astype(bf16))

    scale_two = lax.rsqrt(jnp.mean(middle * middle, axis=-1, keepdims=True) + EPSILON)
    normed_two = gather_plane((middle * scale_two * gain_two).astype(bf16))
    gate_up = mat_dot(normed_two, full_gu)
    act_f, glu_pull = jax.vjp(swiglu, gate_up[:, :hidden_units], gate_up[:, hidden_units:])
    activated = act_f.astype(bf16)
    block_out = middle + scatter_plane(mat_dot(activated, full_down).astype(bf16))
    teacher_own = lax.dynamic_slice(teacher[0], (core * own_rows, 0), (own_rows, width))
    d_out = (
        2.0
        * total_tokens
        / token_count
        * mask_rows.astype(jnp.float32)[:, None]
        * (block_out - teacher_own.astype(jnp.float32))
    )
    d_mlp = gather_plane(d_out.astype(bf16))

    def sum_columns(grads):
        chunks = grads.astype(bf16).reshape(grads.shape[0], data_count * GROUP, slice_rows)
        return lax.psum_scatter(
            chunks.transpose(1, 0, 2), "dp", scatter_dimension=0, tiled=True
        )

    def sum_rows(grads):
        summed = lax.psum_scatter(grads.astype(bf16), "dp", scatter_dimension=0, tiled=True)
        return summed.reshape(GROUP, slice_rows, grads.shape[1])

    grad_down = sum_columns(dot_left_t(activated, d_mlp))
    d_gate, d_up = glu_pull(dot_right_t(d_mlp, full_down))
    d_gate_up = jnp.concatenate([d_gate.astype(bf16), d_up.astype(bf16)], axis=1)
    grad_gate_up = sum_rows(dot_left_t(normed_two, d_gate_up))
    d_normed_two = scatter_plane(dot_right_t(d_gate_up, full_gu).astype(bf16))
    grad_gain_two = jnp.sum(d_normed_two * middle * scale_two, axis=0)
    d_scaled = d_normed_two * gain_two
    d_middle = (
        d_out
        + scale_two * d_scaled
        - middle * scale_two**3 * jnp.mean(d_scaled * middle, axis=-1, keepdims=True)
    )
    d_branch = gather_plane(d_middle.astype(bf16))
    grad_out = sum_columns(dot_left_t(outs, d_branch))
    d_outs = dot_right_t(d_branch, full_out)
    d_query_rot, d_key_part, d_val_part = attend(
        attend_backward_kernel,
        (
            queries,
            keys,
            vals,
            seg_column,
            seg_row,
            log_total,
            d_outs[:, width_x:].astype(bf16),
        ),
        (((length, HD), jnp.float32),) * 3,
    )
    d_kv = sum_from_chips(
        jnp.stack(
            [
                jnp.concatenate(
                    [
                        d_key_part[:, quarter * chip : quarter * (chip + 1)],
                        d_key_part[:, HD // 2 + quarter * chip : HD // 2 + quarter * (chip + 1)],
                        d_val_part[:, 2 * quarter * chip : 2 * quarter * (chip + 1)],
                    ],
                    axis=1,
                ).astype(bf16)
                for chip in range(GROUP)
            ]
        )
    )
    d_query = jnp.concatenate(
        turn(cosine, -sine_part, d_query_rot[:, : HD // 2], d_query_rot[:, HD // 2 :]), axis=1
    )
    d_key_first, d_key_second = turn(
        cos_part, -sin_part, d_kv[:, :quarter], d_kv[:, quarter : 2 * quarter]
    )
    (
        d_heads_x,
        d_b_rows,
        d_c_rows,
        d_gate_z,
        row_sums,
        d_leave,
        d_enter,
        column_sums,
        d_carry,
        d_skip_lanes,
        d_gain_lanes,
    ) = ssd_backward(ssd_arrays, ssm, states, d_outs[:, :width_x])

    def untall(values):
        return values.reshape(laps, CHUNK, 8)[:, :, :HEADS]

    column_sums = column_sums.transpose(0, 2, 1)[:, :, :HEADS]
    d_leave, d_enter = untall(d_leave), untall(d_enter)
    d_left = d_leave * leave
    d_cumul = untall(row_sums) - column_sums * dt_laps + d_enter * enter - d_left
    d_carried = jnp.sum(d_carry.reshape(laps, HEADS, HP), axis=-1) * enter[:, -1]
    d_cumul = d_cumul.at[:, -1].add(jnp.sum(d_left, axis=1) + d_carried)
    d_log = lax.cumsum(d_cumul, axis=1, reverse=True)
    d_dt = column_sums + d_leave * leave_bare - rate * d_log
    d_dt_f = d_dt.reshape(length, HEADS) * jax.nn.sigmoid(dt_raw + dt_bias_loc[None, :])
    grad_dtb = jnp.sum(d_dt_f, axis=0)
    grad_alog = -rate * jnp.sum(d_log * dt_laps, axis=(0, 1))
    grad_skip = jnp.sum(d_skip_lanes.reshape(HEADS, HP), axis=-1)
    grad_group = d_gain_lanes.reshape(HEADS, HP)
    d_ext, grad_conv_loc, grad_bias_loc = conv_pull(
        jnp.concatenate([d_heads_x, d_b_rows, d_c_rows], axis=1)
    )
    d_pre = d_ext[KC - 1 :]
    d_pre_bc = d_pre[:, width_x:]
    d_projected = jnp.concatenate(
        [
            d_gate_z,
            d_pre[:, :width_x].astype(bf16),
            d_query.astype(bf16),
            d_key_first.astype(bf16),
            d_key_second.astype(bf16),
            d_kv[:, 2 * quarter :].astype(bf16),
            d_dt_f.astype(bf16),
            jnp.zeros((length, 128 - 4 * quarter - HEADS), bf16),
        ],
        axis=1,
    )
    d_normed_part = dot_right_t(d_projected, full_in) + dot_right_t(d_pre_bc.astype(bf16), w_bc)
    grad_in = sum_rows(dot_left_t(normed, d_projected))
    d_normed = scatter_plane(d_normed_part.astype(bf16))
    grad_gain_one = jnp.sum(d_normed * hidden_own * lax.rsqrt(jnp.mean(hidden_own * hidden_own, axis=-1, keepdims=True) + EPSILON), axis=0)
    scale_own = lax.rsqrt(jnp.mean(hidden_own * hidden_own, axis=-1, keepdims=True) + EPSILON)
    d_scaled_one = d_normed * gain_one
    grad_input = (
        d_middle
        + scale_own * d_scaled_one
        - hidden_own * scale_own**3 * jnp.mean(d_scaled_one * hidden_own, axis=-1, keepdims=True)
    )

    bc_cols = 2 * NS // (2 * GROUP)
    d_bc_parts = d_pre_bc.reshape(length, 2 * GROUP, bc_cols).transpose(1, 0, 2)
    d_bc = lax.psum_scatter(d_bc_parts, ("seq", "tensor"), scatter_dimension=0, tiled=True)[0]
    grad_bc = lax.psum_scatter(
        dot_left_t(normed, d_bc.astype(bf16)), "dp", scatter_dimension=0, tiled=True
    )
    grad_bc = lax.all_gather(grad_bc, "dp", axis=0, tiled=True)
    grad_bc = lax.all_gather(grad_bc, ("seq", "tensor"), axis=1, tiled=True)

    back_gu, back_down = exchange_plane(
        (block_move(0, 0), block_move(1, 1)),
        (grad_gate_up, grad_down),
        [grad_gate_up.shape, grad_down.shape],
        5,
    )
    back_in, back_out = exchange_plane(
        (block_move(0, 0), block_move(1, 1)),
        (grad_in, grad_out),
        [grad_in.shape, grad_out.shape],
        6,
    )

    def columns(back, start, size):
        return jnp.concatenate(
            [back[chip, :, start : start + size] for chip in range(GROUP)], axis=1
        ).astype(jnp.float32)

    def rows(back, start, size):
        return back[:, start : start + size].reshape(GROUP * size, slice_rows).astype(jnp.float32)

    start_kv = 2 * width_x + HD
    grad_key = jnp.concatenate(
        [columns(back_in, start_kv, quarter), columns(back_in, start_kv + quarter, quarter)], axis=1
    )

    def placed(values, rows_all, start):
        return lax.dynamic_update_slice_in_dim(
            jnp.zeros((rows_all,) + values.shape[1:], jnp.float32), values, start, 0
        )

    grad_conv = jnp.concatenate(
        [placed(grad_conv_loc[:width_x], MH * HP, head_start * HP), grad_conv_loc[width_x:]], axis=0
    )
    grad_bias = jnp.concatenate(
        [placed(grad_bias_loc[:width_x], MH * HP, head_start * HP), grad_bias_loc[width_x:]], axis=0
    )
    small = [
        grad_gain_one,
        grad_gain_two,
        grad_conv.reshape(-1),
        grad_bias,
        placed(grad_dtb, MH, head_start),
        placed(grad_alog, MH, head_start),
        placed(grad_skip, MH, head_start),
        placed(grad_group, MH, head_start).reshape(-1),
    ]
    sizes = [values.shape[0] for values in small]
    summed = lax.psum(jnp.concatenate(small), ("dp", "seq", "tensor"))
    parts = []
    start = 0
    for size in sizes:
        parts.append(summed[start : start + size])
        start += size
    sum_one, sum_two, sum_conv, sum_bias, sum_dtb, sum_alog, sum_skip, sum_group = parts
    gain_start = (data_rank * GROUP + place) * slice_rows
    return (
        both_cores(block_out.astype(bf16))[None],
        both_cores(grad_input)[None],
        lax.dynamic_slice_in_dim(sum_one, gain_start, slice_rows),
        columns(back_in, 0, width_x),
        columns(back_in, width_x, width_x),
        grad_bc,
        columns(back_in, start_kv + 4 * quarter, HEADS),
        sum_conv.reshape(conv_weight.shape),
        sum_bias,
        sum_dtb,
        sum_alog,
        sum_skip,
        sum_group.reshape(MH, HP),
        rows(back_out, 0, width_x),
        columns(back_in, 2 * width_x, HD),
        grad_key,
        columns(back_in, start_kv + 2 * quarter, 2 * quarter),
        rows(back_out, width_x, HD),
        lax.dynamic_slice_in_dim(sum_two, gain_start, slice_rows),
        columns(back_gu, 0, hidden_units),
        columns(back_gu, hidden_units, hidden_units),
        rows(back_down, 0, hidden_units),
    )


def solution(mesh):
    placed = (
        P("dp", "seq", None),
        P("dp", "seq", None),
        P("dp", None),
        P(),
        P(("dp", "seq")),
        P(("dp", "seq"), "tensor"),
        P(("dp", "seq"), "tensor"),
        P(),
        P(("dp", "seq"), "tensor"),
        P(),
        P(),
        P(),
        P(),
        P(),
        P(),
        P("tensor", ("dp", "seq")),
        P(("dp", "seq"), "tensor"),
        P(("dp", "seq"), "tensor"),
        P(("dp", "seq"), "tensor"),
        P("tensor", ("dp", "seq")),
        P(("dp", "seq")),
        P(("dp", "seq"), "tensor"),
        P(("dp", "seq"), "tensor"),
        P("tensor", ("dp", "seq")),
    )
    whole_row = mesh.shape["seq"] == GROUP and mesh.shape["tensor"] == 2
    return jax.shard_map(
        heads_local_plan if whole_row else local,
        mesh=mesh,
        in_specs=placed,
        out_specs=(
            P("dp", "seq", None),
            P("dp", "seq", None),
            P(("dp", "seq")),
            P(("dp", "seq"), "tensor"),
            P(("dp", "seq"), "tensor"),
            P(),
            P(("dp", "seq"), "tensor"),
            P(),
            P(),
            P(),
            P(),
            P(),
            P(),
            P("tensor", ("dp", "seq")),
            P(("dp", "seq"), "tensor"),
            P(("dp", "seq"), "tensor"),
            P(("dp", "seq"), "tensor"),
            P("tensor", ("dp", "seq")),
            P(("dp", "seq")),
            P(("dp", "seq"), "tensor"),
            P(("dp", "seq"), "tensor"),
            P("tensor", ("dp", "seq")),
        ),
        check_vma=False,
    )
```

```python
from functools import partial

import jax
import jax.numpy as jnp
from jax import lax
from jax.experimental import pallas as pl
from jax.experimental.pallas import tpu as pltpu
from jax.sharding import PartitionSpec as P

MH = 48
HP = 64
NS = 256
KC = 4
HD = 128


EPSILON = 1e-06
GROUP_EPSILON = 1e-05
ROPE_BASE = 10000.0
HIGHEST = lax.Precision.HIGHEST


def shifted(block, axis, distance):
    devices = range(lax.axis_size(axis))
    route = [(i - distance, i) for i in devices if i - distance in devices]
    return lax.ppermute(block, axis, route)


def carried_in(part, axis, combine, identity, reverse):
    count = lax.axis_size(axis)
    place = lax.axis_index(axis)
    ahead = count - 1 - place if reverse else place
    gathered = jax.tree.map(lambda a: lax.all_gather(a, axis), part)
    state = jax.tree.map(lambda a, e: jnp.zeros_like(a) + jnp.asarray(e, a.dtype), part, identity)

    def one(lap, state):
        source = count - 1 - lap if reverse else lap
        return combine(
            state, jax.tree.map(lambda a: lax.dynamic_index_in_dim(a, source, 0, False), gathered)
        )

    return lax.fori_loop(0, ahead, one, state)


def mat_dot(left_side, right_side):
    return jnp.dot(left_side, right_side, preferred_element_type=jnp.float32)


def dot_left_t(left_side, right_side):
    return lax.dot_general(
        left_side, right_side, (((0,), (0,)), ((), ())), preferred_element_type=jnp.float32
    )


def dot_right_t(left_side, right_side):
    return lax.dot_general(
        left_side, right_side, (((1,), (1,)), ((), ())), preferred_element_type=jnp.float32
    )


def rms_norm(values, gain_row):
    scale_row = lax.rsqrt(jnp.mean(values * values, axis=-1, keepdims=True) + EPSILON)
    return values * scale_row * gain_row


def rotate(positions, values):
    half_dim = values.shape[-1] // 2
    frequency = ROPE_BASE ** (-2.0 * jnp.arange(half_dim).astype(jnp.float32) / values.shape[-1])
    angles = positions.astype(jnp.float32)[:, None] * frequency[None, :]
    cosine = jnp.cos(angles)[:, None, :]
    sine_part = jnp.sin(angles)[:, None, :]
    first_half = values[..., :half_dim]
    second = values[..., half_dim:]
    return jnp.concatenate(
        [first_half * cosine - second * sine_part, second * cosine + first_half * sine_part],
        axis=-1,
    )


def conv_silu(seg_ext, seg_rows, extended, weights, bias_row):
    size_rows = seg_rows.shape[0]
    summed = jnp.zeros((size_rows, weights.shape[0]), jnp.float32) + bias_row[None, :]
    for tap_index in range(weights.shape[1]):
        window = lax.slice_in_dim(extended, tap_index, tap_index + size_rows, axis=0)
        keep_mask = (
            lax.slice_in_dim(seg_ext, tap_index, tap_index + size_rows) == seg_rows
        ).astype(jnp.float32)
        summed = summed + window * weights[:, tap_index][None, :] * keep_mask[:, None]
    return jax.nn.silu(summed)


def group_gate(ssm_out, gate_z, group_gain):
    mixed_val = ssm_out * jax.nn.silu(gate_z)
    return (
        mixed_val
        * lax.rsqrt(jnp.mean(mixed_val * mixed_val, axis=-1, keepdims=True) + GROUP_EPSILON)
        * group_gain[None]
    )


def swiglu(gate_pre, up_pre):
    return jax.nn.silu(gate_pre) * up_pre


def split_mixed(mixed_in, heads_local):
    size_rows = mixed_in.shape[0]
    width_x = heads_local * HP
    heads_x = mixed_in[:, :width_x].reshape(size_rows, heads_local, HP)
    return (heads_x, mixed_in[:, width_x : width_x + NS], mixed_in[:, width_x + NS :])


def ssd_main(seg_rows, seg_before, mixed_in, dt_raw, dt_bias_row, a_log_row, d_skip_row):
    size_rows = seg_rows.shape[0]
    heads_x, b_rows, c_rows = split_mixed(mixed_in, dt_raw.shape[1])
    dt_rows = jax.nn.softplus(dt_raw + dt_bias_row[None, :])
    cumul = jnp.cumsum(-jnp.exp(a_log_row)[None, :] * dt_rows, axis=0)
    order_pos = jnp.arange(size_rows)
    allowed = (seg_rows[:, None] == seg_rows[None, :]) & (order_pos[:, None] >= order_pos[None, :])
    differ = cumul[:, None, :] - cumul[None, :, :]
    decay = jnp.exp(jnp.where(allowed[:, :, None], differ, -jnp.inf))
    gram = jnp.dot(c_rows, b_rows.T, precision=HIGHEST, preferred_element_type=jnp.float32)
    mixing = gram[:, :, None] * decay * dt_rows[None, :, :]
    outputs = jnp.einsum("tsh,shp->thp", mixing, heads_x, precision=HIGHEST)
    outputs = outputs + d_skip_row[None, :, None] * heads_x
    tail_keep = (seg_rows == seg_rows[-1]).astype(jnp.float32)
    tail_weight = jnp.exp(cumul[-1][None, :] - cumul) * tail_keep[:, None] * dt_rows
    local_state = jnp.einsum("sh,shp,sn->hpn", tail_weight, heads_x, b_rows, precision=HIGHEST)
    carry_factor = jnp.exp(cumul[-1]) * (seg_rows[-1] == seg_before).astype(jnp.float32)
    return (outputs, carry_factor, local_state)


def ssd_state(seg_rows, seg_before, mixed_in, dt_raw, dt_bias_row, a_log_row, entry_state):
    heads_x, b_rows, c_rows = split_mixed(mixed_in, dt_raw.shape[1])
    dt_rows = jax.nn.softplus(dt_raw + dt_bias_row[None, :])
    cumul = jnp.cumsum(-jnp.exp(a_log_row)[None, :] * dt_rows, axis=0)
    entry_keep = (seg_rows == seg_before).astype(jnp.float32)
    entry_part = jnp.einsum("tn,hpn->thp", c_rows, entry_state, precision=HIGHEST)
    return jnp.exp(cumul)[:, :, None] * entry_keep[:, None, None] * entry_part


def chain_states(earlier, later):
    return (earlier[0] * later[0], later[0][:, None, None] * earlier[1] + later[1])


def block_scores(queries, keys_all, vals_all, seg_full, query_pos, seg_query, block_index, key_len):
    key_blk = keys_all[block_index * key_len : (block_index + 1) * key_len]
    val_blk = vals_all[block_index * key_len : (block_index + 1) * key_len]
    seg_key = seg_full[block_index * key_len : (block_index + 1) * key_len]
    key_pos = block_index * key_len + jnp.arange(key_len)
    scores = jnp.einsum(
        "tkgd,skd->kgts", queries, key_blk, preferred_element_type=jnp.float32
    ) * HD ** (-0.5)
    allowed = (query_pos[:, None] >= key_pos[None, :]) & (seg_query[:, None] == seg_key[None, :])
    return (key_blk, val_blk, jnp.where(allowed[None, None], scores, -jnp.inf))


def attend_forward(queries, keys_all, vals_all, seg_full, query_pos, seg_query, block_count):
    key_len = keys_all.shape[0] // block_count
    stat_shape = (queries.shape[1], queries.shape[2], queries.shape[0])
    running_max = jnp.full(stat_shape, -1e30, jnp.float32)
    running_sum = jnp.zeros(stat_shape, jnp.float32)
    for block_index in range(block_count):
        needed = block_index * key_len <= query_pos[-1]

        def stat_step(stats, block_index=block_index):
            old_max, old_sum = stats
            key_blk, val_blk, scores = block_scores(
                queries, keys_all, vals_all, seg_full, query_pos, seg_query, block_index, key_len
            )
            new_max = jnp.maximum(old_max, jnp.max(scores, axis=-1))
            new_sum = old_sum * jnp.exp(old_max - new_max) + jnp.sum(
                jnp.exp(scores - new_max[..., None]), axis=-1
            )
            return (new_max, new_sum)

        running_max, running_sum = lax.cond(
            needed, stat_step, lambda stats: stats, (running_max, running_sum)
        )
    log_total = running_max + jnp.log(running_sum)
    attended = jnp.zeros(queries.shape, jnp.float32)
    for block_index in range(block_count):
        needed = block_index * key_len <= query_pos[-1]

        def value_step(total, block_index=block_index):
            key_blk, val_blk, scores = block_scores(
                queries, keys_all, vals_all, seg_full, query_pos, seg_query, block_index, key_len
            )
            probs = jnp.exp(scores - log_total[..., None]).astype(jnp.bfloat16)
            return total + jnp.einsum(
                "kgts,skd->tkgd", probs, val_blk, preferred_element_type=jnp.float32
            )

        attended = lax.cond(needed, value_step, lambda total: total, attended)
    return (log_total, attended)


def attend_backward(
    queries, keys_all, vals_all, seg_full, query_pos, seg_query, block_count, grad_out, log_total
):
    key_len = keys_all.shape[0] // block_count
    delta = jnp.zeros(log_total.shape, jnp.float32)
    for block_index in range(block_count):
        needed = block_index * key_len <= query_pos[-1]

        def delta_step(total, block_index=block_index):
            key_blk, val_blk, scores = block_scores(
                queries, keys_all, vals_all, seg_full, query_pos, seg_query, block_index, key_len
            )
            probs = jnp.exp(scores - log_total[..., None])
            grad_probs = jnp.einsum(
                "tkgd,skd->kgts", grad_out, val_blk, preferred_element_type=jnp.float32
            )
            return total + jnp.sum(probs * grad_probs, axis=-1)

        delta = lax.cond(needed, delta_step, lambda total: total, delta)
    grad_query = jnp.zeros(queries.shape, jnp.float32)
    empty_part = jnp.zeros((key_len, keys_all.shape[1], keys_all.shape[2]), jnp.float32)
    key_parts = []
    val_parts = []
    for block_index in range(block_count):
        needed = block_index * key_len <= query_pos[-1]

        def grad_step(total, block_index=block_index):
            key_blk, val_blk, scores = block_scores(
                queries, keys_all, vals_all, seg_full, query_pos, seg_query, block_index, key_len
            )
            probs = jnp.exp(scores - log_total[..., None])
            grad_probs = jnp.einsum(
                "tkgd,skd->kgts", grad_out, val_blk, preferred_element_type=jnp.float32
            )
            grad_scores = (probs * (grad_probs - delta[..., None])).astype(jnp.bfloat16)
            new_total = total + jnp.einsum(
                "kgts,skd->tkgd", grad_scores, key_blk, preferred_element_type=jnp.float32
            ) * HD ** (-0.5)
            key_part = jnp.einsum(
                "kgts,tkgd->skd", grad_scores, queries, preferred_element_type=jnp.float32
            ) * HD ** (-0.5)
            val_part = jnp.einsum(
                "kgts,tkgd->skd",
                probs.astype(jnp.bfloat16),
                grad_out,
                preferred_element_type=jnp.float32,
            )
            return (new_total, key_part, val_part)

        grad_query, key_part, val_part = lax.cond(
            needed, grad_step, lambda total: (total, empty_part, empty_part), grad_query
        )
        key_parts.append(key_part)
        val_parts.append(val_part)
    return (grad_query, jnp.concatenate(key_parts, axis=0), jnp.concatenate(val_parts, axis=0))


def local(
    hidden_in,
    teacher,
    segment_ids,
    valid_mask,
    norm1_gain,
    w_z,
    w_x,
    w_bc,
    w_dt,
    conv_weight,
    conv_bias,
    dt_bias,
    a_log,
    d_skip,
    group_gain,
    w_mamba_out,
    w_query,
    w_key,
    w_value,
    w_attn_out,
    norm2_gain,
    w_gate,
    w_up,
    w_down,
):
    tensor_rank = lax.axis_index("tensor")
    seq_rank = lax.axis_index("seq")
    data_rank = lax.axis_index("dp")
    seq_count = lax.axis_size("seq")
    tensor_count = lax.axis_size("tensor")
    size_rows = hidden_in.shape[1]
    full_length = segment_ids.shape[1]
    row_start = seq_rank * size_rows
    seg_full = segment_ids[0]
    seg_local = lax.dynamic_slice_in_dim(seg_full, row_start, size_rows)
    seg_padded = jnp.concatenate([jnp.full((KC - 1,), -1, jnp.int32), seg_full])
    seg_ext = lax.dynamic_slice_in_dim(seg_padded, row_start, size_rows + KC - 1)
    seg_prev = lax.dynamic_index_in_dim(seg_padded, row_start + KC - 2, keepdims=False)
    token_count = jnp.sum(valid_mask).astype(jnp.float32)
    mask_rows = lax.dynamic_slice(valid_mask, (data_rank, row_start), (1, size_rows))[0].astype(
        jnp.float32
    )
    total_tokens = float(valid_mask.shape[0] * valid_mask.shape[1])
    (
        gain_one,
        full_z,
        full_x,
        full_dt,
        full_mo,
        full_q,
        full_k,
        full_v,
        full_ao,
        gain_two,
        full_gate,
        full_up,
        full_down,
    ) = (
        lax.all_gather(norm1_gain, ("dp", "seq"), axis=0, tiled=True),
        lax.all_gather(w_z, ("dp", "seq"), axis=0, tiled=True),
        lax.all_gather(w_x, ("dp", "seq"), axis=0, tiled=True),
        lax.all_gather(w_dt, ("dp", "seq"), axis=0, tiled=True),
        lax.all_gather(w_mamba_out, ("dp", "seq"), axis=1, tiled=True),
        lax.all_gather(w_query, ("dp", "seq"), axis=0, tiled=True),
        lax.all_gather(w_key, ("dp", "seq"), axis=0, tiled=True),
        lax.all_gather(w_value, ("dp", "seq"), axis=0, tiled=True),
        lax.all_gather(w_attn_out, ("dp", "seq"), axis=1, tiled=True),
        lax.all_gather(norm2_gain, ("dp", "seq"), axis=0, tiled=True),
        lax.all_gather(w_gate, ("dp", "seq"), axis=0, tiled=True),
        lax.all_gather(w_up, ("dp", "seq"), axis=0, tiled=True),
        lax.all_gather(w_down, ("dp", "seq"), axis=1, tiled=True),
    )
    heads_local = MH // tensor_count
    width_x = heads_local * HP
    head_start = tensor_rank * heads_local
    hidden = hidden_in[0].astype(jnp.float32)
    normed_f, norm_one_pull = jax.vjp(rms_norm, hidden, gain_one.astype(jnp.float32))
    normed = normed_f.astype(jnp.bfloat16)
    gate_z = mat_dot(normed, full_z)
    pre_x = mat_dot(normed, full_x).astype(jnp.bfloat16)
    pre_bc = mat_dot(normed, w_bc).astype(jnp.bfloat16)
    dt_raw = mat_dot(normed, full_dt)
    pre_all = jnp.concatenate([pre_x, pre_bc], axis=1)
    rim_rows = shifted(pre_all[size_rows - (KC - 1) :], "seq", 1)
    extended = jnp.concatenate([rim_rows, pre_all], axis=0).astype(jnp.float32)
    conv_local = jnp.concatenate(
        [
            lax.dynamic_slice_in_dim(conv_weight, head_start * HP, width_x, 0),
            conv_weight[MH * HP :],
        ],
        axis=0,
    )
    bias_local = jnp.concatenate(
        [lax.dynamic_slice_in_dim(conv_bias, head_start * HP, width_x, 0), conv_bias[MH * HP :]],
        axis=0,
    )
    mixed_f, conv_pull = jax.vjp(
        partial(conv_silu, seg_ext, seg_local), extended, conv_local, bias_local
    )
    mixed_in = lax.optimization_barrier(mixed_f.astype(jnp.bfloat16)).astype(jnp.float32)
    dt_bias_loc = lax.dynamic_slice_in_dim(dt_bias, head_start, heads_local)
    a_log_loc = lax.dynamic_slice_in_dim(a_log, head_start, heads_local)
    d_skip_loc = lax.dynamic_slice_in_dim(d_skip, head_start, heads_local)
    group_loc = lax.dynamic_slice_in_dim(group_gain, head_start, heads_local, 0)
    (ssm_local, carry_dev, state_dev), main_pull = jax.vjp(
        partial(ssd_main, seg_local, seg_prev), mixed_in, dt_raw, dt_bias_loc, a_log_loc, d_skip_loc
    )
    identity = (jnp.ones_like(carry_dev), jnp.zeros_like(state_dev))
    entry_state = carried_in((carry_dev, state_dev), "seq", chain_states, identity, False)[1]
    ssm_entry, state_pull = jax.vjp(
        partial(ssd_state, seg_local, seg_prev),
        mixed_in,
        dt_raw,
        dt_bias_loc,
        a_log_loc,
        entry_state,
    )
    ssm_out = ssm_local + ssm_entry
    gated_f, gate_pull = jax.vjp(
        group_gate, ssm_out, gate_z.reshape(size_rows, heads_local, HP), group_loc
    )
    gated = gated_f.reshape(size_rows, width_x).astype(jnp.bfloat16)
    mamba_part = mat_dot(gated, full_mo)
    positions = row_start + jnp.arange(size_rows)
    heads_q = full_q.shape[1] // HD
    heads_kv = full_k.shape[1] // HD
    groups = heads_q // heads_kv
    query_rot, query_pull = jax.vjp(
        partial(rotate, positions), mat_dot(normed, full_q).reshape(size_rows, heads_q, HD)
    )
    queries = query_rot.astype(jnp.bfloat16).reshape(size_rows, heads_kv, groups, HD)
    key_rot, key_pull = jax.vjp(
        partial(rotate, positions), mat_dot(normed, full_k).reshape(size_rows, heads_kv, HD)
    )
    keys_local = key_rot.astype(jnp.bfloat16).reshape(size_rows, heads_kv * HD)
    vals_local = mat_dot(normed, full_v).astype(jnp.bfloat16)
    keys_all, vals_all = (
        lax.all_gather(keys_local, "seq", axis=0, tiled=True),
        lax.all_gather(vals_local, "seq", axis=0, tiled=True),
    )
    keys_all = keys_all.reshape(full_length, heads_kv, HD)
    vals_all = vals_all.reshape(full_length, heads_kv, HD)
    block_count = seq_count // 4
    log_total, attended_f = attend_forward(
        queries, keys_all, vals_all, seg_full, positions, seg_local, block_count
    )
    attended = attended_f.reshape(size_rows, heads_q * HD).astype(jnp.bfloat16)
    branch = lax.psum(mamba_part + mat_dot(attended, full_ao), "tensor")
    middle = hidden + branch
    normed_two_f, norm_two_pull = jax.vjp(rms_norm, middle, gain_two.astype(jnp.float32))
    normed_two = normed_two_f.astype(jnp.bfloat16)
    act_f, glu_pull = jax.vjp(swiglu, mat_dot(normed_two, full_gate), mat_dot(normed_two, full_up))
    activated = act_f.astype(jnp.bfloat16)
    block_out = middle + lax.psum(mat_dot(activated, full_down), "tensor")
    (
        back_z,
        back_x,
        back_dt,
        back_mo,
        back_q,
        back_k,
        back_v,
        back_ao,
        back_gate,
        back_up,
        back_down,
    ) = (
        lax.all_gather(w_z, ("dp", "seq"), axis=0, tiled=True),
        lax.all_gather(w_x, ("dp", "seq"), axis=0, tiled=True),
        lax.all_gather(w_dt, ("dp", "seq"), axis=0, tiled=True),
        lax.all_gather(w_mamba_out, ("dp", "seq"), axis=1, tiled=True),
        lax.all_gather(w_query, ("dp", "seq"), axis=0, tiled=True),
        lax.all_gather(w_key, ("dp", "seq"), axis=0, tiled=True),
        lax.all_gather(w_value, ("dp", "seq"), axis=0, tiled=True),
        lax.all_gather(w_attn_out, ("dp", "seq"), axis=1, tiled=True),
        lax.all_gather(w_gate, ("dp", "seq"), axis=0, tiled=True),
        lax.all_gather(w_up, ("dp", "seq"), axis=0, tiled=True),
        lax.all_gather(w_down, ("dp", "seq"), axis=1, tiled=True),
    )
    d_out = (
        2.0
        * total_tokens
        / token_count
        * mask_rows[:, None]
        * (block_out - teacher[0].astype(jnp.float32))
    )
    d_mlp = d_out.astype(jnp.bfloat16)
    grad_down = dot_left_t(activated, d_mlp)
    d_gate_f, d_up_f = glu_pull(dot_right_t(d_mlp, back_down))
    d_gate = d_gate_f.astype(jnp.bfloat16)
    d_up = d_up_f.astype(jnp.bfloat16)
    grad_gate = dot_left_t(normed_two, d_gate)
    grad_up = dot_left_t(normed_two, d_up)
    d_normed_two = lax.psum(dot_right_t(d_gate, back_gate) + dot_right_t(d_up, back_up), "tensor")
    d_middle_n, grad_gain_two = norm_two_pull(d_normed_two)
    d_middle = d_out + d_middle_n
    d_branch = d_middle.astype(jnp.bfloat16)
    grad_ao = dot_left_t(attended, d_branch)
    grad_mo = dot_left_t(gated, d_branch)
    d_attended = (
        dot_right_t(d_branch, back_ao).astype(jnp.bfloat16).reshape(size_rows, heads_kv, groups, HD)
    )
    d_gated = dot_right_t(d_branch, back_mo).reshape(size_rows, heads_local, HP)
    d_ssm, d_gate_z_f, grad_group = gate_pull(d_gated)
    d_gate_z = d_gate_z_f.reshape(size_rows, width_x).astype(jnp.bfloat16)
    d_mixed_s, d_dt_s, d_dtb_s, d_alog_s, d_entry = state_pull(d_ssm)
    state_grad = carried_in((carry_dev, d_entry), "seq", chain_states, identity, True)[1]
    d_carry = jnp.sum(state_grad * entry_state, axis=(1, 2))
    d_mixed_m, d_dt_m, d_dtb_m, d_alog_m, grad_skip = main_pull((d_ssm, d_carry, state_grad))
    d_dt_raw = (d_dt_s + d_dt_m).astype(jnp.bfloat16)
    d_ext, grad_conv_loc, grad_bias_loc = conv_pull(d_mixed_s + d_mixed_m)
    rim_grad = shifted(d_ext[: KC - 1], "seq", -1)
    d_pre = d_ext[KC - 1 :] + jnp.pad(rim_grad, ((size_rows - (KC - 1), 0), (0, 0)))
    d_pre_x = d_pre[:, :width_x].astype(jnp.bfloat16)
    d_pre_bc = d_pre[:, width_x:]
    grad_query_rot, key_grads_all, val_grads_all = attend_backward(
        queries,
        keys_all,
        vals_all,
        seg_full,
        positions,
        seg_local,
        block_count,
        d_attended,
        log_total,
    )
    key_grad, val_grad = (
        lax.psum_scatter(
            key_grads_all.reshape(full_length, heads_kv * HD).astype(jnp.bfloat16),
            "seq",
            scatter_dimension=0,
            tiled=True,
        ).astype(jnp.float32),
        lax.psum_scatter(
            val_grads_all.reshape(full_length, heads_kv * HD).astype(jnp.bfloat16),
            "seq",
            scatter_dimension=0,
            tiled=True,
        ).astype(jnp.float32),
    )
    d_query = (
        query_pull(grad_query_rot.reshape(size_rows, heads_q, HD))[0]
        .reshape(size_rows, heads_q * HD)
        .astype(jnp.bfloat16)
    )
    d_key = (
        key_pull(key_grad.reshape(size_rows, heads_kv, HD))[0]
        .reshape(size_rows, heads_kv * HD)
        .astype(jnp.bfloat16)
    )
    d_value = val_grad.astype(jnp.bfloat16)
    grad_z = dot_left_t(normed, d_gate_z)
    grad_x = dot_left_t(normed, d_pre_x)
    grad_dt = dot_left_t(normed, d_dt_raw)
    grad_q = dot_left_t(normed, d_query)
    grad_k = dot_left_t(normed, d_key)
    grad_v = dot_left_t(normed, d_value)
    normed_wide = normed.astype(jnp.float32)
    bc_weight = w_bc.astype(jnp.float32)
    grad_bc = jnp.dot(
        normed_wide.T, d_pre_bc, precision=HIGHEST, preferred_element_type=jnp.float32
    )
    d_normed_part = (
        dot_right_t(d_gate_z, back_z)
        + dot_right_t(d_pre_x, back_x)
        + dot_right_t(d_dt_raw, back_dt)
        + dot_right_t(d_query, back_q)
        + dot_right_t(d_key, back_k)
        + dot_right_t(d_value, back_v)
        + jnp.dot(d_pre_bc, bc_weight.T, precision=HIGHEST, preferred_element_type=jnp.float32)
    )
    d_normed = lax.psum(d_normed_part.astype(jnp.bfloat16), "tensor").astype(jnp.float32)
    d_hidden_n, grad_gain_one = norm_one_pull(d_normed)
    grad_input = d_middle + d_hidden_n
    conv_x_full = lax.dynamic_update_slice_in_dim(
        jnp.zeros((MH * HP, KC), jnp.float32), grad_conv_loc[:width_x], head_start * HP, 0
    )
    grad_conv_full = jnp.concatenate([conv_x_full, grad_conv_loc[width_x:]], axis=0)
    bias_x_full = lax.dynamic_update_slice_in_dim(
        jnp.zeros((MH * HP,), jnp.float32), grad_bias_loc[:width_x], head_start * HP, 0
    )
    grad_bias_full = jnp.concatenate([bias_x_full, grad_bias_loc[width_x:]], axis=0)
    grad_dtb_full = lax.dynamic_update_slice_in_dim(
        jnp.zeros((MH,), jnp.float32), d_dtb_s + d_dtb_m, head_start, 0
    )
    grad_alog_full = lax.dynamic_update_slice_in_dim(
        jnp.zeros((MH,), jnp.float32), d_alog_s + d_alog_m, head_start, 0
    )
    grad_skip_full = lax.dynamic_update_slice_in_dim(
        jnp.zeros((MH,), jnp.float32), grad_skip, head_start, 0
    )
    grad_group_full = lax.dynamic_update_slice_in_dim(
        jnp.zeros((MH, HP), jnp.float32), grad_group, head_start, 0
    )
    sum_bc, sum_conv, sum_bias, sum_dtb, sum_alog, sum_skip, sum_group = lax.psum(
        (
            grad_bc,
            grad_conv_full,
            grad_bias_full,
            grad_dtb_full,
            grad_alog_full,
            grad_skip_full,
            grad_group_full,
        ),
        ("dp", "seq", "tensor"),
    )
    (
        out_gain_one,
        out_z,
        out_x,
        out_dt,
        out_mo,
        out_q,
        out_k,
        out_v,
        out_ao,
        out_gain_two,
        out_gate,
        out_up,
        out_down,
    ) = (
        lax.psum_scatter(grad_gain_one, ("dp", "seq"), scatter_dimension=0, tiled=True),
        lax.psum_scatter(grad_z, ("dp", "seq"), scatter_dimension=0, tiled=True),
        lax.psum_scatter(grad_x, ("dp", "seq"), scatter_dimension=0, tiled=True),
        lax.psum_scatter(grad_dt, ("dp", "seq"), scatter_dimension=0, tiled=True),
        lax.psum_scatter(grad_mo, ("dp", "seq"), scatter_dimension=1, tiled=True),
        lax.psum_scatter(grad_q, ("dp", "seq"), scatter_dimension=0, tiled=True),
        lax.psum_scatter(grad_k, ("dp", "seq"), scatter_dimension=0, tiled=True),
        lax.psum_scatter(grad_v, ("dp", "seq"), scatter_dimension=0, tiled=True),
        lax.psum_scatter(grad_ao, ("dp", "seq"), scatter_dimension=1, tiled=True),
        lax.psum_scatter(grad_gain_two, ("dp", "seq"), scatter_dimension=0, tiled=True),
        lax.psum_scatter(grad_gate, ("dp", "seq"), scatter_dimension=0, tiled=True),
        lax.psum_scatter(grad_up, ("dp", "seq"), scatter_dimension=0, tiled=True),
        lax.psum_scatter(grad_down, ("dp", "seq"), scatter_dimension=1, tiled=True),
    )
    return (
        block_out.astype(jnp.bfloat16)[None],
        grad_input[None],
        out_gain_one,
        out_z,
        out_x,
        sum_bc,
        out_dt,
        sum_conv,
        sum_bias,
        sum_dtb,
        sum_alog,
        sum_skip,
        sum_group,
        out_mo,
        out_q,
        out_k,
        out_v,
        out_ao,
        out_gain_two,
        out_gate,
        out_up,
        out_down,
    )


GROUP = 4
CHUNK = 128
HEADS = 6
MESH_ID = pl.DeviceIdType.MESH
VMEM_BYTES = 56 * 1024 * 1024


def dot_f32(left_side, right_side, left_dim, right_dim):
    return lax.dot_general(
        left_side,
        right_side,
        (((left_dim,), (right_dim,)), ((), ())),
        preferred_element_type=jnp.float32,
    )


def halves(values):
    high = values.astype(jnp.bfloat16)
    return (high, (values - high.astype(jnp.float32)).astype(jnp.bfloat16))


def dot_split(exact, parts, left_dim, right_dim):
    high, low = parts
    return dot_f32(exact, high, left_dim, right_dim) + dot_f32(exact, low, left_dim, right_dim)


def dot_split_left(parts, exact, left_dim, right_dim):
    high, low = parts
    return dot_f32(high, exact, left_dim, right_dim) + dot_f32(low, exact, left_dim, right_dim)


def dot_splits(left_parts, right_parts, left_dim, right_dim):
    left_high, left_low = left_parts
    right_high, right_low = right_parts
    return dot_f32(left_high, right_high, left_dim, right_dim) + (
        dot_f32(left_high, right_low, left_dim, right_dim)
        + dot_f32(left_low, right_high, left_dim, right_dim)
    )


def plane_place():
    data, place, core = lax.axis_index("dp"), lax.axis_index("seq"), lax.axis_index("tensor")
    along_x = place + 1 - 2 * lax.rem(place, 2)
    along_y = lax.rem(place + 2, GROUP)
    across = GROUP - 1 - place
    return (data, place, core, along_x, along_y, across)


def meet(devices):
    barrier = pltpu.get_barrier_semaphore()
    for device in devices:
        pl.semaphore_signal(barrier, inc=1, device_id=device, device_id_type=MESH_ID)
    pl.semaphore_wait(barrier, len(devices))


def remote(source, target, send_sem, recv_sem, device):
    return pltpu.make_async_remote_copy(
        src_ref=source,
        dst_ref=target,
        send_sem=send_sem,
        recv_sem=recv_sem,
        device_id=device,
        device_id_type=MESH_ID,
    )


def lasting(microseconds):
    return pl.CostEstimate(
        flops=int(microseconds * 9e8),
        bytes_accessed=int(microseconds * 3e6),
        transcendentals=0,
    )


def any_specs(count):
    return [pl.BlockSpec(memory_space=pl.ANY)] * count


def vmem_specs(count):
    return [pl.BlockSpec(memory_space=pltpu.VMEM)] * count


def gather_kernel(apply, count_in, count_out, own_ref, *refs):
    inputs, all_ref = refs[:count_in], refs[count_in]
    outputs = refs[count_in + 1 : count_in + 1 + count_out]
    send_sems, recv_sems = refs[count_in + 1 + count_out :]
    data, place, core, along_x, along_y, across = plane_place()
    height = own_ref.shape[0]
    half = height // 2
    to_x, to_y, partner = (data, along_x, core), (data, along_y, core), (data, place, 1 - core)

    def block(chip, part):
        return all_ref.at[2 * chip + core, pl.ds(part * half, half)]

    def work(chip, side):
        if apply is not None:
            index = 2 * chip + side
            rows = pl.ds(pl.multiple_of(index * height, 16), height)
            apply(all_ref[index], rows, inputs, outputs)

    meet((to_x, to_y, partner))

    def push(index, source, target, device):
        copy = remote(source, target, send_sems.at[index], recv_sems.at[index], device)
        copy.start()
        return copy

    first, second = own_ref.at[pl.ds(0, half)], own_ref.at[pl.ds(half, half)]
    x_first = push(0, first, block(place, 0), to_x)
    y_second = push(1, second, block(place, 1), to_y)
    x_second = push(2, second, block(place, 1), to_x)
    y_first = push(3, first, block(place, 0), to_y)
    pair_own = push(4, own_ref, all_ref.at[2 * place + core], partner)
    all_ref[2 * place + core] = own_ref[...]
    work(place, core)
    pair_own.wait_recv()
    work(place, 1 - core)
    x_first.wait_recv()
    over_y = push(5, block(along_x, 0), block(along_x, 0), to_y)
    y_second.wait_recv()
    over_x = push(6, block(along_y, 1), block(along_y, 1), to_x)
    x_second.wait_recv()
    mine_x = all_ref.at[2 * along_x + core]
    pair_x = push(7, mine_x, mine_x, partner)
    y_first.wait_recv()
    mine_y = all_ref.at[2 * along_y + core]
    pair_y = push(8, mine_y, mine_y, partner)
    work(along_x, core)
    work(along_y, core)
    pair_x.wait_recv()
    work(along_x, 1 - core)
    pair_y.wait_recv()
    work(along_y, 1 - core)
    over_y.wait_recv()
    pair_a = push(9, block(across, 0), block(across, 0), partner)
    over_x.wait_recv()
    pair_b = push(10, block(across, 1), block(across, 1), partner)
    work(across, core)
    pair_a.wait_recv()
    pair_b.wait_recv()
    work(across, 1 - core)
    for copy in (
        x_first,
        y_second,
        x_second,
        y_first,
        pair_own,
        over_y,
        over_x,
        pair_x,
        pair_y,
        pair_a,
        pair_b,
    ):
        copy.wait_send()


def gather_plane(own, identity=1, apply=None, inputs=(), outputs=()):
    rows, width = own.shape
    gathered, *results = pl.pallas_call(
        partial(gather_kernel, apply, len(inputs), len(outputs)),
        out_shape=[jax.ShapeDtypeStruct((2 * GROUP, rows, width), own.dtype)]
        + [jax.ShapeDtypeStruct(shape, dtype) for shape, dtype in outputs],
        in_specs=vmem_specs(1 + len(inputs)),
        out_specs=vmem_specs(1 + len(outputs)),
        scratch_shapes=[pltpu.SemaphoreType.DMA((11,)), pltpu.SemaphoreType.DMA((11,))],
        cost_estimate=lasting(35),
        compiler_params=pltpu.CompilerParams(
            collective_id=identity, has_side_effects=True, vmem_limit_bytes=VMEM_BYTES
        ),
    )(own, *inputs)
    gathered = gathered.reshape(2 * GROUP * rows, width)
    return (gathered, *results) if results else gathered


def apply_gate_up(block, rows, inputs, outputs):
    weights, (both_ref, act_ref) = inputs[0], outputs
    units = act_ref.shape[1]
    both = jnp.dot(block, weights[...], preferred_element_type=jnp.float32)
    both_ref[rows] = both
    gate = both[:, :units]
    act_ref[rows] = (gate * jax.nn.sigmoid(gate) * both[:, units:]).astype(jnp.bfloat16)


def apply_down_back(block, rows, inputs, outputs):
    weights, both_ref = inputs
    units = weights.shape[1]
    d_act = jnp.dot(block, weights[...], preferred_element_type=jnp.float32)
    gate, up = both_ref[rows, :units], both_ref[rows, units:]
    sigmoid = jax.nn.sigmoid(gate)
    silu = gate * sigmoid
    d_gate = d_act * up * (sigmoid * (1.0 + gate * (1.0 - sigmoid)))
    outputs[0][rows, :units] = d_gate.astype(jnp.bfloat16)
    outputs[0][rows, units:] = (d_act * silu).astype(jnp.bfloat16)


def apply_out_back(block, rows, inputs, outputs):
    outputs[0][rows] = jnp.dot(block, inputs[0][...], preferred_element_type=jnp.float32)


def scatter_kernel(count, left_ref, right_ref, *refs):
    data, place, core, along_x, along_y, across = plane_place()
    partner = (data, place, 1 - core)
    to_x, to_y = (data, along_x, core), (data, along_y, core)
    order = (across, along_x, along_y, place)
    extra, sums = refs[: count - 1], refs[count - 1 : 2 * count - 1]
    parts, scratch = refs[2 * count - 1 : 3 * count - 1], refs[3 * count - 1 :]
    step = 16
    meet((partner, to_x, to_y))

    def multiply(at, chip, side):
        part = parts[at]
        index = 2 * chip + side
        height, columns = part.shape[1:]
        if at == 0:
            rows = pl.ds(pl.multiple_of(index * height, 16), height)
            block = dot_f32(left_ref[rows], right_ref[...], 1, 1)
        else:
            start = left_ref.shape[1] - GROUP * height
            turned = pl.ds(pl.multiple_of(start + chip * height, 128), height)
            along = pl.ds(pl.multiple_of(side * columns, 128), columns)
            block = dot_f32(left_ref[:, turned], extra[at - 1][:, along], 0, 0)
        part[index] = block.astype(jnp.bfloat16)

    def one_array(at, part_ref, sum_ref, own_refs):
        pair_in, send_a, send_x, send_y, got_x, got_y, pair_s, pair_r, send_s, recv_s = own_refs
        half = part_ref.shape[1] // 2
        pair = []

        def send_pair(index):
            chip = order[index]
            multiply(at, chip, 1 - core)
            copy = remote(
                part_ref.at[2 * chip + 1 - core],
                pair_in.at[index],
                pair_s.at[index],
                pair_r.at[index],
                partner,
            )
            copy.start()
            pair.append(copy)
            multiply(at, chip, core)

        def own_rows(index, rows):
            return part_ref[2 * order[index] + core, rows].astype(jnp.float32) + pair_in[
                index, rows
            ].astype(jnp.float32)

        def fill(target, index, first, extra=None):
            def one(lap, carry):
                rows = pl.ds(pl.multiple_of(lap * step, step), step)
                total = own_rows(index, pl.ds(pl.multiple_of(first + lap * step, step), step))
                if extra is not None:
                    total = total + extra[rows].astype(jnp.float32)
                target[rows] = total.astype(jnp.bfloat16)
                return carry

            lax.fori_loop(0, half // step, one, 0)

        def push(index, source, target, device):
            copy = remote(source, target, send_s.at[index], recv_s.at[index], device)
            copy.start()
            return copy

        send_pair(0)
        pair[0].wait_recv()
        fill(send_a.at[0], 0, 0)
        far_x = push(0, send_a.at[0], got_x.at[0], to_x)
        fill(send_a.at[1], 0, half)
        far_y = push(1, send_a.at[1], got_y.at[0], to_y)
        send_pair(1)
        pair[1].wait_recv()
        fill(send_x.at[0], 1, 0)
        near_x = push(2, send_x.at[0], got_x.at[1], to_x)
        send_pair(2)
        pair[2].wait_recv()
        fill(send_y.at[0], 2, half)
        near_y = push(3, send_y.at[0], got_y.at[1], to_y)
        send_pair(3)
        yield
        far_x.wait_recv()
        fill(send_y.at[1], 2, 0, got_x.at[0])
        last_y = push(4, send_y.at[1], got_y.at[2], to_y)
        far_y.wait_recv()
        fill(send_x.at[1], 1, half, got_y.at[0])
        last_x = push(5, send_x.at[1], got_x.at[2], to_x)
        yield
        pair[3].wait_recv()
        near_x.wait_recv()
        near_y.wait_recv()
        last_y.wait_recv()
        last_x.wait_recv()

        def finish(first, near, last):
            def one(lap, carry):
                rows = pl.ds(pl.multiple_of(lap * step, step), step)
                place_rows = pl.ds(pl.multiple_of(first + lap * step, step), step)
                sum_ref[place_rows] = (
                    own_rows(3, place_rows)
                    + near[rows].astype(jnp.float32)
                    + last[rows].astype(jnp.float32)
                )
                return carry

            lax.fori_loop(0, half // step, one, 0)

        finish(0, got_x.at[1], got_y.at[2])
        finish(half, got_y.at[1], got_x.at[2])
        for copy in pair + [far_x, far_y, near_x, near_y, last_x, last_y]:
            copy.wait_send()

    each = len(scratch) // count
    runs = [
        one_array(at, parts[at], sums[at], scratch[each * at : each * (at + 1)]) for at in range(count)
    ]
    for run in runs:
        next(run)
    for run in runs:
        next(run)
    for run in runs:
        for _ in run:
            pass


def scatter_plane(left, right, identity, extra=()):
    height, width = left.shape[0] // (2 * GROUP), right.shape[0]
    sizes = [(height, width)] + [size for _, *size in extra]
    shapes = []
    scratch = [pltpu.VMEM((2 * GROUP, *size), jnp.bfloat16) for size in sizes]
    for rows, columns in sizes:
        half = (rows // 2, columns)
        shapes.append(jax.ShapeDtypeStruct((rows, columns), jnp.float32))
        scratch += [
            pltpu.VMEM((4, rows, columns), jnp.bfloat16),
            pltpu.VMEM((2,) + half, jnp.bfloat16),
            pltpu.VMEM((2,) + half, jnp.bfloat16),
            pltpu.VMEM((2,) + half, jnp.bfloat16),
            pltpu.VMEM((3,) + half, jnp.bfloat16),
            pltpu.VMEM((3,) + half, jnp.bfloat16),
            pltpu.SemaphoreType.DMA((4,)),
            pltpu.SemaphoreType.DMA((4,)),
            pltpu.SemaphoreType.DMA((6,)),
            pltpu.SemaphoreType.DMA((6,)),
        ]
    count = 1 + len(extra)
    return pl.pallas_call(
        partial(scatter_kernel, count),
        out_shape=shapes,
        in_specs=vmem_specs(1 + count),
        out_specs=vmem_specs(count),
        scratch_shapes=scratch,
        cost_estimate=lasting(35),
        compiler_params=pltpu.CompilerParams(
            collective_id=identity, has_side_effects=True, vmem_limit_bytes=VMEM_BYTES
        ),
    )(left, right, *[array for array, *_ in extra])


def finish_kernel(count_bulk, *refs):
    small_ref, bc_ref, own_ref, out_ref = refs[:4]
    bulk = refs[4 : 4 + count_bulk]
    small_sum, bc_all, both_ref, both_out = refs[4 + count_bulk : 8 + count_bulk]
    bulk_back = refs[8 + count_bulk : 8 + 2 * count_bulk]
    small_in, bc_send, bc_in, line_in, bc_line, own_sems, send_s, recv_s = refs[8 + 2 * count_bulk :]
    data, place, core, along_x, along_y, across = plane_place()
    count = lax.axis_size("dp")
    mine = 2 * place + core
    partner = (data, place, 1 - core)
    others = (across, along_x, along_y)
    plane = []
    for turn_by in range(1, 2 * GROUP):
        other = lax.rem(mine + turn_by, 2 * GROUP)
        plane.append((other, (data, other // 2, lax.rem(other, 2))))
    line = []
    for turn_by in range(1, count):
        other = lax.rem(data + turn_by, count)
        line.append((other, (other, place, core)))
    meet([device for _, device in plane + line])

    sent = 0
    started = []

    def push(source, target, device):
        nonlocal sent
        copy = remote(source, target, send_s.at[sent], recv_s.at[sent], device)
        copy.start()
        sent += 1
        started.append(copy)
        return copy

    piece = small_in.shape[2]
    rows = bc_in.shape[1]

    def piece_of(ref, index):
        return ref.at[:, pl.ds(pl.multiple_of(index * piece, 128), piece)]

    def rows_of(ref, index):
        return ref.at[pl.ds(pl.multiple_of(index * rows, 16), rows)]

    bc_send[...] = bc_ref[...].astype(jnp.bfloat16)
    first = [push(rows_of(bc_send, other), bc_in.at[data], device) for other, device in line]
    first += [push(piece_of(small_ref, other), small_in.at[mine], device) for other, device in plane]
    late = []
    for source, target in ((own_ref, both_ref), (out_ref, both_out)):
        late.append(push(source, target.at[core], partner))
    own = []
    for index, (source, target) in enumerate(zip(bulk, bulk_back)):
        for chip in others:
            late.append(push(source.at[chip], target.at[place], (data, chip, core)))
        copy = pltpu.make_async_copy(source.at[place], target.at[place], own_sems.at[index])
        copy.start()
        own.append(copy)
    small_in[mine] = piece_of(small_ref, mine)[...]
    bc_in[data] = rows_of(bc_send, data)[...]
    both_ref[core] = own_ref[...]
    both_out[core] = out_ref[...]
    for copy in first:
        copy.wait_recv()
    total = small_in[0]
    for index in range(1, 2 * GROUP):
        total = total + small_in[index]
    line_in[data] = total
    total = bc_in[0].astype(jnp.float32)
    for index in range(1, count):
        total = total + bc_in[index].astype(jnp.float32)
    bc_line[data] = total.astype(jnp.bfloat16)
    second = [push(bc_line.at[data], bc_line.at[data], device) for _, device in line]
    second += [push(line_in.at[data], line_in.at[data], device) for _, device in line]
    for copy in second:
        copy.wait_recv()
    total = line_in[0]
    for index in range(1, count):
        total = total + line_in[index]
    piece_of(small_sum, mine)[...] = total
    third = [push(bc_line, bc_all.at[mine], (data, chip, core)) for chip in others]
    late += [
        push(piece_of(small_sum, mine), piece_of(small_sum, mine), device) for _, device in plane
    ]
    late.append(push(bc_line, bc_all.at[mine], partner))
    bc_all[mine] = bc_line[...]
    for copy, chip in zip(third, others):
        copy.wait_recv()
        held = bc_all.at[2 * chip + core]
        late.append(push(held, held, partner))
    for copy in late:
        copy.wait_recv()
    for copy in started:
        copy.wait_send()
    for copy in own:
        copy.wait()


def finish_all(small, bc_sum, own_rows, out_rows, bulk):
    count = lax.axis_size("dp")
    places = 2 * GROUP
    pushes = (count - 1) * 4 + (places - 1) * 2 + 2 * GROUP + 1 + 3 * len(bulk)
    shaped = jax.ShapeDtypeStruct
    piece, line_rows = small.shape[1] // places, bc_sum.shape[0] // count
    width = bc_sum.shape[1]
    return pl.pallas_call(
        partial(finish_kernel, len(bulk)),
        out_shape=[
            shaped(small.shape, jnp.float32),
            shaped((places, count, line_rows, width), jnp.bfloat16),
            shaped((2,) + own_rows.shape, own_rows.dtype),
            shaped((2,) + out_rows.shape, out_rows.dtype),
        ]
        + [shaped(array.shape, array.dtype) for array in bulk],
        in_specs=vmem_specs(4) + any_specs(len(bulk)),
        out_specs=vmem_specs(4) + any_specs(len(bulk)),
        scratch_shapes=[
            pltpu.VMEM((places, 8, piece), jnp.float32),
            pltpu.VMEM(bc_sum.shape, jnp.bfloat16),
            pltpu.VMEM((count, line_rows, width), jnp.bfloat16),
            pltpu.VMEM((count, 8, piece), jnp.float32),
            pltpu.VMEM((count, line_rows, width), jnp.bfloat16),
            pltpu.SemaphoreType.DMA((len(bulk),)),
            pltpu.SemaphoreType.DMA((pushes,)),
            pltpu.SemaphoreType.DMA((pushes,)),
        ],
        cost_estimate=lasting(45),
        compiler_params=pltpu.CompilerParams(
            collective_id=7, has_side_effects=True, vmem_limit_bytes=VMEM_BYTES
        ),
    )(small, bc_sum, own_rows, out_rows, *bulk)


def unpack_kernel(
    gu_ref,
    down_ref,
    out_ref,
    in_ref,
    bc_ref,
    taps_ref,
    gate_ref,
    up_ref,
    d_ref,
    mo_ref,
    ao_ref,
    z_ref,
    x_ref,
    q_ref,
    k_ref,
    v_ref,
    dt_ref,
    grad_bc_ref,
    grad_conv_ref,
):
    units, width, part = down_ref.shape[2], HEADS * HP, HD // 4
    grad_conv_ref[...] = taps_ref[...].T[:, :KC]
    for chip in range(GROUP):
        columns = slice(units * chip, units * (chip + 1))
        gate_ref[:, columns] = gu_ref[chip, :, :units].astype(jnp.float32)
        up_ref[:, columns] = gu_ref[chip, :, units:].astype(jnp.float32)
        d_ref[columns] = down_ref[chip].astype(jnp.float32).T
        turned = out_ref[chip].astype(jnp.float32).T
        mo_ref[width * chip : width * (chip + 1)] = turned[:width]
        ao_ref[HD * chip : HD * (chip + 1)] = turned[width:]
        high, wide = bc_ref.shape[1:]
        for core in range(2):
            grad_bc_ref[wide * core : wide * (core + 1), high * chip : high * (chip + 1)] = (
                bc_ref[2 * chip + core].astype(jnp.float32).T
            )
    for chip in range(GROUP):
        columns = slice(width * chip, width * (chip + 1))
        z_ref[:, columns] = in_ref[chip, :, :width].astype(jnp.float32)
        x_ref[:, columns] = in_ref[chip, :, width + HD : 2 * width + HD].astype(jnp.float32)
        q_ref[:, HD * chip : HD * (chip + 1)] = in_ref[chip, :, width : width + HD].astype(
            jnp.float32
        )
    held = [in_ref[chip, :, 2 * width + HD :].astype(jnp.float32) for chip in range(GROUP)]
    k_ref[...] = jnp.concatenate(
        [
            held[0][:, :part],
            held[1][:, :part],
            held[0][:, part : 2 * part],
            held[1][:, part : 2 * part],
        ],
        axis=1,
    )
    v_ref[...] = jnp.concatenate([held[2][:, : 2 * part], held[3][:, : 2 * part]], axis=1)
    dt_ref[...] = jnp.concatenate(
        [values[:, DT_LANE : DT_LANE + HEADS] for values in held], axis=1
    )


def exchange_kernel(moves, count_in, spread, *refs):
    data, place, core, along_x, along_y, across = plane_place()
    sources, targets = refs[:count_in], refs[count_in:-3]
    local_sems, send_sems, recv_sems = refs[-3:]
    count = lax.axis_size("dp")
    others = (across, along_x, along_y)
    devices = [(data, chip, core) for chip in others]
    if spread:
        mine = GROUP * data + place
        all_places = GROUP * count
        devices = []
        for turn_by in range(1, all_places):
            other = lax.rem(mine + turn_by, all_places)
            devices.append((other // GROUP, lax.rem(other, GROUP), core))
    meet(devices)
    copies = []
    for index, chip in enumerate(others):
        for at, move in enumerate(moves):
            source, target = move(sources, targets, place, chip)
            slot = index * len(moves) + at
            copy = remote(
                source, target, send_sems.at[slot], recv_sems.at[slot], (data, chip, core)
            )
            copy.start()
            copies.append(copy)
    own = []
    if spread:
        first = 3 * len(moves)
        for index, device in enumerate(devices):
            copy = remote(
                sources[-1],
                targets[-1].at[mine],
                send_sems.at[first + index],
                recv_sems.at[first + index],
                device,
            )
            copy.start()
            copies.append(copy)
        copy = pltpu.make_async_copy(sources[-1], targets[-1].at[mine], local_sems.at[len(moves)])
        copy.start()
        own.append(copy)
    for at, move in enumerate(moves):
        source, target = move(sources, targets, place, place)
        copy = pltpu.make_async_copy(source, target, local_sems.at[at])
        copy.start()
        own.append(copy)
    for copy in own:
        copy.wait()
    for copy in copies:
        copy.wait()


def exchange_plane(moves, arrays, out_shapes, identity, spread=False):
    shapes = [jax.ShapeDtypeStruct(shape, jnp.bfloat16) for shape in out_shapes]
    count = 3 * len(moves)
    if spread:
        places = GROUP * lax.axis_size("dp")
        shapes.append(jax.ShapeDtypeStruct((places,) + arrays[-1].shape, arrays[-1].dtype))
        count += places - 1
    return pl.pallas_call(
        partial(exchange_kernel, moves, len(arrays), spread),
        out_shape=shapes,
        in_specs=any_specs(len(arrays)),
        out_specs=any_specs(len(shapes)),
        scratch_shapes=[
            pltpu.SemaphoreType.DMA((len(moves) + 1,)),
            pltpu.SemaphoreType.DMA((count,)),
            pltpu.SemaphoreType.DMA((count,)),
        ],
        cost_estimate=lasting(25),
        compiler_params=pltpu.CompilerParams(collective_id=identity, has_side_effects=True),
    )(*arrays)


def column_move(source, target, start, width):
    def move(sources, targets, place, chip):
        columns = pl.ds(pl.multiple_of(chip * width, 128), width)
        return (
            sources[source].at[:, columns],
            targets[target].at[place, :, pl.ds(start, width)],
        )

    return move


def block_move(source, target):
    def move(sources, targets, place, chip):
        return (sources[source].at[chip], targets[target].at[place])

    return move


def misc_move(source, target, start):
    def move(sources, targets, place, chip):
        return (
            sources[source].at[chip],
            targets[target].at[place, :, pl.ds(start, 128)],
        )

    return move


def lane_masks():
    lane = lax.broadcasted_iota(jnp.int32, (1, 2 * HP), 1)
    return (lane < HP, lane >= HP)


DT_LANE = HP


def at_lane(lane, values):
    row = lax.broadcasted_iota(jnp.int32, (1, 2 * HP), 1)
    return jnp.where(row == lane, values, 0.0)


def at_row(row, values):
    rows = lax.broadcasted_iota(jnp.int32, (values.shape[1], 1), 0)
    return jnp.where(rows == row, values, 0.0)


def pair_columns(values, pair):
    low, high = lane_masks()
    lane = DT_LANE + 2 * pair
    return jnp.where(low, values[:, lane : lane + 1], values[:, lane + 1 : lane + 2])


def head_sums(values):
    low, high = lane_masks()
    first = jnp.sum(jnp.where(low, values, 0.0), axis=1, keepdims=True)
    second = jnp.sum(jnp.where(high, values, 0.0), axis=1, keepdims=True)
    return (first, second)


def head_means(values):
    low, high = lane_masks()
    first, second = head_sums(values)
    return jnp.where(low, first, second) * (1.0 / HP)


def stack_heads(values):
    low, high = lane_masks()
    zero = jnp.zeros_like(values)
    return jnp.concatenate([jnp.where(low, values, zero), jnp.where(high, values, zero)], axis=0)


def order_in(size):
    row = lax.broadcasted_iota(jnp.int32, (size, size), 0)
    column = lax.broadcasted_iota(jnp.int32, (size, size), 1)
    return (row, column)


def exact_sum(ones, values):
    high = values.astype(jnp.bfloat16)
    rest = values - high.astype(jnp.float32)
    middle = rest.astype(jnp.bfloat16)
    low = (rest - middle.astype(jnp.float32)).astype(jnp.bfloat16)
    return dot_f32(ones, high, 1, 0) + (dot_f32(ones, middle, 1, 0) + dot_f32(ones, low, 1, 0))


def chunk_decays(proj_ref, heads_ref, keeps_ref):
    size, width = proj_ref.shape
    raw = proj_ref[:, width - 2 * HP :] + heads_ref[0:1]
    dt_rows = jnp.maximum(raw, 0.0) + jnp.log1p(jnp.exp(-jnp.abs(raw)))
    row, column = order_in(size)
    lower = jnp.where(row >= column, 1.0, 0.0).astype(jnp.bfloat16)
    cumul = exact_sum(lower, -heads_ref[1:2] * dt_rows)
    enter = jnp.exp(cumul) * keeps_ref[:, 0:1]
    leave_bare = jnp.exp(cumul[size - 1 :] - cumul) * keeps_ref[:, 1:2]
    return (raw, dt_rows, cumul, enter, leave_bare)


def conv_windows(block, proj_ref, before_ref, bc_ref, bc_before_ref):
    if block < HEADS // 2:
        start = proj_ref.shape[1] - 2 * HP * (1 + HEADS // 2 - block)
        lanes = slice(start, start + 2 * HP)
        now, before = proj_ref[:, lanes], before_ref[:, lanes]
        now, before = now.astype(jnp.bfloat16), before.astype(jnp.bfloat16)
    else:
        start = 2 * HP * (block - HEADS // 2)
        lanes = slice(start, start + 2 * HP)
        now, before = bc_ref[:, lanes], bc_before_ref[8:, lanes]
    now, before = now.astype(jnp.float32), before.astype(jnp.float32)
    size = now.shape[0]
    extended = jnp.concatenate([before, now], axis=0)
    return [now] + [extended[8 - back : 8 - back + size] for back in range(1, KC)]


def conv_sum(windows, taps_ref, lanes, keeps_ref):
    total = taps_ref[KC : KC + 1, lanes] + taps_ref[KC - 1 : KC, lanes] * windows[0]
    for back in range(1, KC):
        total = total + taps_ref[KC - 1 - back : KC - back, lanes] * (
            windows[back] * keeps_ref[:, 1 + back : 2 + back]
        )
    return total


def head_decay(allowed, cumul, cumul_t, head):
    lane = DT_LANE + head
    differ = cumul[:, lane : lane + 1] - cumul_t[lane : lane + 1, :]
    return jnp.exp(jnp.where(allowed, differ, -jnp.inf))


def ssd_forward_kernel(
    proj_ref,
    before_ref,
    bc_ref,
    bc_before_ref,
    taps_ref,
    heads_ref,
    keeps_ref,
    segc_ref,
    segr_ref,
    skip_ref,
    gain_ref,
    gated_ref,
    ssm_ref,
    states_ref,
    mixed_ref,
    state,
):
    @pl.when(pl.program_id(0) == 0)
    def _():
        state[...] = jnp.zeros_like(state)

    size = proj_ref.shape[0]
    width = HEADS * HP
    for block in range(mixed_ref.shape[1] // (2 * HP)):
        lanes = slice(2 * HP * block, 2 * HP * (block + 1))
        windows = conv_windows(block, proj_ref, before_ref, bc_ref, bc_before_ref)
        summed = conv_sum(windows, taps_ref, lanes, keeps_ref)
        mixed_ref[:, lanes] = (summed * jax.nn.sigmoid(summed)).astype(jnp.bfloat16)
    raw, dt_rows, cumul, enter_all, leave_bare = chunk_decays(proj_ref, heads_ref, keeps_ref)
    leave_all = leave_bare * dt_rows
    cumul_t, dt_t = cumul.T, dt_rows.T
    entry = state[...]
    states_ref[0] = entry
    b_rows, c_rows = mixed_ref[:, width : width + NS], mixed_ref[:, width + NS :]
    gram = dot_f32(c_rows, b_rows, 1, 1)
    row, column = order_in(size)
    allowed = (segc_ref[...] == segr_ref[0]) & (row >= column)
    entered = dot_split(c_rows, halves(entry), 1, 0)
    for pair in range(HEADS // 2):
        lanes = slice(2 * HP * pair, 2 * HP * (pair + 1))
        heads_x = mixed_ref[:, lanes]
        mixing = []
        for head in (2 * pair, 2 * pair + 1):
            lane = DT_LANE + head
            decay = head_decay(allowed, cumul, cumul_t, head)
            mixing.append(gram * decay * dt_t[lane : lane + 1, :])
        out = dot_split_left(
            halves(jnp.concatenate(mixing, axis=1)), stack_heads(heads_x), 1, 0
        )
        wide_x = heads_x.astype(jnp.float32)
        enter = pair_columns(enter_all, pair)
        out = out + enter * entered[:, lanes] + skip_ref[:, lanes] * wide_x
        ssm_ref[:, lanes] = out
        gate = proj_ref[:, lanes]
        value = out * (gate * jax.nn.sigmoid(gate))
        scale = lax.rsqrt(head_means(value * value) + GROUP_EPSILON)
        gated_ref[:, lanes] = (value * scale * gain_ref[:, lanes]).astype(jnp.bfloat16)
        weighted = halves(pair_columns(leave_all, pair) * wide_x)
        state[:, lanes] = enter[size - 1 :, :] * entry[:, lanes] + dot_split(
            b_rows, weighted, 0, 0
        )


def ssd_backward_kernel(
    proj_ref,
    before_ref,
    bc_ref,
    bc_before_ref,
    taps_ref,
    heads_ref,
    keeps_ref,
    segc_ref,
    segr_ref,
    skip_ref,
    gain_ref,
    mixed_ref,
    ssm_ref,
    states_ref,
    dgated_ref,
    dq_ref,
    dproj_ref,
    dtaps_ref,
    dheads_ref,
    dskip_ref,
    dgain_ref,
    state,
    d_mixed,
    next_rows,
):
    @pl.when(pl.program_id(0) == 0)
    def _():
        state[...] = jnp.zeros_like(state)
        next_rows[...] = jnp.zeros_like(next_rows)
        dtaps_ref[...] = jnp.zeros_like(dtaps_ref)
        dheads_ref[...] = jnp.zeros_like(dheads_ref)
        dskip_ref[...] = jnp.zeros_like(dskip_ref)
        dgain_ref[...] = jnp.zeros_like(dgain_ref)

    size = proj_ref.shape[0]
    width = HEADS * HP
    raw, dt_rows, cumul, enter_all, leave_bare = chunk_decays(proj_ref, heads_ref, keeps_ref)
    leave_all = leave_bare * dt_rows
    cumul_t, dt_t = cumul.T, dt_rows.T
    later = state[...]
    later_parts = halves(later)
    entry = states_ref[0]
    entry_parts = halves(entry)
    carried = jnp.sum(later * entry, axis=0, keepdims=True)
    b_rows, c_rows = mixed_ref[:, width : width + NS], mixed_ref[:, width + NS :]
    gram = dot_f32(c_rows, b_rows, 1, 1)
    row, column = order_in(size)
    allowed = (segc_ref[...] == segr_ref[0]) & (row >= column)
    entered = dot_split(c_rows, entry_parts, 1, 0)
    d_weighted = dot_split(b_rows, later_parts, 1, 0)
    d_gram = jnp.zeros((size, size), jnp.float32)
    d_c = jnp.zeros(c_rows.shape, jnp.float32)
    d_b = jnp.zeros(b_rows.shape, jnp.float32)
    row_sums = jnp.zeros((size, 2 * HP), jnp.float32)
    d_leave = jnp.zeros((size, 2 * HP), jnp.float32)
    d_enter = jnp.zeros((size, 2 * HP), jnp.float32)
    column_sums = jnp.zeros((2 * HP, size), jnp.float32)
    d_carried = jnp.zeros((1, 2 * HP), jnp.float32)
    for pair in range(HEADS // 2):
        lanes = slice(2 * HP * pair, 2 * HP * (pair + 1))
        heads_x = mixed_ref[:, lanes]
        wide_x = heads_x.astype(jnp.float32)
        ssm, gate, gain = ssm_ref[:, lanes], proj_ref[:, lanes], gain_ref[:, lanes]
        d_gated = dgated_ref[:, lanes]
        sigmoid = jax.nn.sigmoid(gate)
        silu = gate * sigmoid
        value = ssm * silu
        scale = lax.rsqrt(head_means(value * value) + GROUP_EPSILON)
        dgain_ref[:, lanes] += jnp.sum(d_gated * value * scale, axis=0, keepdims=True)
        d_scaled = d_gated * gain
        d_value = scale * d_scaled - value * (scale * scale * scale) * head_means(d_scaled * value)
        d_out = d_value * silu
        dproj_ref[:, lanes] = (d_value * ssm * (sigmoid * (1.0 + gate * (1.0 - sigmoid)))).astype(
            jnp.bfloat16
        )
        dskip_ref[:, lanes] += jnp.sum(d_out * wide_x, axis=0, keepdims=True)
        enter, leave = pair_columns(enter_all, pair), pair_columns(leave_all, pair)
        d_out_parts = [stack_heads(half) for half in halves(d_out)]
        mixing = []
        for side in range(2):
            head = 2 * pair + side
            lane = DT_LANE + head
            d_mixing = dot_split_left(
                [half[size * side : size * (side + 1)] for half in d_out_parts], heads_x, 1, 1
            )
            decay = head_decay(allowed, cumul, cumul_t, head)
            dt_row = dt_t[lane : lane + 1, :]
            weighted_gram = gram * decay
            mixing.append(weighted_gram * dt_row)
            d_gram = d_gram + d_mixing * (decay * dt_row)
            product = d_mixing * weighted_gram
            column_sums = column_sums + at_row(lane, jnp.sum(product, axis=0, keepdims=True))
            row_sums = row_sums + at_lane(lane, jnp.sum(product * dt_row, axis=1, keepdims=True))
        d_x = dot_splits(halves(jnp.concatenate(mixing, axis=0)), d_out_parts, 0, 0)
        first_lane = DT_LANE + 2 * pair
        first, second = head_sums(d_out * entered[:, lanes])
        d_enter = d_enter + at_lane(first_lane, first) + at_lane(first_lane + 1, second)
        first, second = head_sums(d_weighted[:, lanes] * wide_x)
        d_leave = d_leave + at_lane(first_lane, first) + at_lane(first_lane + 1, second)
        first, second = head_sums(carried[:, lanes])
        d_carried = d_carried + at_lane(first_lane, first) + at_lane(first_lane + 1, second)
        d_mixed[:, lanes] = d_x + skip_ref[:, lanes] * d_out + leave * d_weighted[:, lanes]
        d_entered = halves(enter * d_out)
        weighted = halves(leave * wide_x)
        d_c = d_c + dot_splits(d_entered, [half[:, lanes] for half in entry_parts], 1, 1)
        d_b = d_b + dot_splits(weighted, [half[:, lanes] for half in later_parts], 1, 1)
        state[:, lanes] = enter[size - 1 :, :] * later[:, lanes] + dot_split(
            c_rows, d_entered, 0, 0
        )
    d_gram_parts = halves(d_gram)
    d_mixed[:, width : width + NS] = d_b + dot_split_left(d_gram_parts, c_rows, 0, 0)
    d_mixed[:, width + NS :] = d_c + dot_split_left(d_gram_parts, b_rows, 1, 0)

    column_sums = column_sums.T
    d_left = d_leave * leave_all
    d_cumul = row_sums - column_sums * dt_rows + d_enter * enter_all - d_left
    at_last = jnp.sum(d_left, axis=0, keepdims=True) + d_carried * enter_all[size - 1 :]
    last_row = lax.broadcasted_iota(jnp.int32, (size, 1), 0) == size - 1
    d_cumul = d_cumul + jnp.where(last_row, at_last, 0.0)
    upper = jnp.where(row <= column, 1.0, 0.0).astype(jnp.bfloat16)
    d_log = exact_sum(upper, d_cumul)
    rate = heads_ref[1:2]
    d_raw = (column_sums + d_leave * leave_bare - rate * d_log) * jax.nn.sigmoid(raw)
    lane_row = lax.broadcasted_iota(jnp.int32, (1, 2 * HP), 1)
    d_raw = jnp.where((lane_row >= DT_LANE) & (lane_row < DT_LANE + HEADS), d_raw, 0.0)
    dheads_ref[0:1] += jnp.sum(d_raw, axis=0, keepdims=True)
    dheads_ref[1:2] += -rate * jnp.sum(d_log * dt_rows, axis=0, keepdims=True)
    total = proj_ref.shape[1]
    dproj_ref[:, total - 2 * HP : total] = jnp.concatenate(
        [jnp.zeros((size, DT_LANE), jnp.bfloat16), d_raw[:, DT_LANE:].astype(jnp.bfloat16)], axis=1
    )
    dproj_ref[:, width : width + HD] = dq_ref[...]

    for block in range(mixed_ref.shape[1] // (2 * HP)):
        lanes = slice(2 * HP * block, 2 * HP * (block + 1))
        windows = conv_windows(block, proj_ref, before_ref, bc_ref, bc_before_ref)
        summed = conv_sum(windows, taps_ref, lanes, keeps_ref)
        sigmoid = jax.nn.sigmoid(summed)
        d_sum = d_mixed[:, lanes] * (sigmoid * (1.0 + summed * (1.0 - sigmoid)))
        dtaps_ref[KC : KC + 1, lanes] += jnp.sum(d_sum, axis=0, keepdims=True)
        dtaps_ref[KC - 1 : KC, lanes] += jnp.sum(d_sum * windows[0], axis=0, keepdims=True)
        d_pre = taps_ref[KC - 1 : KC, lanes] * d_sum
        for back in range(1, KC):
            tap = KC - 1 - back
            kept = d_sum * keeps_ref[:, 1 + back : 2 + back]
            dtaps_ref[tap : tap + 1, lanes] += jnp.sum(
                kept * windows[back], axis=0, keepdims=True
            )
            extended = jnp.concatenate([kept, next_rows[back - 1, :, lanes]], axis=0)
            d_pre = d_pre + taps_ref[tap : tap + 1, lanes] * extended[back : back + size]
            next_rows[back - 1, :, lanes] = kept[:8]
        if block < HEADS // 2:
            start = total - 2 * HP * (1 + HEADS // 2 - block)
            dproj_ref[:, start : start + 2 * HP] = d_pre.astype(jnp.bfloat16)
        else:
            start = total + 2 * HP * (block - HEADS // 2)
            dproj_ref[:, start : start + 2 * HP] = d_pre.astype(jnp.bfloat16)


def ssd_specs(length, reverse, width_in, width_all, width):
    laps = length // CHUNK

    def at(lap):
        return laps - 1 - lap if reverse else lap

    def tall(columns):
        return pl.BlockSpec((CHUNK, columns), lambda lap: (at(lap), 0))

    def rim(rows, columns):
        each = CHUNK // rows
        return pl.BlockSpec((rows, columns), lambda lap: (jnp.maximum(each * at(lap) - 1, 0), 0))

    def whole(rows, columns):
        return pl.BlockSpec((rows, columns), lambda lap: (0, 0))

    def slab(rows, columns):
        return pl.BlockSpec((1, rows, columns), lambda lap: (at(lap), 0, 0))

    specs = [
        tall(width_in),
        rim(8, width_in),
        tall(2 * NS),
        rim(16, 2 * NS),
        whole(8, width_all),
        whole(8, 2 * HP),
        tall(8),
        tall(1),
        slab(1, CHUNK),
        whole(1, width),
        whole(1, width),
    ]
    return (laps, tall, whole, slab, specs)


def ssd_forward(arrays):
    length, width_in = arrays[0].shape
    width, width_all = HEADS * HP, HEADS * HP + 2 * NS
    laps, tall, whole, slab, specs = ssd_specs(length, False, width_in, width_all, width)
    shaped = jax.ShapeDtypeStruct
    return pl.pallas_call(
        ssd_forward_kernel,
        grid=(laps,),
        in_specs=specs,
        out_specs=[tall(width), tall(width), slab(NS, width), tall(width_all)],
        out_shape=[
            shaped((length, width), jnp.bfloat16),
            shaped((length, width), jnp.float32),
            shaped((laps, NS, width), jnp.float32),
            shaped((length, width_all), jnp.bfloat16),
        ],
        scratch_shapes=[pltpu.VMEM((NS, width), jnp.float32)],
        cost_estimate=lasting(6),
        compiler_params=pltpu.CompilerParams(vmem_limit_bytes=VMEM_BYTES),
    )(*arrays)


def ssd_backward(arrays, mixed, ssm, states, d_outs, d_query):
    length, width_in = arrays[0].shape
    width, width_all = HEADS * HP, HEADS * HP + 2 * NS
    laps, tall, whole, slab, specs = ssd_specs(length, True, width_in, width_all, width)
    shaped = jax.ShapeDtypeStruct
    return pl.pallas_call(
        ssd_backward_kernel,
        grid=(laps,),
        in_specs=specs
        + [
            tall(width_all),
            tall(width),
            slab(NS, width),
            tall(d_outs.shape[1]),
            tall(HD),
        ],
        out_specs=[
            tall(width_in + 2 * NS),
            whole(8, width_all),
            whole(8, 2 * HP),
            whole(1, width),
            whole(1, width),
        ],
        out_shape=[
            shaped((length, width_in + 2 * NS), jnp.bfloat16),
            shaped((8, width_all), jnp.float32),
            shaped((8, 2 * HP), jnp.float32),
            shaped((1, width), jnp.float32),
            shaped((1, width), jnp.float32),
        ],
        scratch_shapes=[
            pltpu.VMEM((NS, width), jnp.float32),
            pltpu.VMEM((CHUNK, width_all), jnp.float32),
            pltpu.VMEM((KC - 1, 8, width_all), jnp.float32),
        ],
        cost_estimate=lasting(48),
        compiler_params=pltpu.CompilerParams(vmem_limit_bytes=VMEM_BYTES),
    )(*arrays, mixed, ssm, states, d_outs, d_query)


QUERY_ROWS = 256


def masked_scores(q_rows, k_ref, segc_ref, segr_ref, start, reach):
    rows = q_rows.shape[0]
    scores = dot_f32(q_rows, k_ref[:reach], 1, 1) * HD ** (-0.5)
    row = lax.broadcasted_iota(jnp.int32, (rows, reach), 0) + start
    column = lax.broadcasted_iota(jnp.int32, (rows, reach), 1)
    allowed = (segc_ref[start : start + rows] == segr_ref[:, :reach]) & (row >= column)
    return jnp.where(allowed, scores, -jnp.inf)


def rotate_rows(values, cos_ref, sin_ref, sign):
    return values * cos_ref[...] + sign * (pltpu.roll(values, HD // 2, 1) * sin_ref[...])


def swap_middle(values):
    lane = lax.broadcasted_iota(jnp.int32, (1, HD), 1) // (HD // 4)
    up = pltpu.roll(values, HD // 4, 1)
    down = pltpu.roll(values, HD - HD // 4, 1)
    return jnp.where(lane == 1, down, jnp.where(lane == 2, up, values))


def join_halves(ref, first):
    half = ref.shape[2] // 2
    one, two = ref[first], ref[first + 1]
    early = jnp.concatenate([one[:, :half], two[:, :half]], axis=1)
    late = jnp.concatenate([one[:, half:], two[:, half:]], axis=1)
    return jnp.concatenate([early, late], axis=0)


def fold_rows(values):
    rows = values.shape[0] // 2
    return jnp.concatenate([values[:rows], values[rows:]], axis=1)


def unfold_rows(values):
    columns = values.shape[1] // 2
    return jnp.concatenate([values[:, :columns], values[:, columns:]], axis=0)


def attend_forward_kernel(
    raw_ref, cos_ref, sin_ref, kv_ref, segc_ref, segr_ref, out_ref, total_ref, q_ref, k_ref, v_ref
):
    q_ref[...] = swap_middle(rotate_rows(raw_ref[...], cos_ref, sin_ref, 1.0)).astype(jnp.bfloat16)
    k_ref[...] = join_halves(kv_ref, 0)
    v_ref[...] = join_halves(kv_ref, 2)
    for start in range(0, q_ref.shape[0], QUERY_ROWS):
        reach = start + QUERY_ROWS
        rows = slice(start, reach)
        scores = masked_scores(q_ref[rows], k_ref, segc_ref, segr_ref, start, reach)
        top = jnp.max(scores, axis=1, keepdims=True)
        powers = jnp.exp(scores - top)
        total = jnp.sum(powers, axis=1, keepdims=True)
        probs = (powers * (1.0 / total)).astype(jnp.bfloat16)
        out_ref[rows] = dot_f32(probs, v_ref[:reach], 1, 0).astype(jnp.bfloat16)
        total_ref[rows] = top + jnp.log(total)


def attend_backward_kernel(
    q_ref,
    k_ref,
    v_ref,
    cos_ref,
    sin_ref,
    segc_ref,
    segr_ref,
    total_ref,
    dout_ref,
    dq_ref,
    dkv_ref,
    dq_sum,
    dk_sum,
    dv_sum,
):
    dk_sum[...] = jnp.zeros_like(dk_sum)
    dv_sum[...] = jnp.zeros_like(dv_sum)
    for start in range(0, q_ref.shape[0], QUERY_ROWS):
        reach = start + QUERY_ROWS
        rows = slice(start, reach)
        q_rows, d_out = q_ref[rows], dout_ref[rows].astype(jnp.bfloat16)
        scores = masked_scores(q_rows, k_ref, segc_ref, segr_ref, start, reach)
        probs = jnp.exp(scores - total_ref[rows])
        d_probs = dot_f32(d_out, v_ref[:reach], 1, 1)
        delta = jnp.sum(probs * d_probs, axis=1, keepdims=True)
        d_scores = (probs * (d_probs - delta)).astype(jnp.bfloat16)
        dq_sum[rows] = dot_f32(d_scores, k_ref[:reach], 1, 0) * HD ** (-0.5)
        dk_sum[:reach] += dot_f32(d_scores, q_rows, 0, 0) * HD ** (-0.5)
        dv_sum[:reach] += dot_f32(probs.astype(jnp.bfloat16), d_out, 0, 0)
    dq_ref[...] = rotate_rows(swap_middle(dq_sum[...]), cos_ref, sin_ref, -1.0).astype(jnp.bfloat16)
    half = HD // 2
    dkv_ref[0] = fold_rows(dk_sum[:, :half]).astype(jnp.bfloat16)
    dkv_ref[1] = fold_rows(dk_sum[:, half:]).astype(jnp.bfloat16)
    dkv_ref[2] = fold_rows(dv_sum[:, :half]).astype(jnp.bfloat16)
    dkv_ref[3] = fold_rows(dv_sum[:, half:]).astype(jnp.bfloat16)


def place_kv_kernel(lane_ref, cos_ref, sin_ref, *refs):
    parts, out_ref = refs[:-1], refs[-1]
    total = parts[0][...].astype(jnp.float32)
    for part in parts[1:]:
        total = total + part[...].astype(jnp.float32)
    total = unfold_rows(total)
    part = cos_ref.shape[1]
    turned = turn(cos_ref[...], -sin_ref[...], total[:, :part], total[:, part:])
    out_ref[:, : 2 * part] = jnp.concatenate(turned, axis=1).astype(jnp.bfloat16)
    out_ref[:, 2 * part :] = lane_ref[:, 2 * part :]


def place_kv(d_projected, parts, cos_part, sin_part, width_in):
    length = d_projected.shape[0]
    lanes = pl.BlockSpec((length, HD), lambda step: (0, width_in // HD - 1))

    def whole(array):
        return pl.BlockSpec(array.shape, lambda step: (0, 0))

    arrays = (cos_part, sin_part, *parts)
    return pl.pallas_call(
        place_kv_kernel,
        grid=(1,),
        in_specs=[lanes] + [whole(array) for array in arrays],
        out_specs=lanes,
        out_shape=jax.ShapeDtypeStruct(d_projected.shape, d_projected.dtype),
        input_output_aliases={0: 0},
        cost_estimate=lasting(3),
        compiler_params=pltpu.CompilerParams(vmem_limit_bytes=VMEM_BYTES),
    )(d_projected, *arrays)


def attend(kernel, arrays, out_shapes, scratch=()):
    return pl.pallas_call(
        kernel,
        in_specs=vmem_specs(len(arrays)),
        out_specs=vmem_specs(len(out_shapes)),
        out_shape=[jax.ShapeDtypeStruct(shape, dtype) for shape, dtype in out_shapes],
        scratch_shapes=[pltpu.VMEM(shape, dtype) for shape, dtype in scratch],
        cost_estimate=lasting(9),
        compiler_params=pltpu.CompilerParams(vmem_limit_bytes=VMEM_BYTES),
    )(*arrays)


def turn(cosine, sine_part, first_half, second):
    return (
        first_half * cosine - second * sine_part,
        second * cosine + first_half * sine_part,
    )


def after(value, *earlier):
    return lax.optimization_barrier((value,) + earlier)[0]


def over_chips(block):
    place = lax.axis_index("seq")
    count = lax.axis_size("seq")
    stacked = jnp.zeros((count,) + block.shape, block.dtype)
    stacked = lax.dynamic_update_index_in_dim(stacked, block, place, 0)
    for mask in range(1, count):
        moved = lax.ppermute(block, "seq", [(i, i ^ mask) for i in range(count)])
        stacked = lax.dynamic_update_index_in_dim(stacked, moved, place ^ mask, 0)
    return stacked


def from_chips(blocks):
    place = lax.axis_index("seq")
    count = lax.axis_size("seq")
    moved = [lax.dynamic_index_in_dim(blocks, place, 0, False)]
    for mask in range(1, count):
        block = lax.dynamic_index_in_dim(blocks, place ^ mask, 0, False)
        moved.append(lax.ppermute(block, "seq", [(i, i ^ mask) for i in range(count)]))
    return moved


def heads_local_plan(
    hidden_in,
    teacher,
    segment_ids,
    valid_mask,
    norm1_gain,
    w_z,
    w_x,
    w_bc,
    w_dt,
    conv_weight,
    conv_bias,
    dt_bias,
    a_log,
    d_skip,
    group_gain,
    w_mamba_out,
    w_query,
    w_key,
    w_value,
    w_attn_out,
    norm2_gain,
    w_gate,
    w_up,
    w_down,
):
    place, core, data_rank = (
        lax.axis_index("seq"),
        lax.axis_index("tensor"),
        lax.axis_index("dp"),
    )
    data_count = lax.axis_size("dp")
    chip_rows, width = hidden_in.shape[1:]
    own_rows = chip_rows // 2
    length = segment_ids.shape[1]
    slice_rows = w_z.shape[0]
    width_x = HEADS * HP
    hidden_units = w_gate.shape[1] // GROUP
    segment = segment_ids[0]
    seg_column, seg_row = segment[:, None], segment[None, :]
    own_start = place * chip_rows + core * own_rows
    token_count = jnp.sum(valid_mask).astype(jnp.float32)
    mask_rows = lax.dynamic_slice(valid_mask, (data_rank, own_start), (1, own_rows))[0]
    total_tokens = float(valid_mask.shape[0] * valid_mask.shape[1])
    bf16 = jnp.bfloat16

    half, part = HD // 2, HD // 4
    kv_columns = (
        (w_key[:, :part], w_key[:, half : half + part]),
        (w_key[:, part:half], w_key[:, half + part :]),
        (w_value[:, :half],),
        (w_value[:, half:],),
    )
    misc = jnp.stack(
        [
            jnp.concatenate(
                kv_columns[chip]
                + (
                    w_dt[:, HEADS * chip : HEADS * (chip + 1)],
                    jnp.zeros((slice_rows, half - HEADS), bf16),
                ),
                axis=1,
            )
            for chip in range(GROUP)
        ]
    )
    gains = jnp.concatenate(
        [norm1_gain[None], norm2_gain[None], jnp.zeros((6, slice_rows), bf16)]
    ).astype(jnp.float32)
    width_in = 2 * width_x + 2 * HD
    in_slices, gains_all = exchange_plane(
        (
            column_move(0, 0, 0, width_x),
            column_move(1, 0, width_x, HD),
            column_move(2, 0, width_x + HD, width_x),
            misc_move(3, 0, 2 * width_x + HD),
        ),
        (w_z, w_query, w_x, misc, gains),
        [(GROUP, slice_rows, width_in)],
        3,
        True,
    )
    gain_one, gain_two = gains_all[:, 0].reshape(width), gains_all[:, 1].reshape(width)
    full_in = lax.all_gather(in_slices, "dp", axis=0, tiled=True).reshape(width, width_in)
    hidden_own = lax.dynamic_slice(hidden_in[0], (core * own_rows, 0), (own_rows, width))
    hidden_own = after(hidden_own, in_slices)
    hidden_all = gather_plane(hidden_own)
    hidden_own = hidden_own.astype(jnp.float32)
    width_out = width_x + HD
    out_slices, gu_slices, down_slices = exchange_plane(
        (
            column_move(0, 0, 0, width_x),
            column_move(1, 0, width_x, HD),
            column_move(2, 1, 0, hidden_units),
            column_move(3, 1, hidden_units, hidden_units),
            column_move(4, 2, 0, hidden_units),
        ),
        (after(w_mamba_out.T, hidden_all), w_attn_out.T, w_gate, w_up, w_down.T),
        [
            (GROUP, slice_rows, width_out),
            (GROUP, slice_rows, 2 * hidden_units),
            (GROUP, slice_rows, hidden_units),
        ],
        4,
    )
    hidden = after(hidden_all, out_slices).astype(jnp.float32)
    out_gathered = lax.all_gather(after(out_slices, full_in), "dp", axis=0, tiled=True)
    full_out = out_gathered.reshape(width, width_out)

    scale_one = lax.rsqrt(jnp.mean(hidden * hidden, axis=-1, keepdims=True) + EPSILON)
    normed = (hidden * scale_one * gain_one).astype(bf16)
    pre_bc = mat_dot(normed, w_bc).astype(bf16)
    positions = jnp.arange(length)
    frequency = ROPE_BASE ** (-2.0 * jnp.arange(half).astype(jnp.float32) / HD)
    angles = positions.astype(jnp.float32)[:, None] * frequency[None, :]
    cosine, sine_part = jnp.cos(angles), jnp.sin(angles)
    cos_wide = jnp.concatenate([cosine, cosine], axis=1)
    sin_wide = jnp.concatenate([-sine_part, sine_part], axis=1)
    on_key = place < 2
    cos_part = lax.dynamic_slice_in_dim(cosine, part * lax.rem(place, 2), part, 1)
    sin_part = lax.dynamic_slice_in_dim(sine_part, part * lax.rem(place, 2), part, 1)
    cos_part = jnp.where(on_key, cos_part, 1.0)
    sin_part = jnp.where(on_key, sin_part, 0.0)
    head_start = core * (MH // 2) + place * HEADS

    def local_rows(values, width_head):
        return jnp.concatenate(
            [
                lax.dynamic_slice_in_dim(values, head_start * width_head, HEADS * width_head, 0),
                values[MH * width_head :],
            ],
            axis=0,
        )

    taps = jnp.concatenate(
        [local_rows(conv_weight, HP).T, local_rows(conv_bias, HP)[None]], axis=0
    )
    taps = jnp.pad(taps, ((0, 8 - KC - 1), (0, 0)))
    rate = jnp.exp(local_rows(a_log, 1))
    head_rows = jnp.zeros((8, HD), jnp.float32)
    head_rows = head_rows.at[0, DT_LANE : DT_LANE + HEADS].set(local_rows(dt_bias, 1))
    head_rows = head_rows.at[1, DT_LANE : DT_LANE + HEADS].set(rate)
    skip_row = jnp.repeat(local_rows(d_skip, 1), HP)[None, :]
    gain_row = lax.dynamic_slice_in_dim(group_gain, head_start, HEADS, 0).reshape(1, width_x)
    laps = length // CHUNK
    seg_laps = segment.reshape(laps, CHUNK)
    seg_last = seg_laps[:, -1:]
    seg_before = jnp.concatenate([jnp.full((1, 1), -1, jnp.int32), seg_last[:-1]])
    seg_ext = jnp.concatenate([jnp.full((KC - 1,), -1, jnp.int32), segment])
    keeps = [(seg_laps == seg_before).reshape(length), (seg_laps == seg_last).reshape(length)]
    keeps += [seg_ext[KC - 1 - back : KC - 1 - back + length] == segment for back in range(1, KC)]
    keeps = jnp.stack(keeps + [jnp.zeros((length,), bool)] * 3, axis=1).astype(jnp.float32)

    normed_in, pre_bc = lax.optimization_barrier((normed, pre_bc, keeps, cos_wide, sin_wide))[:2]
    projected = mat_dot(normed_in, full_in)
    full_all = jnp.concatenate([full_in, w_bc], axis=1)
    kv_raw = projected[:, 2 * width_x + HD : 2 * width_x + HD + half]
    kv_own = jnp.concatenate(
        turn(cos_part, sin_part, kv_raw[:, :part], kv_raw[:, part:]), axis=1
    ).astype(bf16)
    kv_all = over_chips(fold_rows(kv_own))

    ssd_arrays = (
        projected,
        projected,
        pre_bc,
        pre_bc,
        taps,
        head_rows,
        keeps,
        seg_column,
        seg_laps[:, None, :],
        skip_row,
        gain_row,
    )
    gated, ssm, states, mixed = ssd_forward(ssd_arrays)
    gu_gathered = lax.all_gather(after(gu_slices, out_gathered, gated), "dp", axis=0, tiled=True)
    down_gathered = lax.all_gather(after(down_slices, gu_gathered), "dp", axis=0, tiled=True)
    full_gu = gu_gathered.reshape(width, 2 * hidden_units)
    full_down = down_gathered.reshape(width, hidden_units)
    attended, log_total, queries, keys, vals = attend(
        attend_forward_kernel,
        (
            projected[:, width_x : width_x + HD],
            cos_wide,
            sin_wide,
            after(kv_all, out_gathered),
            seg_column,
            seg_row,
        ),
        (
            ((length, HD), bf16),
            ((length, 1), jnp.float32),
            ((length, HD), bf16),
            ((length, HD), bf16),
            ((length, HD), bf16),
        ),
    )
    outs = jnp.concatenate([gated, attended], axis=1)
    middle = hidden_own + scatter_plane(outs, full_out, 2)[0]

    scale_two = lax.rsqrt(jnp.mean(middle * middle, axis=-1, keepdims=True) + EPSILON)
    normed_two, gate_up, activated = gather_plane(
        after((middle * scale_two * gain_two).astype(bf16), gu_gathered, full_all),
        9,
        apply_gate_up,
        (full_gu,),
        (((length, 2 * hidden_units), jnp.float32), ((length, hidden_units), bf16)),
    )
    block_out = middle + scatter_plane(activated, full_down, 2)[0]
    teacher_own = lax.dynamic_slice(teacher[0], (core * own_rows, 0), (own_rows, width))
    d_out = (
        2.0
        * total_tokens
        / token_count
        * mask_rows.astype(jnp.float32)[:, None]
        * (block_out - teacher_own.astype(jnp.float32))
    )
    d_mlp, d_gate_up = gather_plane(
        d_out.astype(bf16),
        10,
        apply_down_back,
        (full_down, gate_up),
        (((length, 2 * hidden_units), bf16),),
    )

    def sum_rows(grads):
        summed = lax.psum_scatter(grads.astype(bf16), "dp", scatter_dimension=0, tiled=True)
        return summed.reshape(GROUP, slice_rows, grads.shape[1])

    grad_down = sum_rows(dot_left_t(d_mlp, activated))
    d_normed_two = scatter_plane(d_gate_up, full_gu, 11)[0]
    grad_gate_up = sum_rows(
        after(dot_left_t(normed_two, d_gate_up).astype(bf16), grad_down, d_normed_two)
    )
    grad_gain_two = jnp.sum(d_normed_two * middle * scale_two, axis=0)
    d_scaled = d_normed_two * gain_two
    d_middle = (
        d_out
        + scale_two * d_scaled
        - middle * scale_two**3 * jnp.mean(d_scaled * middle, axis=-1, keepdims=True)
    )
    d_branch, d_outs = gather_plane(
        after(d_middle.astype(bf16), grad_down),
        12,
        apply_out_back,
        (full_out,),
        (((length, width_out), jnp.float32),),
    )
    d_query, d_kv = attend(
        attend_backward_kernel,
        (
            queries,
            keys,
            vals,
            cos_wide,
            sin_wide,
            seg_column,
            seg_row,
            log_total,
            d_outs[:, width_x:],
        ),
        (((length, HD), bf16), ((GROUP, length // 2, HD), bf16)),
        (((length, HD), jnp.float32),) * 3,
    )
    d_kv_parts = from_chips(d_kv)
    grad_out = sum_rows(
        after(dot_left_t(d_branch, outs).astype(bf16), grad_gate_up, d_query)
    )
    d_projected, grad_taps, grad_heads, d_skip_lanes, d_gain_lanes = ssd_backward(
        ssd_arrays, mixed, ssm, states, after(d_outs, grad_gate_up), d_query
    )
    d_kv_parts = lax.optimization_barrier((d_projected, *d_kv_parts))[1:]
    d_projected = place_kv(d_projected, d_kv_parts, cos_part, sin_part, width_in)
    grad_skip = jnp.sum(d_skip_lanes.reshape(HEADS, HP), axis=-1)
    grad_group = d_gain_lanes.reshape(HEADS, HP)
    grad_in = sum_rows(
        after(dot_left_t(normed, d_projected[:, :width_in]).astype(bf16), grad_out)
    )
    bc_cols = 2 * NS // GROUP
    d_normed, bc_sum = scatter_plane(
        after(d_projected, grad_out), full_all, 8, ((normed, bc_cols, width // 2),)
    )
    scale_own = lax.rsqrt(jnp.mean(hidden_own * hidden_own, axis=-1, keepdims=True) + EPSILON)
    grad_gain_one = jnp.sum(d_normed * hidden_own * scale_own, axis=0)
    d_scaled_one = d_normed * gain_one
    grad_input = (
        d_middle
        + scale_own * d_scaled_one
        - hidden_own * scale_own**3 * jnp.mean(d_scaled_one * hidden_own, axis=-1, keepdims=True)
    )
    taps_all = jnp.concatenate(
        [
            lax.dynamic_update_slice(
                jnp.zeros((8, MH * HP), jnp.float32), grad_taps[:, :width_x], (0, head_start * HP)
            ),
            grad_taps[:, width_x:],
        ],
        axis=1,
    )
    heads_all = lax.dynamic_update_slice(
        jnp.zeros((8, 128), jnp.float32),
        jnp.concatenate([grad_heads[:2, DT_LANE : DT_LANE + HEADS], grad_skip[None]]),
        (0, head_start),
    )
    group_all = lax.dynamic_update_slice(
        jnp.zeros((MH, HP), jnp.float32), grad_group, (head_start, 0)
    )
    small = [taps_all, heads_all]
    small += [
        values.reshape(8, -1) for values in (grad_gain_one, grad_gain_two, group_all)
    ]
    small = jnp.concatenate(small, axis=1)
    small_width = -(-small.shape[1] // (2 * GROUP * 128)) * 2 * GROUP * 128
    small = jnp.pad(small, ((0, 0), (0, small_width - small.shape[1])))
    summed, bc_all, both_input, both_output, *back = finish_all(
        small,
        bc_sum,
        grad_input,
        block_out.astype(bf16),
        [grad_gate_up, grad_down, grad_out],
    )
    (back_in,) = exchange_plane(
        (block_move(0, 0),), (after(grad_in, both_input),), [grad_in.shape], 6
    )
    width_taps = MH * HP + 2 * NS
    sum_taps = summed[:, :width_taps]
    sum_heads = summed[:, width_taps : width_taps + 128]
    summed = summed[:, width_taps + 128 :]
    sum_one = summed[:, : width // 8].reshape(width)
    sum_two = summed[:, width // 8 : width // 4].reshape(width)
    sum_group = summed[:, width // 4 :][:, : MH * HP // 8].reshape(MH, HP)
    gain_start = (data_rank * GROUP + place) * slice_rows

    (
        grad_gate,
        grad_up,
        grad_down,
        grad_mo,
        grad_ao,
        grad_z,
        grad_x,
        grad_q,
        grad_k,
        grad_v,
        grad_dt,
        grad_bc,
        grad_conv,
    ) = attend(
        unpack_kernel,
        (*back, back_in, bc_all.reshape(2 * GROUP, bc_cols, width // 2), sum_taps),
        [
            (array.shape, jnp.float32)
            for array in (
                w_gate,
                w_up,
                w_down,
                w_mamba_out,
                w_attn_out,
                w_z,
                w_x,
                w_query,
                w_key,
                w_value,
                w_dt,
                w_bc,
                conv_weight,
            )
        ],
    )
    return (
        both_output.reshape(1, chip_rows, width),
        both_input.reshape(1, chip_rows, width),
        lax.dynamic_slice_in_dim(sum_one, gain_start, slice_rows),
        grad_z,
        grad_x,
        grad_bc,
        grad_dt,
        grad_conv,
        sum_taps[KC],
        sum_heads[0, :MH],
        sum_heads[1, :MH],
        sum_heads[2, :MH],
        sum_group,
        grad_mo,
        grad_q,
        grad_k,
        grad_v,
        grad_ao,
        lax.dynamic_slice_in_dim(sum_two, gain_start, slice_rows),
        grad_gate,
        grad_up,
        grad_down,
    )


def solution(mesh):
    placed = (
        P("dp", "seq", None),
        P("dp", "seq", None),
        P("dp", None),
        P(),
        P(("dp", "seq")),
        P(("dp", "seq"), "tensor"),
        P(("dp", "seq"), "tensor"),
        P(),
        P(("dp", "seq"), "tensor"),
        P(),
        P(),
        P(),
        P(),
        P(),
        P(),
        P("tensor", ("dp", "seq")),
        P(("dp", "seq"), "tensor"),
        P(("dp", "seq"), "tensor"),
        P(("dp", "seq"), "tensor"),
        P("tensor", ("dp", "seq")),
        P(("dp", "seq")),
        P(("dp", "seq"), "tensor"),
        P(("dp", "seq"), "tensor"),
        P("tensor", ("dp", "seq")),
    )
    whole_row = mesh.shape["seq"] == GROUP and mesh.shape["tensor"] == 2
    return jax.shard_map(
        heads_local_plan if whole_row else local,
        mesh=mesh,
        in_specs=placed,
        out_specs=(
            P("dp", "seq", None),
            P("dp", "seq", None),
            P(("dp", "seq")),
            P(("dp", "seq"), "tensor"),
            P(("dp", "seq"), "tensor"),
            P(),
            P(("dp", "seq"), "tensor"),
            P(),
            P(),
            P(),
            P(),
            P(),
            P(),
            P("tensor", ("dp", "seq")),
            P(("dp", "seq"), "tensor"),
            P(("dp", "seq"), "tensor"),
            P(("dp", "seq"), "tensor"),
            P("tensor", ("dp", "seq")),
            P(("dp", "seq")),
            P(("dp", "seq"), "tensor"),
            P(("dp", "seq"), "tensor"),
            P("tensor", ("dp", "seq")),
        ),
        check_vma=False,
    )
```

```python
from functools import partial

import jax
import jax.numpy as jnp
import numpy as np
from jax import lax
from jax.experimental import pallas as pl
from jax.experimental.pallas import tpu as pltpu
from jax.sharding import PartitionSpec as P

MH = 48
HP = 64
NS = 256
KC = 4
HD = 128


EPSILON = 1e-06
GROUP_EPSILON = 1e-05
ROPE_BASE = 10000.0
HIGHEST = lax.Precision.HIGHEST


def shifted(block, axis, distance):
    devices = range(lax.axis_size(axis))
    route = [(i - distance, i) for i in devices if i - distance in devices]
    return lax.ppermute(block, axis, route)


def carried_in(part, axis, combine, identity, reverse):
    count = lax.axis_size(axis)
    place = lax.axis_index(axis)
    ahead = count - 1 - place if reverse else place
    gathered = jax.tree.map(lambda a: lax.all_gather(a, axis), part)
    state = jax.tree.map(lambda a, e: jnp.zeros_like(a) + jnp.asarray(e, a.dtype), part, identity)

    def one(lap, state):
        source = count - 1 - lap if reverse else lap
        return combine(
            state, jax.tree.map(lambda a: lax.dynamic_index_in_dim(a, source, 0, False), gathered)
        )

    return lax.fori_loop(0, ahead, one, state)


def mat_dot(left_side, right_side):
    return jnp.dot(left_side, right_side, preferred_element_type=jnp.float32)


def dot_left_t(left_side, right_side):
    return lax.dot_general(
        left_side, right_side, (((0,), (0,)), ((), ())), preferred_element_type=jnp.float32
    )


def dot_right_t(left_side, right_side):
    return lax.dot_general(
        left_side, right_side, (((1,), (1,)), ((), ())), preferred_element_type=jnp.float32
    )


def rms_norm(values, gain_row):
    scale_row = lax.rsqrt(jnp.mean(values * values, axis=-1, keepdims=True) + EPSILON)
    return values * scale_row * gain_row


def rotate(positions, values):
    half_dim = values.shape[-1] // 2
    frequency = ROPE_BASE ** (-2.0 * jnp.arange(half_dim).astype(jnp.float32) / values.shape[-1])
    angles = positions.astype(jnp.float32)[:, None] * frequency[None, :]
    cosine = jnp.cos(angles)[:, None, :]
    sine_part = jnp.sin(angles)[:, None, :]
    first_half = values[..., :half_dim]
    second = values[..., half_dim:]
    return jnp.concatenate(
        [first_half * cosine - second * sine_part, second * cosine + first_half * sine_part],
        axis=-1,
    )


def conv_silu(seg_ext, seg_rows, extended, weights, bias_row):
    size_rows = seg_rows.shape[0]
    summed = jnp.zeros((size_rows, weights.shape[0]), jnp.float32) + bias_row[None, :]
    for tap_index in range(weights.shape[1]):
        window = lax.slice_in_dim(extended, tap_index, tap_index + size_rows, axis=0)
        keep_mask = (
            lax.slice_in_dim(seg_ext, tap_index, tap_index + size_rows) == seg_rows
        ).astype(jnp.float32)
        summed = summed + window * weights[:, tap_index][None, :] * keep_mask[:, None]
    return jax.nn.silu(summed)


def group_gate(ssm_out, gate_z, group_gain):
    mixed_val = ssm_out * jax.nn.silu(gate_z)
    return (
        mixed_val
        * lax.rsqrt(jnp.mean(mixed_val * mixed_val, axis=-1, keepdims=True) + GROUP_EPSILON)
        * group_gain[None]
    )


def swiglu(gate_pre, up_pre):
    return jax.nn.silu(gate_pre) * up_pre


def split_mixed(mixed_in, heads_local):
    size_rows = mixed_in.shape[0]
    width_x = heads_local * HP
    heads_x = mixed_in[:, :width_x].reshape(size_rows, heads_local, HP)
    return (heads_x, mixed_in[:, width_x : width_x + NS], mixed_in[:, width_x + NS :])


def ssd_main(seg_rows, seg_before, mixed_in, dt_raw, dt_bias_row, a_log_row, d_skip_row):
    size_rows = seg_rows.shape[0]
    heads_x, b_rows, c_rows = split_mixed(mixed_in, dt_raw.shape[1])
    dt_rows = jax.nn.softplus(dt_raw + dt_bias_row[None, :])
    cumul = jnp.cumsum(-jnp.exp(a_log_row)[None, :] * dt_rows, axis=0)
    order_pos = jnp.arange(size_rows)
    allowed = (seg_rows[:, None] == seg_rows[None, :]) & (order_pos[:, None] >= order_pos[None, :])
    differ = cumul[:, None, :] - cumul[None, :, :]
    decay = jnp.exp(jnp.where(allowed[:, :, None], differ, -jnp.inf))
    gram = jnp.dot(c_rows, b_rows.T, precision=HIGHEST, preferred_element_type=jnp.float32)
    mixing = gram[:, :, None] * decay * dt_rows[None, :, :]
    outputs = jnp.einsum("tsh,shp->thp", mixing, heads_x, precision=HIGHEST)
    outputs = outputs + d_skip_row[None, :, None] * heads_x
    tail_keep = (seg_rows == seg_rows[-1]).astype(jnp.float32)
    tail_weight = jnp.exp(cumul[-1][None, :] - cumul) * tail_keep[:, None] * dt_rows
    local_state = jnp.einsum("sh,shp,sn->hpn", tail_weight, heads_x, b_rows, precision=HIGHEST)
    carry_factor = jnp.exp(cumul[-1]) * (seg_rows[-1] == seg_before).astype(jnp.float32)
    return (outputs, carry_factor, local_state)


def ssd_state(seg_rows, seg_before, mixed_in, dt_raw, dt_bias_row, a_log_row, entry_state):
    heads_x, b_rows, c_rows = split_mixed(mixed_in, dt_raw.shape[1])
    dt_rows = jax.nn.softplus(dt_raw + dt_bias_row[None, :])
    cumul = jnp.cumsum(-jnp.exp(a_log_row)[None, :] * dt_rows, axis=0)
    entry_keep = (seg_rows == seg_before).astype(jnp.float32)
    entry_part = jnp.einsum("tn,hpn->thp", c_rows, entry_state, precision=HIGHEST)
    return jnp.exp(cumul)[:, :, None] * entry_keep[:, None, None] * entry_part


def chain_states(earlier, later):
    return (earlier[0] * later[0], later[0][:, None, None] * earlier[1] + later[1])


def block_scores(queries, keys_all, vals_all, seg_full, query_pos, seg_query, block_index, key_len):
    key_blk = keys_all[block_index * key_len : (block_index + 1) * key_len]
    val_blk = vals_all[block_index * key_len : (block_index + 1) * key_len]
    seg_key = seg_full[block_index * key_len : (block_index + 1) * key_len]
    key_pos = block_index * key_len + jnp.arange(key_len)
    scores = jnp.einsum(
        "tkgd,skd->kgts", queries, key_blk, preferred_element_type=jnp.float32
    ) * HD ** (-0.5)
    allowed = (query_pos[:, None] >= key_pos[None, :]) & (seg_query[:, None] == seg_key[None, :])
    return (key_blk, val_blk, jnp.where(allowed[None, None], scores, -jnp.inf))


def attend_forward(queries, keys_all, vals_all, seg_full, query_pos, seg_query, block_count):
    key_len = keys_all.shape[0] // block_count
    stat_shape = (queries.shape[1], queries.shape[2], queries.shape[0])
    running_max = jnp.full(stat_shape, -1e30, jnp.float32)
    running_sum = jnp.zeros(stat_shape, jnp.float32)
    for block_index in range(block_count):
        needed = block_index * key_len <= query_pos[-1]

        def stat_step(stats, block_index=block_index):
            old_max, old_sum = stats
            key_blk, val_blk, scores = block_scores(
                queries, keys_all, vals_all, seg_full, query_pos, seg_query, block_index, key_len
            )
            new_max = jnp.maximum(old_max, jnp.max(scores, axis=-1))
            new_sum = old_sum * jnp.exp(old_max - new_max) + jnp.sum(
                jnp.exp(scores - new_max[..., None]), axis=-1
            )
            return (new_max, new_sum)

        running_max, running_sum = lax.cond(
            needed, stat_step, lambda stats: stats, (running_max, running_sum)
        )
    log_total = running_max + jnp.log(running_sum)
    attended = jnp.zeros(queries.shape, jnp.float32)
    for block_index in range(block_count):
        needed = block_index * key_len <= query_pos[-1]

        def value_step(total, block_index=block_index):
            key_blk, val_blk, scores = block_scores(
                queries, keys_all, vals_all, seg_full, query_pos, seg_query, block_index, key_len
            )
            probs = jnp.exp(scores - log_total[..., None]).astype(jnp.bfloat16)
            return total + jnp.einsum(
                "kgts,skd->tkgd", probs, val_blk, preferred_element_type=jnp.float32
            )

        attended = lax.cond(needed, value_step, lambda total: total, attended)
    return (log_total, attended)


def attend_backward(
    queries, keys_all, vals_all, seg_full, query_pos, seg_query, block_count, grad_out, log_total
):
    key_len = keys_all.shape[0] // block_count
    delta = jnp.zeros(log_total.shape, jnp.float32)
    for block_index in range(block_count):
        needed = block_index * key_len <= query_pos[-1]

        def delta_step(total, block_index=block_index):
            key_blk, val_blk, scores = block_scores(
                queries, keys_all, vals_all, seg_full, query_pos, seg_query, block_index, key_len
            )
            probs = jnp.exp(scores - log_total[..., None])
            grad_probs = jnp.einsum(
                "tkgd,skd->kgts", grad_out, val_blk, preferred_element_type=jnp.float32
            )
            return total + jnp.sum(probs * grad_probs, axis=-1)

        delta = lax.cond(needed, delta_step, lambda total: total, delta)
    grad_query = jnp.zeros(queries.shape, jnp.float32)
    empty_part = jnp.zeros((key_len, keys_all.shape[1], keys_all.shape[2]), jnp.float32)
    key_parts = []
    val_parts = []
    for block_index in range(block_count):
        needed = block_index * key_len <= query_pos[-1]

        def grad_step(total, block_index=block_index):
            key_blk, val_blk, scores = block_scores(
                queries, keys_all, vals_all, seg_full, query_pos, seg_query, block_index, key_len
            )
            probs = jnp.exp(scores - log_total[..., None])
            grad_probs = jnp.einsum(
                "tkgd,skd->kgts", grad_out, val_blk, preferred_element_type=jnp.float32
            )
            grad_scores = (probs * (grad_probs - delta[..., None])).astype(jnp.bfloat16)
            new_total = total + jnp.einsum(
                "kgts,skd->tkgd", grad_scores, key_blk, preferred_element_type=jnp.float32
            ) * HD ** (-0.5)
            key_part = jnp.einsum(
                "kgts,tkgd->skd", grad_scores, queries, preferred_element_type=jnp.float32
            ) * HD ** (-0.5)
            val_part = jnp.einsum(
                "kgts,tkgd->skd",
                probs.astype(jnp.bfloat16),
                grad_out,
                preferred_element_type=jnp.float32,
            )
            return (new_total, key_part, val_part)

        grad_query, key_part, val_part = lax.cond(
            needed, grad_step, lambda total: (total, empty_part, empty_part), grad_query
        )
        key_parts.append(key_part)
        val_parts.append(val_part)
    return (grad_query, jnp.concatenate(key_parts, axis=0), jnp.concatenate(val_parts, axis=0))


def local(
    hidden_in,
    teacher,
    segment_ids,
    valid_mask,
    norm1_gain,
    w_z,
    w_x,
    w_bc,
    w_dt,
    conv_weight,
    conv_bias,
    dt_bias,
    a_log,
    d_skip,
    group_gain,
    w_mamba_out,
    w_query,
    w_key,
    w_value,
    w_attn_out,
    norm2_gain,
    w_gate,
    w_up,
    w_down,
):
    tensor_rank = lax.axis_index("tensor")
    seq_rank = lax.axis_index("seq")
    data_rank = lax.axis_index("dp")
    seq_count = lax.axis_size("seq")
    tensor_count = lax.axis_size("tensor")
    size_rows = hidden_in.shape[1]
    full_length = segment_ids.shape[1]
    row_start = seq_rank * size_rows
    seg_full = segment_ids[0]
    seg_local = lax.dynamic_slice_in_dim(seg_full, row_start, size_rows)
    seg_padded = jnp.concatenate([jnp.full((KC - 1,), -1, jnp.int32), seg_full])
    seg_ext = lax.dynamic_slice_in_dim(seg_padded, row_start, size_rows + KC - 1)
    seg_prev = lax.dynamic_index_in_dim(seg_padded, row_start + KC - 2, keepdims=False)
    token_count = jnp.sum(valid_mask).astype(jnp.float32)
    mask_rows = lax.dynamic_slice(valid_mask, (data_rank, row_start), (1, size_rows))[0].astype(
        jnp.float32
    )
    total_tokens = float(valid_mask.shape[0] * valid_mask.shape[1])
    (
        gain_one,
        full_z,
        full_x,
        full_dt,
        full_mo,
        full_q,
        full_k,
        full_v,
        full_ao,
        gain_two,
        full_gate,
        full_up,
        full_down,
    ) = (
        lax.all_gather(norm1_gain, ("dp", "seq"), axis=0, tiled=True),
        lax.all_gather(w_z, ("dp", "seq"), axis=0, tiled=True),
        lax.all_gather(w_x, ("dp", "seq"), axis=0, tiled=True),
        lax.all_gather(w_dt, ("dp", "seq"), axis=0, tiled=True),
        lax.all_gather(w_mamba_out, ("dp", "seq"), axis=1, tiled=True),
        lax.all_gather(w_query, ("dp", "seq"), axis=0, tiled=True),
        lax.all_gather(w_key, ("dp", "seq"), axis=0, tiled=True),
        lax.all_gather(w_value, ("dp", "seq"), axis=0, tiled=True),
        lax.all_gather(w_attn_out, ("dp", "seq"), axis=1, tiled=True),
        lax.all_gather(norm2_gain, ("dp", "seq"), axis=0, tiled=True),
        lax.all_gather(w_gate, ("dp", "seq"), axis=0, tiled=True),
        lax.all_gather(w_up, ("dp", "seq"), axis=0, tiled=True),
        lax.all_gather(w_down, ("dp", "seq"), axis=1, tiled=True),
    )
    heads_local = MH // tensor_count
    width_x = heads_local * HP
    head_start = tensor_rank * heads_local
    hidden = hidden_in[0].astype(jnp.float32)
    normed_f, norm_one_pull = jax.vjp(rms_norm, hidden, gain_one.astype(jnp.float32))
    normed = normed_f.astype(jnp.bfloat16)
    gate_z = mat_dot(normed, full_z)
    pre_x = mat_dot(normed, full_x).astype(jnp.bfloat16)
    pre_bc = mat_dot(normed, w_bc).astype(jnp.bfloat16)
    dt_raw = mat_dot(normed, full_dt)
    pre_all = jnp.concatenate([pre_x, pre_bc], axis=1)
    rim_rows = shifted(pre_all[size_rows - (KC - 1) :], "seq", 1)
    extended = jnp.concatenate([rim_rows, pre_all], axis=0).astype(jnp.float32)
    conv_local = jnp.concatenate(
        [
            lax.dynamic_slice_in_dim(conv_weight, head_start * HP, width_x, 0),
            conv_weight[MH * HP :],
        ],
        axis=0,
    )
    bias_local = jnp.concatenate(
        [lax.dynamic_slice_in_dim(conv_bias, head_start * HP, width_x, 0), conv_bias[MH * HP :]],
        axis=0,
    )
    mixed_f, conv_pull = jax.vjp(
        partial(conv_silu, seg_ext, seg_local), extended, conv_local, bias_local
    )
    mixed_in = lax.optimization_barrier(mixed_f.astype(jnp.bfloat16)).astype(jnp.float32)
    dt_bias_loc = lax.dynamic_slice_in_dim(dt_bias, head_start, heads_local)
    a_log_loc = lax.dynamic_slice_in_dim(a_log, head_start, heads_local)
    d_skip_loc = lax.dynamic_slice_in_dim(d_skip, head_start, heads_local)
    group_loc = lax.dynamic_slice_in_dim(group_gain, head_start, heads_local, 0)
    (ssm_local, carry_dev, state_dev), main_pull = jax.vjp(
        partial(ssd_main, seg_local, seg_prev), mixed_in, dt_raw, dt_bias_loc, a_log_loc, d_skip_loc
    )
    identity = (jnp.ones_like(carry_dev), jnp.zeros_like(state_dev))
    entry_state = carried_in((carry_dev, state_dev), "seq", chain_states, identity, False)[1]
    ssm_entry, state_pull = jax.vjp(
        partial(ssd_state, seg_local, seg_prev),
        mixed_in,
        dt_raw,
        dt_bias_loc,
        a_log_loc,
        entry_state,
    )
    ssm_out = ssm_local + ssm_entry
    gated_f, gate_pull = jax.vjp(
        group_gate, ssm_out, gate_z.reshape(size_rows, heads_local, HP), group_loc
    )
    gated = gated_f.reshape(size_rows, width_x).astype(jnp.bfloat16)
    mamba_part = mat_dot(gated, full_mo)
    positions = row_start + jnp.arange(size_rows)
    heads_q = full_q.shape[1] // HD
    heads_kv = full_k.shape[1] // HD
    groups = heads_q // heads_kv
    query_rot, query_pull = jax.vjp(
        partial(rotate, positions), mat_dot(normed, full_q).reshape(size_rows, heads_q, HD)
    )
    queries = query_rot.astype(jnp.bfloat16).reshape(size_rows, heads_kv, groups, HD)
    key_rot, key_pull = jax.vjp(
        partial(rotate, positions), mat_dot(normed, full_k).reshape(size_rows, heads_kv, HD)
    )
    keys_local = key_rot.astype(jnp.bfloat16).reshape(size_rows, heads_kv * HD)
    vals_local = mat_dot(normed, full_v).astype(jnp.bfloat16)
    keys_all, vals_all = (
        lax.all_gather(keys_local, "seq", axis=0, tiled=True),
        lax.all_gather(vals_local, "seq", axis=0, tiled=True),
    )
    keys_all = keys_all.reshape(full_length, heads_kv, HD)
    vals_all = vals_all.reshape(full_length, heads_kv, HD)
    block_count = seq_count // 4
    log_total, attended_f = attend_forward(
        queries, keys_all, vals_all, seg_full, positions, seg_local, block_count
    )
    attended = attended_f.reshape(size_rows, heads_q * HD).astype(jnp.bfloat16)
    branch = lax.psum(mamba_part + mat_dot(attended, full_ao), "tensor")
    middle = hidden + branch
    normed_two_f, norm_two_pull = jax.vjp(rms_norm, middle, gain_two.astype(jnp.float32))
    normed_two = normed_two_f.astype(jnp.bfloat16)
    act_f, glu_pull = jax.vjp(swiglu, mat_dot(normed_two, full_gate), mat_dot(normed_two, full_up))
    activated = act_f.astype(jnp.bfloat16)
    block_out = middle + lax.psum(mat_dot(activated, full_down), "tensor")
    (
        back_z,
        back_x,
        back_dt,
        back_mo,
        back_q,
        back_k,
        back_v,
        back_ao,
        back_gate,
        back_up,
        back_down,
    ) = (
        lax.all_gather(w_z, ("dp", "seq"), axis=0, tiled=True),
        lax.all_gather(w_x, ("dp", "seq"), axis=0, tiled=True),
        lax.all_gather(w_dt, ("dp", "seq"), axis=0, tiled=True),
        lax.all_gather(w_mamba_out, ("dp", "seq"), axis=1, tiled=True),
        lax.all_gather(w_query, ("dp", "seq"), axis=0, tiled=True),
        lax.all_gather(w_key, ("dp", "seq"), axis=0, tiled=True),
        lax.all_gather(w_value, ("dp", "seq"), axis=0, tiled=True),
        lax.all_gather(w_attn_out, ("dp", "seq"), axis=1, tiled=True),
        lax.all_gather(w_gate, ("dp", "seq"), axis=0, tiled=True),
        lax.all_gather(w_up, ("dp", "seq"), axis=0, tiled=True),
        lax.all_gather(w_down, ("dp", "seq"), axis=1, tiled=True),
    )
    d_out = (
        2.0
        * total_tokens
        / token_count
        * mask_rows[:, None]
        * (block_out - teacher[0].astype(jnp.float32))
    )
    d_mlp = d_out.astype(jnp.bfloat16)
    grad_down = dot_left_t(activated, d_mlp)
    d_gate_f, d_up_f = glu_pull(dot_right_t(d_mlp, back_down))
    d_gate = d_gate_f.astype(jnp.bfloat16)
    d_up = d_up_f.astype(jnp.bfloat16)
    grad_gate = dot_left_t(normed_two, d_gate)
    grad_up = dot_left_t(normed_two, d_up)
    d_normed_two = lax.psum(dot_right_t(d_gate, back_gate) + dot_right_t(d_up, back_up), "tensor")
    d_middle_n, grad_gain_two = norm_two_pull(d_normed_two)
    d_middle = d_out + d_middle_n
    d_branch = d_middle.astype(jnp.bfloat16)
    grad_ao = dot_left_t(attended, d_branch)
    grad_mo = dot_left_t(gated, d_branch)
    d_attended = (
        dot_right_t(d_branch, back_ao).astype(jnp.bfloat16).reshape(size_rows, heads_kv, groups, HD)
    )
    d_gated = dot_right_t(d_branch, back_mo).reshape(size_rows, heads_local, HP)
    d_ssm, d_gate_z_f, grad_group = gate_pull(d_gated)
    d_gate_z = d_gate_z_f.reshape(size_rows, width_x).astype(jnp.bfloat16)
    d_mixed_s, d_dt_s, d_dtb_s, d_alog_s, d_entry = state_pull(d_ssm)
    state_grad = carried_in((carry_dev, d_entry), "seq", chain_states, identity, True)[1]
    d_carry = jnp.sum(state_grad * entry_state, axis=(1, 2))
    d_mixed_m, d_dt_m, d_dtb_m, d_alog_m, grad_skip = main_pull((d_ssm, d_carry, state_grad))
    d_dt_raw = (d_dt_s + d_dt_m).astype(jnp.bfloat16)
    d_ext, grad_conv_loc, grad_bias_loc = conv_pull(d_mixed_s + d_mixed_m)
    rim_grad = shifted(d_ext[: KC - 1], "seq", -1)
    d_pre = d_ext[KC - 1 :] + jnp.pad(rim_grad, ((size_rows - (KC - 1), 0), (0, 0)))
    d_pre_x = d_pre[:, :width_x].astype(jnp.bfloat16)
    d_pre_bc = d_pre[:, width_x:]
    grad_query_rot, key_grads_all, val_grads_all = attend_backward(
        queries,
        keys_all,
        vals_all,
        seg_full,
        positions,
        seg_local,
        block_count,
        d_attended,
        log_total,
    )
    key_grad, val_grad = (
        lax.psum_scatter(
            key_grads_all.reshape(full_length, heads_kv * HD).astype(jnp.bfloat16),
            "seq",
            scatter_dimension=0,
            tiled=True,
        ).astype(jnp.float32),
        lax.psum_scatter(
            val_grads_all.reshape(full_length, heads_kv * HD).astype(jnp.bfloat16),
            "seq",
            scatter_dimension=0,
            tiled=True,
        ).astype(jnp.float32),
    )
    d_query = (
        query_pull(grad_query_rot.reshape(size_rows, heads_q, HD))[0]
        .reshape(size_rows, heads_q * HD)
        .astype(jnp.bfloat16)
    )
    d_key = (
        key_pull(key_grad.reshape(size_rows, heads_kv, HD))[0]
        .reshape(size_rows, heads_kv * HD)
        .astype(jnp.bfloat16)
    )
    d_value = val_grad.astype(jnp.bfloat16)
    grad_z = dot_left_t(normed, d_gate_z)
    grad_x = dot_left_t(normed, d_pre_x)
    grad_dt = dot_left_t(normed, d_dt_raw)
    grad_q = dot_left_t(normed, d_query)
    grad_k = dot_left_t(normed, d_key)
    grad_v = dot_left_t(normed, d_value)
    normed_wide = normed.astype(jnp.float32)
    bc_weight = w_bc.astype(jnp.float32)
    grad_bc = jnp.dot(
        normed_wide.T, d_pre_bc, precision=HIGHEST, preferred_element_type=jnp.float32
    )
    d_normed_part = (
        dot_right_t(d_gate_z, back_z)
        + dot_right_t(d_pre_x, back_x)
        + dot_right_t(d_dt_raw, back_dt)
        + dot_right_t(d_query, back_q)
        + dot_right_t(d_key, back_k)
        + dot_right_t(d_value, back_v)
        + jnp.dot(d_pre_bc, bc_weight.T, precision=HIGHEST, preferred_element_type=jnp.float32)
    )
    d_normed = lax.psum(d_normed_part.astype(jnp.bfloat16), "tensor").astype(jnp.float32)
    d_hidden_n, grad_gain_one = norm_one_pull(d_normed)
    grad_input = d_middle + d_hidden_n
    conv_x_full = lax.dynamic_update_slice_in_dim(
        jnp.zeros((MH * HP, KC), jnp.float32), grad_conv_loc[:width_x], head_start * HP, 0
    )
    grad_conv_full = jnp.concatenate([conv_x_full, grad_conv_loc[width_x:]], axis=0)
    bias_x_full = lax.dynamic_update_slice_in_dim(
        jnp.zeros((MH * HP,), jnp.float32), grad_bias_loc[:width_x], head_start * HP, 0
    )
    grad_bias_full = jnp.concatenate([bias_x_full, grad_bias_loc[width_x:]], axis=0)
    grad_dtb_full = lax.dynamic_update_slice_in_dim(
        jnp.zeros((MH,), jnp.float32), d_dtb_s + d_dtb_m, head_start, 0
    )
    grad_alog_full = lax.dynamic_update_slice_in_dim(
        jnp.zeros((MH,), jnp.float32), d_alog_s + d_alog_m, head_start, 0
    )
    grad_skip_full = lax.dynamic_update_slice_in_dim(
        jnp.zeros((MH,), jnp.float32), grad_skip, head_start, 0
    )
    grad_group_full = lax.dynamic_update_slice_in_dim(
        jnp.zeros((MH, HP), jnp.float32), grad_group, head_start, 0
    )
    sum_bc, sum_conv, sum_bias, sum_dtb, sum_alog, sum_skip, sum_group = lax.psum(
        (
            grad_bc,
            grad_conv_full,
            grad_bias_full,
            grad_dtb_full,
            grad_alog_full,
            grad_skip_full,
            grad_group_full,
        ),
        ("dp", "seq", "tensor"),
    )
    (
        out_gain_one,
        out_z,
        out_x,
        out_dt,
        out_mo,
        out_q,
        out_k,
        out_v,
        out_ao,
        out_gain_two,
        out_gate,
        out_up,
        out_down,
    ) = (
        lax.psum_scatter(grad_gain_one, ("dp", "seq"), scatter_dimension=0, tiled=True),
        lax.psum_scatter(grad_z, ("dp", "seq"), scatter_dimension=0, tiled=True),
        lax.psum_scatter(grad_x, ("dp", "seq"), scatter_dimension=0, tiled=True),
        lax.psum_scatter(grad_dt, ("dp", "seq"), scatter_dimension=0, tiled=True),
        lax.psum_scatter(grad_mo, ("dp", "seq"), scatter_dimension=1, tiled=True),
        lax.psum_scatter(grad_q, ("dp", "seq"), scatter_dimension=0, tiled=True),
        lax.psum_scatter(grad_k, ("dp", "seq"), scatter_dimension=0, tiled=True),
        lax.psum_scatter(grad_v, ("dp", "seq"), scatter_dimension=0, tiled=True),
        lax.psum_scatter(grad_ao, ("dp", "seq"), scatter_dimension=1, tiled=True),
        lax.psum_scatter(grad_gain_two, ("dp", "seq"), scatter_dimension=0, tiled=True),
        lax.psum_scatter(grad_gate, ("dp", "seq"), scatter_dimension=0, tiled=True),
        lax.psum_scatter(grad_up, ("dp", "seq"), scatter_dimension=0, tiled=True),
        lax.psum_scatter(grad_down, ("dp", "seq"), scatter_dimension=1, tiled=True),
    )
    return (
        block_out.astype(jnp.bfloat16)[None],
        grad_input[None],
        out_gain_one,
        out_z,
        out_x,
        sum_bc,
        out_dt,
        sum_conv,
        sum_bias,
        sum_dtb,
        sum_alog,
        sum_skip,
        sum_group,
        out_mo,
        out_q,
        out_k,
        out_v,
        out_ao,
        out_gain_two,
        out_gate,
        out_up,
        out_down,
    )


GROUP = 4
CHUNK = 256
HEADS = 6
MESH_ID = pl.DeviceIdType.MESH
VMEM_BYTES = 56 * 1024 * 1024


def dot_f32(left_side, right_side, left_dim, right_dim):
    return lax.dot_general(
        left_side,
        right_side,
        (((left_dim,), (right_dim,)), ((), ())),
        preferred_element_type=jnp.float32,
    )


def halves(values):
    high = values.astype(jnp.bfloat16)
    return (high, (values - high.astype(jnp.float32)).astype(jnp.bfloat16))


def plane_place():
    data, place, core = lax.axis_index("dp"), lax.axis_index("seq"), lax.axis_index("tensor")
    along_x = place + 1 - 2 * lax.rem(place, 2)
    along_y = lax.rem(place + 2, GROUP)
    across = GROUP - 1 - place
    return (data, place, core, along_x, along_y, across)


def meet(devices):
    barrier = pltpu.get_barrier_semaphore()
    for device in devices:
        pl.semaphore_signal(barrier, inc=1, device_id=device, device_id_type=MESH_ID)
    pl.semaphore_wait(barrier, len(devices))


def remote(source, target, send_sem, recv_sem, device):
    return pltpu.make_async_remote_copy(
        src_ref=source,
        dst_ref=target,
        send_sem=send_sem,
        recv_sem=recv_sem,
        device_id=device,
        device_id_type=MESH_ID,
    )


def lasting(microseconds):
    return pl.CostEstimate(
        flops=int(microseconds * 9e8),
        bytes_accessed=int(microseconds * 3e6),
        transcendentals=0,
    )


def any_specs(count):
    return [pl.BlockSpec(memory_space=pl.ANY)] * count


def vmem_specs(count):
    return [pl.BlockSpec(memory_space=pltpu.VMEM)] * count


def gather_kernel(apply, count_in, count_out, own_ref, *refs):
    inputs, all_ref = refs[:count_in], refs[count_in]
    outputs = refs[count_in + 1 : count_in + 1 + count_out]
    send_sems, recv_sems = refs[count_in + 1 + count_out :]
    data, place, core, along_x, along_y, across = plane_place()
    height = own_ref.shape[0]
    half = height // 2
    to_x, to_y, partner = (data, along_x, core), (data, along_y, core), (data, place, 1 - core)

    def block(chip, part):
        return all_ref.at[2 * chip + core, pl.ds(part * half, half)]

    def work(chip, side):
        if apply is not None:
            index = 2 * chip + side
            rows = pl.ds(pl.multiple_of(index * height, 16), height)
            apply(all_ref[index], rows, inputs, outputs)

    meet((to_x, to_y, partner))

    def push(index, source, target, device):
        copy = remote(source, target, send_sems.at[index], recv_sems.at[index], device)
        copy.start()
        return copy

    first, second = own_ref.at[pl.ds(0, half)], own_ref.at[pl.ds(half, half)]
    x_first = push(0, first, block(place, 0), to_x)
    y_second = push(1, second, block(place, 1), to_y)
    x_second = push(2, second, block(place, 1), to_x)
    y_first = push(3, first, block(place, 0), to_y)
    pair_own = push(4, own_ref, all_ref.at[2 * place + core], partner)
    all_ref[2 * place + core] = own_ref[...]
    work(place, core)
    pair_own.wait_recv()
    work(place, 1 - core)
    x_first.wait_recv()
    over_y = push(5, block(along_x, 0), block(along_x, 0), to_y)
    y_second.wait_recv()
    over_x = push(6, block(along_y, 1), block(along_y, 1), to_x)
    x_second.wait_recv()
    mine_x = all_ref.at[2 * along_x + core]
    pair_x = push(7, mine_x, mine_x, partner)
    y_first.wait_recv()
    mine_y = all_ref.at[2 * along_y + core]
    pair_y = push(8, mine_y, mine_y, partner)
    work(along_x, core)
    work(along_y, core)
    pair_x.wait_recv()
    work(along_x, 1 - core)
    pair_y.wait_recv()
    work(along_y, 1 - core)
    over_y.wait_recv()
    pair_a = push(9, block(across, 0), block(across, 0), partner)
    over_x.wait_recv()
    pair_b = push(10, block(across, 1), block(across, 1), partner)
    work(across, core)
    pair_a.wait_recv()
    pair_b.wait_recv()
    work(across, 1 - core)
    for copy in (
        x_first,
        y_second,
        x_second,
        y_first,
        pair_own,
        over_y,
        over_x,
        pair_x,
        pair_y,
        pair_a,
        pair_b,
    ):
        copy.wait_send()


def gather_plane(own, identity=1, apply=None, inputs=(), outputs=()):
    rows, width = own.shape
    gathered, *results = pl.pallas_call(
        partial(gather_kernel, apply, len(inputs), len(outputs)),
        out_shape=[jax.ShapeDtypeStruct((2 * GROUP, rows, width), own.dtype)]
        + [jax.ShapeDtypeStruct(shape, dtype) for shape, dtype in outputs],
        in_specs=vmem_specs(1 + len(inputs)),
        out_specs=vmem_specs(1 + len(outputs)),
        scratch_shapes=[pltpu.SemaphoreType.DMA((11,)), pltpu.SemaphoreType.DMA((11,))],
        cost_estimate=lasting(35),
        compiler_params=pltpu.CompilerParams(
            collective_id=identity, has_side_effects=True, vmem_limit_bytes=VMEM_BYTES
        ),
    )(own, *inputs)
    gathered = gathered.reshape(2 * GROUP * rows, width)
    return (gathered, *results) if results else gathered


def apply_gate_up(block, rows, inputs, outputs):
    weights, (both_ref, act_ref) = inputs[0], outputs
    units = act_ref.shape[1]
    both = jnp.dot(block, weights[...], preferred_element_type=jnp.float32)
    both_ref[rows] = both
    gate = both[:, :units]
    act_ref[rows] = (gate * jax.nn.sigmoid(gate) * both[:, units:]).astype(jnp.bfloat16)


def apply_down_back(block, rows, inputs, outputs):
    weights, both_ref = inputs
    units = weights.shape[1]
    d_act = jnp.dot(block, weights[...], preferred_element_type=jnp.float32)
    gate, up = both_ref[rows, :units], both_ref[rows, units:]
    sigmoid = jax.nn.sigmoid(gate)
    silu = gate * sigmoid
    d_gate = d_act * up * (sigmoid * (1.0 + gate * (1.0 - sigmoid)))
    outputs[0][rows, :units] = d_gate.astype(jnp.bfloat16)
    outputs[0][rows, units:] = (d_act * silu).astype(jnp.bfloat16)


def apply_out_back(block, rows, inputs, outputs):
    both = jnp.dot(block, inputs[0][...], preferred_element_type=jnp.float32)
    width = outputs[0].shape[1]
    outputs[0][rows] = both[:, :width]
    outputs[1][rows] = both[:, width:].astype(jnp.bfloat16)


def apply_norm(block, rows, inputs, outputs):
    gain_ref, weights = inputs
    values = block.astype(jnp.float32)
    scale = lax.rsqrt(jnp.mean(values * values, axis=-1, keepdims=True) + EPSILON)
    normed = (values * scale * gain_ref[...]).astype(jnp.bfloat16)
    outputs[0][rows] = normed
    outputs[1][rows] = jnp.dot(normed, weights[...], preferred_element_type=jnp.float32).astype(
        jnp.bfloat16
    )


def scatter_kernel(count, left_ref, right_ref, *refs):
    data, place, core, along_x, along_y, across = plane_place()
    partner = (data, place, 1 - core)
    to_x, to_y = (data, along_x, core), (data, along_y, core)
    order = (across, along_x, along_y, place)
    count_in = 0 if count == 1 else count
    extra, sums = refs[:count_in], refs[count_in : count_in + count]
    parts, scratch = refs[count_in + count : count_in + 2 * count], refs[count_in + 2 * count :]
    step = 16
    meet((partner, to_x, to_y))

    def multiply(at, chip, side):
        part = parts[at]
        index = 2 * chip + side
        height, columns = part.shape[1:]
        if at == 0:
            rows = pl.ds(pl.multiple_of(index * height, 16), height)
            depth = right_ref.shape[1]
            block = dot_f32(left_ref[rows, :depth], right_ref[...], 1, 1)
            if count > 1:
                block = block + dot_f32(left_ref[rows, depth:], extra[-1][...], 1, 1)
        else:
            start = left_ref.shape[1] - GROUP * height
            turned = pl.ds(pl.multiple_of(start + chip * height, 128), height)
            along = pl.ds(pl.multiple_of(side * columns, 128), columns)
            block = dot_f32(left_ref[:, turned], extra[at - 1][:, along], 0, 0)
        part[index] = block.astype(jnp.bfloat16)

    def one_array(at, part_ref, sum_ref, own_refs):
        pair_in, send_a, send_x, send_y, got_x, got_y, pair_s, pair_r, send_s, recv_s = own_refs
        half = part_ref.shape[1] // 2
        pair = []

        def send_pair(index):
            chip = order[index]
            multiply(at, chip, 1 - core)
            copy = remote(
                part_ref.at[2 * chip + 1 - core],
                pair_in.at[index],
                pair_s.at[index],
                pair_r.at[index],
                partner,
            )
            copy.start()
            pair.append(copy)
            multiply(at, chip, core)

        def own_rows(index, rows):
            return part_ref[2 * order[index] + core, rows].astype(jnp.float32) + pair_in[
                index, rows
            ].astype(jnp.float32)

        def fill(target, index, first, extra=None):
            def one(lap, carry):
                rows = pl.ds(pl.multiple_of(lap * step, step), step)
                total = own_rows(index, pl.ds(pl.multiple_of(first + lap * step, step), step))
                if extra is not None:
                    total = total + extra[rows].astype(jnp.float32)
                target[rows] = total.astype(jnp.bfloat16)
                return carry

            lax.fori_loop(0, half // step, one, 0)

        def push(index, source, target, device):
            copy = remote(source, target, send_s.at[index], recv_s.at[index], device)
            copy.start()
            return copy

        send_pair(0)
        pair[0].wait_recv()
        fill(send_a.at[0], 0, 0)
        far_x = push(0, send_a.at[0], got_x.at[0], to_x)
        fill(send_a.at[1], 0, half)
        far_y = push(1, send_a.at[1], got_y.at[0], to_y)
        send_pair(1)
        pair[1].wait_recv()
        fill(send_x.at[0], 1, 0)
        near_x = push(2, send_x.at[0], got_x.at[1], to_x)
        send_pair(2)
        pair[2].wait_recv()
        fill(send_y.at[0], 2, half)
        near_y = push(3, send_y.at[0], got_y.at[1], to_y)
        send_pair(3)
        yield
        far_x.wait_recv()
        fill(send_y.at[1], 2, 0, got_x.at[0])
        last_y = push(4, send_y.at[1], got_y.at[2], to_y)
        far_y.wait_recv()
        fill(send_x.at[1], 1, half, got_y.at[0])
        last_x = push(5, send_x.at[1], got_x.at[2], to_x)
        yield
        pair[3].wait_recv()
        near_x.wait_recv()
        near_y.wait_recv()
        last_y.wait_recv()
        last_x.wait_recv()

        def finish(first, near, last):
            def one(lap, carry):
                rows = pl.ds(pl.multiple_of(lap * step, step), step)
                place_rows = pl.ds(pl.multiple_of(first + lap * step, step), step)
                sum_ref[place_rows] = (
                    own_rows(3, place_rows)
                    + near[rows].astype(jnp.float32)
                    + last[rows].astype(jnp.float32)
                )
                return carry

            lax.fori_loop(0, half // step, one, 0)

        finish(0, got_x.at[1], got_y.at[2])
        finish(half, got_y.at[1], got_x.at[2])
        for copy in pair + [far_x, far_y, near_x, near_y, last_x, last_y]:
            copy.wait_send()

    each = len(scratch) // count
    runs = [
        one_array(at, parts[at], sums[at], scratch[each * at : each * (at + 1)]) for at in range(count)
    ]
    for run in runs:
        next(run)
    for run in runs:
        next(run)
    for run in runs:
        for _ in run:
            pass


def scatter_plane(left, right, identity, extra=(), beside=()):
    height, width = left.shape[0] // (2 * GROUP), right.shape[0]
    sizes = [(height, width)] + [size for _, *size in extra]
    shapes = []
    scratch = [pltpu.VMEM((2 * GROUP, *size), jnp.bfloat16) for size in sizes]
    for rows, columns in sizes:
        half = (rows // 2, columns)
        shapes.append(jax.ShapeDtypeStruct((rows, columns), jnp.float32))
        scratch += [
            pltpu.VMEM((4, rows, columns), jnp.bfloat16),
            pltpu.VMEM((2,) + half, jnp.bfloat16),
            pltpu.VMEM((2,) + half, jnp.bfloat16),
            pltpu.VMEM((2,) + half, jnp.bfloat16),
            pltpu.VMEM((3,) + half, jnp.bfloat16),
            pltpu.VMEM((3,) + half, jnp.bfloat16),
            pltpu.SemaphoreType.DMA((4,)),
            pltpu.SemaphoreType.DMA((4,)),
            pltpu.SemaphoreType.DMA((6,)),
            pltpu.SemaphoreType.DMA((6,)),
        ]
    count = 1 + len(extra)
    return pl.pallas_call(
        partial(scatter_kernel, count),
        out_shape=shapes,
        in_specs=vmem_specs(2 if count == 1 else 2 + count),
        out_specs=vmem_specs(count),
        scratch_shapes=scratch,
        cost_estimate=lasting(35),
        compiler_params=pltpu.CompilerParams(
            collective_id=identity, has_side_effects=True, vmem_limit_bytes=VMEM_BYTES
        ),
    )(left, right, *[array for array, *_ in extra], *beside)


def plane_sum_kernel(
    small_ref, own_ref, out_ref, bulk, sum_ref, both_ref, both_out, back, small_in, own_sem, send_s, recv_s
):
    data, place, core, along_x, along_y, across = plane_place()
    mine = 2 * place + core
    partner = (data, place, 1 - core)
    plane = []
    for turn_by in range(1, 2 * GROUP):
        other = lax.rem(mine + turn_by, 2 * GROUP)
        plane.append((other, (data, other // 2, lax.rem(other, 2))))
    meet([device for _, device in plane])
    started = []

    def push(source, target, device):
        slot = len(started)
        copy = remote(source, target, send_s.at[slot], recv_s.at[slot], device)
        copy.start()
        started.append(copy)

    piece = small_in.shape[2]

    def piece_of(index):
        return small_ref.at[:, pl.ds(pl.multiple_of(index * piece, 128), piece)]

    for other, device in plane:
        push(piece_of(other), small_in.at[mine], device)
    for source, target in ((own_ref, both_ref), (out_ref, both_out)):
        push(source, target.at[core], partner)
    for chip in (across, along_x, along_y):
        push(bulk.at[chip], back.at[place], (data, chip, core))
    own = pltpu.make_async_copy(bulk.at[place], back.at[place], own_sem)
    own.start()
    small_in[mine] = piece_of(mine)[...]
    both_ref[core] = own_ref[...]
    both_out[core] = out_ref[...]
    for copy in started:
        copy.wait()
    own.wait()
    total = small_in[0]
    for index in range(1, 2 * GROUP):
        total = total + small_in[index]
    sum_ref[...] = total


def plane_sum(small, own_rows, out_rows, bulk):
    places = 2 * GROUP
    pushes = places - 1 + 2 + 3
    shaped = jax.ShapeDtypeStruct
    piece = small.shape[1] // places
    return pl.pallas_call(
        plane_sum_kernel,
        out_shape=[
            shaped((8, piece), jnp.float32),
            shaped((2,) + own_rows.shape, own_rows.dtype),
            shaped((2,) + out_rows.shape, out_rows.dtype),
            shaped(bulk.shape, bulk.dtype),
        ],
        in_specs=vmem_specs(3) + any_specs(1),
        out_specs=vmem_specs(3) + any_specs(1),
        scratch_shapes=[
            pltpu.VMEM((places, 8, piece), jnp.float32),
            pltpu.SemaphoreType.DMA,
            pltpu.SemaphoreType.DMA((pushes,)),
            pltpu.SemaphoreType.DMA((pushes,)),
        ],
        cost_estimate=lasting(20),
        compiler_params=pltpu.CompilerParams(
            collective_id=7, has_side_effects=True, vmem_limit_bytes=VMEM_BYTES
        ),
    )(small, own_rows, out_rows, bulk)


def finish_kernel(
    piece_ref,
    bc_ref,
    bulk,
    small_all,
    bc_all,
    back,
    bc_send,
    bc_in,
    bc_line,
    line_in,
    own_sem,
    send_s,
    recv_s,
):
    data, place, core, along_x, along_y, across = plane_place()
    count = lax.axis_size("dp")
    mine = 2 * place + core
    partner = (data, place, 1 - core)
    others = (across, along_x, along_y)
    chips = [(data, chip, core) for chip in others]
    plane = []
    for turn_by in range(1, 2 * GROUP):
        other = lax.rem(mine + turn_by, 2 * GROUP)
        plane.append((data, other // 2, lax.rem(other, 2)))
    line = []
    for turn_by in range(1, count):
        other = lax.rem(data + turn_by, count)
        line.append((other, (other, place, core)))
    meet(plane + [device for _, device in line])
    started = []

    def push(source, target, device):
        slot = len(started)
        copy = remote(source, target, send_s.at[slot], recv_s.at[slot], device)
        copy.start()
        started.append(copy)
        return copy

    rows = bc_in.shape[1]

    def rows_of(index):
        return bc_send.at[pl.ds(pl.multiple_of(index * rows, 16), rows)]

    bc_send[...] = bc_ref[...].astype(jnp.bfloat16)
    first = [push(rows_of(other), bc_in.at[data], device) for other, device in line]
    small = [push(piece_ref, line_in.at[data], device) for _, device in line]
    late = []
    for chip, device in zip(others, chips):
        late.append(push(bulk.at[chip], back.at[place], device))
    own = pltpu.make_async_copy(bulk.at[place], back.at[place], own_sem)
    own.start()
    bc_in[data] = rows_of(data)[...]
    line_in[data] = piece_ref[...]
    for copy in first:
        copy.wait_recv()
    total = bc_in[0].astype(jnp.float32)
    for index in range(1, count):
        total = total + bc_in[index].astype(jnp.float32)
    bc_line[data] = total.astype(jnp.bfloat16)
    second = [push(bc_line.at[data], bc_line.at[data], device) for _, device in line]
    for copy in small:
        copy.wait_recv()
    total = line_in[0]
    for index in range(1, count):
        total = total + line_in[index]
    small_all[mine] = total
    late += [push(small_all.at[mine], small_all.at[mine], device) for device in plane]
    for copy in second:
        copy.wait_recv()
    third = [push(bc_line, bc_all.at[mine], device) for device in chips]
    late.append(push(bc_line, bc_all.at[mine], partner))
    bc_all[mine] = bc_line[...]
    for copy, chip in zip(third, others):
        copy.wait_recv()
        held = bc_all.at[2 * chip + core]
        late.append(push(held, held, partner))
    for copy in late:
        copy.wait_recv()
    for copy in started:
        copy.wait_send()
    own.wait()


def finish_all(piece, bc_sum, bulk):
    count = lax.axis_size("dp")
    places = 2 * GROUP
    pushes = 3 * (count - 1) + (places - 1) + 2 * (GROUP - 1) + GROUP
    shaped = jax.ShapeDtypeStruct
    blocks = (count, bc_sum.shape[0] // count, bc_sum.shape[1])
    return pl.pallas_call(
        finish_kernel,
        out_shape=[
            shaped((places,) + piece.shape, jnp.float32),
            shaped((places,) + blocks, jnp.bfloat16),
            shaped(bulk.shape, bulk.dtype),
        ],
        in_specs=vmem_specs(2) + any_specs(1),
        out_specs=vmem_specs(2) + any_specs(1),
        scratch_shapes=[
            pltpu.VMEM(bc_sum.shape, jnp.bfloat16),
            pltpu.VMEM(blocks, jnp.bfloat16),
            pltpu.VMEM(blocks, jnp.bfloat16),
            pltpu.VMEM((count,) + piece.shape, jnp.float32),
            pltpu.SemaphoreType.DMA,
            pltpu.SemaphoreType.DMA((pushes,)),
            pltpu.SemaphoreType.DMA((pushes,)),
        ],
        cost_estimate=lasting(30),
        compiler_params=pltpu.CompilerParams(
            collective_id=6, has_side_effects=True, vmem_limit_bytes=VMEM_BYTES
        ),
    )(piece, bc_sum, bulk)


def unpack_kernel(
    gu_ref,
    down_ref,
    out_ref,
    in_ref,
    bc_ref,
    misc_ref,
    pieces_ref,
    gate_ref,
    up_ref,
    d_ref,
    mo_ref,
    ao_ref,
    z_ref,
    x_ref,
    q_ref,
    grad_bc_ref,
    k_ref,
    v_ref,
    dt_ref,
    conv_ref,
    bias_ref,
    dtb_ref,
    alog_ref,
    skip_ref,
    group_ref,
    one_ref,
    two_ref,
    sums_ref,
):
    units, width, part = down_ref.shape[2], HEADS * HP, HD // 4
    gate_ref[...] = gu_ref[0, :, :units].astype(jnp.float32)
    up_ref[...] = gu_ref[0, :, units:].astype(jnp.float32)
    d_ref[...] = down_ref[0].astype(jnp.float32).T
    turned = out_ref[0].astype(jnp.float32).T
    mo_ref[...] = turned[:width]
    ao_ref[...] = turned[width:]
    z_ref[...] = in_ref[0, :, :width].astype(jnp.float32)
    q_ref[...] = in_ref[0, :, width : width + HD].astype(jnp.float32)
    x_ref[...] = in_ref[0, :, width + HD : 2 * width + HD].astype(jnp.float32)
    wide = bc_ref.shape[2]
    for core in range(2):
        grad_bc_ref[wide * core : wide * (core + 1)] = bc_ref[core].astype(jnp.float32).T

    @pl.when(pl.program_id(0) == 0)
    def _():
        for index in range(2 * GROUP):
            piece = pieces_ref.shape[2]
            sums_ref[:, piece * index : piece * (index + 1)] = pieces_ref[index]
        held = [misc_ref[chip].astype(jnp.float32) for chip in range(GROUP)]
        k_ref[...] = jnp.concatenate(
            [
                held[0][:, :part],
                held[1][:, :part],
                held[0][:, part : 2 * part],
                held[1][:, part : 2 * part],
            ],
            axis=1,
        )
        v_ref[...] = jnp.concatenate([held[2][:, : 2 * part], held[3][:, : 2 * part]], axis=1)
        dt_ref[...] = jnp.concatenate(
            [values[:, DT_LANE : DT_LANE + HEADS] for values in held], axis=1
        ).T
        taps = bias_ref.shape[1]
        conv_ref[...] = sums_ref[:KC, :taps]
        bias_ref[...] = sums_ref[KC : KC + 1, :taps]
        dtb_ref[...] = sums_ref[0:1, taps : taps + MH]
        alog_ref[...] = sums_ref[1:2, taps : taps + MH]
        skip_ref[...] = sums_ref[2:3, taps : taps + MH]
        start = taps + 128
        mine = GROUP * lax.axis_index("dp") + lax.axis_index("seq")
        slice_rows = one_ref.shape[1]
        each = slice_rows * GROUP * lax.axis_size("dp") // 8
        for ref in (one_ref, two_ref):
            gains = sums_ref[:, start : start + each]
            row = lax.broadcasted_iota(jnp.int32, (8, 1), 0)
            total = jnp.zeros((1, slice_rows), jnp.float32)
            for at in range(each // slice_rows):
                block = gains[:, slice_rows * at : slice_rows * (at + 1)]
                wanted = row * (each // slice_rows) + at == mine
                total = total + jnp.sum(jnp.where(wanted, block, 0.0), axis=0, keepdims=True)
            ref[...] = total
            start += each
        per_row = MH // 8
        for head in range(MH):
            row, lane = head // per_row, start + HP * (head % per_row)
            group_ref[head : head + 1, :] = sums_ref[row : row + 1, lane : lane + HP]


def unpack_all(back, bc_all, sums, shapes):
    gu, down, out, in_all = back

    def per_chip(array, rows=1):
        return pl.BlockSpec((rows,) + array.shape[1:], lambda chip: (chip, 0, 0))

    def across(shape):
        return pl.BlockSpec((shape[0], shape[1] // GROUP), lambda chip: (0, chip))

    def down_along(shape):
        return pl.BlockSpec((shape[0] // GROUP, shape[1]), lambda chip: (chip, 0))

    def once(shape):
        return pl.BlockSpec(shape, lambda chip: (0,) * len(shape))

    misc_block = (GROUP, in_all.shape[1], HD)
    kinds = [across, across, down_along, down_along, down_along, across, across, across, across]
    kinds += [once] * (len(shapes) - len(kinds))
    return pl.pallas_call(
        unpack_kernel,
        grid=(GROUP,),
        in_specs=[
            per_chip(gu),
            per_chip(down),
            per_chip(out),
            per_chip(in_all),
            per_chip(bc_all, 2),
            pl.BlockSpec(misc_block, lambda chip: (0, 0, in_all.shape[2] // HD - 1)),
            once(sums.shape),
        ],
        out_specs=[kind(shape) for kind, shape in zip(kinds, shapes)],
        out_shape=[jax.ShapeDtypeStruct(shape, jnp.float32) for shape in shapes],
        scratch_shapes=[pltpu.VMEM((8, 2 * GROUP * sums.shape[2]), jnp.float32)],
        cost_estimate=lasting(8),
        compiler_params=pltpu.CompilerParams(vmem_limit_bytes=VMEM_BYTES),
    )(gu, down, out, in_all, bc_all, in_all, sums)


def push_moves(moves, sources, targets, local_sems, send_sems, recv_sems, first=0):
    data, place, core, along_x, along_y, across = plane_place()
    copies = []
    for index, chip in enumerate((across, along_x, along_y)):
        for at, move in enumerate(moves):
            source, target = move(sources, targets, place, chip)
            slot = first + index * len(moves) + at
            copy = remote(
                source, target, send_sems.at[slot], recv_sems.at[slot], (data, chip, core)
            )
            copy.start()
            copies.append(copy)
    for at, move in enumerate(moves):
        source, target = move(sources, targets, place, place)
        copy = pltpu.make_async_copy(source, target, local_sems.at[at])
        copy.start()
        copies.append(copy)
    return copies


def plane_peers():
    data, place, core, along_x, along_y, across = plane_place()
    return [(data, chip, core) for chip in (across, along_x, along_y)]


def exchange_kernel(moves, count_in, *refs):
    sources, targets = refs[:count_in], refs[count_in:-3]
    meet(plane_peers())
    for copy in push_moves(moves, sources, targets, *refs[-3:]):
        copy.wait()


def first_exchange_kernel(
    moves,
    z_ref,
    q_ref,
    x_ref,
    key_ref,
    value_ref,
    dt_ref,
    one_ref,
    two_ref,
    in_ref,
    gains_ref,
    misc,
    gains,
    local_sems,
    send_sems,
    recv_sems,
):
    data, place, core, along_x, along_y, across = plane_place()
    places = GROUP * lax.axis_size("dp")
    mine = GROUP * data + place
    devices = []
    for turn_by in range(1, places):
        other = lax.rem(mine + turn_by, places)
        devices.append((other // GROUP, lax.rem(other, GROUP), core))
    meet(devices)
    half, part = HD // 2, HD // 4
    keys, values = key_ref[...], value_ref[...]
    steps = dt_ref[...].astype(jnp.float32).T.astype(keys.dtype)
    columns = (
        (keys[:, :part], keys[:, half : half + part]),
        (keys[:, part:half], keys[:, half + part :]),
        (values[:, :half],),
        (values[:, half:],),
    )
    for chip in range(GROUP):
        heads = steps[:, HEADS * chip : HEADS * (chip + 1)]
        rest = jnp.zeros((keys.shape[0], half - HEADS), keys.dtype)
        misc[chip] = jnp.concatenate([*columns[chip], heads, rest], axis=1)
    gains[...] = jnp.zeros_like(gains)
    gains[0:1] = one_ref[...].astype(jnp.float32)
    gains[1:2] = two_ref[...].astype(jnp.float32)
    sources = (z_ref, q_ref, x_ref, misc)
    copies = push_moves(moves, sources, (in_ref,), local_sems, send_sems, recv_sems)
    for index, device in enumerate(devices):
        slot = 3 * len(moves) + index
        copy = remote(
            gains, gains_ref.at[mine], send_sems.at[slot], recv_sems.at[slot], device
        )
        copy.start()
        copies.append(copy)
    gains_ref[mine] = gains[...]
    for copy in copies:
        copy.wait()


def first_exchange(moves, arrays, width_in):
    places = GROUP * lax.axis_size("dp")
    slice_rows = arrays[0].shape[0]
    count = 3 * len(moves) + places - 1
    return pl.pallas_call(
        partial(first_exchange_kernel, moves),
        out_shape=[
            jax.ShapeDtypeStruct((GROUP, slice_rows, width_in), jnp.bfloat16),
            jax.ShapeDtypeStruct((places, 8, slice_rows), jnp.float32),
        ],
        in_specs=any_specs(3) + vmem_specs(5),
        out_specs=any_specs(1) + vmem_specs(1),
        scratch_shapes=[
            pltpu.VMEM((GROUP, slice_rows, HD), jnp.bfloat16),
            pltpu.VMEM((8, slice_rows), jnp.float32),
            pltpu.SemaphoreType.DMA((len(moves),)),
            pltpu.SemaphoreType.DMA((count,)),
            pltpu.SemaphoreType.DMA((count,)),
        ],
        cost_estimate=lasting(20),
        compiler_params=pltpu.CompilerParams(collective_id=3, has_side_effects=True),
    )(*arrays)


def exchange_plane(moves, arrays, out_shapes, identity):
    count = 3 * len(moves)
    return pl.pallas_call(
        partial(exchange_kernel, moves, len(arrays)),
        out_shape=[jax.ShapeDtypeStruct(shape, jnp.bfloat16) for shape in out_shapes],
        in_specs=any_specs(len(arrays)),
        out_specs=any_specs(len(out_shapes)),
        scratch_shapes=[
            pltpu.SemaphoreType.DMA((len(moves),)),
            pltpu.SemaphoreType.DMA((count,)),
            pltpu.SemaphoreType.DMA((count,)),
        ],
        cost_estimate=lasting(25),
        compiler_params=pltpu.CompilerParams(collective_id=identity, has_side_effects=True),
    )(*arrays)


def column_move(source, target, start, width):
    def move(sources, targets, place, chip):
        columns = pl.ds(pl.multiple_of(chip * width, 128), width)
        return (
            sources[source].at[:, columns],
            targets[target].at[place, :, pl.ds(start, width)],
        )

    return move


def block_move(source, target):
    def move(sources, targets, place, chip):
        return (sources[source].at[chip], targets[target].at[place])

    return move


def misc_move(source, target, start):
    def move(sources, targets, place, chip):
        return (
            sources[source].at[chip],
            targets[target].at[place, :, pl.ds(start, 128)],
        )

    return move


def lane_masks():
    lane = lax.broadcasted_iota(jnp.int32, (1, 2 * HP), 1)
    return (lane < HP, lane >= HP)


DT_LANE = HP


def at_lane(lane, values):
    row = lax.broadcasted_iota(jnp.int32, (1, 2 * HP), 1)
    return jnp.where(row == lane, values, 0.0)


def dot_beside(exact, values, left_dim):
    width = values.shape[1]
    both = dot_f32(exact, jnp.concatenate(halves(values), axis=1), left_dim, 0)
    return both[:, :width] + both[:, width:]


def dot_along(left, right):
    left_high, left_low = halves(left)
    right_high, right_low = halves(right)
    return dot_f32(
        jnp.concatenate([left_high, left_high, left_low], axis=1),
        jnp.concatenate([right_high, right_low, right_high], axis=1),
        1,
        1,
    )


def spread_heads(*columns):
    width = HEADS * HP
    row = lax.rem(lax.broadcasted_iota(jnp.int32, (4 * HP, width), 0), 2 * HP)
    head = lax.broadcasted_iota(jnp.int32, (4 * HP, width), 1) // HP
    pick = jnp.where(row == DT_LANE + head, 1.0, 0.0).astype(jnp.bfloat16)
    parts = [jnp.concatenate(halves(values), axis=1) for values in columns]
    wide = dot_f32(jnp.concatenate(parts, axis=0), pick, 1, 0)
    size = columns[0].shape[0]
    return [wide[size * at : size * (at + 1)] for at in range(len(columns))]


def wide_keeps(keeps_ref):
    size = keeps_ref.shape[0]
    return [None] + [
        jnp.broadcast_to(keeps_ref[:, 1 + back : 2 + back], (size, 2 * HP))
        for back in range(1, KC)
    ]


def head_sums(values):
    low, high = lane_masks()
    first = jnp.sum(jnp.where(low, values, 0.0), axis=1, keepdims=True)
    second = jnp.sum(jnp.where(high, values, 0.0), axis=1, keepdims=True)
    return (first, second)


def head_means(values):
    low, high = lane_masks()
    first, second = head_sums(values)
    return jnp.where(low, first, second) * (1.0 / HP)


def stack_heads(values):
    low, high = lane_masks()
    zero = jnp.zeros_like(values)
    return jnp.concatenate([jnp.where(low, values, zero), jnp.where(high, values, zero)], axis=0)


def order_in(size):
    row = lax.broadcasted_iota(jnp.int32, (size, size), 0)
    column = lax.broadcasted_iota(jnp.int32, (size, size), 1)
    return (row, column)


def exact_sum(ones, values):
    high = values.astype(jnp.bfloat16)
    rest = values - high.astype(jnp.float32)
    middle = rest.astype(jnp.bfloat16)
    low = (rest - middle.astype(jnp.float32)).astype(jnp.bfloat16)
    return dot_f32(ones, high, 1, 0) + (dot_f32(ones, middle, 1, 0) + dot_f32(ones, low, 1, 0))


def chunk_decays(proj_ref, heads_ref, keeps_ref):
    size, width = proj_ref.shape
    raw = proj_ref[:, width - 2 * HP :] + heads_ref[0:1]
    dt_rows = jnp.maximum(raw, 0.0) + jnp.log1p(jnp.exp(-jnp.abs(raw)))
    row, column = order_in(size)
    lower = jnp.where(row >= column, 1.0, 0.0).astype(jnp.bfloat16)
    cumul = exact_sum(lower, -heads_ref[1:2] * dt_rows)
    enter = jnp.exp(cumul) * keeps_ref[:, 0:1]
    leave_bare = jnp.exp(cumul[size - 1 :] - cumul) * keeps_ref[:, 1:2]
    return (raw, dt_rows, cumul, enter, leave_bare)


def conv_windows(block, proj_ref, before_ref, bc_ref, bc_before_ref):
    if block < HEADS // 2:
        start = proj_ref.shape[1] - 2 * HP * (1 + HEADS // 2 - block)
        lanes = slice(start, start + 2 * HP)
        now, before = proj_ref[:, lanes], before_ref[:, lanes]
        now, before = now.astype(jnp.bfloat16), before.astype(jnp.bfloat16)
    else:
        start = 2 * HP * (block - HEADS // 2)
        lanes = slice(start, start + 2 * HP)
        now, before = bc_ref[:, lanes], bc_before_ref[8:, lanes]
    now, before = now.astype(jnp.float32), before.astype(jnp.float32)
    size = now.shape[0]
    extended = jnp.concatenate([before, now], axis=0)
    return [now] + [extended[8 - back : 8 - back + size] for back in range(1, KC)]


def conv_sum(windows, taps_ref, lanes, keeps):
    total = taps_ref[KC : KC + 1, lanes] + taps_ref[KC - 1 : KC, lanes] * windows[0]
    for back in range(1, KC):
        total = total + taps_ref[KC - 1 - back : KC - back, lanes] * (
            windows[back] * keeps[back]
        )
    return total


def head_decay(allowed, cumul, cumul_t, head):
    lane = DT_LANE + head
    differ = cumul[:, lane : lane + 1] - cumul_t[lane : lane + 1, :]
    return jnp.exp(jnp.where(allowed, differ, -jnp.inf))


def ssd_forward_kernel(
    proj_ref,
    before_ref,
    bc_ref,
    bc_before_ref,
    taps_ref,
    heads_ref,
    keeps_ref,
    segc_ref,
    segr_ref,
    skip_ref,
    gain_ref,
    cos_ref,
    sin_ref,
    gated_ref,
    ssm_ref,
    states_ref,
    mixed_ref,
    kv_ref,
    state,
):
    @pl.when(pl.program_id(0) == 0)
    def _():
        state[...] = jnp.zeros_like(state)

    size = proj_ref.shape[0]
    width = HEADS * HP
    keeps = wide_keeps(keeps_ref)
    for block in range(mixed_ref.shape[1] // (2 * HP)):
        lanes = slice(2 * HP * block, 2 * HP * (block + 1))
        windows = conv_windows(block, proj_ref, before_ref, bc_ref, bc_before_ref)
        summed = conv_sum(windows, taps_ref, lanes, keeps)
        mixed_ref[:, lanes] = (summed * jax.nn.sigmoid(summed)).astype(jnp.bfloat16)
    raw, dt_rows, cumul, enter_all, leave_bare = chunk_decays(proj_ref, heads_ref, keeps_ref)
    enter_all, leave_all = spread_heads(enter_all, leave_bare * dt_rows)
    cumul_t, dt_t = cumul.T, dt_rows.T
    entry = state[...]
    states_ref[0] = entry
    b_rows, c_rows = mixed_ref[:, width : width + NS], mixed_ref[:, width + NS :]
    gram = dot_f32(c_rows, b_rows, 1, 1)
    row, column = order_in(size)
    allowed = (segc_ref[...] == segr_ref[0]) & (row >= column)
    entered = dot_beside(c_rows, entry, 1)
    weighted = []
    for pair in range(HEADS // 2):
        lanes = slice(2 * HP * pair, 2 * HP * (pair + 1))
        heads_x = mixed_ref[:, lanes]
        mixing = []
        for head in (2 * pair, 2 * pair + 1):
            lane = DT_LANE + head
            decay = head_decay(allowed, cumul, cumul_t, head)
            mixing.append(gram * decay * dt_t[lane : lane + 1, :])
        stacked = stack_heads(heads_x)
        out = dot_f32(
            jnp.concatenate(halves(jnp.concatenate(mixing, axis=1)), axis=1),
            jnp.concatenate([stacked, stacked], axis=0),
            1,
            0,
        )
        wide_x = heads_x.astype(jnp.float32)
        enter = enter_all[:, lanes]
        out = out + enter * entered[:, lanes] + skip_ref[:, lanes] * wide_x
        ssm_ref[:, lanes] = out
        gate = proj_ref[:, lanes]
        value = out * (gate * jax.nn.sigmoid(gate))
        scale = lax.rsqrt(head_means(value * value) + GROUP_EPSILON)
        gated_ref[:, lanes] = (value * scale * gain_ref[:, lanes]).astype(jnp.bfloat16)
        weighted.append(leave_all[:, lanes] * wide_x)
        state[:, lanes] = enter[size - 1 :, :] * entry[:, lanes]
    state[...] += dot_beside(b_rows, jnp.concatenate(weighted, axis=1), 0)
    kv = proj_ref[:, proj_ref.shape[1] - 2 * HP :][:, :HP]
    kv = jnp.concatenate([kv[: size // 2], kv[size // 2 :]], axis=1)
    kv_ref[...] = turn_folded(kv, cos_ref[...], sin_ref[...]).astype(jnp.bfloat16)


def ssd_backward_kernel(
    moves,
    proj_ref,
    before_ref,
    bc_ref,
    bc_before_ref,
    taps_ref,
    heads_ref,
    keeps_ref,
    segc_ref,
    segr_ref,
    skip_ref,
    gain_ref,
    mixed_ref,
    ssm_ref,
    states_ref,
    dgated_ref,
    dq_ref,
    gu_ref,
    down_ref,
    dproj_ref,
    dtaps_ref,
    dheads_ref,
    dskip_ref,
    dgain_ref,
    gu_back,
    down_back,
    state,
    d_mixed,
    next_rows,
    *sems,
):
    def transfers(act):
        data, place, core, along_x, along_y, across = plane_place()
        sources, targets = (gu_ref, down_ref), (gu_back, down_back)
        local_sems, send_sems, recv_sems = sems
        for index, chip in enumerate((across, along_x, along_y)):
            for at, move in enumerate(moves):
                source, target = move(sources, targets, place, chip)
                slot = index * len(moves) + at
                act(
                    remote(
                        source, target, send_sems.at[slot], recv_sems.at[slot], (data, chip, core)
                    )
                )
        for at, move in enumerate(moves):
            source, target = move(sources, targets, place, place)
            act(pltpu.make_async_copy(source, target, local_sems.at[at]))

    @pl.when(pl.program_id(0) == 0)
    def _():
        meet(plane_peers())
        transfers(lambda copy: copy.start())
        state[...] = jnp.zeros_like(state)
        next_rows[...] = jnp.zeros_like(next_rows)
        dtaps_ref[...] = jnp.zeros_like(dtaps_ref)
        dheads_ref[...] = jnp.zeros_like(dheads_ref)
        dskip_ref[...] = jnp.zeros_like(dskip_ref)
        dgain_ref[...] = jnp.zeros_like(dgain_ref)

    size = proj_ref.shape[0]
    width = HEADS * HP
    raw, dt_rows, cumul, enter_all, leave_bare = chunk_decays(proj_ref, heads_ref, keeps_ref)
    cumul_t, dt_t = cumul.T, dt_rows.T
    later = state[...]
    entry = states_ref[0]
    carried = jnp.sum(later * entry, axis=0, keepdims=True)
    b_rows, c_rows = mixed_ref[:, width : width + NS], mixed_ref[:, width + NS :]
    gram = dot_f32(c_rows, b_rows, 1, 1)
    row, column = order_in(size)
    allowed = (segc_ref[...] == segr_ref[0]) & (row >= column)
    d_weighted = dot_beside(b_rows, later, 1)
    enter_all, bare_all, dt_all = spread_heads(enter_all, leave_bare, dt_rows)
    d_gram = jnp.zeros((size, size), jnp.float32)
    row_sums = jnp.zeros((size, 2 * HP), jnp.float32)
    column_sums = jnp.zeros((size, 2 * HP), jnp.float32)
    at_last = jnp.zeros((1, 2 * HP), jnp.float32)
    d_entered, weighted = [], []
    for pair in range(HEADS // 2):
        lanes = slice(2 * HP * pair, 2 * HP * (pair + 1))
        heads_x = mixed_ref[:, lanes]
        wide_x = heads_x.astype(jnp.float32)
        ssm, gate, gain = ssm_ref[:, lanes], proj_ref[:, lanes], gain_ref[:, lanes]
        d_gated = dgated_ref[:, lanes]
        sigmoid = jax.nn.sigmoid(gate)
        silu = gate * sigmoid
        value = ssm * silu
        scale = lax.rsqrt(head_means(value * value) + GROUP_EPSILON)
        dgain_ref[:, lanes] += jnp.sum(d_gated * value * scale, axis=0, keepdims=True)
        d_scaled = d_gated * gain
        d_value = scale * d_scaled - value * (scale * scale * scale) * head_means(d_scaled * value)
        d_out = d_value * silu
        dproj_ref[:, lanes] = (d_value * ssm * (sigmoid * (1.0 + gate * (1.0 - sigmoid)))).astype(
            jnp.bfloat16
        )
        dskip_ref[:, lanes] += jnp.sum(d_out * wide_x, axis=0, keepdims=True)
        enter, bare, dt_pair = enter_all[:, lanes], bare_all[:, lanes], dt_all[:, lanes]
        high, low = [stack_heads(half) for half in halves(d_out)]
        d_mixing = dot_f32(jnp.concatenate([high, low], axis=0), heads_x, 1, 1)
        grams = []
        for side in range(2):
            head = 2 * pair + side
            lane = DT_LANE + head
            decay = head_decay(allowed, cumul, cumul_t, head)
            grams.append(gram * decay)
            first = size * side
            d_mix = d_mixing[first : first + size] + d_mixing[2 * size + first : 3 * size + first]
            d_gram = d_gram + d_mix * (decay * dt_t[lane : lane + 1, :])
        gram_high, gram_low = halves(jnp.concatenate(grams, axis=0))
        bare_x = dot_f32(
            jnp.concatenate([gram_high, gram_high, gram_low], axis=0),
            jnp.concatenate([high, low, high], axis=0),
            0,
            0,
        )
        left = bare * d_weighted[:, lanes]
        d_x = bare_x + left
        first_lane = DT_LANE + 2 * pair
        first, second = head_sums(d_out * (ssm - skip_ref[:, lanes] * wide_x))
        row_sums = row_sums + at_lane(first_lane, first) + at_lane(first_lane + 1, second)
        first, second = head_sums(d_x * wide_x)
        column_sums = column_sums + at_lane(first_lane, first) + at_lane(first_lane + 1, second)
        last = jnp.sum(dt_pair * left * wide_x, axis=0, keepdims=True)
        last = last + carried[:, lanes] * enter[size - 1 :]
        first, second = head_sums(last)
        at_last = at_last + at_lane(first_lane, first) + at_lane(first_lane + 1, second)
        d_mixed[:, lanes] = dt_pair * d_x + skip_ref[:, lanes] * d_out
        d_entered.append(enter * d_out)
        weighted.append(bare * dt_pair * wide_x)
        state[:, lanes] = enter[size - 1 :, :] * later[:, lanes]
    d_entered = jnp.concatenate(d_entered, axis=1)
    state[...] += dot_beside(c_rows, d_entered, 0)
    d_gram_parts = halves(d_gram)
    d_b = dot_along(jnp.concatenate(weighted, axis=1), later)
    d_mixed[:, width : width + NS] = d_b + dot_f32(
        jnp.concatenate(d_gram_parts, axis=0),
        jnp.concatenate([c_rows, c_rows], axis=0),
        0,
        0,
    )
    d_c = dot_along(d_entered, entry)
    d_mixed[:, width + NS :] = d_c + dot_f32(
        jnp.concatenate(d_gram_parts, axis=1),
        jnp.concatenate([b_rows, b_rows], axis=0),
        1,
        0,
    )

    d_cumul = row_sums - column_sums * dt_rows
    last_row = lax.broadcasted_iota(jnp.int32, (size, 1), 0) == size - 1
    d_cumul = d_cumul + jnp.where(last_row, at_last, 0.0)
    upper = jnp.where(row <= column, 1.0, 0.0).astype(jnp.bfloat16)
    d_log = exact_sum(upper, d_cumul)
    rate = heads_ref[1:2]
    d_raw = (column_sums - rate * d_log) * jax.nn.sigmoid(raw)
    lane_row = lax.broadcasted_iota(jnp.int32, (1, 2 * HP), 1)
    d_raw = jnp.where((lane_row >= DT_LANE) & (lane_row < DT_LANE + HEADS), d_raw, 0.0)
    dheads_ref[0:1] += jnp.sum(d_raw, axis=0, keepdims=True)
    dheads_ref[1:2] += -rate * jnp.sum(d_log * dt_rows, axis=0, keepdims=True)
    total = proj_ref.shape[1]
    dproj_ref[:, total - 2 * HP : total] = jnp.concatenate(
        [jnp.zeros((size, DT_LANE), jnp.bfloat16), d_raw[:, DT_LANE:].astype(jnp.bfloat16)], axis=1
    )
    dproj_ref[:, width : width + HD] = dq_ref[...]

    keeps = wide_keeps(keeps_ref)
    for block in range(mixed_ref.shape[1] // (2 * HP)):
        lanes = slice(2 * HP * block, 2 * HP * (block + 1))
        windows = conv_windows(block, proj_ref, before_ref, bc_ref, bc_before_ref)
        summed = conv_sum(windows, taps_ref, lanes, keeps)
        sigmoid = jax.nn.sigmoid(summed)
        d_sum = d_mixed[:, lanes] * (sigmoid * (1.0 + summed * (1.0 - sigmoid)))
        dtaps_ref[KC : KC + 1, lanes] += jnp.sum(d_sum, axis=0, keepdims=True)
        dtaps_ref[KC - 1 : KC, lanes] += jnp.sum(d_sum * windows[0], axis=0, keepdims=True)
        d_pre = taps_ref[KC - 1 : KC, lanes] * d_sum
        for back in range(1, KC):
            tap = KC - 1 - back
            kept = d_sum * keeps[back]
            dtaps_ref[tap : tap + 1, lanes] += jnp.sum(
                kept * windows[back], axis=0, keepdims=True
            )
            extended = jnp.concatenate([kept, next_rows[back - 1, :, lanes]], axis=0)
            d_pre = d_pre + taps_ref[tap : tap + 1, lanes] * extended[back : back + size]
            next_rows[back - 1, :, lanes] = kept[:8]
        if block < HEADS // 2:
            start = total - 2 * HP * (1 + HEADS // 2 - block)
            dproj_ref[:, start : start + 2 * HP] = d_pre.astype(jnp.bfloat16)
        else:
            start = total + 2 * HP * (block - HEADS // 2)
            dproj_ref[:, start : start + 2 * HP] = d_pre.astype(jnp.bfloat16)

    @pl.when(pl.program_id(0) == pl.num_programs(0) - 1)
    def _():
        transfers(lambda copy: copy.wait())


def ssd_specs(length, reverse, width_in, width_all, width):
    laps = length // CHUNK

    def at(lap):
        return laps - 1 - lap if reverse else lap

    def tall(columns):
        return pl.BlockSpec((CHUNK, columns), lambda lap: (at(lap), 0))

    def rim(rows, columns):
        each = CHUNK // rows
        return pl.BlockSpec((rows, columns), lambda lap: (lax.rem(each * (at(lap) + laps) - 1, each * laps), 0))

    def whole(rows, columns):
        return pl.BlockSpec((rows, columns), lambda lap: (0, 0))

    def slab(rows, columns):
        return pl.BlockSpec((1, rows, columns), lambda lap: (at(lap), 0, 0))

    specs = [
        tall(width_in),
        rim(8, width_in),
        tall(2 * NS),
        rim(16, 2 * NS),
        whole(8, width_all),
        whole(8, 2 * HP),
        tall(8),
        tall(1),
        slab(1, CHUNK),
        whole(1, width),
        whole(1, width),
    ]
    return (laps, tall, whole, slab, specs)


def ssd_forward(arrays, cos_part, sin_part):
    length, width_in = arrays[0].shape
    width, width_all = HEADS * HP, HEADS * HP + 2 * NS
    laps, tall, whole, slab, specs = ssd_specs(length, False, width_in, width_all, width)
    shaped = jax.ShapeDtypeStruct
    fold = pl.BlockSpec((CHUNK // 2, 2 * HP), lambda lap: (lap, 0))
    return pl.pallas_call(
        ssd_forward_kernel,
        grid=(laps,),
        in_specs=specs + [fold, fold],
        out_specs=[
            tall(width),
            tall(width),
            slab(NS, width),
            tall(width_all),
            fold,
        ],
        out_shape=[
            shaped((length, width), jnp.bfloat16),
            shaped((length, width), jnp.float32),
            shaped((laps, NS, width), jnp.float32),
            shaped((length, width_all), jnp.bfloat16),
            shaped((length // 2, 2 * HP), jnp.bfloat16),
        ],
        scratch_shapes=[pltpu.VMEM((NS, width), jnp.float32)],
        cost_estimate=lasting(6),
        compiler_params=pltpu.CompilerParams(vmem_limit_bytes=VMEM_BYTES),
    )(*arrays, cos_part, sin_part)


def ssd_backward(arrays, mixed, ssm, states, d_outs, d_query, grads):
    length, width_in = arrays[0].shape
    width, width_all = HEADS * HP, HEADS * HP + 2 * NS
    laps, tall, whole, slab, specs = ssd_specs(length, True, width_in, width_all, width)
    shaped = jax.ShapeDtypeStruct
    moves = (block_move(0, 0), block_move(1, 1))
    return pl.pallas_call(
        partial(ssd_backward_kernel, moves),
        grid=(laps,),
        in_specs=specs
        + [
            tall(width_all),
            tall(width),
            slab(NS, width),
            tall(width),
            tall(HD),
        ]
        + any_specs(2),
        out_specs=[
            tall(width_in + 2 * NS),
            whole(8, width_all),
            whole(8, 2 * HP),
            whole(1, width),
            whole(1, width),
        ]
        + any_specs(2),
        out_shape=[
            shaped((length, width_in + 2 * NS), jnp.bfloat16),
            shaped((8, width_all), jnp.float32),
            shaped((8, 2 * HP), jnp.float32),
            shaped((1, width), jnp.float32),
            shaped((1, width), jnp.float32),
        ]
        + [shaped(array.shape, array.dtype) for array in grads],
        scratch_shapes=[
            pltpu.VMEM((NS, width), jnp.float32),
            pltpu.VMEM((CHUNK, width_all), jnp.float32),
            pltpu.VMEM((KC - 1, 8, width_all), jnp.float32),
            pltpu.SemaphoreType.DMA((len(moves),)),
            pltpu.SemaphoreType.DMA((3 * len(moves),)),
            pltpu.SemaphoreType.DMA((3 * len(moves),)),
        ],
        cost_estimate=lasting(48),
        compiler_params=pltpu.CompilerParams(
            collective_id=13, has_side_effects=True, vmem_limit_bytes=VMEM_BYTES
        ),
    )(*arrays, mixed, ssm, states, d_outs, d_query, *grads)


QUERY_ROWS = 256


def masked_scores(q_rows, k_ref, segc_ref, segr_ref, start, reach):
    rows = q_rows.shape[0]
    scores = dot_f32(q_rows, k_ref[:reach], 1, 1) * HD ** (-0.5)
    row = lax.broadcasted_iota(jnp.int32, (rows, reach), 0) + start
    column = lax.broadcasted_iota(jnp.int32, (rows, reach), 1)
    allowed = (segc_ref[start : start + rows] == segr_ref[:, :reach]) & (row >= column)
    return jnp.where(allowed, scores, -jnp.inf)


def rotate_rows(values, cos_ref, sin_ref, sign):
    return values * cos_ref[...] + sign * (pltpu.roll(values, HD // 2, 1) * sin_ref[...])


def swap_middle(values):
    lane = lax.broadcasted_iota(jnp.int32, (1, HD), 1) // (HD // 4)
    up = pltpu.roll(values, HD // 4, 1)
    down = pltpu.roll(values, HD - HD // 4, 1)
    return jnp.where(lane == 1, down, jnp.where(lane == 2, up, values))


def unfold_rows(values, write):
    step, columns = CHUNK // 2, values.shape[1] // 2
    for start in range(0, values.shape[0], step):
        rows = values[start : start + step]
        write(2 * start, rows[:, :columns])
        write(2 * start + step, rows[:, columns:])


def fold_rows(ref, index, values):
    step = CHUNK // 2
    for start in range(0, values.shape[0] // 2, step):
        ref[index, start : start + step] = jnp.concatenate(
            [values[2 * start : 2 * start + step], values[2 * start + step : 2 * start + 2 * step]],
            axis=1,
        ).astype(ref.dtype)


def join_halves(ref, first, target):
    half = HD // 2

    def write_at(lanes):
        def write(start, rows):
            target[start : start + rows.shape[0], lanes] = rows

        return write

    unfold_rows(ref[first], write_at(slice(0, half)))
    unfold_rows(ref[first + 1], write_at(slice(half, HD)))


def attend_forward_kernel(
    raw_ref, cos_ref, sin_ref, kv_ref, segc_ref, segr_ref, out_ref, total_ref, q_ref, k_ref, v_ref
):
    q_ref[...] = swap_middle(rotate_rows(raw_ref[...], cos_ref, sin_ref, 1.0)).astype(jnp.bfloat16)
    join_halves(kv_ref, 0, k_ref)
    join_halves(kv_ref, 2, v_ref)
    for start in range(0, q_ref.shape[0], QUERY_ROWS):
        reach = start + QUERY_ROWS
        rows = slice(start, reach)
        scores = masked_scores(q_ref[rows], k_ref, segc_ref, segr_ref, start, reach)
        top = jnp.max(scores, axis=1, keepdims=True)
        powers = jnp.exp(scores - top)
        total = jnp.sum(powers, axis=1, keepdims=True)
        probs = (powers * (1.0 / total)).astype(jnp.bfloat16)
        out_ref[rows] = dot_f32(probs, v_ref[:reach], 1, 0).astype(jnp.bfloat16)
        total_ref[rows] = top + jnp.log(total)


def attend_backward_kernel(
    q_ref,
    k_ref,
    v_ref,
    cos_ref,
    sin_ref,
    segc_ref,
    segr_ref,
    total_ref,
    dout_ref,
    dq_ref,
    dkv_ref,
    dq_sum,
    dk_sum,
    dv_sum,
):
    dk_sum[...] = jnp.zeros_like(dk_sum)
    dv_sum[...] = jnp.zeros_like(dv_sum)
    for start in range(0, q_ref.shape[0], QUERY_ROWS):
        reach = start + QUERY_ROWS
        rows = slice(start, reach)
        q_rows, d_out = q_ref[rows], dout_ref[rows]
        scores = masked_scores(q_rows, k_ref, segc_ref, segr_ref, start, reach)
        probs = jnp.exp(scores - total_ref[rows])
        d_probs = dot_f32(d_out, v_ref[:reach], 1, 1)
        delta = jnp.sum(probs * d_probs, axis=1, keepdims=True)
        d_scores = (probs * (d_probs - delta)).astype(jnp.bfloat16)
        dq_sum[rows] = dot_f32(d_scores, k_ref[:reach], 1, 0) * HD ** (-0.5)
        dk_sum[:reach] += dot_f32(d_scores, q_rows, 0, 0) * HD ** (-0.5)
        dv_sum[:reach] += dot_f32(probs.astype(jnp.bfloat16), d_out, 0, 0)
    dq_ref[...] = rotate_rows(swap_middle(dq_sum[...]), cos_ref, sin_ref, -1.0).astype(jnp.bfloat16)
    half = HD // 2
    fold_rows(dkv_ref, 0, dk_sum[:, :half])
    fold_rows(dkv_ref, 1, dk_sum[:, half:])
    fold_rows(dkv_ref, 2, dv_sum[:, :half])
    fold_rows(dkv_ref, 3, dv_sum[:, half:])


def rotation_tables(length):
    half, part = HD // 2, HD // 4
    frequency = np.float32(ROPE_BASE) ** (
        np.float32(-2.0) * np.arange(half).astype(np.float32) / np.float32(HD)
    )
    angles = np.arange(length).astype(np.float32)[:, None] * frequency[None, :]
    cosine, sine_part = np.cos(angles), np.sin(angles)

    def folded(values):
        rows = values.reshape(length // CHUNK, 2, CHUNK // 2, half)
        return rows.transpose(0, 2, 1, 3).reshape(length // 2, HD)

    cos_kinds, sin_kinds = [], []
    for start in (0, part):
        columns = slice(start, start + part)
        cos_part, sin_part = cosine[:, columns], sine_part[:, columns]
        cos_kinds.append(folded(np.concatenate([cos_part, cos_part], axis=1)))
        sin_kinds.append(folded(np.concatenate([-sin_part, sin_part], axis=1)))
    cos_kinds.append(np.ones_like(cos_kinds[0]))
    sin_kinds.append(np.zeros_like(sin_kinds[0]))
    tables = (
        np.concatenate([cosine, cosine], axis=1),
        np.concatenate([-sine_part, sine_part], axis=1),
        np.stack(cos_kinds),
        np.stack(sin_kinds),
    )
    return [jnp.asarray(table.astype(np.float32)) for table in tables]


def turn_folded(values, cosine, sine_part):
    lane = lax.rem(lax.broadcasted_iota(jnp.int32, (1, HD), 1), HD // 2)
    quarter = HD // 4
    other = jnp.where(
        lane < quarter, pltpu.roll(values, HD - quarter, 1), pltpu.roll(values, quarter, 1)
    )
    return values * cosine + other * sine_part


def place_kv_kernel(lane_ref, cos_ref, sin_ref, *refs):
    parts, out_ref = refs[:-1], refs[-1]
    total = parts[0][...].astype(jnp.float32)
    for part in parts[1:]:
        total = total + part[...].astype(jnp.float32)
    half = HD // 2
    total = turn_folded(total, cos_ref[...], -sin_ref[...])

    def write(start, values):
        out_ref[start : start + values.shape[0], :half] = values.astype(jnp.bfloat16)

    unfold_rows(total, write)
    out_ref[:, half:] = lane_ref[:, half:]


def place_kv(d_projected, parts, cos_part, sin_part, width_in):
    length = d_projected.shape[0]
    lanes = pl.BlockSpec((length, HD), lambda step: (0, width_in // HD - 1))

    def whole(array):
        return pl.BlockSpec(array.shape, lambda step: (0, 0))

    arrays = (cos_part, sin_part, *parts)
    return pl.pallas_call(
        place_kv_kernel,
        grid=(1,),
        in_specs=[lanes] + [whole(array) for array in arrays],
        out_specs=lanes,
        out_shape=jax.ShapeDtypeStruct(d_projected.shape, d_projected.dtype),
        input_output_aliases={0: 0},
        cost_estimate=lasting(3),
        compiler_params=pltpu.CompilerParams(vmem_limit_bytes=VMEM_BYTES),
    )(d_projected, *arrays)


def whole_block(shape):
    return pl.BlockSpec(shape, lambda step: (0,) * len(shape))


def attend(kernel, arrays, out_shapes, scratch=(), blocks=None):
    return pl.pallas_call(
        kernel,
        grid=(1,),
        in_specs=[
            whole_block(array.shape) if blocks is None or blocks[at] is None else blocks[at]
            for at, array in enumerate(arrays)
        ],
        out_specs=[whole_block(shape) for shape, _ in out_shapes],
        out_shape=[jax.ShapeDtypeStruct(shape, dtype) for shape, dtype in out_shapes],
        scratch_shapes=[pltpu.VMEM(shape, dtype) for shape, dtype in scratch],
        cost_estimate=lasting(9),
        compiler_params=pltpu.CompilerParams(vmem_limit_bytes=VMEM_BYTES),
    )(*arrays)


def after(value, *earlier):
    return lax.optimization_barrier((value,) + earlier)[0]


def over_chips(block):
    place = lax.axis_index("seq")
    count = lax.axis_size("seq")
    stacked = jnp.zeros((count,) + block.shape, block.dtype)
    stacked = lax.dynamic_update_index_in_dim(stacked, block, place, 0)
    for mask in range(1, count):
        moved = lax.ppermute(block, "seq", [(i, i ^ mask) for i in range(count)])
        stacked = lax.dynamic_update_index_in_dim(stacked, moved, place ^ mask, 0)
    return stacked


def from_chips(blocks):
    place = lax.axis_index("seq")
    count = lax.axis_size("seq")
    moved = [lax.dynamic_index_in_dim(blocks, place, 0, False)]
    for mask in range(1, count):
        block = lax.dynamic_index_in_dim(blocks, place ^ mask, 0, False)
        moved.append(lax.ppermute(block, "seq", [(i, i ^ mask) for i in range(count)]))
    return moved


def heads_local_plan(
    hidden_in,
    teacher,
    segment_ids,
    valid_mask,
    norm1_gain,
    w_z,
    w_x,
    w_bc,
    w_dt,
    conv_weight,
    conv_bias,
    dt_bias,
    a_log,
    d_skip,
    group_gain,
    w_mamba_out,
    w_query,
    w_key,
    w_value,
    w_attn_out,
    norm2_gain,
    w_gate,
    w_up,
    w_down,
):
    place, core, data_rank = (
        lax.axis_index("seq"),
        lax.axis_index("tensor"),
        lax.axis_index("dp"),
    )
    data_count = lax.axis_size("dp")
    chip_rows, width = hidden_in.shape[1:]
    own_rows = chip_rows // 2
    length = segment_ids.shape[1]
    slice_rows = w_z.shape[0]
    width_x = HEADS * HP
    hidden_units = w_gate.shape[1] // GROUP
    segment = segment_ids[0]
    own_start = place * chip_rows + core * own_rows
    token_count = jnp.sum(valid_mask).astype(jnp.float32)
    mask_rows = lax.dynamic_slice(valid_mask, (data_rank, own_start), (1, own_rows))[0]
    total_tokens = float(valid_mask.shape[0] * valid_mask.shape[1])
    bf16 = jnp.bfloat16

    half, part = HD // 2, HD // 4
    width_in = 2 * width_x + 2 * HD
    in_slices, gains_all = first_exchange(
        (
            column_move(0, 0, 0, width_x),
            column_move(1, 0, width_x, HD),
            column_move(2, 0, width_x + HD, width_x),
            misc_move(3, 0, 2 * width_x + HD),
        ),
        (w_z, w_query, w_x, w_key, w_value, w_dt.T, norm1_gain[None], norm2_gain[None]),
        width_in,
    )
    gain_one, gain_two = gains_all[:, 0].reshape(width), gains_all[:, 1].reshape(width)
    full_in = lax.all_gather(in_slices, "dp", axis=0, tiled=True).reshape(width, width_in)
    hidden_own = lax.dynamic_slice(hidden_in[0], (core * own_rows, 0), (own_rows, width))
    hidden_own = after(hidden_own, in_slices)
    hidden_all, normed, pre_bc = gather_plane(
        hidden_own,
        1,
        apply_norm,
        (gain_one[None], w_bc),
        (((length, width), bf16), ((length, 2 * NS), bf16)),
    )
    hidden_own = hidden_own.astype(jnp.float32)
    width_out = width_x + HD
    out_slices, gu_slices, down_slices = exchange_plane(
        (
            column_move(0, 0, 0, width_x),
            column_move(1, 0, width_x, HD),
            column_move(2, 1, 0, hidden_units),
            column_move(3, 1, hidden_units, hidden_units),
            column_move(4, 2, 0, hidden_units),
        ),
        (after(w_mamba_out.T, normed), w_attn_out.T, w_gate, w_up, w_down.T),
        [
            (GROUP, slice_rows, width_out),
            (GROUP, slice_rows, 2 * hidden_units),
            (GROUP, slice_rows, hidden_units),
        ],
        4,
    )
    out_gathered = lax.all_gather(after(out_slices, full_in), "dp", axis=0, tiled=True)
    full_out = out_gathered.reshape(width, width_out)

    segment, conv_weight, conv_bias, dt_bias, a_log, d_skip, group_gain = (
        lax.optimization_barrier(
            (segment, conv_weight, conv_bias, dt_bias, a_log, d_skip, group_gain, out_slices)
        )[:7]
    )
    seg_column, seg_row = segment[:, None], segment[None, :]
    cos_wide, sin_wide, cos_folded, sin_folded = rotation_tables(length)
    kind = jnp.minimum(place, 2)
    cos_folded = lax.dynamic_index_in_dim(cos_folded, kind, 0, False)
    sin_folded = lax.dynamic_index_in_dim(sin_folded, kind, 0, False)
    head_start = core * (MH // 2) + place * HEADS

    def local_rows(values, width_head):
        return jnp.concatenate(
            [
                lax.dynamic_slice_in_dim(values, head_start * width_head, HEADS * width_head, 0),
                values[MH * width_head :],
            ],
            axis=0,
        )

    taps = jnp.concatenate(
        [local_rows(conv_weight, HP).T, local_rows(conv_bias, HP)[None]], axis=0
    )
    taps = jnp.pad(taps, ((0, 8 - KC - 1), (0, 0)))
    rate = jnp.exp(local_rows(a_log, 1))
    head_rows = jnp.stack([local_rows(dt_bias, 1), rate])
    head_rows = jnp.pad(head_rows, ((0, 6), (DT_LANE, HD - DT_LANE - HEADS)))
    skip_row = jnp.repeat(local_rows(d_skip, 1), HP)[None, :]
    gain_row = lax.dynamic_slice_in_dim(group_gain, head_start, HEADS, 0).reshape(1, width_x)
    laps = length // CHUNK
    seg_laps = segment.reshape(laps, CHUNK)
    seg_last = seg_laps[:, -1:]
    seg_before = jnp.concatenate([jnp.full((1, 1), -1, jnp.int32), seg_last[:-1]])
    seg_ext = jnp.concatenate([jnp.full((KC - 1,), -1, jnp.int32), segment])
    keeps = [(seg_laps == seg_before).reshape(length), (seg_laps == seg_last).reshape(length)]
    keeps += [seg_ext[KC - 1 - back : KC - 1 - back + length] == segment for back in range(1, KC)]
    keeps = jnp.stack(keeps + [jnp.zeros((length,), bool)] * 3, axis=1).astype(jnp.float32)

    projected = mat_dot(normed, full_in)

    ssd_arrays = (
        projected,
        projected,
        pre_bc,
        pre_bc,
        taps,
        head_rows,
        keeps,
        seg_column,
        seg_laps[:, None, :],
        skip_row,
        gain_row,
    )
    gated, ssm, states, mixed, kv_own = ssd_forward(ssd_arrays, cos_folded, sin_folded)
    kv_all = over_chips(kv_own)
    gu_gathered = lax.all_gather(after(gu_slices, out_gathered, gated), "dp", axis=0, tiled=True)
    down_gathered = lax.all_gather(after(down_slices, gu_gathered), "dp", axis=0, tiled=True)
    full_gu = gu_gathered.reshape(width, 2 * hidden_units)
    full_down = down_gathered.reshape(width, hidden_units)
    attended, log_total, queries, keys, vals = attend(
        attend_forward_kernel,
        (
            projected,
            cos_wide,
            sin_wide,
            after(kv_all, out_gathered),
            seg_column,
            seg_row,
        ),
        (
            ((length, HD), bf16),
            ((length, 1), jnp.float32),
            ((length, HD), bf16),
            ((length, HD), bf16),
            ((length, HD), bf16),
        ),
        blocks=[pl.BlockSpec((length, HD), lambda step: (0, width_x // HD))] + [None] * 5,
    )
    outs = jnp.concatenate([gated, attended], axis=1)
    middle = hidden_own + scatter_plane(outs, full_out, 2)[0]

    scale_two = lax.rsqrt(jnp.mean(middle * middle, axis=-1, keepdims=True) + EPSILON)
    normed_two, gate_up, activated = gather_plane(
        after((middle * scale_two * gain_two).astype(bf16), gu_gathered),
        9,
        apply_gate_up,
        (full_gu,),
        (((length, 2 * hidden_units), jnp.float32), ((length, hidden_units), bf16)),
    )
    block_out = middle + scatter_plane(activated, full_down, 2)[0]
    teacher_own = lax.dynamic_slice(teacher[0], (core * own_rows, 0), (own_rows, width))
    d_out = (
        2.0
        * total_tokens
        / token_count
        * mask_rows.astype(jnp.float32)[:, None]
        * (block_out - teacher_own.astype(jnp.float32))
    )
    d_mlp, d_gate_up = gather_plane(
        d_out.astype(bf16),
        10,
        apply_down_back,
        (full_down, gate_up),
        (((length, 2 * hidden_units), bf16),),
    )

    def sum_rows(grads):
        summed = lax.psum_scatter(grads.astype(bf16), "dp", scatter_dimension=0, tiled=True)
        return summed.reshape(GROUP, slice_rows, grads.shape[1])

    grad_down = sum_rows(dot_left_t(d_mlp, activated))
    d_normed_two = scatter_plane(d_gate_up, full_gu, 11)[0]
    grad_gate_up = sum_rows(
        after(dot_left_t(normed_two, d_gate_up).astype(bf16), grad_down, d_normed_two)
    )
    grad_gain_two = jnp.sum(d_normed_two * middle * scale_two, axis=0)
    d_scaled = d_normed_two * gain_two
    d_middle = (
        d_out
        + scale_two * d_scaled
        - middle * scale_two**3 * jnp.mean(d_scaled * middle, axis=-1, keepdims=True)
    )
    d_branch, d_gated, d_attended = gather_plane(
        after(d_middle.astype(bf16), grad_down),
        12,
        apply_out_back,
        (full_out,),
        (((length, width_x), jnp.float32), ((length, HD), bf16)),
    )
    d_query, d_kv = attend(
        attend_backward_kernel,
        (
            queries,
            keys,
            vals,
            cos_wide,
            sin_wide,
            seg_column,
            seg_row,
            log_total,
            d_attended,
        ),
        (((length, HD), bf16), ((GROUP, length // 2, HD), bf16)),
        (((length, HD), jnp.float32),) * 3,
    )
    d_kv_parts = from_chips(d_kv)
    grad_out = sum_rows(
        after(dot_left_t(d_branch, outs).astype(bf16), grad_gate_up, d_query)
    )
    (
        d_projected,
        grad_taps,
        grad_heads,
        d_skip_lanes,
        d_gain_lanes,
        back_gate_up,
        back_down,
    ) = ssd_backward(
        ssd_arrays, mixed, ssm, states, d_gated, d_query, (grad_gate_up, grad_down)
    )
    d_kv_parts = lax.optimization_barrier((d_projected, *d_kv_parts))[1:]
    d_projected = place_kv(d_projected, d_kv_parts, cos_folded, sin_folded, width_in)
    grad_skip = jnp.sum(d_skip_lanes.reshape(HEADS, HP), axis=-1)
    grad_group = d_gain_lanes.reshape(HEADS, HP)
    grad_in = sum_rows(
        after(dot_left_t(normed, d_projected[:, :width_in]).astype(bf16), grad_out)
    )
    bc_cols = 2 * NS // GROUP
    d_normed, bc_sum = scatter_plane(
        after(d_projected, grad_out), full_in, 8, ((normed, bc_cols, width // 2),), (w_bc,)
    )
    scale_own = lax.rsqrt(jnp.mean(hidden_own * hidden_own, axis=-1, keepdims=True) + EPSILON)
    grad_gain_one = jnp.sum(d_normed * hidden_own * scale_own, axis=0)
    d_scaled_one = d_normed * gain_one
    grad_input = (
        d_middle
        + scale_own * d_scaled_one
        - hidden_own * scale_own**3 * jnp.mean(d_scaled_one * hidden_own, axis=-1, keepdims=True)
    )
    taps_all = jnp.concatenate(
        [
            lax.dynamic_update_slice(
                jnp.zeros((8, MH * HP), jnp.float32), grad_taps[:, :width_x], (0, head_start * HP)
            ),
            grad_taps[:, width_x:],
        ],
        axis=1,
    )
    heads_all = lax.dynamic_update_slice(
        jnp.zeros((8, 128), jnp.float32),
        jnp.concatenate([grad_heads[:2, DT_LANE : DT_LANE + HEADS], grad_skip[None]]),
        (0, head_start),
    )
    group_all = lax.dynamic_update_slice(
        jnp.zeros((MH, HP), jnp.float32), grad_group, (head_start, 0)
    )
    small = [taps_all, heads_all]
    small += [
        values.reshape(8, -1) for values in (grad_gain_one, grad_gain_two, group_all)
    ]
    small = jnp.concatenate(small, axis=1)
    small_width = -(-small.shape[1] // (2 * GROUP * 128)) * 2 * GROUP * 128
    small = jnp.pad(small, ((0, 0), (0, small_width - small.shape[1])))
    piece, both_input, both_output, back_out = plane_sum(
        small, grad_input, block_out.astype(bf16), grad_out
    )
    small_all, bc_all, back_in = finish_all(piece, bc_sum, grad_in)
    bc_all = bc_all.reshape(2 * GROUP, bc_cols, width // 2)
    shapes = [
        array.shape
        for array in (
            w_gate,
            w_up,
            w_down,
            w_mamba_out,
            w_attn_out,
            w_z,
            w_x,
            w_query,
            w_bc,
            w_key,
            w_value,
            w_dt.T,
            conv_weight.T,
        )
    ]
    shapes += [(1, conv_bias.shape[0])] + [(1, MH)] * 3 + [(MH, HP)] + [(1, slice_rows)] * 2
    (
        grad_gate,
        grad_up,
        grad_down,
        grad_mo,
        grad_ao,
        grad_z,
        grad_x,
        grad_q,
        grad_bc,
        grad_k,
        grad_v,
        grad_dt,
        grad_conv,
        grad_bias,
        grad_dtb,
        grad_alog,
        grad_skip,
        grad_group,
        grad_one,
        grad_two,
    ) = unpack_all(
        (back_gate_up, back_down, back_out, back_in), bc_all, small_all, shapes
    )
    return (
        both_output.reshape(1, chip_rows, width),
        both_input.reshape(1, chip_rows, width),
        grad_one[0],
        grad_z,
        grad_x,
        grad_bc,
        grad_dt.T,
        grad_conv.T,
        grad_bias[0],
        grad_dtb[0],
        grad_alog[0],
        grad_skip[0],
        grad_group,
        grad_mo,
        grad_q,
        grad_k,
        grad_v,
        grad_ao,
        grad_two[0],
        grad_gate,
        grad_up,
        grad_down,
    )


def solution(mesh):
    placed = (
        P("dp", "seq", None),
        P("dp", "seq", None),
        P("dp", None),
        P(),
        P(("dp", "seq")),
        P(("dp", "seq"), "tensor"),
        P(("dp", "seq"), "tensor"),
        P(),
        P(("dp", "seq"), "tensor"),
        P(),
        P(),
        P(),
        P(),
        P(),
        P(),
        P("tensor", ("dp", "seq")),
        P(("dp", "seq"), "tensor"),
        P(("dp", "seq"), "tensor"),
        P(("dp", "seq"), "tensor"),
        P("tensor", ("dp", "seq")),
        P(("dp", "seq")),
        P(("dp", "seq"), "tensor"),
        P(("dp", "seq"), "tensor"),
        P("tensor", ("dp", "seq")),
    )
    whole_row = mesh.shape["seq"] == GROUP and mesh.shape["tensor"] == 2
    return jax.shard_map(
        heads_local_plan if whole_row else local,
        mesh=mesh,
        in_specs=placed,
        out_specs=(
            P("dp", "seq", None),
            P("dp", "seq", None),
            P(("dp", "seq")),
            P(("dp", "seq"), "tensor"),
            P(("dp", "seq"), "tensor"),
            P(),
            P(("dp", "seq"), "tensor"),
            P(),
            P(),
            P(),
            P(),
            P(),
            P(),
            P("tensor", ("dp", "seq")),
            P(("dp", "seq"), "tensor"),
            P(("dp", "seq"), "tensor"),
            P(("dp", "seq"), "tensor"),
            P("tensor", ("dp", "seq")),
            P(("dp", "seq")),
            P(("dp", "seq"), "tensor"),
            P(("dp", "seq"), "tensor"),
            P("tensor", ("dp", "seq")),
        ),
        check_vma=False,
    )
```

```python
from functools import partial

import jax
import jax.numpy as jnp
import numpy as np
from jax import lax
from jax.experimental import pallas as pl
from jax.experimental.pallas import tpu as pltpu
from jax.sharding import PartitionSpec as P

MH = 48
HP = 64
NS = 256
KC = 4
HD = 128


EPSILON = 1e-06
GROUP_EPSILON = 1e-05
ROPE_BASE = 10000.0
HIGHEST = lax.Precision.HIGHEST


def shifted(block, axis, distance):
    devices = range(lax.axis_size(axis))
    route = [(i - distance, i) for i in devices if i - distance in devices]
    return lax.ppermute(block, axis, route)


def carried_in(part, axis, combine, identity, reverse):
    count = lax.axis_size(axis)
    place = lax.axis_index(axis)
    ahead = count - 1 - place if reverse else place
    gathered = jax.tree.map(lambda a: lax.all_gather(a, axis), part)
    state = jax.tree.map(lambda a, e: jnp.zeros_like(a) + jnp.asarray(e, a.dtype), part, identity)

    def one(lap, state):
        source = count - 1 - lap if reverse else lap
        return combine(
            state, jax.tree.map(lambda a: lax.dynamic_index_in_dim(a, source, 0, False), gathered)
        )

    return lax.fori_loop(0, ahead, one, state)


def mat_dot(left_side, right_side):
    return jnp.dot(left_side, right_side, preferred_element_type=jnp.float32)


def dot_left_t(left_side, right_side):
    return lax.dot_general(
        left_side, right_side, (((0,), (0,)), ((), ())), preferred_element_type=jnp.float32
    )


def dot_right_t(left_side, right_side):
    return lax.dot_general(
        left_side, right_side, (((1,), (1,)), ((), ())), preferred_element_type=jnp.float32
    )


def rms_norm(values, gain_row):
    scale_row = lax.rsqrt(jnp.mean(values * values, axis=-1, keepdims=True) + EPSILON)
    return values * scale_row * gain_row


def rotate(positions, values):
    half_dim = values.shape[-1] // 2
    frequency = ROPE_BASE ** (-2.0 * jnp.arange(half_dim).astype(jnp.float32) / values.shape[-1])
    angles = positions.astype(jnp.float32)[:, None] * frequency[None, :]
    cosine = jnp.cos(angles)[:, None, :]
    sine_part = jnp.sin(angles)[:, None, :]
    first_half = values[..., :half_dim]
    second = values[..., half_dim:]
    return jnp.concatenate(
        [first_half * cosine - second * sine_part, second * cosine + first_half * sine_part],
        axis=-1,
    )


def conv_silu(seg_ext, seg_rows, extended, weights, bias_row):
    size_rows = seg_rows.shape[0]
    summed = jnp.zeros((size_rows, weights.shape[0]), jnp.float32) + bias_row[None, :]
    for tap_index in range(weights.shape[1]):
        window = lax.slice_in_dim(extended, tap_index, tap_index + size_rows, axis=0)
        keep_mask = (
            lax.slice_in_dim(seg_ext, tap_index, tap_index + size_rows) == seg_rows
        ).astype(jnp.float32)
        summed = summed + window * weights[:, tap_index][None, :] * keep_mask[:, None]
    return jax.nn.silu(summed)


def group_gate(ssm_out, gate_z, group_gain):
    mixed_val = ssm_out * jax.nn.silu(gate_z)
    return (
        mixed_val
        * lax.rsqrt(jnp.mean(mixed_val * mixed_val, axis=-1, keepdims=True) + GROUP_EPSILON)
        * group_gain[None]
    )


def swiglu(gate_pre, up_pre):
    return jax.nn.silu(gate_pre) * up_pre


def split_mixed(mixed_in, heads_local):
    size_rows = mixed_in.shape[0]
    width_x = heads_local * HP
    heads_x = mixed_in[:, :width_x].reshape(size_rows, heads_local, HP)
    return (heads_x, mixed_in[:, width_x : width_x + NS], mixed_in[:, width_x + NS :])


def ssd_main(seg_rows, seg_before, mixed_in, dt_raw, dt_bias_row, a_log_row, d_skip_row):
    size_rows = seg_rows.shape[0]
    heads_x, b_rows, c_rows = split_mixed(mixed_in, dt_raw.shape[1])
    dt_rows = jax.nn.softplus(dt_raw + dt_bias_row[None, :])
    cumul = jnp.cumsum(-jnp.exp(a_log_row)[None, :] * dt_rows, axis=0)
    order_pos = jnp.arange(size_rows)
    allowed = (seg_rows[:, None] == seg_rows[None, :]) & (order_pos[:, None] >= order_pos[None, :])
    differ = cumul[:, None, :] - cumul[None, :, :]
    decay = jnp.exp(jnp.where(allowed[:, :, None], differ, -jnp.inf))
    gram = jnp.dot(c_rows, b_rows.T, precision=HIGHEST, preferred_element_type=jnp.float32)
    mixing = gram[:, :, None] * decay * dt_rows[None, :, :]
    outputs = jnp.einsum("tsh,shp->thp", mixing, heads_x, precision=HIGHEST)
    outputs = outputs + d_skip_row[None, :, None] * heads_x
    tail_keep = (seg_rows == seg_rows[-1]).astype(jnp.float32)
    tail_weight = jnp.exp(cumul[-1][None, :] - cumul) * tail_keep[:, None] * dt_rows
    local_state = jnp.einsum("sh,shp,sn->hpn", tail_weight, heads_x, b_rows, precision=HIGHEST)
    carry_factor = jnp.exp(cumul[-1]) * (seg_rows[-1] == seg_before).astype(jnp.float32)
    return (outputs, carry_factor, local_state)


def ssd_state(seg_rows, seg_before, mixed_in, dt_raw, dt_bias_row, a_log_row, entry_state):
    heads_x, b_rows, c_rows = split_mixed(mixed_in, dt_raw.shape[1])
    dt_rows = jax.nn.softplus(dt_raw + dt_bias_row[None, :])
    cumul = jnp.cumsum(-jnp.exp(a_log_row)[None, :] * dt_rows, axis=0)
    entry_keep = (seg_rows == seg_before).astype(jnp.float32)
    entry_part = jnp.einsum("tn,hpn->thp", c_rows, entry_state, precision=HIGHEST)
    return jnp.exp(cumul)[:, :, None] * entry_keep[:, None, None] * entry_part


def chain_states(earlier, later):
    return (earlier[0] * later[0], later[0][:, None, None] * earlier[1] + later[1])


def block_scores(queries, keys_all, vals_all, seg_full, query_pos, seg_query, block_index, key_len):
    key_blk = keys_all[block_index * key_len : (block_index + 1) * key_len]
    val_blk = vals_all[block_index * key_len : (block_index + 1) * key_len]
    seg_key = seg_full[block_index * key_len : (block_index + 1) * key_len]
    key_pos = block_index * key_len + jnp.arange(key_len)
    scores = jnp.einsum(
        "tkgd,skd->kgts", queries, key_blk, preferred_element_type=jnp.float32
    ) * HD ** (-0.5)
    allowed = (query_pos[:, None] >= key_pos[None, :]) & (seg_query[:, None] == seg_key[None, :])
    return (key_blk, val_blk, jnp.where(allowed[None, None], scores, -jnp.inf))


def attend_forward(queries, keys_all, vals_all, seg_full, query_pos, seg_query, block_count):
    key_len = keys_all.shape[0] // block_count
    stat_shape = (queries.shape[1], queries.shape[2], queries.shape[0])
    running_max = jnp.full(stat_shape, -1e30, jnp.float32)
    running_sum = jnp.zeros(stat_shape, jnp.float32)
    for block_index in range(block_count):
        needed = block_index * key_len <= query_pos[-1]

        def stat_step(stats, block_index=block_index):
            old_max, old_sum = stats
            key_blk, val_blk, scores = block_scores(
                queries, keys_all, vals_all, seg_full, query_pos, seg_query, block_index, key_len
            )
            new_max = jnp.maximum(old_max, jnp.max(scores, axis=-1))
            new_sum = old_sum * jnp.exp(old_max - new_max) + jnp.sum(
                jnp.exp(scores - new_max[..., None]), axis=-1
            )
            return (new_max, new_sum)

        running_max, running_sum = lax.cond(
            needed, stat_step, lambda stats: stats, (running_max, running_sum)
        )
    log_total = running_max + jnp.log(running_sum)
    attended = jnp.zeros(queries.shape, jnp.float32)
    for block_index in range(block_count):
        needed = block_index * key_len <= query_pos[-1]

        def value_step(total, block_index=block_index):
            key_blk, val_blk, scores = block_scores(
                queries, keys_all, vals_all, seg_full, query_pos, seg_query, block_index, key_len
            )
            probs = jnp.exp(scores - log_total[..., None]).astype(jnp.bfloat16)
            return total + jnp.einsum(
                "kgts,skd->tkgd", probs, val_blk, preferred_element_type=jnp.float32
            )

        attended = lax.cond(needed, value_step, lambda total: total, attended)
    return (log_total, attended)


def attend_backward(
    queries, keys_all, vals_all, seg_full, query_pos, seg_query, block_count, grad_out, log_total
):
    key_len = keys_all.shape[0] // block_count
    delta = jnp.zeros(log_total.shape, jnp.float32)
    for block_index in range(block_count):
        needed = block_index * key_len <= query_pos[-1]

        def delta_step(total, block_index=block_index):
            key_blk, val_blk, scores = block_scores(
                queries, keys_all, vals_all, seg_full, query_pos, seg_query, block_index, key_len
            )
            probs = jnp.exp(scores - log_total[..., None])
            grad_probs = jnp.einsum(
                "tkgd,skd->kgts", grad_out, val_blk, preferred_element_type=jnp.float32
            )
            return total + jnp.sum(probs * grad_probs, axis=-1)

        delta = lax.cond(needed, delta_step, lambda total: total, delta)
    grad_query = jnp.zeros(queries.shape, jnp.float32)
    empty_part = jnp.zeros((key_len, keys_all.shape[1], keys_all.shape[2]), jnp.float32)
    key_parts = []
    val_parts = []
    for block_index in range(block_count):
        needed = block_index * key_len <= query_pos[-1]

        def grad_step(total, block_index=block_index):
            key_blk, val_blk, scores = block_scores(
                queries, keys_all, vals_all, seg_full, query_pos, seg_query, block_index, key_len
            )
            probs = jnp.exp(scores - log_total[..., None])
            grad_probs = jnp.einsum(
                "tkgd,skd->kgts", grad_out, val_blk, preferred_element_type=jnp.float32
            )
            grad_scores = (probs * (grad_probs - delta[..., None])).astype(jnp.bfloat16)
            new_total = total + jnp.einsum(
                "kgts,skd->tkgd", grad_scores, key_blk, preferred_element_type=jnp.float32
            ) * HD ** (-0.5)
            key_part = jnp.einsum(
                "kgts,tkgd->skd", grad_scores, queries, preferred_element_type=jnp.float32
            ) * HD ** (-0.5)
            val_part = jnp.einsum(
                "kgts,tkgd->skd",
                probs.astype(jnp.bfloat16),
                grad_out,
                preferred_element_type=jnp.float32,
            )
            return (new_total, key_part, val_part)

        grad_query, key_part, val_part = lax.cond(
            needed, grad_step, lambda total: (total, empty_part, empty_part), grad_query
        )
        key_parts.append(key_part)
        val_parts.append(val_part)
    return (grad_query, jnp.concatenate(key_parts, axis=0), jnp.concatenate(val_parts, axis=0))


def local(
    hidden_in,
    teacher,
    segment_ids,
    valid_mask,
    norm1_gain,
    w_z,
    w_x,
    w_bc,
    w_dt,
    conv_weight,
    conv_bias,
    dt_bias,
    a_log,
    d_skip,
    group_gain,
    w_mamba_out,
    w_query,
    w_key,
    w_value,
    w_attn_out,
    norm2_gain,
    w_gate,
    w_up,
    w_down,
):
    tensor_rank = lax.axis_index("tensor")
    seq_rank = lax.axis_index("seq")
    data_rank = lax.axis_index("dp")
    seq_count = lax.axis_size("seq")
    tensor_count = lax.axis_size("tensor")
    size_rows = hidden_in.shape[1]
    full_length = segment_ids.shape[1]
    row_start = seq_rank * size_rows
    seg_full = segment_ids[0]
    seg_local = lax.dynamic_slice_in_dim(seg_full, row_start, size_rows)
    seg_padded = jnp.concatenate([jnp.full((KC - 1,), -1, jnp.int32), seg_full])
    seg_ext = lax.dynamic_slice_in_dim(seg_padded, row_start, size_rows + KC - 1)
    seg_prev = lax.dynamic_index_in_dim(seg_padded, row_start + KC - 2, keepdims=False)
    token_count = jnp.sum(valid_mask).astype(jnp.float32)
    mask_rows = lax.dynamic_slice(valid_mask, (data_rank, row_start), (1, size_rows))[0].astype(
        jnp.float32
    )
    total_tokens = float(valid_mask.shape[0] * valid_mask.shape[1])
    (
        gain_one,
        full_z,
        full_x,
        full_dt,
        full_mo,
        full_q,
        full_k,
        full_v,
        full_ao,
        gain_two,
        full_gate,
        full_up,
        full_down,
    ) = (
        lax.all_gather(norm1_gain, ("dp", "seq"), axis=0, tiled=True),
        lax.all_gather(w_z, ("dp", "seq"), axis=0, tiled=True),
        lax.all_gather(w_x, ("dp", "seq"), axis=0, tiled=True),
        lax.all_gather(w_dt, ("dp", "seq"), axis=0, tiled=True),
        lax.all_gather(w_mamba_out, ("dp", "seq"), axis=1, tiled=True),
        lax.all_gather(w_query, ("dp", "seq"), axis=0, tiled=True),
        lax.all_gather(w_key, ("dp", "seq"), axis=0, tiled=True),
        lax.all_gather(w_value, ("dp", "seq"), axis=0, tiled=True),
        lax.all_gather(w_attn_out, ("dp", "seq"), axis=1, tiled=True),
        lax.all_gather(norm2_gain, ("dp", "seq"), axis=0, tiled=True),
        lax.all_gather(w_gate, ("dp", "seq"), axis=0, tiled=True),
        lax.all_gather(w_up, ("dp", "seq"), axis=0, tiled=True),
        lax.all_gather(w_down, ("dp", "seq"), axis=1, tiled=True),
    )
    heads_local = MH // tensor_count
    width_x = heads_local * HP
    head_start = tensor_rank * heads_local
    hidden = hidden_in[0].astype(jnp.float32)
    normed_f, norm_one_pull = jax.vjp(rms_norm, hidden, gain_one.astype(jnp.float32))
    normed = normed_f.astype(jnp.bfloat16)
    gate_z = mat_dot(normed, full_z)
    pre_x = mat_dot(normed, full_x).astype(jnp.bfloat16)
    pre_bc = mat_dot(normed, w_bc).astype(jnp.bfloat16)
    dt_raw = mat_dot(normed, full_dt)
    pre_all = jnp.concatenate([pre_x, pre_bc], axis=1)
    rim_rows = shifted(pre_all[size_rows - (KC - 1) :], "seq", 1)
    extended = jnp.concatenate([rim_rows, pre_all], axis=0).astype(jnp.float32)
    conv_local = jnp.concatenate(
        [
            lax.dynamic_slice_in_dim(conv_weight, head_start * HP, width_x, 0),
            conv_weight[MH * HP :],
        ],
        axis=0,
    )
    bias_local = jnp.concatenate(
        [lax.dynamic_slice_in_dim(conv_bias, head_start * HP, width_x, 0), conv_bias[MH * HP :]],
        axis=0,
    )
    mixed_f, conv_pull = jax.vjp(
        partial(conv_silu, seg_ext, seg_local), extended, conv_local, bias_local
    )
    mixed_in = lax.optimization_barrier(mixed_f.astype(jnp.bfloat16)).astype(jnp.float32)
    dt_bias_loc = lax.dynamic_slice_in_dim(dt_bias, head_start, heads_local)
    a_log_loc = lax.dynamic_slice_in_dim(a_log, head_start, heads_local)
    d_skip_loc = lax.dynamic_slice_in_dim(d_skip, head_start, heads_local)
    group_loc = lax.dynamic_slice_in_dim(group_gain, head_start, heads_local, 0)
    (ssm_local, carry_dev, state_dev), main_pull = jax.vjp(
        partial(ssd_main, seg_local, seg_prev), mixed_in, dt_raw, dt_bias_loc, a_log_loc, d_skip_loc
    )
    identity = (jnp.ones_like(carry_dev), jnp.zeros_like(state_dev))
    entry_state = carried_in((carry_dev, state_dev), "seq", chain_states, identity, False)[1]
    ssm_entry, state_pull = jax.vjp(
        partial(ssd_state, seg_local, seg_prev),
        mixed_in,
        dt_raw,
        dt_bias_loc,
        a_log_loc,
        entry_state,
    )
    ssm_out = ssm_local + ssm_entry
    gated_f, gate_pull = jax.vjp(
        group_gate, ssm_out, gate_z.reshape(size_rows, heads_local, HP), group_loc
    )
    gated = gated_f.reshape(size_rows, width_x).astype(jnp.bfloat16)
    mamba_part = mat_dot(gated, full_mo)
    positions = row_start + jnp.arange(size_rows)
    heads_q = full_q.shape[1] // HD
    heads_kv = full_k.shape[1] // HD
    groups = heads_q // heads_kv
    query_rot, query_pull = jax.vjp(
        partial(rotate, positions), mat_dot(normed, full_q).reshape(size_rows, heads_q, HD)
    )
    queries = query_rot.astype(jnp.bfloat16).reshape(size_rows, heads_kv, groups, HD)
    key_rot, key_pull = jax.vjp(
        partial(rotate, positions), mat_dot(normed, full_k).reshape(size_rows, heads_kv, HD)
    )
    keys_local = key_rot.astype(jnp.bfloat16).reshape(size_rows, heads_kv * HD)
    vals_local = mat_dot(normed, full_v).astype(jnp.bfloat16)
    keys_all, vals_all = (
        lax.all_gather(keys_local, "seq", axis=0, tiled=True),
        lax.all_gather(vals_local, "seq", axis=0, tiled=True),
    )
    keys_all = keys_all.reshape(full_length, heads_kv, HD)
    vals_all = vals_all.reshape(full_length, heads_kv, HD)
    block_count = seq_count // 4
    log_total, attended_f = attend_forward(
        queries, keys_all, vals_all, seg_full, positions, seg_local, block_count
    )
    attended = attended_f.reshape(size_rows, heads_q * HD).astype(jnp.bfloat16)
    branch = lax.psum(mamba_part + mat_dot(attended, full_ao), "tensor")
    middle = hidden + branch
    normed_two_f, norm_two_pull = jax.vjp(rms_norm, middle, gain_two.astype(jnp.float32))
    normed_two = normed_two_f.astype(jnp.bfloat16)
    act_f, glu_pull = jax.vjp(swiglu, mat_dot(normed_two, full_gate), mat_dot(normed_two, full_up))
    activated = act_f.astype(jnp.bfloat16)
    block_out = middle + lax.psum(mat_dot(activated, full_down), "tensor")
    (
        back_z,
        back_x,
        back_dt,
        back_mo,
        back_q,
        back_k,
        back_v,
        back_ao,
        back_gate,
        back_up,
        back_down,
    ) = (
        lax.all_gather(w_z, ("dp", "seq"), axis=0, tiled=True),
        lax.all_gather(w_x, ("dp", "seq"), axis=0, tiled=True),
        lax.all_gather(w_dt, ("dp", "seq"), axis=0, tiled=True),
        lax.all_gather(w_mamba_out, ("dp", "seq"), axis=1, tiled=True),
        lax.all_gather(w_query, ("dp", "seq"), axis=0, tiled=True),
        lax.all_gather(w_key, ("dp", "seq"), axis=0, tiled=True),
        lax.all_gather(w_value, ("dp", "seq"), axis=0, tiled=True),
        lax.all_gather(w_attn_out, ("dp", "seq"), axis=1, tiled=True),
        lax.all_gather(w_gate, ("dp", "seq"), axis=0, tiled=True),
        lax.all_gather(w_up, ("dp", "seq"), axis=0, tiled=True),
        lax.all_gather(w_down, ("dp", "seq"), axis=1, tiled=True),
    )
    d_out = (
        2.0
        * total_tokens
        / token_count
        * mask_rows[:, None]
        * (block_out - teacher[0].astype(jnp.float32))
    )
    d_mlp = d_out.astype(jnp.bfloat16)
    grad_down = dot_left_t(activated, d_mlp)
    d_gate_f, d_up_f = glu_pull(dot_right_t(d_mlp, back_down))
    d_gate = d_gate_f.astype(jnp.bfloat16)
    d_up = d_up_f.astype(jnp.bfloat16)
    grad_gate = dot_left_t(normed_two, d_gate)
    grad_up = dot_left_t(normed_two, d_up)
    d_normed_two = lax.psum(dot_right_t(d_gate, back_gate) + dot_right_t(d_up, back_up), "tensor")
    d_middle_n, grad_gain_two = norm_two_pull(d_normed_two)
    d_middle = d_out + d_middle_n
    d_branch = d_middle.astype(jnp.bfloat16)
    grad_ao = dot_left_t(attended, d_branch)
    grad_mo = dot_left_t(gated, d_branch)
    d_attended = (
        dot_right_t(d_branch, back_ao).astype(jnp.bfloat16).reshape(size_rows, heads_kv, groups, HD)
    )
    d_gated = dot_right_t(d_branch, back_mo).reshape(size_rows, heads_local, HP)
    d_ssm, d_gate_z_f, grad_group = gate_pull(d_gated)
    d_gate_z = d_gate_z_f.reshape(size_rows, width_x).astype(jnp.bfloat16)
    d_mixed_s, d_dt_s, d_dtb_s, d_alog_s, d_entry = state_pull(d_ssm)
    state_grad = carried_in((carry_dev, d_entry), "seq", chain_states, identity, True)[1]
    d_carry = jnp.sum(state_grad * entry_state, axis=(1, 2))
    d_mixed_m, d_dt_m, d_dtb_m, d_alog_m, grad_skip = main_pull((d_ssm, d_carry, state_grad))
    d_dt_raw = (d_dt_s + d_dt_m).astype(jnp.bfloat16)
    d_ext, grad_conv_loc, grad_bias_loc = conv_pull(d_mixed_s + d_mixed_m)
    rim_grad = shifted(d_ext[: KC - 1], "seq", -1)
    d_pre = d_ext[KC - 1 :] + jnp.pad(rim_grad, ((size_rows - (KC - 1), 0), (0, 0)))
    d_pre_x = d_pre[:, :width_x].astype(jnp.bfloat16)
    d_pre_bc = d_pre[:, width_x:]
    grad_query_rot, key_grads_all, val_grads_all = attend_backward(
        queries,
        keys_all,
        vals_all,
        seg_full,
        positions,
        seg_local,
        block_count,
        d_attended,
        log_total,
    )
    key_grad, val_grad = (
        lax.psum_scatter(
            key_grads_all.reshape(full_length, heads_kv * HD).astype(jnp.bfloat16),
            "seq",
            scatter_dimension=0,
            tiled=True,
        ).astype(jnp.float32),
        lax.psum_scatter(
            val_grads_all.reshape(full_length, heads_kv * HD).astype(jnp.bfloat16),
            "seq",
            scatter_dimension=0,
            tiled=True,
        ).astype(jnp.float32),
    )
    d_query = (
        query_pull(grad_query_rot.reshape(size_rows, heads_q, HD))[0]
        .reshape(size_rows, heads_q * HD)
        .astype(jnp.bfloat16)
    )
    d_key = (
        key_pull(key_grad.reshape(size_rows, heads_kv, HD))[0]
        .reshape(size_rows, heads_kv * HD)
        .astype(jnp.bfloat16)
    )
    d_value = val_grad.astype(jnp.bfloat16)
    grad_z = dot_left_t(normed, d_gate_z)
    grad_x = dot_left_t(normed, d_pre_x)
    grad_dt = dot_left_t(normed, d_dt_raw)
    grad_q = dot_left_t(normed, d_query)
    grad_k = dot_left_t(normed, d_key)
    grad_v = dot_left_t(normed, d_value)
    normed_wide = normed.astype(jnp.float32)
    bc_weight = w_bc.astype(jnp.float32)
    grad_bc = jnp.dot(
        normed_wide.T, d_pre_bc, precision=HIGHEST, preferred_element_type=jnp.float32
    )
    d_normed_part = (
        dot_right_t(d_gate_z, back_z)
        + dot_right_t(d_pre_x, back_x)
        + dot_right_t(d_dt_raw, back_dt)
        + dot_right_t(d_query, back_q)
        + dot_right_t(d_key, back_k)
        + dot_right_t(d_value, back_v)
        + jnp.dot(d_pre_bc, bc_weight.T, precision=HIGHEST, preferred_element_type=jnp.float32)
    )
    d_normed = lax.psum(d_normed_part.astype(jnp.bfloat16), "tensor").astype(jnp.float32)
    d_hidden_n, grad_gain_one = norm_one_pull(d_normed)
    grad_input = d_middle + d_hidden_n
    conv_x_full = lax.dynamic_update_slice_in_dim(
        jnp.zeros((MH * HP, KC), jnp.float32), grad_conv_loc[:width_x], head_start * HP, 0
    )
    grad_conv_full = jnp.concatenate([conv_x_full, grad_conv_loc[width_x:]], axis=0)
    bias_x_full = lax.dynamic_update_slice_in_dim(
        jnp.zeros((MH * HP,), jnp.float32), grad_bias_loc[:width_x], head_start * HP, 0
    )
    grad_bias_full = jnp.concatenate([bias_x_full, grad_bias_loc[width_x:]], axis=0)
    grad_dtb_full = lax.dynamic_update_slice_in_dim(
        jnp.zeros((MH,), jnp.float32), d_dtb_s + d_dtb_m, head_start, 0
    )
    grad_alog_full = lax.dynamic_update_slice_in_dim(
        jnp.zeros((MH,), jnp.float32), d_alog_s + d_alog_m, head_start, 0
    )
    grad_skip_full = lax.dynamic_update_slice_in_dim(
        jnp.zeros((MH,), jnp.float32), grad_skip, head_start, 0
    )
    grad_group_full = lax.dynamic_update_slice_in_dim(
        jnp.zeros((MH, HP), jnp.float32), grad_group, head_start, 0
    )
    sum_bc, sum_conv, sum_bias, sum_dtb, sum_alog, sum_skip, sum_group = lax.psum(
        (
            grad_bc,
            grad_conv_full,
            grad_bias_full,
            grad_dtb_full,
            grad_alog_full,
            grad_skip_full,
            grad_group_full,
        ),
        ("dp", "seq", "tensor"),
    )
    (
        out_gain_one,
        out_z,
        out_x,
        out_dt,
        out_mo,
        out_q,
        out_k,
        out_v,
        out_ao,
        out_gain_two,
        out_gate,
        out_up,
        out_down,
    ) = (
        lax.psum_scatter(grad_gain_one, ("dp", "seq"), scatter_dimension=0, tiled=True),
        lax.psum_scatter(grad_z, ("dp", "seq"), scatter_dimension=0, tiled=True),
        lax.psum_scatter(grad_x, ("dp", "seq"), scatter_dimension=0, tiled=True),
        lax.psum_scatter(grad_dt, ("dp", "seq"), scatter_dimension=0, tiled=True),
        lax.psum_scatter(grad_mo, ("dp", "seq"), scatter_dimension=1, tiled=True),
        lax.psum_scatter(grad_q, ("dp", "seq"), scatter_dimension=0, tiled=True),
        lax.psum_scatter(grad_k, ("dp", "seq"), scatter_dimension=0, tiled=True),
        lax.psum_scatter(grad_v, ("dp", "seq"), scatter_dimension=0, tiled=True),
        lax.psum_scatter(grad_ao, ("dp", "seq"), scatter_dimension=1, tiled=True),
        lax.psum_scatter(grad_gain_two, ("dp", "seq"), scatter_dimension=0, tiled=True),
        lax.psum_scatter(grad_gate, ("dp", "seq"), scatter_dimension=0, tiled=True),
        lax.psum_scatter(grad_up, ("dp", "seq"), scatter_dimension=0, tiled=True),
        lax.psum_scatter(grad_down, ("dp", "seq"), scatter_dimension=1, tiled=True),
    )
    return (
        block_out.astype(jnp.bfloat16)[None],
        grad_input[None],
        out_gain_one,
        out_z,
        out_x,
        sum_bc,
        out_dt,
        sum_conv,
        sum_bias,
        sum_dtb,
        sum_alog,
        sum_skip,
        sum_group,
        out_mo,
        out_q,
        out_k,
        out_v,
        out_ao,
        out_gain_two,
        out_gate,
        out_up,
        out_down,
    )


GROUP = 4
CHUNK = 128
HEADS = 6
MESH_ID = pl.DeviceIdType.MESH
VMEM_BYTES = 56 * 1024 * 1024


def dot_f32(left_side, right_side, left_dim, right_dim):
    return lax.dot_general(
        left_side,
        right_side,
        (((left_dim,), (right_dim,)), ((), ())),
        preferred_element_type=jnp.float32,
    )


def halves(values):
    high = values.astype(jnp.bfloat16)
    return (high, (values - high.astype(jnp.float32)).astype(jnp.bfloat16))


def plane_place():
    data, place, core = lax.axis_index("dp"), lax.axis_index("seq"), lax.axis_index("tensor")
    along_x = place + 1 - 2 * lax.rem(place, 2)
    along_y = lax.rem(place + 2, GROUP)
    across = GROUP - 1 - place
    return (data, place, core, along_x, along_y, across)


def meet(devices):
    barrier = pltpu.get_barrier_semaphore()
    for device in devices:
        pl.semaphore_signal(barrier, inc=1, device_id=device, device_id_type=MESH_ID)
    pl.semaphore_wait(barrier, len(devices))


def remote(source, target, send_sem, recv_sem, device):
    return pltpu.make_async_remote_copy(
        src_ref=source,
        dst_ref=target,
        send_sem=send_sem,
        recv_sem=recv_sem,
        device_id=device,
        device_id_type=MESH_ID,
    )


def lasting(microseconds):
    return pl.CostEstimate(
        flops=int(microseconds * 9e8),
        bytes_accessed=int(microseconds * 3e6),
        transcendentals=0,
    )


def any_specs(count):
    return [pl.BlockSpec(memory_space=pl.ANY)] * count


def vmem_specs(count):
    return [pl.BlockSpec(memory_space=pltpu.VMEM)] * count


def gather_kernel(apply, count_in, count_out, own_ref, *refs):
    inputs, all_ref = refs[:count_in], refs[count_in]
    outputs = refs[count_in + 1 : count_in + 1 + count_out]
    send_sems, recv_sems = refs[count_in + 1 + count_out :]
    data, place, core, along_x, along_y, across = plane_place()
    to_x, to_y, partner = (data, along_x, core), (data, along_y, core), (data, place, 1 - core)
    meet((to_x, to_y, partner))
    gather_steps(apply, own_ref, inputs, all_ref, outputs, send_sems, recv_sems)


def gather_steps(apply, own_ref, inputs, all_ref, outputs, send_sems, recv_sems, ready=None):
    data, place, core, along_x, along_y, across = plane_place()
    height = own_ref.shape[0]
    half = height // 2
    to_x, to_y, partner = (data, along_x, core), (data, along_y, core), (data, place, 1 - core)

    def block(chip, part):
        return all_ref.at[2 * chip + core, pl.ds(part * half, half)]

    def work(chip, side):
        if apply is not None:
            index = 2 * chip + side
            rows = pl.ds(pl.multiple_of(index * height, 16), height)
            apply(all_ref[index], rows, inputs, outputs)

    def push(index, source, target, device):
        copy = remote(source, target, send_sems.at[index], recv_sems.at[index], device)
        copy.start()
        return copy

    first, second = own_ref.at[pl.ds(0, half)], own_ref.at[pl.ds(half, half)]
    x_first = push(0, first, block(place, 0), to_x)
    y_second = push(1, second, block(place, 1), to_y)
    x_second = push(2, second, block(place, 1), to_x)
    y_first = push(3, first, block(place, 0), to_y)
    pair_own = push(4, own_ref, all_ref.at[2 * place + core], partner)
    all_ref[2 * place + core] = own_ref[...]
    work(place, core)
    pair_own.wait_recv()
    work(place, 1 - core)
    if ready is not None:
        ready(place, 0)
    x_first.wait_recv()
    over_y = push(5, block(along_x, 0), block(along_x, 0), to_y)
    y_second.wait_recv()
    over_x = push(6, block(along_y, 1), block(along_y, 1), to_x)
    x_second.wait_recv()
    mine_x = all_ref.at[2 * along_x + core]
    pair_x = push(7, mine_x, mine_x, partner)
    y_first.wait_recv()
    mine_y = all_ref.at[2 * along_y + core]
    pair_y = push(8, mine_y, mine_y, partner)
    work(along_x, core)
    work(along_y, core)
    pair_x.wait_recv()
    work(along_x, 1 - core)
    if ready is not None:
        ready(along_x, 1)
    pair_y.wait_recv()
    work(along_y, 1 - core)
    if ready is not None:
        ready(along_y, 2)
    over_y.wait_recv()
    pair_a = push(9, block(across, 0), block(across, 0), partner)
    over_x.wait_recv()
    pair_b = push(10, block(across, 1), block(across, 1), partner)
    work(across, core)
    pair_a.wait_recv()
    pair_b.wait_recv()
    work(across, 1 - core)
    if ready is not None:
        ready(across, 3)
    for copy in (
        x_first,
        y_second,
        x_second,
        y_first,
        pair_own,
        over_y,
        over_x,
        pair_x,
        pair_y,
        pair_a,
        pair_b,
    ):
        copy.wait_send()


def gather_plane(own, identity=1, apply=None, inputs=(), outputs=()):
    rows, width = own.shape
    gathered, *results = pl.pallas_call(
        partial(gather_kernel, apply, len(inputs), len(outputs)),
        out_shape=[jax.ShapeDtypeStruct((2 * GROUP, rows, width), own.dtype)]
        + [jax.ShapeDtypeStruct(shape, dtype) for shape, dtype in outputs],
        in_specs=vmem_specs(1 + len(inputs)),
        out_specs=vmem_specs(1 + len(outputs)),
        scratch_shapes=[pltpu.SemaphoreType.DMA((11,)), pltpu.SemaphoreType.DMA((11,))],
        cost_estimate=lasting(35),
        compiler_params=pltpu.CompilerParams(
            collective_id=identity, has_side_effects=True, vmem_limit_bytes=VMEM_BYTES
        ),
    )(own, *inputs)
    gathered = gathered.reshape(2 * GROUP * rows, width)
    return (gathered, *results) if results else gathered


def apply_gate_up(block, rows, inputs, outputs):
    weights, (both_ref, act_ref) = inputs[0], outputs
    units = act_ref.shape[1]
    both = jnp.dot(block, weights[...], preferred_element_type=jnp.float32)
    both_ref[rows] = both
    gate = both[:, :units]
    act_ref[rows] = (gate * jax.nn.sigmoid(gate) * both[:, units:]).astype(jnp.bfloat16)


def apply_down_back(block, rows, inputs, outputs):
    weights, both_ref = inputs
    units = weights.shape[1]
    d_act = jnp.dot(block, weights[...], preferred_element_type=jnp.float32)
    gate, up = both_ref[rows, :units], both_ref[rows, units:]
    sigmoid = jax.nn.sigmoid(gate)
    silu = gate * sigmoid
    d_gate = d_act * up * (sigmoid * (1.0 + gate * (1.0 - sigmoid)))
    outputs[0][rows, :units] = d_gate.astype(jnp.bfloat16)
    outputs[0][rows, units:] = (d_act * silu).astype(jnp.bfloat16)


def apply_out_back(block, rows, inputs, outputs):
    both = jnp.dot(block, inputs[0][...], preferred_element_type=jnp.float32)
    width = outputs[0].shape[1]
    outputs[0][rows] = both[:, :width]
    outputs[1][rows] = both[:, width:].astype(jnp.bfloat16)


def apply_norm(block, rows, inputs, outputs):
    gain_ref, weights = inputs
    values = block.astype(jnp.float32)
    scale = lax.rsqrt(jnp.mean(values * values, axis=-1, keepdims=True) + EPSILON)
    normed = (values * scale * gain_ref[...]).astype(jnp.bfloat16)
    outputs[0][rows] = normed
    outputs[1][rows] = jnp.dot(normed, weights[...], preferred_element_type=jnp.float32).astype(
        jnp.bfloat16
    )


def scatter_kernel(count, left_ref, right_ref, *refs, store=None, between=None):
    data, place, core, along_x, along_y, across = plane_place()
    partner = (data, place, 1 - core)
    to_x, to_y = (data, along_x, core), (data, along_y, core)
    order = (across, along_x, along_y, place)
    count_in = 0 if count == 1 else count
    extra, sums = refs[:count_in], refs[count_in : count_in + count]
    parts, scratch = refs[count_in + count : count_in + 2 * count], refs[count_in + 2 * count :]
    step = 16
    meet((partner, to_x, to_y))

    def multiply(at, chip, side):
        part = parts[at]
        index = 2 * chip + side
        height, columns = part.shape[1:]
        if at == 0:
            rows = pl.ds(pl.multiple_of(index * height, 16), height)
            depth = right_ref.shape[1]
            block = dot_f32(left_ref[rows, :depth], right_ref[...], 1, 1)
            if count > 1:
                block = block + dot_f32(left_ref[rows, depth:], extra[-1][...], 1, 1)
        else:
            start = left_ref.shape[1] - GROUP * height
            turned = pl.ds(pl.multiple_of(start + chip * height, 128), height)
            along = pl.ds(pl.multiple_of(side * columns, 128), columns)
            block = dot_f32(left_ref[:, turned], extra[at - 1][:, along], 0, 0)
        part[index] = block.astype(jnp.bfloat16)

    def one_array(at, part_ref, sum_ref, own_refs):
        pair_in, send_a, send_x, send_y, got_x, got_y, pair_s, pair_r, send_s, recv_s = own_refs
        half = part_ref.shape[1] // 2
        pair = []

        def send_pair(index):
            chip = order[index]
            multiply(at, chip, 1 - core)
            copy = remote(
                part_ref.at[2 * chip + 1 - core],
                pair_in.at[index],
                pair_s.at[index],
                pair_r.at[index],
                partner,
            )
            copy.start()
            pair.append(copy)
            multiply(at, chip, core)

        def own_rows(index, rows):
            return part_ref[2 * order[index] + core, rows].astype(jnp.float32) + pair_in[
                index, rows
            ].astype(jnp.float32)

        def fill(target, index, first, extra=None):
            def one(lap, carry):
                rows = pl.ds(pl.multiple_of(lap * step, step), step)
                total = own_rows(index, pl.ds(pl.multiple_of(first + lap * step, step), step))
                if extra is not None:
                    total = total + extra[rows].astype(jnp.float32)
                target[rows] = total.astype(jnp.bfloat16)
                return carry

            lax.fori_loop(0, half // step, one, 0)

        def push(index, source, target, device):
            copy = remote(source, target, send_s.at[index], recv_s.at[index], device)
            copy.start()
            return copy

        send_pair(0)
        pair[0].wait_recv()
        fill(send_a.at[0], 0, 0)
        far_x = push(0, send_a.at[0], got_x.at[0], to_x)
        fill(send_a.at[1], 0, half)
        far_y = push(1, send_a.at[1], got_y.at[0], to_y)
        send_pair(1)
        pair[1].wait_recv()
        fill(send_x.at[0], 1, 0)
        near_x = push(2, send_x.at[0], got_x.at[1], to_x)
        send_pair(2)
        pair[2].wait_recv()
        fill(send_y.at[0], 2, half)
        near_y = push(3, send_y.at[0], got_y.at[1], to_y)
        send_pair(3)
        yield
        far_x.wait_recv()
        fill(send_y.at[1], 2, 0, got_x.at[0])
        last_y = push(4, send_y.at[1], got_y.at[2], to_y)
        far_y.wait_recv()
        fill(send_x.at[1], 1, half, got_y.at[0])
        last_x = push(5, send_x.at[1], got_x.at[2], to_x)
        yield
        pair[3].wait_recv()
        near_x.wait_recv()
        near_y.wait_recv()
        last_y.wait_recv()
        last_x.wait_recv()

        def finish(first, near, last):
            def one(lap, carry):
                rows = pl.ds(pl.multiple_of(lap * step, step), step)
                place_rows = pl.ds(pl.multiple_of(first + lap * step, step), step)
                total = (
                    own_rows(3, place_rows)
                    + near[rows].astype(jnp.float32)
                    + last[rows].astype(jnp.float32)
                )
                if store is None:
                    sum_ref[place_rows] = total
                else:
                    store(place_rows, total)
                return carry

            lax.fori_loop(0, half // step, one, 0)

        finish(0, got_x.at[1], got_y.at[2])
        finish(half, got_y.at[1], got_x.at[2])
        for copy in pair + [far_x, far_y, near_x, near_y, last_x, last_y]:
            copy.wait_send()

    each = len(scratch) // count
    runs = [
        one_array(at, parts[at], sums[at], scratch[each * at : each * (at + 1)]) for at in range(count)
    ]
    for stage in range(2):
        for run in runs:
            next(run)
        if between is not None:
            between(stage)
    for run in runs:
        for _ in run:
            pass


def down_and_back_kernel(
    act_ref,
    weights_ref,
    middle_ref,
    teacher_ref,
    factor_ref,
    both_ref,
    out_ref,
    d_out_ref,
    d_mlp_ref,
    d_both_ref,
    grad_ref,
    own_ref,
    grad_sum,
    gather_send,
    gather_recv,
    *scratch,
):
    def store(rows, total):
        out = middle_ref[rows] + total
        out_ref[rows] = out.astype(jnp.bfloat16)
        d_out = factor_ref[rows] * (out - teacher_ref[rows].astype(jnp.float32))
        d_out_ref[rows] = d_out
        own_ref[rows] = d_out.astype(jnp.bfloat16)

    def ready(chip, turn_at):
        blocks = d_mlp_ref[pl.ds(2 * chip, 2)]
        height = blocks.shape[0] * blocks.shape[1]
        rows = pl.ds(pl.multiple_of(chip * height, 16), height)
        part = dot_f32(blocks.reshape(height, blocks.shape[2]), act_ref[rows], 0, 0)
        if turn_at == 0:
            grad_sum[...] = part
        elif turn_at < GROUP - 1:
            grad_sum[...] += part
        else:
            grad_ref[...] = (grad_sum[...] + part).astype(jnp.bfloat16)

    scatter_kernel(1, act_ref, weights_ref, None, *scratch, store=store)
    gather_steps(
        apply_down_back,
        own_ref,
        (weights_ref, both_ref),
        d_mlp_ref,
        (d_both_ref,),
        gather_send,
        gather_recv,
        ready,
    )


def down_and_back(activated, full_down, middle, teacher_own, factor, gate_up):
    rows, width = middle.shape
    shaped = jax.ShapeDtypeStruct
    return pl.pallas_call(
        down_and_back_kernel,
        out_shape=[
            shaped((rows, width), jnp.bfloat16),
            shaped((rows, width), jnp.float32),
            shaped((2 * GROUP, rows, width), jnp.bfloat16),
            shaped(gate_up.shape, jnp.bfloat16),
            shaped(full_down.shape, jnp.bfloat16),
        ],
        in_specs=vmem_specs(6),
        out_specs=vmem_specs(5),
        scratch_shapes=[
            pltpu.VMEM((rows, width), jnp.bfloat16),
            pltpu.VMEM(full_down.shape, jnp.float32),
            pltpu.SemaphoreType.DMA((11,)),
            pltpu.SemaphoreType.DMA((11,)),
        ]
        + scatter_scratch([(rows, width)]),
        cost_estimate=lasting(70),
        compiler_params=pltpu.CompilerParams(
            collective_id=10, has_side_effects=True, vmem_limit_bytes=VMEM_BYTES
        ),
    )(activated, full_down, middle, teacher_own, factor, gate_up)


def up_back_kernel(d_both_ref, weights_ref, normed_ref, sum_ref, grad_ref, *scratch):
    tiles = 4
    width = normed_ref.shape[1] // tiles

    def between(stage):
        for tile in range(2 * stage, 2 * stage + 2):
            columns = slice(width * tile, width * (tile + 1))
            grad_ref[columns] = dot_f32(
                normed_ref[:, columns], d_both_ref[...], 0, 0
            ).astype(jnp.bfloat16)

    scatter_kernel(1, d_both_ref, weights_ref, sum_ref, *scratch, between=between)


def up_back(d_gate_up, full_gu, normed_two):
    rows, width = d_gate_up.shape[0] // (2 * GROUP), full_gu.shape[0]
    return pl.pallas_call(
        up_back_kernel,
        out_shape=[
            jax.ShapeDtypeStruct((rows, width), jnp.float32),
            jax.ShapeDtypeStruct(full_gu.shape, jnp.bfloat16),
        ],
        in_specs=vmem_specs(3),
        out_specs=vmem_specs(2),
        scratch_shapes=scatter_scratch([(rows, width)]),
        cost_estimate=lasting(38),
        compiler_params=pltpu.CompilerParams(
            collective_id=11, has_side_effects=True, vmem_limit_bytes=VMEM_BYTES
        ),
    )(d_gate_up, full_gu, normed_two)


def scatter_scratch(sizes):
    scratch = [pltpu.VMEM((2 * GROUP, *size), jnp.bfloat16) for size in sizes]
    for rows, columns in sizes:
        half = (rows // 2, columns)
        scratch += [
            pltpu.VMEM((4, rows, columns), jnp.bfloat16),
            pltpu.VMEM((2,) + half, jnp.bfloat16),
            pltpu.VMEM((2,) + half, jnp.bfloat16),
            pltpu.VMEM((2,) + half, jnp.bfloat16),
            pltpu.VMEM((3,) + half, jnp.bfloat16),
            pltpu.VMEM((3,) + half, jnp.bfloat16),
            pltpu.SemaphoreType.DMA((4,)),
            pltpu.SemaphoreType.DMA((4,)),
            pltpu.SemaphoreType.DMA((6,)),
            pltpu.SemaphoreType.DMA((6,)),
        ]
    return scratch


def scatter_plane(left, right, identity, extra=(), beside=()):
    height, width = left.shape[0] // (2 * GROUP), right.shape[0]
    sizes = [(height, width)] + [tuple(size) for _, *size in extra]
    shapes = [jax.ShapeDtypeStruct(size, jnp.float32) for size in sizes]
    count = 1 + len(extra)
    return pl.pallas_call(
        partial(scatter_kernel, count),
        out_shape=shapes,
        in_specs=vmem_specs(2 if count == 1 else 2 + count),
        out_specs=vmem_specs(count),
        scratch_shapes=scatter_scratch(sizes),
        cost_estimate=lasting(35),
        compiler_params=pltpu.CompilerParams(
            collective_id=identity, has_side_effects=True, vmem_limit_bytes=VMEM_BYTES
        ),
    )(left, right, *[array for array, *_ in extra], *beside)


def plane_sum_kernel(
    small_ref, own_ref, out_ref, bulk, sum_ref, both_ref, both_out, back, small_in, own_sem, send_s, recv_s
):
    data, place, core, along_x, along_y, across = plane_place()
    mine = 2 * place + core
    partner = (data, place, 1 - core)
    plane = []
    for turn_by in range(1, 2 * GROUP):
        other = lax.rem(mine + turn_by, 2 * GROUP)
        plane.append((other, (data, other // 2, lax.rem(other, 2))))
    meet([device for _, device in plane])
    started = []

    def push(source, target, device):
        slot = len(started)
        copy = remote(source, target, send_s.at[slot], recv_s.at[slot], device)
        copy.start()
        started.append(copy)

    piece = small_in.shape[2]

    def piece_of(index):
        return small_ref.at[:, pl.ds(pl.multiple_of(index * piece, 128), piece)]

    for other, device in plane:
        push(piece_of(other), small_in.at[mine], device)
    for source, target in ((own_ref, both_ref), (out_ref, both_out)):
        push(source, target.at[core], partner)
    for chip in (across, along_x, along_y):
        push(bulk.at[chip], back.at[place], (data, chip, core))
    own = pltpu.make_async_copy(bulk.at[place], back.at[place], own_sem)
    own.start()
    small_in[mine] = piece_of(mine)[...]
    both_ref[core] = own_ref[...]
    both_out[core] = out_ref[...]
    for copy in started:
        copy.wait()
    own.wait()
    total = small_in[0]
    for index in range(1, 2 * GROUP):
        total = total + small_in[index]
    sum_ref[...] = total


def plane_sum(small, own_rows, out_rows, bulk):
    places = 2 * GROUP
    pushes = places - 1 + 2 + 3
    shaped = jax.ShapeDtypeStruct
    piece = small.shape[1] // places
    return pl.pallas_call(
        plane_sum_kernel,
        out_shape=[
            shaped((8, piece), jnp.float32),
            shaped((2,) + own_rows.shape, own_rows.dtype),
            shaped((2,) + out_rows.shape, out_rows.dtype),
            shaped(bulk.shape, bulk.dtype),
        ],
        in_specs=vmem_specs(3) + any_specs(1),
        out_specs=vmem_specs(3) + any_specs(1),
        scratch_shapes=[
            pltpu.VMEM((places, 8, piece), jnp.float32),
            pltpu.SemaphoreType.DMA,
            pltpu.SemaphoreType.DMA((pushes,)),
            pltpu.SemaphoreType.DMA((pushes,)),
        ],
        cost_estimate=lasting(20),
        compiler_params=pltpu.CompilerParams(
            collective_id=7, has_side_effects=True, vmem_limit_bytes=VMEM_BYTES
        ),
    )(small, own_rows, out_rows, bulk)


def finish_kernel(
    piece_ref,
    bc_ref,
    bulk,
    small_all,
    bc_all,
    back,
    bc_send,
    bc_in,
    bc_line,
    line_in,
    own_sem,
    send_s,
    recv_s,
):
    data, place, core, along_x, along_y, across = plane_place()
    count = lax.axis_size("dp")
    mine = 2 * place + core
    partner = (data, place, 1 - core)
    others = (across, along_x, along_y)
    chips = [(data, chip, core) for chip in others]
    plane = []
    for turn_by in range(1, 2 * GROUP):
        other = lax.rem(mine + turn_by, 2 * GROUP)
        plane.append((data, other // 2, lax.rem(other, 2)))
    line = []
    for turn_by in range(1, count):
        other = lax.rem(data + turn_by, count)
        line.append((other, (other, place, core)))
    meet(plane + [device for _, device in line])
    started = []

    def push(source, target, device):
        slot = len(started)
        copy = remote(source, target, send_s.at[slot], recv_s.at[slot], device)
        copy.start()
        started.append(copy)
        return copy

    rows = bc_in.shape[1]

    def rows_of(index):
        return bc_send.at[pl.ds(pl.multiple_of(index * rows, 16), rows)]

    bc_send[...] = bc_ref[...].astype(jnp.bfloat16)
    first = [push(rows_of(other), bc_in.at[data], device) for other, device in line]
    small = [push(piece_ref, line_in.at[data], device) for _, device in line]
    late = []
    for chip, device in zip(others, chips):
        late.append(push(bulk.at[chip], back.at[place], device))
    own = pltpu.make_async_copy(bulk.at[place], back.at[place], own_sem)
    own.start()
    bc_in[data] = rows_of(data)[...]
    line_in[data] = piece_ref[...]
    for copy in first:
        copy.wait_recv()
    total = bc_in[0].astype(jnp.float32)
    for index in range(1, count):
        total = total + bc_in[index].astype(jnp.float32)
    bc_line[data] = total.astype(jnp.bfloat16)
    second = [push(bc_line.at[data], bc_line.at[data], device) for _, device in line]
    for copy in small:
        copy.wait_recv()
    total = line_in[0]
    for index in range(1, count):
        total = total + line_in[index]
    small_all[mine] = total
    late += [push(small_all.at[mine], small_all.at[mine], device) for device in plane]
    for copy in second:
        copy.wait_recv()
    half = count // 2

    def half_of(chip, at):
        return bc_all.at[2 * chip + core, pl.ds(at * half, half)]

    def send_half(chip, at, device):
        held = half_of(chip, at)
        return push(held, held, device)

    to_x, to_y = (data, along_x, core), (data, along_y, core)
    bc_all[mine] = bc_line[...]
    x_first = send_half(place, 0, to_x)
    y_second = send_half(place, 1, to_y)
    x_second = send_half(place, 1, to_x)
    y_first = send_half(place, 0, to_y)
    late.append(push(bc_all.at[mine], bc_all.at[mine], partner))
    x_first.wait_recv()
    over_y = send_half(along_x, 0, to_y)
    y_second.wait_recv()
    over_x = send_half(along_y, 1, to_x)
    for copies, chip in (((x_second,), along_x), ((y_first,), along_y), ((over_x, over_y), across)):
        for copy in copies:
            copy.wait_recv()
        held = bc_all.at[2 * chip + core]
        late.append(push(held, held, partner))
    for copy in late:
        copy.wait_recv()
    for copy in started:
        copy.wait_send()
    own.wait()


def finish_all(piece, bc_sum, bulk):
    count = lax.axis_size("dp")
    places = 2 * GROUP
    pushes = 3 * (count - 1) + (places - 1) + (GROUP - 1) + 6 + GROUP
    shaped = jax.ShapeDtypeStruct
    blocks = (count, bc_sum.shape[0] // count, bc_sum.shape[1])
    return pl.pallas_call(
        finish_kernel,
        out_shape=[
            shaped((places,) + piece.shape, jnp.float32),
            shaped((places,) + blocks, jnp.bfloat16),
            shaped(bulk.shape, bulk.dtype),
        ],
        in_specs=vmem_specs(2) + any_specs(1),
        out_specs=vmem_specs(2) + any_specs(1),
        scratch_shapes=[
            pltpu.VMEM(bc_sum.shape, jnp.bfloat16),
            pltpu.VMEM(blocks, jnp.bfloat16),
            pltpu.VMEM(blocks, jnp.bfloat16),
            pltpu.VMEM((count,) + piece.shape, jnp.float32),
            pltpu.SemaphoreType.DMA,
            pltpu.SemaphoreType.DMA((pushes,)),
            pltpu.SemaphoreType.DMA((pushes,)),
        ],
        cost_estimate=lasting(30),
        compiler_params=pltpu.CompilerParams(
            collective_id=6, has_side_effects=True, vmem_limit_bytes=VMEM_BYTES
        ),
    )(piece, bc_sum, bulk)


def unpack_kernel(
    gu_ref,
    down_ref,
    out_ref,
    in_ref,
    bc_ref,
    misc_ref,
    both_ref,
    both_out,
    pieces_ref,
    gate_ref,
    up_ref,
    d_ref,
    mo_ref,
    ao_ref,
    z_ref,
    x_ref,
    q_ref,
    grad_bc_ref,
    k_ref,
    v_ref,
    dt_ref,
    conv_ref,
    bias_ref,
    dtb_ref,
    alog_ref,
    skip_ref,
    group_ref,
    one_ref,
    two_ref,
    input_ref,
    output_ref,
    sums_ref,
):
    units, width, part = down_ref.shape[2], HEADS * HP, HD // 4
    input_ref[...] = both_ref[0]
    output_ref[...] = both_out[0]
    gate_ref[...] = gu_ref[0, :, :units].astype(jnp.float32)
    up_ref[...] = gu_ref[0, :, units:].astype(jnp.float32)
    d_ref[...] = down_ref[0].astype(jnp.float32).T
    turned = out_ref[0].astype(jnp.float32).T
    mo_ref[...] = turned[:width]
    ao_ref[...] = turned[width:]
    z_ref[...] = in_ref[0, :, :width].astype(jnp.float32)
    q_ref[...] = in_ref[0, :, width : width + HD].astype(jnp.float32)
    x_ref[...] = in_ref[0, :, width + HD : 2 * width + HD].astype(jnp.float32)
    wide = bc_ref.shape[2]
    for core in range(2):
        grad_bc_ref[wide * core : wide * (core + 1)] = bc_ref[core].astype(jnp.float32).T

    @pl.when(pl.program_id(0) == 0)
    def _():
        for index in range(2 * GROUP):
            piece = pieces_ref.shape[2]
            sums_ref[:, piece * index : piece * (index + 1)] = pieces_ref[index]
        held = [misc_ref[chip].astype(jnp.float32) for chip in range(GROUP)]
        k_ref[...] = jnp.concatenate(
            [
                held[0][:, :part],
                held[1][:, :part],
                held[0][:, part : 2 * part],
                held[1][:, part : 2 * part],
            ],
            axis=1,
        )
        v_ref[...] = jnp.concatenate([held[2][:, : 2 * part], held[3][:, : 2 * part]], axis=1)
        dt_ref[...] = jnp.concatenate(
            [values[:, DT_LANE : DT_LANE + HEADS] for values in held], axis=1
        ).T
        taps = bias_ref.shape[1]
        conv_ref[...] = sums_ref[:KC, :taps]
        bias_ref[...] = sums_ref[KC : KC + 1, :taps]
        dtb_ref[...] = sums_ref[0:1, taps : taps + MH]
        alog_ref[...] = sums_ref[1:2, taps : taps + MH]
        skip_ref[...] = sums_ref[2:3, taps : taps + MH]
        start = taps + 128
        mine = GROUP * lax.axis_index("dp") + lax.axis_index("seq")
        slice_rows = one_ref.shape[1]
        each = slice_rows * GROUP * lax.axis_size("dp") // 8
        for ref in (one_ref, two_ref):
            gains = sums_ref[:, start : start + each]
            row = lax.broadcasted_iota(jnp.int32, (8, 1), 0)
            total = jnp.zeros((1, slice_rows), jnp.float32)
            for at in range(each // slice_rows):
                block = gains[:, slice_rows * at : slice_rows * (at + 1)]
                wanted = row * (each // slice_rows) + at == mine
                total = total + jnp.sum(jnp.where(wanted, block, 0.0), axis=0, keepdims=True)
            ref[...] = total
            start += each
        per_row = MH // 8
        for head in range(MH):
            row, lane = head // per_row, start + HP * (head % per_row)
            group_ref[head : head + 1, :] = sums_ref[row : row + 1, lane : lane + HP]


def unpack_all(back, bc_all, both, sums, shapes):
    gu, down, out, in_all = back

    def per_chip(array, rows=1):
        return pl.BlockSpec((rows,) + array.shape[1:], lambda chip: (chip, 0, 0))

    def across(shape):
        return pl.BlockSpec((shape[0], shape[1] // GROUP), lambda chip: (0, chip))

    def down_along(shape):
        return pl.BlockSpec((shape[0] // GROUP, shape[1]), lambda chip: (chip, 0))

    def once(shape):
        return pl.BlockSpec(shape, lambda chip: (0,) * len(shape))

    misc_block = (GROUP, in_all.shape[1], HD)
    kinds = [across, across, down_along, down_along, down_along, across, across, across, across]
    kinds += [once] * (len(shapes) - len(kinds))
    out_shape = [jax.ShapeDtypeStruct(shape, jnp.float32) for shape in shapes]
    rows, width = both[0].shape[1:]
    step = 2 * rows // GROUP
    rows_in = pl.BlockSpec((1, step, width), lambda chip: (chip // 2, lax.rem(chip, 2), 0))
    out_shape += [jax.ShapeDtypeStruct((2 * rows, width), array.dtype) for array in both]
    out_specs = [kind(shape) for kind, shape in zip(kinds, shapes)]
    out_specs += [pl.BlockSpec((step, width), lambda chip: (chip, 0))] * 2
    return pl.pallas_call(
        unpack_kernel,
        grid=(GROUP,),
        in_specs=[
            per_chip(gu),
            per_chip(down),
            per_chip(out),
            per_chip(in_all),
            per_chip(bc_all, 2),
            pl.BlockSpec(misc_block, lambda chip: (0, 0, in_all.shape[2] // HD - 1)),
            rows_in,
            rows_in,
            once(sums.shape),
        ],
        out_specs=out_specs,
        out_shape=out_shape,
        scratch_shapes=[pltpu.VMEM((8, 2 * GROUP * sums.shape[2]), jnp.float32)],
        cost_estimate=lasting(8),
        compiler_params=pltpu.CompilerParams(vmem_limit_bytes=VMEM_BYTES),
    )(gu, down, out, in_all, bc_all, in_all, *both, sums)


def push_moves(moves, sources, targets, local_sems, send_sems, recv_sems, first=0):
    data, place, core, along_x, along_y, across = plane_place()
    copies = []
    for index, chip in enumerate((across, along_x, along_y)):
        for at, move in enumerate(moves):
            source, target = move(sources, targets, place, chip)
            slot = first + index * len(moves) + at
            copy = remote(
                source, target, send_sems.at[slot], recv_sems.at[slot], (data, chip, core)
            )
            copy.start()
            copies.append(copy)
    for at, move in enumerate(moves):
        source, target = move(sources, targets, place, place)
        copy = pltpu.make_async_copy(source, target, local_sems.at[at])
        copy.start()
        copies.append(copy)
    return copies


def plane_peers():
    data, place, core, along_x, along_y, across = plane_place()
    return [(data, chip, core) for chip in (across, along_x, along_y)]


def exchange_kernel(moves, count_in, *refs):
    sources, targets = refs[:count_in], refs[count_in:-3]
    meet(plane_peers())
    for copy in push_moves(moves, sources, targets, *refs[-3:]):
        copy.wait()


def first_exchange_kernel(
    moves,
    z_ref,
    q_ref,
    x_ref,
    key_ref,
    value_ref,
    dt_ref,
    one_ref,
    two_ref,
    in_ref,
    gains_ref,
    misc,
    gains,
    local_sems,
    send_sems,
    recv_sems,
):
    data, place, core, along_x, along_y, across = plane_place()
    places = GROUP * lax.axis_size("dp")
    mine = GROUP * data + place
    devices = []
    for turn_by in range(1, places):
        other = lax.rem(mine + turn_by, places)
        devices.append((other // GROUP, lax.rem(other, GROUP), core))
    meet(devices)
    half, part = HD // 2, HD // 4
    keys, values = key_ref[...], value_ref[...]
    steps = dt_ref[...].astype(jnp.float32).T.astype(keys.dtype)
    columns = (
        (keys[:, :part], keys[:, half : half + part]),
        (keys[:, part:half], keys[:, half + part :]),
        (values[:, :half],),
        (values[:, half:],),
    )
    for chip in range(GROUP):
        heads = steps[:, HEADS * chip : HEADS * (chip + 1)]
        rest = jnp.zeros((keys.shape[0], half - HEADS), keys.dtype)
        misc[chip] = jnp.concatenate([*columns[chip], heads, rest], axis=1)
    gains[...] = jnp.zeros_like(gains)
    gains[0:1] = one_ref[...].astype(jnp.float32)
    gains[1:2] = two_ref[...].astype(jnp.float32)
    sources = (z_ref, q_ref, x_ref, misc)
    copies = push_moves(moves, sources, (in_ref,), local_sems, send_sems, recv_sems)
    for index, device in enumerate(devices):
        slot = 3 * len(moves) + index
        copy = remote(
            gains, gains_ref.at[mine], send_sems.at[slot], recv_sems.at[slot], device
        )
        copy.start()
        copies.append(copy)
    gains_ref[mine] = gains[...]
    for copy in copies:
        copy.wait()


def first_exchange(moves, arrays, width_in):
    places = GROUP * lax.axis_size("dp")
    slice_rows = arrays[0].shape[0]
    count = 3 * len(moves) + places - 1
    return pl.pallas_call(
        partial(first_exchange_kernel, moves),
        out_shape=[
            jax.ShapeDtypeStruct((GROUP, slice_rows, width_in), jnp.bfloat16),
            jax.ShapeDtypeStruct((places, 8, slice_rows), jnp.float32),
        ],
        in_specs=any_specs(3) + vmem_specs(5),
        out_specs=any_specs(1) + vmem_specs(1),
        scratch_shapes=[
            pltpu.VMEM((GROUP, slice_rows, HD), jnp.bfloat16),
            pltpu.VMEM((8, slice_rows), jnp.float32),
            pltpu.SemaphoreType.DMA((len(moves),)),
            pltpu.SemaphoreType.DMA((count,)),
            pltpu.SemaphoreType.DMA((count,)),
        ],
        cost_estimate=lasting(20),
        compiler_params=pltpu.CompilerParams(collective_id=3, has_side_effects=True),
    )(*arrays)


def exchange_plane(moves, arrays, out_shapes, identity):
    count = 3 * len(moves)
    return pl.pallas_call(
        partial(exchange_kernel, moves, len(arrays)),
        out_shape=[jax.ShapeDtypeStruct(shape, jnp.bfloat16) for shape in out_shapes],
        in_specs=any_specs(len(arrays)),
        out_specs=any_specs(len(out_shapes)),
        scratch_shapes=[
            pltpu.SemaphoreType.DMA((len(moves),)),
            pltpu.SemaphoreType.DMA((count,)),
            pltpu.SemaphoreType.DMA((count,)),
        ],
        cost_estimate=lasting(25),
        compiler_params=pltpu.CompilerParams(collective_id=identity, has_side_effects=True),
    )(*arrays)


def column_move(source, target, start, width):
    def move(sources, targets, place, chip):
        columns = pl.ds(pl.multiple_of(chip * width, 128), width)
        return (
            sources[source].at[:, columns],
            targets[target].at[place, :, pl.ds(start, width)],
        )

    return move


def block_move(source, target):
    def move(sources, targets, place, chip):
        return (sources[source].at[chip], targets[target].at[place])

    return move


def misc_move(source, target, start):
    def move(sources, targets, place, chip):
        return (
            sources[source].at[chip],
            targets[target].at[place, :, pl.ds(start, 128)],
        )

    return move


def lane_masks():
    lane = lax.broadcasted_iota(jnp.int32, (1, 2 * HP), 1)
    return (lane < HP, lane >= HP)


DT_LANE = HP


def at_lane(lane, values):
    row = lax.broadcasted_iota(jnp.int32, (1, 2 * HP), 1)
    return jnp.where(row == lane, values, 0.0)


def dot_beside(exact, values, left_dim):
    width = values.shape[1]
    both = dot_f32(exact, jnp.concatenate(halves(values), axis=1), left_dim, 0)
    return both[:, :width] + both[:, width:]


def dot_along(left, right):
    left_high, left_low = halves(left)
    right_high, right_low = halves(right)
    return dot_f32(
        jnp.concatenate([left_high, left_high, left_low], axis=1),
        jnp.concatenate([right_high, right_low, right_high], axis=1),
        1,
        1,
    )


def spread_heads(*columns):
    width = HEADS * HP
    row = lax.rem(lax.broadcasted_iota(jnp.int32, (4 * HP, width), 0), 2 * HP)
    head = lax.broadcasted_iota(jnp.int32, (4 * HP, width), 1) // HP
    pick = jnp.where(row == DT_LANE + head, 1.0, 0.0).astype(jnp.bfloat16)
    parts = [jnp.concatenate(halves(values), axis=1) for values in columns]
    wide = dot_f32(jnp.concatenate(parts, axis=0), pick, 1, 0)
    size = columns[0].shape[0]
    return [wide[size * at : size * (at + 1)] for at in range(len(columns))]


def wide_keeps(keeps_ref):
    size = keeps_ref.shape[0]
    return [None] + [
        jnp.broadcast_to(keeps_ref[:, 1 + back : 2 + back], (size, 2 * HP))
        for back in range(1, KC)
    ]


def head_sums(values):
    low, high = lane_masks()
    first = jnp.sum(jnp.where(low, values, 0.0), axis=1, keepdims=True)
    second = jnp.sum(jnp.where(high, values, 0.0), axis=1, keepdims=True)
    return (first, second)


def head_means(values):
    low, high = lane_masks()
    first, second = head_sums(values)
    return jnp.where(low, first, second) * (1.0 / HP)


def stack_heads(values):
    low, high = lane_masks()
    zero = jnp.zeros_like(values)
    return jnp.concatenate([jnp.where(low, values, zero), jnp.where(high, values, zero)], axis=0)


def order_in(size):
    row = lax.broadcasted_iota(jnp.int32, (size, size), 0)
    column = lax.broadcasted_iota(jnp.int32, (size, size), 1)
    return (row, column)


def exact_sum(ones, values):
    high = values.astype(jnp.bfloat16)
    rest = values - high.astype(jnp.float32)
    middle = rest.astype(jnp.bfloat16)
    low = (rest - middle.astype(jnp.float32)).astype(jnp.bfloat16)
    return dot_f32(ones, high, 1, 0) + (dot_f32(ones, middle, 1, 0) + dot_f32(ones, low, 1, 0))


def chunk_decays(proj_ref, heads_ref, keeps_ref):
    size, width = proj_ref.shape
    raw = proj_ref[:, width - 2 * HP :] + heads_ref[0:1]
    dt_rows = jnp.maximum(raw, 0.0) + jnp.log1p(jnp.exp(-jnp.abs(raw)))
    row, column = order_in(size)
    lower = jnp.where(row >= column, 1.0, 0.0).astype(jnp.bfloat16)
    cumul = exact_sum(lower, -heads_ref[1:2] * dt_rows)
    enter = jnp.exp(cumul) * keeps_ref[:, 0:1]
    leave_bare = jnp.exp(cumul[size - 1 :] - cumul) * keeps_ref[:, 1:2]
    return (raw, dt_rows, cumul, enter, leave_bare)


def conv_windows(block, proj_ref, before_ref, bc_ref, bc_before_ref):
    if block < HEADS // 2:
        start = proj_ref.shape[1] - 2 * HP * (1 + HEADS // 2 - block)
        lanes = slice(start, start + 2 * HP)
        now, before = proj_ref[:, lanes], before_ref[:, lanes]
        now, before = now.astype(jnp.bfloat16), before.astype(jnp.bfloat16)
    else:
        start = 2 * HP * (block - HEADS // 2)
        lanes = slice(start, start + 2 * HP)
        now, before = bc_ref[:, lanes], bc_before_ref[8:, lanes]
    now, before = now.astype(jnp.float32), before.astype(jnp.float32)
    size = now.shape[0]
    extended = jnp.concatenate([before, now], axis=0)
    return [now] + [extended[8 - back : 8 - back + size] for back in range(1, KC)]


def conv_sum(windows, taps_ref, lanes, keeps):
    total = taps_ref[KC : KC + 1, lanes] + taps_ref[KC - 1 : KC, lanes] * windows[0]
    for back in range(1, KC):
        total = total + taps_ref[KC - 1 - back : KC - back, lanes] * (
            windows[back] * keeps[back]
        )
    return total


def head_decay(allowed, cumul, cumul_t, head):
    lane = DT_LANE + head
    differ = cumul[:, lane : lane + 1] - cumul_t[lane : lane + 1, :]
    return jnp.exp(jnp.where(allowed, differ, -jnp.inf))


def ssd_forward_kernel(
    proj_ref,
    before_ref,
    bc_ref,
    bc_before_ref,
    taps_ref,
    heads_ref,
    keeps_ref,
    segc_ref,
    segr_ref,
    skip_ref,
    gain_ref,
    cos_ref,
    sin_ref,
    gated_ref,
    ssm_ref,
    states_ref,
    mixed_ref,
    slope_ref,
    kv_ref,
    state,
):
    @pl.when(pl.program_id(0) == 0)
    def _():
        state[...] = jnp.zeros_like(state)

    size = proj_ref.shape[0]
    width = HEADS * HP
    keeps = wide_keeps(keeps_ref)
    for block in range(mixed_ref.shape[1] // (2 * HP)):
        lanes = slice(2 * HP * block, 2 * HP * (block + 1))
        windows = conv_windows(block, proj_ref, before_ref, bc_ref, bc_before_ref)
        summed = conv_sum(windows, taps_ref, lanes, keeps)
        sigmoid = jax.nn.sigmoid(summed)
        mixed_ref[:, lanes] = (summed * sigmoid).astype(jnp.bfloat16)
        slope_ref[:, lanes] = sigmoid * (1.0 + summed * (1.0 - sigmoid))
    raw, dt_rows, cumul, enter_all, leave_bare = chunk_decays(proj_ref, heads_ref, keeps_ref)
    enter_all, leave_all = spread_heads(enter_all, leave_bare * dt_rows)
    cumul_t, dt_t = cumul.T, dt_rows.T
    entry = state[...]
    states_ref[0] = entry
    b_rows, c_rows = mixed_ref[:, width : width + NS], mixed_ref[:, width + NS :]
    gram = dot_f32(c_rows, b_rows, 1, 1)
    row, column = order_in(size)
    allowed = (segc_ref[...] == segr_ref[0]) & (row >= column)
    entered = dot_beside(c_rows, entry, 1)
    weighted = []
    for pair in range(HEADS // 2):
        lanes = slice(2 * HP * pair, 2 * HP * (pair + 1))
        heads_x = mixed_ref[:, lanes]
        mixing = []
        for head in (2 * pair, 2 * pair + 1):
            lane = DT_LANE + head
            decay = head_decay(allowed, cumul, cumul_t, head)
            mixing.append(gram * decay * dt_t[lane : lane + 1, :])
        stacked = stack_heads(heads_x)
        out = dot_f32(
            jnp.concatenate(halves(jnp.concatenate(mixing, axis=1)), axis=1),
            jnp.concatenate([stacked, stacked], axis=0),
            1,
            0,
        )
        wide_x = heads_x.astype(jnp.float32)
        enter = enter_all[:, lanes]
        out = out + enter * entered[:, lanes] + skip_ref[:, lanes] * wide_x
        ssm_ref[:, lanes] = out
        gate = proj_ref[:, lanes]
        value = out * (gate * jax.nn.sigmoid(gate))
        scale = lax.rsqrt(head_means(value * value) + GROUP_EPSILON)
        gated_ref[:, lanes] = (value * scale * gain_ref[:, lanes]).astype(jnp.bfloat16)
        weighted.append(leave_all[:, lanes] * wide_x)
        state[:, lanes] = enter[size - 1 :, :] * entry[:, lanes]
    state[...] += dot_beside(b_rows, jnp.concatenate(weighted, axis=1), 0)
    kv = proj_ref[:, proj_ref.shape[1] - 2 * HP :][:, :HP]
    kv = jnp.concatenate([kv[: size // 2], kv[size // 2 :]], axis=1)
    kv_ref[...] = turn_folded(kv, cos_ref[...], sin_ref[...]).astype(jnp.bfloat16)


def ssd_backward_kernel(
    moves,
    proj_ref,
    slope_ref,
    bc_ref,
    taps_ref,
    heads_ref,
    keeps_ref,
    segc_ref,
    segr_ref,
    skip_ref,
    gain_ref,
    mixed_ref,
    ssm_ref,
    states_ref,
    dgated_ref,
    dq_ref,
    kv_own_ref,
    kv_x_ref,
    kv_y_ref,
    kv_a_ref,
    cos_ref,
    sin_ref,
    gu_ref,
    down_ref,
    dproj_ref,
    dtaps_ref,
    dheads_ref,
    dskip_ref,
    dgain_ref,
    gu_back,
    down_back,
    state,
    d_mixed,
    next_rows,
    *sems,
):
    def transfers(act):
        data, place, core, along_x, along_y, across = plane_place()
        sources, targets = (gu_ref, down_ref), (gu_back, down_back)
        local_sems, send_sems, recv_sems = sems
        for index, chip in enumerate((across, along_x, along_y)):
            for at, move in enumerate(moves):
                source, target = move(sources, targets, place, chip)
                slot = index * len(moves) + at
                act(
                    remote(
                        source, target, send_sems.at[slot], recv_sems.at[slot], (data, chip, core)
                    )
                )
        for at, move in enumerate(moves):
            source, target = move(sources, targets, place, place)
            act(pltpu.make_async_copy(source, target, local_sems.at[at]))

    @pl.when(pl.program_id(0) == 0)
    def _():
        meet(plane_peers())
        transfers(lambda copy: copy.start())
        state[...] = jnp.zeros_like(state)
        next_rows[...] = jnp.zeros_like(next_rows)
        dtaps_ref[...] = jnp.zeros_like(dtaps_ref)
        dheads_ref[...] = jnp.zeros_like(dheads_ref)
        dskip_ref[...] = jnp.zeros_like(dskip_ref)
        dgain_ref[...] = jnp.zeros_like(dgain_ref)

    size = proj_ref.shape[0]
    width = HEADS * HP
    raw, dt_rows, cumul, enter_all, leave_bare = chunk_decays(proj_ref, heads_ref, keeps_ref)
    cumul_t, dt_t = cumul.T, dt_rows.T
    later = state[...]
    entry = states_ref[0]
    carried = jnp.sum(later * entry, axis=0, keepdims=True)
    b_rows, c_rows = mixed_ref[:, width : width + NS], mixed_ref[:, width + NS :]
    gram = dot_f32(c_rows, b_rows, 1, 1)
    row, column = order_in(size)
    allowed = (segc_ref[...] == segr_ref[0]) & (row >= column)
    d_weighted = dot_beside(b_rows, later, 1)
    enter_all, bare_all, dt_all = spread_heads(enter_all, leave_bare, dt_rows)
    d_gram = jnp.zeros((size, size), jnp.float32)
    row_sums = jnp.zeros((size, 2 * HP), jnp.float32)
    column_sums = jnp.zeros((size, 2 * HP), jnp.float32)
    at_last = jnp.zeros((1, 2 * HP), jnp.float32)
    d_entered, weighted = [], []
    for pair in range(HEADS // 2):
        lanes = slice(2 * HP * pair, 2 * HP * (pair + 1))
        heads_x = mixed_ref[:, lanes]
        wide_x = heads_x.astype(jnp.float32)
        ssm, gate, gain = ssm_ref[:, lanes], proj_ref[:, lanes], gain_ref[:, lanes]
        d_gated = dgated_ref[:, lanes]
        sigmoid = jax.nn.sigmoid(gate)
        silu = gate * sigmoid
        value = ssm * silu
        scale = lax.rsqrt(head_means(value * value) + GROUP_EPSILON)
        dgain_ref[:, lanes] += jnp.sum(d_gated * value * scale, axis=0, keepdims=True)
        d_scaled = d_gated * gain
        d_value = scale * d_scaled - value * (scale * scale * scale) * head_means(d_scaled * value)
        d_out = d_value * silu
        dproj_ref[:, lanes] = (d_value * ssm * (sigmoid * (1.0 + gate * (1.0 - sigmoid)))).astype(
            jnp.bfloat16
        )
        dskip_ref[:, lanes] += jnp.sum(d_out * wide_x, axis=0, keepdims=True)
        enter, bare, dt_pair = enter_all[:, lanes], bare_all[:, lanes], dt_all[:, lanes]
        high, low = [stack_heads(half) for half in halves(d_out)]
        d_mixing = dot_f32(jnp.concatenate([high, low], axis=0), heads_x, 1, 1)
        grams = []
        for side in range(2):
            head = 2 * pair + side
            lane = DT_LANE + head
            decay = head_decay(allowed, cumul, cumul_t, head)
            grams.append(gram * decay)
            first = size * side
            d_mix = d_mixing[first : first + size] + d_mixing[2 * size + first : 3 * size + first]
            d_gram = d_gram + d_mix * (decay * dt_t[lane : lane + 1, :])
        gram_high, gram_low = halves(jnp.concatenate(grams, axis=0))
        bare_x = dot_f32(
            jnp.concatenate([high, low, high], axis=0),
            jnp.concatenate([gram_high, gram_high, gram_low], axis=0),
            0,
            0,
        ).T
        left = bare * d_weighted[:, lanes]
        d_x = bare_x + left
        first_lane = DT_LANE + 2 * pair
        first, second = head_sums(d_out * (ssm - skip_ref[:, lanes] * wide_x))
        row_sums = row_sums + at_lane(first_lane, first) + at_lane(first_lane + 1, second)
        first, second = head_sums(d_x * wide_x)
        column_sums = column_sums + at_lane(first_lane, first) + at_lane(first_lane + 1, second)
        last = jnp.sum(dt_pair * left * wide_x, axis=0, keepdims=True)
        last = last + carried[:, lanes] * enter[size - 1 :]
        first, second = head_sums(last)
        at_last = at_last + at_lane(first_lane, first) + at_lane(first_lane + 1, second)
        d_mixed[:, lanes] = dt_pair * d_x + skip_ref[:, lanes] * d_out
        d_entered.append(enter * d_out)
        weighted.append(bare * dt_pair * wide_x)
        state[:, lanes] = enter[size - 1 :, :] * later[:, lanes]
    d_entered = jnp.concatenate(d_entered, axis=1)
    state[...] += dot_beside(c_rows, d_entered, 0)
    d_gram_parts = halves(d_gram)
    d_b = dot_along(jnp.concatenate(weighted, axis=1), later)
    d_mixed[:, width : width + NS] = d_b + dot_f32(
        jnp.concatenate(d_gram_parts, axis=0),
        jnp.concatenate([c_rows, c_rows], axis=0),
        0,
        0,
    )
    d_c = dot_along(d_entered, entry)
    d_mixed[:, width + NS :] = d_c + dot_f32(
        jnp.concatenate(d_gram_parts, axis=1),
        jnp.concatenate([b_rows, b_rows], axis=0),
        1,
        0,
    )

    d_cumul = row_sums - column_sums * dt_rows
    last_row = lax.broadcasted_iota(jnp.int32, (size, 1), 0) == size - 1
    d_cumul = d_cumul + jnp.where(last_row, at_last, 0.0)
    upper = jnp.where(row <= column, 1.0, 0.0).astype(jnp.bfloat16)
    d_log = exact_sum(upper, d_cumul)
    rate = heads_ref[1:2]
    d_raw = (column_sums - rate * d_log) * jax.nn.sigmoid(raw)
    lane_row = lax.broadcasted_iota(jnp.int32, (1, 2 * HP), 1)
    d_raw = jnp.where((lane_row >= DT_LANE) & (lane_row < DT_LANE + HEADS), d_raw, 0.0)
    dheads_ref[0:1] += jnp.sum(d_raw, axis=0, keepdims=True)
    dheads_ref[1:2] += -rate * jnp.sum(d_log * dt_rows, axis=0, keepdims=True)
    total = proj_ref.shape[1]
    d_kv = kv_own_ref[...].astype(jnp.float32)
    for ref in (kv_x_ref, kv_y_ref, kv_a_ref):
        d_kv = d_kv + ref[...].astype(jnp.float32)
    d_kv = turn_folded(d_kv, cos_ref[...], -sin_ref[...])
    d_kv = jnp.concatenate([d_kv[:, :DT_LANE], d_kv[:, DT_LANE:]], axis=0)
    dproj_ref[:, total - 2 * HP : total] = jnp.concatenate(
        [d_kv, d_raw[:, DT_LANE:]], axis=1
    ).astype(jnp.bfloat16)
    dproj_ref[:, width : width + HD] = dq_ref[...]

    keeps = wide_keeps(keeps_ref)
    for block in range(mixed_ref.shape[1] // (2 * HP)):
        lanes = slice(2 * HP * block, 2 * HP * (block + 1))
        if block < HEADS // 2:
            start = total - 2 * HP * (1 + HEADS // 2 - block)
            pre = proj_ref[:, start : start + 2 * HP].astype(jnp.bfloat16).astype(jnp.float32)
        else:
            start = 2 * HP * (block - HEADS // 2)
            pre = bc_ref[:, start : start + 2 * HP].astype(jnp.float32)
        d_sum = d_mixed[:, lanes] * slope_ref[:, lanes]
        dtaps_ref[KC : KC + 1, lanes] += jnp.sum(d_sum, axis=0, keepdims=True)
        dtaps_ref[KC - 1 : KC, lanes] += jnp.sum(d_sum * pre, axis=0, keepdims=True)
        d_pre = taps_ref[KC - 1 : KC, lanes] * d_sum
        for back in range(1, KC):
            tap = KC - 1 - back
            kept = d_sum * keeps[back]
            extended = jnp.concatenate([kept, next_rows[back - 1, :, lanes]], axis=0)
            later_rows = extended[back : back + size]
            dtaps_ref[tap : tap + 1, lanes] += jnp.sum(later_rows * pre, axis=0, keepdims=True)
            d_pre = d_pre + taps_ref[tap : tap + 1, lanes] * later_rows
            next_rows[back - 1, :, lanes] = kept[:8]
        if block < HEADS // 2:
            start = total - 2 * HP * (1 + HEADS // 2 - block)
            dproj_ref[:, start : start + 2 * HP] = d_pre.astype(jnp.bfloat16)
        else:
            start = total + 2 * HP * (block - HEADS // 2)
            dproj_ref[:, start : start + 2 * HP] = d_pre.astype(jnp.bfloat16)

    @pl.when(pl.program_id(0) == pl.num_programs(0) - 1)
    def _():
        transfers(lambda copy: copy.wait())


def ssd_specs(length, reverse, width_in, width_all, width):
    laps = length // CHUNK

    def at(lap):
        return laps - 1 - lap if reverse else lap

    def tall(columns):
        return pl.BlockSpec((CHUNK, columns), lambda lap: (at(lap), 0))

    def rim(rows, columns):
        each = CHUNK // rows
        return pl.BlockSpec((rows, columns), lambda lap: (lax.rem(each * (at(lap) + laps) - 1, each * laps), 0))

    def whole(rows, columns):
        return pl.BlockSpec((rows, columns), lambda lap: (0, 0))

    def slab(rows, columns):
        return pl.BlockSpec((1, rows, columns), lambda lap: (at(lap), 0, 0))

    specs = [
        tall(width_in),
        rim(8, width_in),
        tall(2 * NS),
        rim(16, 2 * NS),
        whole(8, width_all),
        whole(8, 2 * HP),
        tall(8),
        tall(1),
        slab(1, CHUNK),
        whole(1, width),
        whole(1, width),
    ]
    return (laps, tall, whole, slab, specs)


def ssd_forward(arrays, cos_part, sin_part):
    length, width_in = arrays[0].shape
    width, width_all = HEADS * HP, HEADS * HP + 2 * NS
    laps, tall, whole, slab, specs = ssd_specs(length, False, width_in, width_all, width)
    shaped = jax.ShapeDtypeStruct
    fold = pl.BlockSpec((CHUNK // 2, 2 * HP), lambda lap: (lap, 0))
    return pl.pallas_call(
        ssd_forward_kernel,
        grid=(laps,),
        in_specs=specs + [fold, fold],
        out_specs=[
            tall(width),
            tall(width),
            slab(NS, width),
            tall(width_all),
            tall(width_all),
            fold,
        ],
        out_shape=[
            shaped((length, width), jnp.bfloat16),
            shaped((length, width), jnp.float32),
            shaped((laps, NS, width), jnp.float32),
            shaped((length, width_all), jnp.bfloat16),
            shaped((length, width_all), jnp.float32),
            shaped((length // 2, 2 * HP), jnp.bfloat16),
        ],
        scratch_shapes=[pltpu.VMEM((NS, width), jnp.float32)],
        cost_estimate=lasting(6),
        compiler_params=pltpu.CompilerParams(vmem_limit_bytes=VMEM_BYTES),
    )(*arrays, cos_part, sin_part)


def ssd_backward(arrays, slope, mixed, ssm, states, d_outs, d_query, d_kv_parts, tables, grads):
    length, width_in = arrays[0].shape
    width, width_all = HEADS * HP, HEADS * HP + 2 * NS
    laps, tall, whole, slab, specs = ssd_specs(length, True, width_in, width_all, width)
    shaped = jax.ShapeDtypeStruct
    moves = (block_move(0, 0), block_move(1, 1))
    fold = pl.BlockSpec((CHUNK // 2, 2 * HP), lambda lap: (laps - 1 - lap, 0))
    return pl.pallas_call(
        partial(ssd_backward_kernel, moves),
        grid=(laps,),
        in_specs=[specs[0], tall(width_all), specs[2], *specs[4:]]
        + [
            tall(width_all),
            tall(width),
            slab(NS, width),
            tall(width),
            tall(HD),
        ]
        + [fold] * 6
        + any_specs(2),
        out_specs=[
            tall(width_in + 2 * NS),
            whole(8, width_all),
            whole(8, 2 * HP),
            whole(1, width),
            whole(1, width),
        ]
        + any_specs(2),
        out_shape=[
            shaped((length, width_in + 2 * NS), jnp.bfloat16),
            shaped((8, width_all), jnp.float32),
            shaped((8, 2 * HP), jnp.float32),
            shaped((1, width), jnp.float32),
            shaped((1, width), jnp.float32),
        ]
        + [shaped(array.shape, array.dtype) for array in grads],
        scratch_shapes=[
            pltpu.VMEM((NS, width), jnp.float32),
            pltpu.VMEM((CHUNK, width_all), jnp.float32),
            pltpu.VMEM((KC - 1, 8, width_all), jnp.float32),
            pltpu.SemaphoreType.DMA((len(moves),)),
            pltpu.SemaphoreType.DMA((3 * len(moves),)),
            pltpu.SemaphoreType.DMA((3 * len(moves),)),
        ],
        cost_estimate=lasting(48),
        compiler_params=pltpu.CompilerParams(
            collective_id=13, has_side_effects=True, vmem_limit_bytes=VMEM_BYTES
        ),
    )(arrays[0], slope, arrays[2], *arrays[4:], mixed, ssm, states, d_outs, d_query, *d_kv_parts, *tables, *grads)


QUERY_ROWS = 256


def masked_scores(q_rows, k_ref, segc_ref, segr_ref, start, reach):
    rows = q_rows.shape[0]
    scores = dot_f32(q_rows, k_ref[:reach], 1, 1) * HD ** (-0.5)
    row = lax.broadcasted_iota(jnp.int32, (rows, reach), 0) + start
    column = lax.broadcasted_iota(jnp.int32, (rows, reach), 1)
    allowed = (segc_ref[start : start + rows] == segr_ref[:, :reach]) & (row >= column)
    return jnp.where(allowed, scores, -jnp.inf)


def rotate_rows(values, cos_ref, sin_ref, sign):
    return values * cos_ref[...] + sign * (pltpu.roll(values, HD // 2, 1) * sin_ref[...])


def swap_middle(values):
    lane = lax.broadcasted_iota(jnp.int32, (1, HD), 1) // (HD // 4)
    up = pltpu.roll(values, HD // 4, 1)
    down = pltpu.roll(values, HD - HD // 4, 1)
    return jnp.where(lane == 1, down, jnp.where(lane == 2, up, values))


def unfold_rows(values, write):
    step, columns = CHUNK // 2, values.shape[1] // 2
    for start in range(0, values.shape[0], step):
        rows = values[start : start + step]
        write(2 * start, rows[:, :columns])
        write(2 * start + step, rows[:, columns:])


def fold_rows(ref, index, values):
    step = CHUNK // 2
    for start in range(0, values.shape[0] // 2, step):
        ref[index, start : start + step] = jnp.concatenate(
            [values[2 * start : 2 * start + step], values[2 * start + step : 2 * start + 2 * step]],
            axis=1,
        ).astype(ref.dtype)


def join_halves(ref, first, target):
    half = HD // 2

    def write_at(lanes):
        def write(start, rows):
            target[start : start + rows.shape[0], lanes] = rows

        return write

    unfold_rows(ref[first], write_at(slice(0, half)))
    unfold_rows(ref[first + 1], write_at(slice(half, HD)))


def attend_forward_kernel(
    raw_ref, cos_ref, sin_ref, kv_ref, segc_ref, segr_ref, out_ref, total_ref, q_ref, k_ref, v_ref
):
    q_ref[...] = swap_middle(rotate_rows(raw_ref[...], cos_ref, sin_ref, 1.0)).astype(jnp.bfloat16)
    join_halves(kv_ref, 0, k_ref)
    join_halves(kv_ref, 2, v_ref)
    for start in range(0, q_ref.shape[0], QUERY_ROWS):
        reach = start + QUERY_ROWS
        rows = slice(start, reach)
        scores = masked_scores(q_ref[rows], k_ref, segc_ref, segr_ref, start, reach)
        top = jnp.max(scores, axis=1, keepdims=True)
        powers = jnp.exp(scores - top)
        total = jnp.sum(powers, axis=1, keepdims=True)
        probs = (powers * (1.0 / total)).astype(jnp.bfloat16)
        out_ref[rows] = dot_f32(probs, v_ref[:reach], 1, 0).astype(jnp.bfloat16)
        total_ref[rows] = top + jnp.log(total)


def attend_backward_kernel(
    q_ref,
    k_ref,
    v_ref,
    cos_ref,
    sin_ref,
    segc_ref,
    segr_ref,
    total_ref,
    dout_ref,
    dq_ref,
    dkv_ref,
    dq_sum,
    dk_sum,
    dv_sum,
):
    dk_sum[...] = jnp.zeros_like(dk_sum)
    dv_sum[...] = jnp.zeros_like(dv_sum)
    for start in range(0, q_ref.shape[0], QUERY_ROWS):
        reach = start + QUERY_ROWS
        rows = slice(start, reach)
        q_rows, d_out = q_ref[rows], dout_ref[rows]
        scores = masked_scores(q_rows, k_ref, segc_ref, segr_ref, start, reach)
        probs = jnp.exp(scores - total_ref[rows])
        d_probs = dot_f32(d_out, v_ref[:reach], 1, 1)
        delta = jnp.sum(probs * d_probs, axis=1, keepdims=True)
        d_scores = (probs * (d_probs - delta)).astype(jnp.bfloat16)
        dq_sum[rows] = dot_f32(d_scores, k_ref[:reach], 1, 0) * HD ** (-0.5)
        dk_sum[:reach] += dot_f32(d_scores, q_rows, 0, 0) * HD ** (-0.5)
        dv_sum[:reach] += dot_f32(probs.astype(jnp.bfloat16), d_out, 0, 0)
    dq_ref[...] = rotate_rows(swap_middle(dq_sum[...]), cos_ref, sin_ref, -1.0).astype(jnp.bfloat16)
    half = HD // 2
    fold_rows(dkv_ref, 0, dk_sum[:, :half])
    fold_rows(dkv_ref, 1, dk_sum[:, half:])
    fold_rows(dkv_ref, 2, dv_sum[:, :half])
    fold_rows(dkv_ref, 3, dv_sum[:, half:])


def rotation_tables(length):
    half, part = HD // 2, HD // 4
    frequency = np.float32(ROPE_BASE) ** (
        np.float32(-2.0) * np.arange(half).astype(np.float32) / np.float32(HD)
    )
    angles = np.arange(length).astype(np.float32)[:, None] * frequency[None, :]
    cosine, sine_part = np.cos(angles), np.sin(angles)

    def folded(values):
        rows = values.reshape(length // CHUNK, 2, CHUNK // 2, half)
        return rows.transpose(0, 2, 1, 3).reshape(length // 2, HD)

    cos_kinds, sin_kinds = [], []
    for start in (0, part):
        columns = slice(start, start + part)
        cos_part, sin_part = cosine[:, columns], sine_part[:, columns]
        cos_kinds.append(folded(np.concatenate([cos_part, cos_part], axis=1)))
        sin_kinds.append(folded(np.concatenate([-sin_part, sin_part], axis=1)))
    cos_kinds.append(np.ones_like(cos_kinds[0]))
    sin_kinds.append(np.zeros_like(sin_kinds[0]))
    tables = (
        np.concatenate([cosine, cosine], axis=1),
        np.concatenate([-sine_part, sine_part], axis=1),
        np.stack(cos_kinds),
        np.stack(sin_kinds),
    )
    return [jnp.asarray(table.astype(np.float32)) for table in tables]


def turn_folded(values, cosine, sine_part):
    lane = lax.rem(lax.broadcasted_iota(jnp.int32, (1, HD), 1), HD // 2)
    quarter = HD // 4
    other = jnp.where(
        lane < quarter, pltpu.roll(values, HD - quarter, 1), pltpu.roll(values, quarter, 1)
    )
    return values * cosine + other * sine_part


def whole_block(shape):
    return pl.BlockSpec(shape, lambda step: (0,) * len(shape))


def attend(kernel, arrays, out_shapes, scratch=(), blocks=None):
    return pl.pallas_call(
        kernel,
        grid=(1,),
        in_specs=[
            whole_block(array.shape) if blocks is None or blocks[at] is None else blocks[at]
            for at, array in enumerate(arrays)
        ],
        out_specs=[whole_block(shape) for shape, _ in out_shapes],
        out_shape=[jax.ShapeDtypeStruct(shape, dtype) for shape, dtype in out_shapes],
        scratch_shapes=[pltpu.VMEM(shape, dtype) for shape, dtype in scratch],
        cost_estimate=lasting(9),
        compiler_params=pltpu.CompilerParams(vmem_limit_bytes=VMEM_BYTES),
    )(*arrays)


def after(value, *earlier):
    return lax.optimization_barrier((value,) + earlier)[0]


def over_chips(block):
    place = lax.axis_index("seq")
    count = lax.axis_size("seq")
    stacked = jnp.zeros((count,) + block.shape, block.dtype)
    stacked = lax.dynamic_update_index_in_dim(stacked, block, place, 0)
    for mask in range(1, count):
        moved = lax.ppermute(block, "seq", [(i, i ^ mask) for i in range(count)])
        stacked = lax.dynamic_update_index_in_dim(stacked, moved, place ^ mask, 0)
    return stacked


def from_chips(blocks):
    place = lax.axis_index("seq")
    count = lax.axis_size("seq")
    moved = [lax.dynamic_index_in_dim(blocks, place, 0, False)]
    for mask in range(1, count):
        block = lax.dynamic_index_in_dim(blocks, place ^ mask, 0, False)
        moved.append(lax.ppermute(block, "seq", [(i, i ^ mask) for i in range(count)]))
    return moved


def heads_local_plan(
    hidden_in,
    teacher,
    segment_ids,
    valid_mask,
    norm1_gain,
    w_z,
    w_x,
    w_bc,
    w_dt,
    conv_weight,
    conv_bias,
    dt_bias,
    a_log,
    d_skip,
    group_gain,
    w_mamba_out,
    w_query,
    w_key,
    w_value,
    w_attn_out,
    norm2_gain,
    w_gate,
    w_up,
    w_down,
):
    place, core, data_rank = (
        lax.axis_index("seq"),
        lax.axis_index("tensor"),
        lax.axis_index("dp"),
    )
    data_count = lax.axis_size("dp")
    chip_rows, width = hidden_in.shape[1:]
    own_rows = chip_rows // 2
    length = segment_ids.shape[1]
    slice_rows = w_z.shape[0]
    width_x = HEADS * HP
    hidden_units = w_gate.shape[1] // GROUP
    segment = segment_ids[0]
    own_start = place * chip_rows + core * own_rows
    token_count = jnp.sum(valid_mask).astype(jnp.float32)
    mask_rows = lax.dynamic_slice(valid_mask, (data_rank, own_start), (1, own_rows))[0]
    total_tokens = float(valid_mask.shape[0] * valid_mask.shape[1])
    bf16 = jnp.bfloat16

    half, part = HD // 2, HD // 4
    width_in = 2 * width_x + 2 * HD
    in_slices, gains_all = first_exchange(
        (
            column_move(0, 0, 0, width_x),
            column_move(1, 0, width_x, HD),
            column_move(2, 0, width_x + HD, width_x),
            misc_move(3, 0, 2 * width_x + HD),
        ),
        (w_z, w_query, w_x, w_key, w_value, w_dt.T, norm1_gain[None], norm2_gain[None]),
        width_in,
    )
    gain_one, gain_two = gains_all[:, 0].reshape(width), gains_all[:, 1].reshape(width)
    full_in = lax.all_gather(in_slices, "dp", axis=0, tiled=True).reshape(width, width_in)
    hidden_own = lax.dynamic_slice(hidden_in[0], (core * own_rows, 0), (own_rows, width))
    hidden_own = after(hidden_own, in_slices)
    hidden_all, normed, pre_bc = gather_plane(
        hidden_own,
        1,
        apply_norm,
        (gain_one[None], w_bc),
        (((length, width), bf16), ((length, 2 * NS), bf16)),
    )
    hidden_own = hidden_own.astype(jnp.float32)
    width_out = width_x + HD
    out_slices, gu_slices, down_slices = exchange_plane(
        (
            column_move(0, 0, 0, width_x),
            column_move(1, 0, width_x, HD),
            column_move(2, 1, 0, hidden_units),
            column_move(3, 1, hidden_units, hidden_units),
            column_move(4, 2, 0, hidden_units),
        ),
        (after(w_mamba_out.T, normed), w_attn_out.T, w_gate, w_up, w_down.T),
        [
            (GROUP, slice_rows, width_out),
            (GROUP, slice_rows, 2 * hidden_units),
            (GROUP, slice_rows, hidden_units),
        ],
        4,
    )
    out_gathered = lax.all_gather(after(out_slices, full_in), "dp", axis=0, tiled=True)
    full_out = out_gathered.reshape(width, width_out)

    segment, conv_weight, conv_bias, dt_bias, a_log, d_skip, group_gain = (
        lax.optimization_barrier(
            (segment, conv_weight, conv_bias, dt_bias, a_log, d_skip, group_gain, out_slices)
        )[:7]
    )
    seg_column, seg_row = segment[:, None], segment[None, :]
    cos_wide, sin_wide, cos_folded, sin_folded = rotation_tables(length)
    kind = jnp.minimum(place, 2)
    cos_folded = lax.dynamic_index_in_dim(cos_folded, kind, 0, False)
    sin_folded = lax.dynamic_index_in_dim(sin_folded, kind, 0, False)
    head_start = core * (MH // 2) + place * HEADS

    def local_rows(values, width_head):
        return jnp.concatenate(
            [
                lax.dynamic_slice_in_dim(values, head_start * width_head, HEADS * width_head, 0),
                values[MH * width_head :],
            ],
            axis=0,
        )

    taps = jnp.concatenate(
        [local_rows(conv_weight, HP).T, local_rows(conv_bias, HP)[None]], axis=0
    )
    taps = jnp.pad(taps, ((0, 8 - KC - 1), (0, 0)))
    rate = jnp.exp(local_rows(a_log, 1))
    head_rows = jnp.stack([local_rows(dt_bias, 1), rate])
    head_rows = jnp.pad(head_rows, ((0, 6), (DT_LANE, HD - DT_LANE - HEADS)))
    skip_row = jnp.repeat(local_rows(d_skip, 1), HP)[None, :]
    gain_row = lax.dynamic_slice_in_dim(group_gain, head_start, HEADS, 0).reshape(1, width_x)
    laps = length // CHUNK
    seg_laps = segment.reshape(laps, CHUNK)
    seg_last = seg_laps[:, -1:]
    seg_before = jnp.concatenate([jnp.full((1, 1), -1, jnp.int32), seg_last[:-1]])
    seg_ext = jnp.concatenate([jnp.full((KC - 1,), -1, jnp.int32), segment])
    keeps = [(seg_laps == seg_before).reshape(length), (seg_laps == seg_last).reshape(length)]
    keeps += [seg_ext[KC - 1 - back : KC - 1 - back + length] == segment for back in range(1, KC)]
    keeps = jnp.stack(keeps + [jnp.zeros((length,), bool)] * 3, axis=1).astype(jnp.float32)

    projected = mat_dot(normed, full_in)

    ssd_arrays = (
        projected,
        projected,
        pre_bc,
        pre_bc,
        taps,
        head_rows,
        keeps,
        seg_column,
        seg_laps[:, None, :],
        skip_row,
        gain_row,
    )
    gated, ssm, states, mixed, slope, kv_own = ssd_forward(ssd_arrays, cos_folded, sin_folded)
    kv_all = over_chips(kv_own)
    gu_gathered = lax.all_gather(after(gu_slices, out_gathered, gated), "dp", axis=0, tiled=True)
    down_gathered = lax.all_gather(after(down_slices, gu_gathered), "dp", axis=0, tiled=True)
    full_gu = gu_gathered.reshape(width, 2 * hidden_units)
    full_down = down_gathered.reshape(width, hidden_units)
    attended, log_total, queries, keys, vals = attend(
        attend_forward_kernel,
        (
            projected,
            cos_wide,
            sin_wide,
            after(kv_all, out_gathered),
            seg_column,
            seg_row,
        ),
        (
            ((length, HD), bf16),
            ((length, 1), jnp.float32),
            ((length, HD), bf16),
            ((length, HD), bf16),
            ((length, HD), bf16),
        ),
        blocks=[pl.BlockSpec((length, HD), lambda step: (0, width_x // HD))] + [None] * 5,
    )
    outs = jnp.concatenate([gated, attended], axis=1)
    middle = hidden_own + scatter_plane(outs, full_out, 2)[0]

    scale_two = lax.rsqrt(jnp.mean(middle * middle, axis=-1, keepdims=True) + EPSILON)
    normed_two, gate_up, activated = gather_plane(
        after((middle * scale_two * gain_two).astype(bf16), gu_gathered),
        9,
        apply_gate_up,
        (full_gu,),
        (((length, 2 * hidden_units), jnp.float32), ((length, hidden_units), bf16)),
    )
    teacher_own = lax.dynamic_slice(teacher[0], (core * own_rows, 0), (own_rows, width))
    factor = 2.0 * total_tokens / token_count * mask_rows.astype(jnp.float32)[:, None]
    block_out, d_out, d_mlp, d_gate_up, grad_down = down_and_back(
        activated, full_down, middle, teacher_own, factor, gate_up
    )

    def sum_rows(grads):
        summed = lax.psum_scatter(grads.astype(bf16), "dp", scatter_dimension=0, tiled=True)
        return summed.reshape(GROUP, slice_rows, grads.shape[1])

    grad_down = sum_rows(grad_down)
    d_normed_two, grad_gate_up = up_back(d_gate_up, full_gu, normed_two)
    grad_gate_up = sum_rows(after(grad_gate_up, grad_down))
    grad_gain_two = jnp.sum(d_normed_two * middle * scale_two, axis=0)
    d_scaled = d_normed_two * gain_two
    d_middle = (
        d_out
        + scale_two * d_scaled
        - middle * scale_two**3 * jnp.mean(d_scaled * middle, axis=-1, keepdims=True)
    )
    d_branch, d_gated, d_attended = gather_plane(
        after(d_middle.astype(bf16), grad_down),
        12,
        apply_out_back,
        (full_out,),
        (((length, width_x), jnp.float32), ((length, HD), bf16)),
    )
    d_query, d_kv = attend(
        attend_backward_kernel,
        (
            queries,
            keys,
            vals,
            cos_wide,
            sin_wide,
            seg_column,
            seg_row,
            log_total,
            d_attended,
        ),
        (((length, HD), bf16), ((GROUP, length // 2, HD), bf16)),
        (((length, HD), jnp.float32),) * 3,
    )
    d_kv_parts = from_chips(d_kv)
    grad_out = sum_rows(
        after(dot_left_t(d_branch, outs).astype(bf16), grad_gate_up, d_query)
    )
    (
        d_projected,
        grad_taps,
        grad_heads,
        d_skip_lanes,
        d_gain_lanes,
        back_gate_up,
        back_down,
    ) = ssd_backward(
        ssd_arrays,
        slope,
        mixed,
        ssm,
        states,
        d_gated,
        d_query,
        d_kv_parts,
        (cos_folded, sin_folded),
        (grad_gate_up, grad_down),
    )
    grad_skip = jnp.sum(d_skip_lanes.reshape(HEADS, HP), axis=-1)
    grad_group = d_gain_lanes.reshape(HEADS, HP)
    grad_in = sum_rows(
        after(dot_left_t(normed, d_projected[:, :width_in]).astype(bf16), grad_out)
    )
    bc_cols = 2 * NS // GROUP
    d_normed, bc_sum = scatter_plane(
        after(d_projected, grad_out), full_in, 8, ((normed, bc_cols, width // 2),), (w_bc,)
    )
    scale_own = lax.rsqrt(jnp.mean(hidden_own * hidden_own, axis=-1, keepdims=True) + EPSILON)
    grad_gain_one = jnp.sum(d_normed * hidden_own * scale_own, axis=0)
    d_scaled_one = d_normed * gain_one
    grad_input = (
        d_middle
        + scale_own * d_scaled_one
        - hidden_own * scale_own**3 * jnp.mean(d_scaled_one * hidden_own, axis=-1, keepdims=True)
    )
    taps_all = jnp.concatenate(
        [
            lax.dynamic_update_slice(
                jnp.zeros((8, MH * HP), jnp.float32), grad_taps[:, :width_x], (0, head_start * HP)
            ),
            grad_taps[:, width_x:],
        ],
        axis=1,
    )
    heads_all = lax.dynamic_update_slice(
        jnp.zeros((8, 128), jnp.float32),
        jnp.concatenate([grad_heads[:2, DT_LANE : DT_LANE + HEADS], grad_skip[None]]),
        (0, head_start),
    )
    group_all = lax.dynamic_update_slice(
        jnp.zeros((MH, HP), jnp.float32), grad_group, (head_start, 0)
    )
    small = [taps_all, heads_all]
    small += [
        values.reshape(8, -1) for values in (grad_gain_one, grad_gain_two, group_all)
    ]
    small = jnp.concatenate(small, axis=1)
    small_width = -(-small.shape[1] // (2 * GROUP * 128)) * 2 * GROUP * 128
    small = jnp.pad(small, ((0, 0), (0, small_width - small.shape[1])))
    piece, both_input, both_output, back_out = plane_sum(small, grad_input, block_out, grad_out)
    small_all, bc_all, back_in = finish_all(piece, bc_sum, grad_in)
    bc_all = bc_all.reshape(2 * GROUP, bc_cols, width // 2)
    shapes = [
        array.shape
        for array in (
            w_gate,
            w_up,
            w_down,
            w_mamba_out,
            w_attn_out,
            w_z,
            w_x,
            w_query,
            w_bc,
            w_key,
            w_value,
            w_dt.T,
            conv_weight.T,
        )
    ]
    shapes += [(1, conv_bias.shape[0])] + [(1, MH)] * 3 + [(MH, HP)] + [(1, slice_rows)] * 2
    (
        grad_gate,
        grad_up,
        grad_down,
        grad_mo,
        grad_ao,
        grad_z,
        grad_x,
        grad_q,
        grad_bc,
        grad_k,
        grad_v,
        grad_dt,
        grad_conv,
        grad_bias,
        grad_dtb,
        grad_alog,
        grad_skip,
        grad_group,
        grad_one,
        grad_two,
        grad_input,
        block_out,
    ) = unpack_all(
        (back_gate_up, back_down, back_out, back_in),
        bc_all,
        (both_input, both_output),
        small_all,
        shapes,
    )
    return (
        block_out[None],
        grad_input[None],
        grad_one[0],
        grad_z,
        grad_x,
        grad_bc,
        grad_dt.T,
        grad_conv.T,
        grad_bias.reshape(-1),
        grad_dtb[0],
        grad_alog[0],
        grad_skip[0],
        grad_group,
        grad_mo,
        grad_q,
        grad_k,
        grad_v,
        grad_ao,
        grad_two[0],
        grad_gate,
        grad_up,
        grad_down,
    )


def solution(mesh):
    placed = (
        P("dp", "seq", None),
        P("dp", "seq", None),
        P("dp", None),
        P(),
        P(("dp", "seq")),
        P(("dp", "seq"), "tensor"),
        P(("dp", "seq"), "tensor"),
        P(),
        P(("dp", "seq"), "tensor"),
        P(),
        P(),
        P(),
        P(),
        P(),
        P(),
        P("tensor", ("dp", "seq")),
        P(("dp", "seq"), "tensor"),
        P(("dp", "seq"), "tensor"),
        P(("dp", "seq"), "tensor"),
        P("tensor", ("dp", "seq")),
        P(("dp", "seq")),
        P(("dp", "seq"), "tensor"),
        P(("dp", "seq"), "tensor"),
        P("tensor", ("dp", "seq")),
    )
    whole_row = mesh.shape["seq"] == GROUP and mesh.shape["tensor"] == 2
    return jax.shard_map(
        heads_local_plan if whole_row else local,
        mesh=mesh,
        in_specs=placed,
        out_specs=(
            P("dp", "seq", None),
            P("dp", "seq", None),
            P(("dp", "seq")),
            P(("dp", "seq"), "tensor"),
            P(("dp", "seq"), "tensor"),
            P(),
            P(("dp", "seq"), "tensor"),
            P(),
            P(),
            P(),
            P(),
            P(),
            P(),
            P("tensor", ("dp", "seq")),
            P(("dp", "seq"), "tensor"),
            P(("dp", "seq"), "tensor"),
            P(("dp", "seq"), "tensor"),
            P("tensor", ("dp", "seq")),
            P(("dp", "seq")),
            P(("dp", "seq"), "tensor"),
            P(("dp", "seq"), "tensor"),
            P("tensor", ("dp", "seq")),
        ),
        check_vma=False,
    )
```

```python
from functools import partial

import jax
import jax.numpy as jnp
import numpy as np
from jax import lax
from jax.experimental import pallas as pl
from jax.experimental.pallas import tpu as pltpu
from jax.sharding import PartitionSpec as P

MH = 48
HP = 64
NS = 256
KC = 4
HD = 128


EPSILON = 1e-06
GROUP_EPSILON = 1e-05
ROPE_BASE = 10000.0
HIGHEST = lax.Precision.HIGHEST


def shifted(block, axis, distance):
    devices = range(lax.axis_size(axis))
    route = [(i - distance, i) for i in devices if i - distance in devices]
    return lax.ppermute(block, axis, route)


def carried_in(part, axis, combine, identity, reverse):
    count = lax.axis_size(axis)
    place = lax.axis_index(axis)
    ahead = count - 1 - place if reverse else place
    gathered = jax.tree.map(lambda a: lax.all_gather(a, axis), part)
    state = jax.tree.map(lambda a, e: jnp.zeros_like(a) + jnp.asarray(e, a.dtype), part, identity)

    def one(lap, state):
        source = count - 1 - lap if reverse else lap
        return combine(
            state, jax.tree.map(lambda a: lax.dynamic_index_in_dim(a, source, 0, False), gathered)
        )

    return lax.fori_loop(0, ahead, one, state)


def mat_dot(left_side, right_side):
    return jnp.dot(left_side, right_side, preferred_element_type=jnp.float32)


def dot_left_t(left_side, right_side):
    return lax.dot_general(
        left_side, right_side, (((0,), (0,)), ((), ())), preferred_element_type=jnp.float32
    )


def dot_right_t(left_side, right_side):
    return lax.dot_general(
        left_side, right_side, (((1,), (1,)), ((), ())), preferred_element_type=jnp.float32
    )


def rms_norm(values, gain_row):
    scale_row = lax.rsqrt(jnp.mean(values * values, axis=-1, keepdims=True) + EPSILON)
    return values * scale_row * gain_row


def rotate(positions, values):
    half_dim = values.shape[-1] // 2
    frequency = ROPE_BASE ** (-2.0 * jnp.arange(half_dim).astype(jnp.float32) / values.shape[-1])
    angles = positions.astype(jnp.float32)[:, None] * frequency[None, :]
    cosine = jnp.cos(angles)[:, None, :]
    sine_part = jnp.sin(angles)[:, None, :]
    first_half = values[..., :half_dim]
    second = values[..., half_dim:]
    return jnp.concatenate(
        [first_half * cosine - second * sine_part, second * cosine + first_half * sine_part],
        axis=-1,
    )


def conv_silu(seg_ext, seg_rows, extended, weights, bias_row):
    size_rows = seg_rows.shape[0]
    summed = jnp.zeros((size_rows, weights.shape[0]), jnp.float32) + bias_row[None, :]
    for tap_index in range(weights.shape[1]):
        window = lax.slice_in_dim(extended, tap_index, tap_index + size_rows, axis=0)
        keep_mask = (
            lax.slice_in_dim(seg_ext, tap_index, tap_index + size_rows) == seg_rows
        ).astype(jnp.float32)
        summed = summed + window * weights[:, tap_index][None, :] * keep_mask[:, None]
    return jax.nn.silu(summed)


def group_gate(ssm_out, gate_z, group_gain):
    mixed_val = ssm_out * jax.nn.silu(gate_z)
    return (
        mixed_val
        * lax.rsqrt(jnp.mean(mixed_val * mixed_val, axis=-1, keepdims=True) + GROUP_EPSILON)
        * group_gain[None]
    )


def swiglu(gate_pre, up_pre):
    return jax.nn.silu(gate_pre) * up_pre


def split_mixed(mixed_in, heads_local):
    size_rows = mixed_in.shape[0]
    width_x = heads_local * HP
    heads_x = mixed_in[:, :width_x].reshape(size_rows, heads_local, HP)
    return (heads_x, mixed_in[:, width_x : width_x + NS], mixed_in[:, width_x + NS :])


def ssd_main(seg_rows, seg_before, mixed_in, dt_raw, dt_bias_row, a_log_row, d_skip_row):
    size_rows = seg_rows.shape[0]
    heads_x, b_rows, c_rows = split_mixed(mixed_in, dt_raw.shape[1])
    dt_rows = jax.nn.softplus(dt_raw + dt_bias_row[None, :])
    cumul = jnp.cumsum(-jnp.exp(a_log_row)[None, :] * dt_rows, axis=0)
    order_pos = jnp.arange(size_rows)
    allowed = (seg_rows[:, None] == seg_rows[None, :]) & (order_pos[:, None] >= order_pos[None, :])
    differ = cumul[:, None, :] - cumul[None, :, :]
    decay = jnp.exp(jnp.where(allowed[:, :, None], differ, -jnp.inf))
    gram = jnp.dot(c_rows, b_rows.T, precision=HIGHEST, preferred_element_type=jnp.float32)
    mixing = gram[:, :, None] * decay * dt_rows[None, :, :]
    outputs = jnp.einsum("tsh,shp->thp", mixing, heads_x, precision=HIGHEST)
    outputs = outputs + d_skip_row[None, :, None] * heads_x
    tail_keep = (seg_rows == seg_rows[-1]).astype(jnp.float32)
    tail_weight = jnp.exp(cumul[-1][None, :] - cumul) * tail_keep[:, None] * dt_rows
    local_state = jnp.einsum("sh,shp,sn->hpn", tail_weight, heads_x, b_rows, precision=HIGHEST)
    carry_factor = jnp.exp(cumul[-1]) * (seg_rows[-1] == seg_before).astype(jnp.float32)
    return (outputs, carry_factor, local_state)


def ssd_state(seg_rows, seg_before, mixed_in, dt_raw, dt_bias_row, a_log_row, entry_state):
    heads_x, b_rows, c_rows = split_mixed(mixed_in, dt_raw.shape[1])
    dt_rows = jax.nn.softplus(dt_raw + dt_bias_row[None, :])
    cumul = jnp.cumsum(-jnp.exp(a_log_row)[None, :] * dt_rows, axis=0)
    entry_keep = (seg_rows == seg_before).astype(jnp.float32)
    entry_part = jnp.einsum("tn,hpn->thp", c_rows, entry_state, precision=HIGHEST)
    return jnp.exp(cumul)[:, :, None] * entry_keep[:, None, None] * entry_part


def chain_states(earlier, later):
    return (earlier[0] * later[0], later[0][:, None, None] * earlier[1] + later[1])


def block_scores(queries, keys_all, vals_all, seg_full, query_pos, seg_query, block_index, key_len):
    key_blk = keys_all[block_index * key_len : (block_index + 1) * key_len]
    val_blk = vals_all[block_index * key_len : (block_index + 1) * key_len]
    seg_key = seg_full[block_index * key_len : (block_index + 1) * key_len]
    key_pos = block_index * key_len + jnp.arange(key_len)
    scores = jnp.einsum(
        "tkgd,skd->kgts", queries, key_blk, preferred_element_type=jnp.float32
    ) * HD ** (-0.5)
    allowed = (query_pos[:, None] >= key_pos[None, :]) & (seg_query[:, None] == seg_key[None, :])
    return (key_blk, val_blk, jnp.where(allowed[None, None], scores, -jnp.inf))


def attend_forward(queries, keys_all, vals_all, seg_full, query_pos, seg_query, block_count):
    key_len = keys_all.shape[0] // block_count
    stat_shape = (queries.shape[1], queries.shape[2], queries.shape[0])
    running_max = jnp.full(stat_shape, -1e30, jnp.float32)
    running_sum = jnp.zeros(stat_shape, jnp.float32)
    for block_index in range(block_count):
        needed = block_index * key_len <= query_pos[-1]

        def stat_step(stats, block_index=block_index):
            old_max, old_sum = stats
            key_blk, val_blk, scores = block_scores(
                queries, keys_all, vals_all, seg_full, query_pos, seg_query, block_index, key_len
            )
            new_max = jnp.maximum(old_max, jnp.max(scores, axis=-1))
            new_sum = old_sum * jnp.exp(old_max - new_max) + jnp.sum(
                jnp.exp(scores - new_max[..., None]), axis=-1
            )
            return (new_max, new_sum)

        running_max, running_sum = lax.cond(
            needed, stat_step, lambda stats: stats, (running_max, running_sum)
        )
    log_total = running_max + jnp.log(running_sum)
    attended = jnp.zeros(queries.shape, jnp.float32)
    for block_index in range(block_count):
        needed = block_index * key_len <= query_pos[-1]

        def value_step(total, block_index=block_index):
            key_blk, val_blk, scores = block_scores(
                queries, keys_all, vals_all, seg_full, query_pos, seg_query, block_index, key_len
            )
            probs = jnp.exp(scores - log_total[..., None]).astype(jnp.bfloat16)
            return total + jnp.einsum(
                "kgts,skd->tkgd", probs, val_blk, preferred_element_type=jnp.float32
            )

        attended = lax.cond(needed, value_step, lambda total: total, attended)
    return (log_total, attended)


def attend_backward(
    queries, keys_all, vals_all, seg_full, query_pos, seg_query, block_count, grad_out, log_total
):
    key_len = keys_all.shape[0] // block_count
    delta = jnp.zeros(log_total.shape, jnp.float32)
    for block_index in range(block_count):
        needed = block_index * key_len <= query_pos[-1]

        def delta_step(total, block_index=block_index):
            key_blk, val_blk, scores = block_scores(
                queries, keys_all, vals_all, seg_full, query_pos, seg_query, block_index, key_len
            )
            probs = jnp.exp(scores - log_total[..., None])
            grad_probs = jnp.einsum(
                "tkgd,skd->kgts", grad_out, val_blk, preferred_element_type=jnp.float32
            )
            return total + jnp.sum(probs * grad_probs, axis=-1)

        delta = lax.cond(needed, delta_step, lambda total: total, delta)
    grad_query = jnp.zeros(queries.shape, jnp.float32)
    empty_part = jnp.zeros((key_len, keys_all.shape[1], keys_all.shape[2]), jnp.float32)
    key_parts = []
    val_parts = []
    for block_index in range(block_count):
        needed = block_index * key_len <= query_pos[-1]

        def grad_step(total, block_index=block_index):
            key_blk, val_blk, scores = block_scores(
                queries, keys_all, vals_all, seg_full, query_pos, seg_query, block_index, key_len
            )
            probs = jnp.exp(scores - log_total[..., None])
            grad_probs = jnp.einsum(
                "tkgd,skd->kgts", grad_out, val_blk, preferred_element_type=jnp.float32
            )
            grad_scores = (probs * (grad_probs - delta[..., None])).astype(jnp.bfloat16)
            new_total = total + jnp.einsum(
                "kgts,skd->tkgd", grad_scores, key_blk, preferred_element_type=jnp.float32
            ) * HD ** (-0.5)
            key_part = jnp.einsum(
                "kgts,tkgd->skd", grad_scores, queries, preferred_element_type=jnp.float32
            ) * HD ** (-0.5)
            val_part = jnp.einsum(
                "kgts,tkgd->skd",
                probs.astype(jnp.bfloat16),
                grad_out,
                preferred_element_type=jnp.float32,
            )
            return (new_total, key_part, val_part)

        grad_query, key_part, val_part = lax.cond(
            needed, grad_step, lambda total: (total, empty_part, empty_part), grad_query
        )
        key_parts.append(key_part)
        val_parts.append(val_part)
    return (grad_query, jnp.concatenate(key_parts, axis=0), jnp.concatenate(val_parts, axis=0))


def local(
    hidden_in,
    teacher,
    segment_ids,
    valid_mask,
    norm1_gain,
    w_z,
    w_x,
    w_bc,
    w_dt,
    conv_weight,
    conv_bias,
    dt_bias,
    a_log,
    d_skip,
    group_gain,
    w_mamba_out,
    w_query,
    w_key,
    w_value,
    w_attn_out,
    norm2_gain,
    w_gate,
    w_up,
    w_down,
):
    tensor_rank = lax.axis_index("tensor")
    seq_rank = lax.axis_index("seq")
    data_rank = lax.axis_index("dp")
    seq_count = lax.axis_size("seq")
    tensor_count = lax.axis_size("tensor")
    size_rows = hidden_in.shape[1]
    full_length = segment_ids.shape[1]
    row_start = seq_rank * size_rows
    seg_full = segment_ids[0]
    seg_local = lax.dynamic_slice_in_dim(seg_full, row_start, size_rows)
    seg_padded = jnp.concatenate([jnp.full((KC - 1,), -1, jnp.int32), seg_full])
    seg_ext = lax.dynamic_slice_in_dim(seg_padded, row_start, size_rows + KC - 1)
    seg_prev = lax.dynamic_index_in_dim(seg_padded, row_start + KC - 2, keepdims=False)
    token_count = jnp.sum(valid_mask).astype(jnp.float32)
    mask_rows = lax.dynamic_slice(valid_mask, (data_rank, row_start), (1, size_rows))[0].astype(
        jnp.float32
    )
    total_tokens = float(valid_mask.shape[0] * valid_mask.shape[1])
    (
        gain_one,
        full_z,
        full_x,
        full_dt,
        full_mo,
        full_q,
        full_k,
        full_v,
        full_ao,
        gain_two,
        full_gate,
        full_up,
        full_down,
    ) = (
        lax.all_gather(norm1_gain, ("dp", "seq"), axis=0, tiled=True),
        lax.all_gather(w_z, ("dp", "seq"), axis=0, tiled=True),
        lax.all_gather(w_x, ("dp", "seq"), axis=0, tiled=True),
        lax.all_gather(w_dt, ("dp", "seq"), axis=0, tiled=True),
        lax.all_gather(w_mamba_out, ("dp", "seq"), axis=1, tiled=True),
        lax.all_gather(w_query, ("dp", "seq"), axis=0, tiled=True),
        lax.all_gather(w_key, ("dp", "seq"), axis=0, tiled=True),
        lax.all_gather(w_value, ("dp", "seq"), axis=0, tiled=True),
        lax.all_gather(w_attn_out, ("dp", "seq"), axis=1, tiled=True),
        lax.all_gather(norm2_gain, ("dp", "seq"), axis=0, tiled=True),
        lax.all_gather(w_gate, ("dp", "seq"), axis=0, tiled=True),
        lax.all_gather(w_up, ("dp", "seq"), axis=0, tiled=True),
        lax.all_gather(w_down, ("dp", "seq"), axis=1, tiled=True),
    )
    heads_local = MH // tensor_count
    width_x = heads_local * HP
    head_start = tensor_rank * heads_local
    hidden = hidden_in[0].astype(jnp.float32)
    normed_f, norm_one_pull = jax.vjp(rms_norm, hidden, gain_one.astype(jnp.float32))
    normed = normed_f.astype(jnp.bfloat16)
    gate_z = mat_dot(normed, full_z)
    pre_x = mat_dot(normed, full_x).astype(jnp.bfloat16)
    pre_bc = mat_dot(normed, w_bc).astype(jnp.bfloat16)
    dt_raw = mat_dot(normed, full_dt)
    pre_all = jnp.concatenate([pre_x, pre_bc], axis=1)
    rim_rows = shifted(pre_all[size_rows - (KC - 1) :], "seq", 1)
    extended = jnp.concatenate([rim_rows, pre_all], axis=0).astype(jnp.float32)
    conv_local = jnp.concatenate(
        [
            lax.dynamic_slice_in_dim(conv_weight, head_start * HP, width_x, 0),
            conv_weight[MH * HP :],
        ],
        axis=0,
    )
    bias_local = jnp.concatenate(
        [lax.dynamic_slice_in_dim(conv_bias, head_start * HP, width_x, 0), conv_bias[MH * HP :]],
        axis=0,
    )
    mixed_f, conv_pull = jax.vjp(
        partial(conv_silu, seg_ext, seg_local), extended, conv_local, bias_local
    )
    mixed_in = lax.optimization_barrier(mixed_f.astype(jnp.bfloat16)).astype(jnp.float32)
    dt_bias_loc = lax.dynamic_slice_in_dim(dt_bias, head_start, heads_local)
    a_log_loc = lax.dynamic_slice_in_dim(a_log, head_start, heads_local)
    d_skip_loc = lax.dynamic_slice_in_dim(d_skip, head_start, heads_local)
    group_loc = lax.dynamic_slice_in_dim(group_gain, head_start, heads_local, 0)
    (ssm_local, carry_dev, state_dev), main_pull = jax.vjp(
        partial(ssd_main, seg_local, seg_prev), mixed_in, dt_raw, dt_bias_loc, a_log_loc, d_skip_loc
    )
    identity = (jnp.ones_like(carry_dev), jnp.zeros_like(state_dev))
    entry_state = carried_in((carry_dev, state_dev), "seq", chain_states, identity, False)[1]
    ssm_entry, state_pull = jax.vjp(
        partial(ssd_state, seg_local, seg_prev),
        mixed_in,
        dt_raw,
        dt_bias_loc,
        a_log_loc,
        entry_state,
    )
    ssm_out = ssm_local + ssm_entry
    gated_f, gate_pull = jax.vjp(
        group_gate, ssm_out, gate_z.reshape(size_rows, heads_local, HP), group_loc
    )
    gated = gated_f.reshape(size_rows, width_x).astype(jnp.bfloat16)
    mamba_part = mat_dot(gated, full_mo)
    positions = row_start + jnp.arange(size_rows)
    heads_q = full_q.shape[1] // HD
    heads_kv = full_k.shape[1] // HD
    groups = heads_q // heads_kv
    query_rot, query_pull = jax.vjp(
        partial(rotate, positions), mat_dot(normed, full_q).reshape(size_rows, heads_q, HD)
    )
    queries = query_rot.astype(jnp.bfloat16).reshape(size_rows, heads_kv, groups, HD)
    key_rot, key_pull = jax.vjp(
        partial(rotate, positions), mat_dot(normed, full_k).reshape(size_rows, heads_kv, HD)
    )
    keys_local = key_rot.astype(jnp.bfloat16).reshape(size_rows, heads_kv * HD)
    vals_local = mat_dot(normed, full_v).astype(jnp.bfloat16)
    keys_all, vals_all = (
        lax.all_gather(keys_local, "seq", axis=0, tiled=True),
        lax.all_gather(vals_local, "seq", axis=0, tiled=True),
    )
    keys_all = keys_all.reshape(full_length, heads_kv, HD)
    vals_all = vals_all.reshape(full_length, heads_kv, HD)
    block_count = seq_count // 4
    log_total, attended_f = attend_forward(
        queries, keys_all, vals_all, seg_full, positions, seg_local, block_count
    )
    attended = attended_f.reshape(size_rows, heads_q * HD).astype(jnp.bfloat16)
    branch = lax.psum(mamba_part + mat_dot(attended, full_ao), "tensor")
    middle = hidden + branch
    normed_two_f, norm_two_pull = jax.vjp(rms_norm, middle, gain_two.astype(jnp.float32))
    normed_two = normed_two_f.astype(jnp.bfloat16)
    act_f, glu_pull = jax.vjp(swiglu, mat_dot(normed_two, full_gate), mat_dot(normed_two, full_up))
    activated = act_f.astype(jnp.bfloat16)
    block_out = middle + lax.psum(mat_dot(activated, full_down), "tensor")
    (
        back_z,
        back_x,
        back_dt,
        back_mo,
        back_q,
        back_k,
        back_v,
        back_ao,
        back_gate,
        back_up,
        back_down,
    ) = (
        lax.all_gather(w_z, ("dp", "seq"), axis=0, tiled=True),
        lax.all_gather(w_x, ("dp", "seq"), axis=0, tiled=True),
        lax.all_gather(w_dt, ("dp", "seq"), axis=0, tiled=True),
        lax.all_gather(w_mamba_out, ("dp", "seq"), axis=1, tiled=True),
        lax.all_gather(w_query, ("dp", "seq"), axis=0, tiled=True),
        lax.all_gather(w_key, ("dp", "seq"), axis=0, tiled=True),
        lax.all_gather(w_value, ("dp", "seq"), axis=0, tiled=True),
        lax.all_gather(w_attn_out, ("dp", "seq"), axis=1, tiled=True),
        lax.all_gather(w_gate, ("dp", "seq"), axis=0, tiled=True),
        lax.all_gather(w_up, ("dp", "seq"), axis=0, tiled=True),
        lax.all_gather(w_down, ("dp", "seq"), axis=1, tiled=True),
    )
    d_out = (
        2.0
        * total_tokens
        / token_count
        * mask_rows[:, None]
        * (block_out - teacher[0].astype(jnp.float32))
    )
    d_mlp = d_out.astype(jnp.bfloat16)
    grad_down = dot_left_t(activated, d_mlp)
    d_gate_f, d_up_f = glu_pull(dot_right_t(d_mlp, back_down))
    d_gate = d_gate_f.astype(jnp.bfloat16)
    d_up = d_up_f.astype(jnp.bfloat16)
    grad_gate = dot_left_t(normed_two, d_gate)
    grad_up = dot_left_t(normed_two, d_up)
    d_normed_two = lax.psum(dot_right_t(d_gate, back_gate) + dot_right_t(d_up, back_up), "tensor")
    d_middle_n, grad_gain_two = norm_two_pull(d_normed_two)
    d_middle = d_out + d_middle_n
    d_branch = d_middle.astype(jnp.bfloat16)
    grad_ao = dot_left_t(attended, d_branch)
    grad_mo = dot_left_t(gated, d_branch)
    d_attended = (
        dot_right_t(d_branch, back_ao).astype(jnp.bfloat16).reshape(size_rows, heads_kv, groups, HD)
    )
    d_gated = dot_right_t(d_branch, back_mo).reshape(size_rows, heads_local, HP)
    d_ssm, d_gate_z_f, grad_group = gate_pull(d_gated)
    d_gate_z = d_gate_z_f.reshape(size_rows, width_x).astype(jnp.bfloat16)
    d_mixed_s, d_dt_s, d_dtb_s, d_alog_s, d_entry = state_pull(d_ssm)
    state_grad = carried_in((carry_dev, d_entry), "seq", chain_states, identity, True)[1]
    d_carry = jnp.sum(state_grad * entry_state, axis=(1, 2))
    d_mixed_m, d_dt_m, d_dtb_m, d_alog_m, grad_skip = main_pull((d_ssm, d_carry, state_grad))
    d_dt_raw = (d_dt_s + d_dt_m).astype(jnp.bfloat16)
    d_ext, grad_conv_loc, grad_bias_loc = conv_pull(d_mixed_s + d_mixed_m)
    rim_grad = shifted(d_ext[: KC - 1], "seq", -1)
    d_pre = d_ext[KC - 1 :] + jnp.pad(rim_grad, ((size_rows - (KC - 1), 0), (0, 0)))
    d_pre_x = d_pre[:, :width_x].astype(jnp.bfloat16)
    d_pre_bc = d_pre[:, width_x:]
    grad_query_rot, key_grads_all, val_grads_all = attend_backward(
        queries,
        keys_all,
        vals_all,
        seg_full,
        positions,
        seg_local,
        block_count,
        d_attended,
        log_total,
    )
    key_grad, val_grad = (
        lax.psum_scatter(
            key_grads_all.reshape(full_length, heads_kv * HD).astype(jnp.bfloat16),
            "seq",
            scatter_dimension=0,
            tiled=True,
        ).astype(jnp.float32),
        lax.psum_scatter(
            val_grads_all.reshape(full_length, heads_kv * HD).astype(jnp.bfloat16),
            "seq",
            scatter_dimension=0,
            tiled=True,
        ).astype(jnp.float32),
    )
    d_query = (
        query_pull(grad_query_rot.reshape(size_rows, heads_q, HD))[0]
        .reshape(size_rows, heads_q * HD)
        .astype(jnp.bfloat16)
    )
    d_key = (
        key_pull(key_grad.reshape(size_rows, heads_kv, HD))[0]
        .reshape(size_rows, heads_kv * HD)
        .astype(jnp.bfloat16)
    )
    d_value = val_grad.astype(jnp.bfloat16)
    grad_z = dot_left_t(normed, d_gate_z)
    grad_x = dot_left_t(normed, d_pre_x)
    grad_dt = dot_left_t(normed, d_dt_raw)
    grad_q = dot_left_t(normed, d_query)
    grad_k = dot_left_t(normed, d_key)
    grad_v = dot_left_t(normed, d_value)
    normed_wide = normed.astype(jnp.float32)
    bc_weight = w_bc.astype(jnp.float32)
    grad_bc = jnp.dot(
        normed_wide.T, d_pre_bc, precision=HIGHEST, preferred_element_type=jnp.float32
    )
    d_normed_part = (
        dot_right_t(d_gate_z, back_z)
        + dot_right_t(d_pre_x, back_x)
        + dot_right_t(d_dt_raw, back_dt)
        + dot_right_t(d_query, back_q)
        + dot_right_t(d_key, back_k)
        + dot_right_t(d_value, back_v)
        + jnp.dot(d_pre_bc, bc_weight.T, precision=HIGHEST, preferred_element_type=jnp.float32)
    )
    d_normed = lax.psum(d_normed_part.astype(jnp.bfloat16), "tensor").astype(jnp.float32)
    d_hidden_n, grad_gain_one = norm_one_pull(d_normed)
    grad_input = d_middle + d_hidden_n
    conv_x_full = lax.dynamic_update_slice_in_dim(
        jnp.zeros((MH * HP, KC), jnp.float32), grad_conv_loc[:width_x], head_start * HP, 0
    )
    grad_conv_full = jnp.concatenate([conv_x_full, grad_conv_loc[width_x:]], axis=0)
    bias_x_full = lax.dynamic_update_slice_in_dim(
        jnp.zeros((MH * HP,), jnp.float32), grad_bias_loc[:width_x], head_start * HP, 0
    )
    grad_bias_full = jnp.concatenate([bias_x_full, grad_bias_loc[width_x:]], axis=0)
    grad_dtb_full = lax.dynamic_update_slice_in_dim(
        jnp.zeros((MH,), jnp.float32), d_dtb_s + d_dtb_m, head_start, 0
    )
    grad_alog_full = lax.dynamic_update_slice_in_dim(
        jnp.zeros((MH,), jnp.float32), d_alog_s + d_alog_m, head_start, 0
    )
    grad_skip_full = lax.dynamic_update_slice_in_dim(
        jnp.zeros((MH,), jnp.float32), grad_skip, head_start, 0
    )
    grad_group_full = lax.dynamic_update_slice_in_dim(
        jnp.zeros((MH, HP), jnp.float32), grad_group, head_start, 0
    )
    sum_bc, sum_conv, sum_bias, sum_dtb, sum_alog, sum_skip, sum_group = lax.psum(
        (
            grad_bc,
            grad_conv_full,
            grad_bias_full,
            grad_dtb_full,
            grad_alog_full,
            grad_skip_full,
            grad_group_full,
        ),
        ("dp", "seq", "tensor"),
    )
    (
        out_gain_one,
        out_z,
        out_x,
        out_dt,
        out_mo,
        out_q,
        out_k,
        out_v,
        out_ao,
        out_gain_two,
        out_gate,
        out_up,
        out_down,
    ) = (
        lax.psum_scatter(grad_gain_one, ("dp", "seq"), scatter_dimension=0, tiled=True),
        lax.psum_scatter(grad_z, ("dp", "seq"), scatter_dimension=0, tiled=True),
        lax.psum_scatter(grad_x, ("dp", "seq"), scatter_dimension=0, tiled=True),
        lax.psum_scatter(grad_dt, ("dp", "seq"), scatter_dimension=0, tiled=True),
        lax.psum_scatter(grad_mo, ("dp", "seq"), scatter_dimension=1, tiled=True),
        lax.psum_scatter(grad_q, ("dp", "seq"), scatter_dimension=0, tiled=True),
        lax.psum_scatter(grad_k, ("dp", "seq"), scatter_dimension=0, tiled=True),
        lax.psum_scatter(grad_v, ("dp", "seq"), scatter_dimension=0, tiled=True),
        lax.psum_scatter(grad_ao, ("dp", "seq"), scatter_dimension=1, tiled=True),
        lax.psum_scatter(grad_gain_two, ("dp", "seq"), scatter_dimension=0, tiled=True),
        lax.psum_scatter(grad_gate, ("dp", "seq"), scatter_dimension=0, tiled=True),
        lax.psum_scatter(grad_up, ("dp", "seq"), scatter_dimension=0, tiled=True),
        lax.psum_scatter(grad_down, ("dp", "seq"), scatter_dimension=1, tiled=True),
    )
    return (
        block_out.astype(jnp.bfloat16)[None],
        grad_input[None],
        out_gain_one,
        out_z,
        out_x,
        sum_bc,
        out_dt,
        sum_conv,
        sum_bias,
        sum_dtb,
        sum_alog,
        sum_skip,
        sum_group,
        out_mo,
        out_q,
        out_k,
        out_v,
        out_ao,
        out_gain_two,
        out_gate,
        out_up,
        out_down,
    )


GROUP = 4
CHUNK = 128
HEADS = 6
MESH_ID = pl.DeviceIdType.MESH
VMEM_BYTES = 56 * 1024 * 1024


def dot_f32(left_side, right_side, left_dim, right_dim):
    return lax.dot_general(
        left_side,
        right_side,
        (((left_dim,), (right_dim,)), ((), ())),
        preferred_element_type=jnp.float32,
    )


def halves(values):
    high = values.astype(jnp.bfloat16)
    return (high, (values - high.astype(jnp.float32)).astype(jnp.bfloat16))


def plane_place():
    data, place, core = lax.axis_index("dp"), lax.axis_index("seq"), lax.axis_index("tensor")
    along_x = place + 1 - 2 * lax.rem(place, 2)
    along_y = lax.rem(place + 2, GROUP)
    across = GROUP - 1 - place
    return (data, place, core, along_x, along_y, across)


def meet(devices):
    barrier = pltpu.get_barrier_semaphore()
    for device in devices:
        pl.semaphore_signal(barrier, inc=1, device_id=device, device_id_type=MESH_ID)
    pl.semaphore_wait(barrier, len(devices))


def remote(source, target, send_sem, recv_sem, device):
    return pltpu.make_async_remote_copy(
        src_ref=source,
        dst_ref=target,
        send_sem=send_sem,
        recv_sem=recv_sem,
        device_id=device,
        device_id_type=MESH_ID,
    )


def lasting(microseconds):
    return pl.CostEstimate(
        flops=int(microseconds * 9e8),
        bytes_accessed=int(microseconds * 3e6),
        transcendentals=0,
    )


def any_specs(count):
    return [pl.BlockSpec(memory_space=pl.ANY)] * count


def vmem_specs(count):
    return [pl.BlockSpec(memory_space=pltpu.VMEM)] * count


def gather_kernel(apply, count_in, count_out, own_ref, *refs):
    inputs, all_ref = refs[:count_in], refs[count_in]
    outputs = refs[count_in + 1 : count_in + 1 + count_out]
    send_sems, recv_sems = refs[count_in + 1 + count_out :]
    data, place, core, along_x, along_y, across = plane_place()
    to_x, to_y, partner = (data, along_x, core), (data, along_y, core), (data, place, 1 - core)
    meet((to_x, to_y, partner))
    gather_steps(apply, own_ref, inputs, all_ref, outputs, send_sems, recv_sems)


def gather_steps(apply, own_ref, inputs, all_ref, outputs, send_sems, recv_sems, ready=None):
    data, place, core, along_x, along_y, across = plane_place()
    height = own_ref.shape[0]
    half = height // 2
    to_x, to_y, partner = (data, along_x, core), (data, along_y, core), (data, place, 1 - core)

    def block(chip, part):
        return all_ref.at[2 * chip + core, pl.ds(part * half, half)]

    def work(chip, side):
        if apply is not None:
            index = 2 * chip + side
            rows = pl.ds(pl.multiple_of(index * height, 16), height)
            apply(all_ref[index], rows, inputs, outputs)

    def push(index, source, target, device):
        copy = remote(source, target, send_sems.at[index], recv_sems.at[index], device)
        copy.start()
        return copy

    first, second = own_ref.at[pl.ds(0, half)], own_ref.at[pl.ds(half, half)]
    x_first = push(0, first, block(place, 0), to_x)
    y_second = push(1, second, block(place, 1), to_y)
    x_second = push(2, second, block(place, 1), to_x)
    y_first = push(3, first, block(place, 0), to_y)
    pair_own = push(4, own_ref, all_ref.at[2 * place + core], partner)
    all_ref[2 * place + core] = own_ref[...]
    work(place, core)
    pair_own.wait_recv()
    work(place, 1 - core)
    if ready is not None:
        ready(place, 0)
    x_first.wait_recv()
    over_y = push(5, block(along_x, 0), block(along_x, 0), to_y)
    y_second.wait_recv()
    over_x = push(6, block(along_y, 1), block(along_y, 1), to_x)
    x_second.wait_recv()
    mine_x = all_ref.at[2 * along_x + core]
    pair_x = push(7, mine_x, mine_x, partner)
    y_first.wait_recv()
    mine_y = all_ref.at[2 * along_y + core]
    pair_y = push(8, mine_y, mine_y, partner)
    work(along_x, core)
    work(along_y, core)
    pair_x.wait_recv()
    work(along_x, 1 - core)
    if ready is not None:
        ready(along_x, 1)
    pair_y.wait_recv()
    work(along_y, 1 - core)
    if ready is not None:
        ready(along_y, 2)
    over_y.wait_recv()
    pair_a = push(9, block(across, 0), block(across, 0), partner)
    over_x.wait_recv()
    pair_b = push(10, block(across, 1), block(across, 1), partner)
    work(across, core)
    pair_a.wait_recv()
    pair_b.wait_recv()
    work(across, 1 - core)
    if ready is not None:
        ready(across, 3)
    for copy in (
        x_first,
        y_second,
        x_second,
        y_first,
        pair_own,
        over_y,
        over_x,
        pair_x,
        pair_y,
        pair_a,
        pair_b,
    ):
        copy.wait_send()


def gather_plane(own, identity=1, apply=None, inputs=(), outputs=()):
    rows, width = own.shape
    gathered, *results = pl.pallas_call(
        partial(gather_kernel, apply, len(inputs), len(outputs)),
        out_shape=[jax.ShapeDtypeStruct((2 * GROUP, rows, width), own.dtype)]
        + [jax.ShapeDtypeStruct(shape, dtype) for shape, dtype in outputs],
        in_specs=vmem_specs(1 + len(inputs)),
        out_specs=vmem_specs(1 + len(outputs)),
        scratch_shapes=[pltpu.SemaphoreType.DMA((11,)), pltpu.SemaphoreType.DMA((11,))],
        cost_estimate=lasting(35),
        compiler_params=pltpu.CompilerParams(
            collective_id=identity, has_side_effects=True, vmem_limit_bytes=VMEM_BYTES
        ),
    )(own, *inputs)
    gathered = gathered.reshape(2 * GROUP * rows, width)
    return (gathered, *results) if results else gathered


def apply_gate_up(block, rows, inputs, outputs):
    weights, (both_ref, act_ref) = inputs[0], outputs
    units = act_ref.shape[1]
    both = jnp.dot(block, weights[...], preferred_element_type=jnp.float32)
    both_ref[rows] = both
    gate = both[:, :units]
    act_ref[rows] = (gate * jax.nn.sigmoid(gate) * both[:, units:]).astype(jnp.bfloat16)


def apply_down_back(block, rows, inputs, outputs):
    weights, both_ref = inputs
    units = weights.shape[1]
    d_act = jnp.dot(block, weights[...], preferred_element_type=jnp.float32)
    gate, up = both_ref[rows, :units], both_ref[rows, units:]
    sigmoid = jax.nn.sigmoid(gate)
    silu = gate * sigmoid
    d_gate = d_act * up * (sigmoid * (1.0 + gate * (1.0 - sigmoid)))
    outputs[0][rows, :units] = d_gate.astype(jnp.bfloat16)
    outputs[0][rows, units:] = (d_act * silu).astype(jnp.bfloat16)


def apply_out_back(block, rows, inputs, outputs):
    both = jnp.dot(block, inputs[0][...], preferred_element_type=jnp.float32)
    width = outputs[0].shape[1]
    outputs[0][rows] = both[:, :width]
    outputs[1][rows] = both[:, width:].astype(jnp.bfloat16)


def apply_norm(block, rows, inputs, outputs):
    gain_ref, weights = inputs
    values = block.astype(jnp.float32)
    scale = lax.rsqrt(jnp.mean(values * values, axis=-1, keepdims=True) + EPSILON)
    normed = (values * scale * gain_ref[...]).astype(jnp.bfloat16)
    outputs[0][rows] = normed
    outputs[1][rows] = jnp.dot(normed, weights[...], preferred_element_type=jnp.float32).astype(
        jnp.bfloat16
    )


def scatter_kernel(
    count, left_ref, right_ref, *refs, store=None, between=None, preparing=None, finishing=None
):
    data, place, core, along_x, along_y, across = plane_place()
    partner = (data, place, 1 - core)
    to_x, to_y = (data, along_x, core), (data, along_y, core)
    order = (across, along_x, along_y, place)
    count_in = 0 if count == 1 else count
    extra, sums = refs[:count_in], refs[count_in : count_in + count]
    parts, scratch = refs[count_in + count : count_in + 2 * count], refs[count_in + 2 * count :]
    step = 16
    meet((partner, to_x, to_y))

    def multiply(at, chip, side):
        part = parts[at]
        index = 2 * chip + side
        height, columns = part.shape[1:]
        if at == 0:
            rows = pl.ds(pl.multiple_of(index * height, 16), height)
            depth = right_ref.shape[1]
            block = dot_f32(left_ref[rows, :depth], right_ref[...], 1, 1)
            if count > 1:
                block = block + dot_f32(left_ref[rows, depth:], extra[-1][...], 1, 1)
        else:
            start = left_ref.shape[1] - GROUP * height
            turned = pl.ds(pl.multiple_of(start + chip * height, 128), height)
            along = pl.ds(pl.multiple_of(side * columns, 128), columns)
            block = dot_f32(left_ref[:, turned], extra[at - 1][:, along], 0, 0)
        part[index] = block.astype(jnp.bfloat16)

    def one_array(at, part_ref, sum_ref, own_refs):
        pair_in, send_a, send_x, send_y, got_x, got_y, pair_s, pair_r, send_s, recv_s = own_refs
        half = part_ref.shape[1] // 2
        pair = []

        def send_pair(index):
            chip = order[index]
            multiply(at, chip, 1 - core)
            copy = remote(
                part_ref.at[2 * chip + 1 - core],
                pair_in.at[index],
                pair_s.at[index],
                pair_r.at[index],
                partner,
            )
            copy.start()
            pair.append(copy)
            multiply(at, chip, core)

        def own_rows(index, rows):
            return part_ref[2 * order[index] + core, rows].astype(jnp.float32) + pair_in[
                index, rows
            ].astype(jnp.float32)

        def fill(target, index, first, extra=None):
            def one(lap, carry):
                rows = pl.ds(pl.multiple_of(lap * step, step), step)
                total = own_rows(index, pl.ds(pl.multiple_of(first + lap * step, step), step))
                if extra is not None:
                    total = total + extra[rows].astype(jnp.float32)
                target[rows] = total.astype(jnp.bfloat16)
                return carry

            lax.fori_loop(0, half // step, one, 0)

        def push(index, source, target, device):
            copy = remote(source, target, send_s.at[index], recv_s.at[index], device)
            copy.start()
            return copy

        send_pair(0)
        pair[0].wait_recv()
        fill(send_a.at[0], 0, 0)
        far_x = push(0, send_a.at[0], got_x.at[0], to_x)
        fill(send_a.at[1], 0, half)
        far_y = push(1, send_a.at[1], got_y.at[0], to_y)
        send_pair(1)
        pair[1].wait_recv()
        fill(send_x.at[0], 1, 0)
        near_x = push(2, send_x.at[0], got_x.at[1], to_x)
        send_pair(2)
        pair[2].wait_recv()
        fill(send_y.at[0], 2, half)
        near_y = push(3, send_y.at[0], got_y.at[1], to_y)
        send_pair(3)
        yield
        far_x.wait_recv()
        fill(send_y.at[1], 2, 0, got_x.at[0])
        last_y = push(4, send_y.at[1], got_y.at[2], to_y)
        far_y.wait_recv()
        fill(send_x.at[1], 1, half, got_y.at[0])
        last_x = push(5, send_x.at[1], got_x.at[2], to_x)
        yield
        pair[3].wait_recv()
        near_x.wait_recv()
        near_y.wait_recv()
        last_y.wait_recv()
        last_x.wait_recv()

        def finish(first, near, last):
            def one(lap, carry):
                rows = pl.ds(pl.multiple_of(lap * step, step), step)
                place_rows = pl.ds(pl.multiple_of(first + lap * step, step), step)
                total = (
                    own_rows(3, place_rows)
                    + near[rows].astype(jnp.float32)
                    + last[rows].astype(jnp.float32)
                )
                if store is None:
                    sum_ref[place_rows] = total
                else:
                    store(at, sum_ref, place_rows, total)
                return carry

            lax.fori_loop(0, half // step, one, 0)

        finish(0, got_x.at[1], got_y.at[2])
        finish(half, got_y.at[1], got_x.at[2])
        for copy in pair + [far_x, far_y, near_x, near_y, last_x, last_y]:
            copy.wait_send()

    each = len(scratch) // count
    runs = [
        one_array(at, parts[at], sums[at], scratch[each * at : each * (at + 1)]) for at in range(count)
    ]
    for stage in range(2):
        for at, run in enumerate(runs):
            if at > 0 and stage == 0 and preparing is not None:
                preparing()
            next(run)
        if between is not None:
            between(stage)
    if finishing is not None:
        finishing()
    for run in runs:
        for _ in run:
            pass


def down_and_back_kernel(
    act_ref,
    weights_ref,
    factor_ref,
    middle_hbm,
    teacher_hbm,
    both_hbm,
    out_ref,
    d_out_ref,
    d_both_ref,
    grad_ref,
    own_ref,
    grad_sum,
    d_mlp_ref,
    middle_ref,
    teacher_ref,
    both_ref,
    load_sems,
    gather_send,
    gather_recv,
    *scratch,
):
    loads = []
    for source, target in (
        (middle_hbm, middle_ref),
        (teacher_hbm, teacher_ref),
        (both_hbm, both_ref),
    ):
        copy = pltpu.make_async_copy(source, target, load_sems.at[len(loads)])
        copy.start()
        loads.append(copy)

    def loaded():
        for copy in loads:
            copy.wait()

    def store(at, target, rows, total):
        out = middle_ref[rows] + total
        out_ref[rows] = out.astype(jnp.bfloat16)
        d_out = factor_ref[rows] * (out - teacher_ref[rows].astype(jnp.float32))
        d_out_ref[rows] = d_out
        own_ref[rows] = d_out.astype(jnp.bfloat16)

    def ready(chip, turn_at):
        blocks = d_mlp_ref[pl.ds(2 * chip, 2)]
        height = blocks.shape[0] * blocks.shape[1]
        rows = pl.ds(pl.multiple_of(chip * height, 16), height)
        part = dot_f32(blocks.reshape(height, blocks.shape[2]), act_ref[rows], 0, 0)
        if turn_at == 0:
            grad_sum[...] = part
        elif turn_at < GROUP - 1:
            grad_sum[...] += part
        else:
            grad_ref[...] = (grad_sum[...] + part).astype(jnp.bfloat16)

    scatter_kernel(1, act_ref, weights_ref, None, *scratch, store=store, finishing=loaded)
    gather_steps(
        apply_down_back,
        own_ref,
        (weights_ref, both_ref),
        d_mlp_ref,
        (d_both_ref,),
        gather_send,
        gather_recv,
        ready,
    )


def down_and_back(activated, full_down, middle, teacher_own, factor, gate_up):
    rows, width = middle.shape
    shaped = jax.ShapeDtypeStruct
    return pl.pallas_call(
        down_and_back_kernel,
        out_shape=[
            shaped((rows, width), jnp.bfloat16),
            shaped((rows, width), jnp.float32),
            shaped(gate_up.shape, jnp.bfloat16),
            shaped(full_down.shape, jnp.bfloat16),
        ],
        in_specs=vmem_specs(3) + any_specs(3),
        out_specs=vmem_specs(4),
        scratch_shapes=[
            pltpu.VMEM((rows, width), jnp.bfloat16),
            pltpu.VMEM(full_down.shape, jnp.float32),
            pltpu.VMEM((2 * GROUP, rows, width), jnp.bfloat16),
            pltpu.VMEM(middle.shape, middle.dtype),
            pltpu.VMEM(teacher_own.shape, teacher_own.dtype),
            pltpu.VMEM(gate_up.shape, gate_up.dtype),
            pltpu.SemaphoreType.DMA((3,)),
            pltpu.SemaphoreType.DMA((11,)),
            pltpu.SemaphoreType.DMA((11,)),
        ]
        + scatter_scratch([(rows, width)]),
        cost_estimate=lasting(70),
        compiler_params=pltpu.CompilerParams(
            collective_id=10, has_side_effects=True, vmem_limit_bytes=VMEM_BYTES
        ),
    )(activated, full_down, factor, middle, teacher_own, gate_up)


def up_back_kernel(d_both_ref, weights_ref, normed_ref, sum_ref, grad_ref, *scratch):
    tiles = 4
    width = normed_ref.shape[1] // tiles

    def between(stage):
        for tile in range(2 * stage, 2 * stage + 2):
            columns = slice(width * tile, width * (tile + 1))
            grad_ref[columns] = dot_f32(
                normed_ref[:, columns], d_both_ref[...], 0, 0
            ).astype(jnp.bfloat16)

    scatter_kernel(1, d_both_ref, weights_ref, sum_ref, *scratch, between=between)


def up_back(d_gate_up, full_gu, normed_two):
    rows, width = d_gate_up.shape[0] // (2 * GROUP), full_gu.shape[0]
    return pl.pallas_call(
        up_back_kernel,
        out_shape=[
            jax.ShapeDtypeStruct((rows, width), jnp.float32),
            jax.ShapeDtypeStruct(full_gu.shape, jnp.bfloat16),
        ],
        in_specs=vmem_specs(3),
        out_specs=vmem_specs(2),
        scratch_shapes=scatter_scratch([(rows, width)]),
        cost_estimate=lasting(38),
        compiler_params=pltpu.CompilerParams(
            collective_id=11, has_side_effects=True, vmem_limit_bytes=VMEM_BYTES
        ),
    )(d_gate_up, full_gu, normed_two)


def input_back_kernel(
    left_ref,
    weights_ref,
    bc_weights_ref,
    gain_ref,
    normed_hbm,
    hidden_hbm,
    d_middle_hbm,
    grad_ref,
    bc_ref,
    gain_sum_ref,
    normed_ref,
    hidden_ref,
    d_middle_ref,
    load_sems,
    *scratch,
):
    loads = []
    for source, target in (
        (normed_hbm, normed_ref),
        (hidden_hbm, hidden_ref),
        (d_middle_hbm, d_middle_ref),
    ):
        copy = pltpu.make_async_copy(source, target, load_sems.at[len(loads)])
        copy.start()
        loads.append(copy)
    gain_sum_ref[...] = jnp.zeros_like(gain_sum_ref)

    def loaded():
        for copy in loads[1:]:
            copy.wait()


    def store(at, target, rows, total):
        if at > 0:
            target[rows] = total
            return
        hidden = hidden_ref[rows].astype(jnp.float32)
        scale = lax.rsqrt(jnp.mean(hidden * hidden, axis=-1, keepdims=True) + EPSILON)
        scaled = total * gain_ref[...]
        inner = jnp.mean(scaled * hidden, axis=-1, keepdims=True)
        grad_ref[rows] = d_middle_ref[rows] + scale * scaled - hidden * (scale**3 * inner)
        product = total * hidden * scale
        gain_sum_ref[...] += product[:8] + product[8:]

    scatter_kernel(
        2,
        left_ref,
        weights_ref,
        normed_ref,
        bc_weights_ref,
        None,
        bc_ref,
        *scratch,
        store=store,
        preparing=loads[0].wait,
        finishing=loaded,
    )


def input_back(d_projected, full_in, normed, w_bc, hidden_own, d_middle, gain, bc_cols):
    rows, width = d_middle.shape
    sizes = [(rows, width), (bc_cols, width // 2)]
    shaped = jax.ShapeDtypeStruct
    return pl.pallas_call(
        input_back_kernel,
        out_shape=[
            shaped((rows, width), jnp.float32),
            shaped(sizes[1], jnp.float32),
            shaped((8, width), jnp.float32),
        ],
        in_specs=vmem_specs(4) + any_specs(3),
        out_specs=vmem_specs(3),
        scratch_shapes=[
            pltpu.VMEM(normed.shape, normed.dtype),
            pltpu.VMEM(hidden_own.shape, hidden_own.dtype),
            pltpu.VMEM(d_middle.shape, d_middle.dtype),
            pltpu.SemaphoreType.DMA((3,)),
        ]
        + scatter_scratch(sizes),
        cost_estimate=lasting(50),
        compiler_params=pltpu.CompilerParams(
            collective_id=8, has_side_effects=True, vmem_limit_bytes=VMEM_BYTES
        ),
    )(d_projected, full_in, w_bc, gain, normed, hidden_own, d_middle)


def scatter_scratch(sizes):
    scratch = [pltpu.VMEM((2 * GROUP, *size), jnp.bfloat16) for size in sizes]
    for rows, columns in sizes:
        half = (rows // 2, columns)
        scratch += [
            pltpu.VMEM((4, rows, columns), jnp.bfloat16),
            pltpu.VMEM((2,) + half, jnp.bfloat16),
            pltpu.VMEM((2,) + half, jnp.bfloat16),
            pltpu.VMEM((2,) + half, jnp.bfloat16),
            pltpu.VMEM((3,) + half, jnp.bfloat16),
            pltpu.VMEM((3,) + half, jnp.bfloat16),
            pltpu.SemaphoreType.DMA((4,)),
            pltpu.SemaphoreType.DMA((4,)),
            pltpu.SemaphoreType.DMA((6,)),
            pltpu.SemaphoreType.DMA((6,)),
        ]
    return scratch


def scatter_plane(left, right, identity, extra=(), beside=()):
    height, width = left.shape[0] // (2 * GROUP), right.shape[0]
    sizes = [(height, width)] + [tuple(size) for _, *size in extra]
    shapes = [jax.ShapeDtypeStruct(size, jnp.float32) for size in sizes]
    count = 1 + len(extra)
    return pl.pallas_call(
        partial(scatter_kernel, count),
        out_shape=shapes,
        in_specs=vmem_specs(2 if count == 1 else 2 + count),
        out_specs=vmem_specs(count),
        scratch_shapes=scatter_scratch(sizes),
        cost_estimate=lasting(35),
        compiler_params=pltpu.CompilerParams(
            collective_id=identity, has_side_effects=True, vmem_limit_bytes=VMEM_BYTES
        ),
    )(left, right, *[array for array, *_ in extra], *beside)


def plane_sum_kernel(
    small_ref, own_ref, out_ref, bulk, sum_ref, both_ref, both_out, back, small_in, own_sem, send_s, recv_s
):
    data, place, core, along_x, along_y, across = plane_place()
    mine = 2 * place + core
    partner = (data, place, 1 - core)
    plane = []
    for turn_by in range(1, 2 * GROUP):
        other = lax.rem(mine + turn_by, 2 * GROUP)
        plane.append((other, (data, other // 2, lax.rem(other, 2))))
    meet([device for _, device in plane])
    started = []

    def push(source, target, device):
        slot = len(started)
        copy = remote(source, target, send_s.at[slot], recv_s.at[slot], device)
        copy.start()
        started.append(copy)

    piece = small_in.shape[2]

    def piece_of(index):
        return small_ref.at[:, pl.ds(pl.multiple_of(index * piece, 128), piece)]

    for other, device in plane:
        push(piece_of(other), small_in.at[mine], device)
    for source, target in ((own_ref, both_ref), (out_ref, both_out)):
        push(source, target.at[core], partner)
    for chip in (across, along_x, along_y):
        push(bulk.at[chip], back.at[place], (data, chip, core))
    own = pltpu.make_async_copy(bulk.at[place], back.at[place], own_sem)
    own.start()
    small_in[mine] = piece_of(mine)[...]
    both_ref[core] = own_ref[...]
    both_out[core] = out_ref[...]
    for copy in started:
        copy.wait()
    own.wait()
    total = small_in[0]
    for index in range(1, 2 * GROUP):
        total = total + small_in[index]
    sum_ref[...] = total


def plane_sum(small, own_rows, out_rows, bulk):
    places = 2 * GROUP
    pushes = places - 1 + 2 + 3
    shaped = jax.ShapeDtypeStruct
    piece = small.shape[1] // places
    return pl.pallas_call(
        plane_sum_kernel,
        out_shape=[
            shaped((8, piece), jnp.float32),
            shaped((2,) + own_rows.shape, own_rows.dtype),
            shaped((2,) + out_rows.shape, out_rows.dtype),
            shaped(bulk.shape, bulk.dtype),
        ],
        in_specs=vmem_specs(3) + any_specs(1),
        out_specs=vmem_specs(3) + any_specs(1),
        scratch_shapes=[
            pltpu.VMEM((places, 8, piece), jnp.float32),
            pltpu.SemaphoreType.DMA,
            pltpu.SemaphoreType.DMA((pushes,)),
            pltpu.SemaphoreType.DMA((pushes,)),
        ],
        cost_estimate=lasting(20),
        compiler_params=pltpu.CompilerParams(
            collective_id=7, has_side_effects=True, vmem_limit_bytes=VMEM_BYTES
        ),
    )(small, own_rows, out_rows, bulk)


def finish_kernel(
    piece_ref,
    bc_ref,
    bulk,
    small_all,
    bc_all,
    back,
    bc_send,
    bc_in,
    bc_line,
    line_in,
    own_sem,
    send_s,
    recv_s,
):
    data, place, core, along_x, along_y, across = plane_place()
    count = lax.axis_size("dp")
    mine = 2 * place + core
    partner = (data, place, 1 - core)
    others = (across, along_x, along_y)
    chips = [(data, chip, core) for chip in others]
    plane = []
    for turn_by in range(1, 2 * GROUP):
        other = lax.rem(mine + turn_by, 2 * GROUP)
        plane.append((data, other // 2, lax.rem(other, 2)))
    line = []
    for turn_by in range(1, count):
        other = lax.rem(data + turn_by, count)
        line.append((other, (other, place, core)))
    meet(plane + [device for _, device in line])
    started = []

    def push(source, target, device):
        slot = len(started)
        copy = remote(source, target, send_s.at[slot], recv_s.at[slot], device)
        copy.start()
        started.append(copy)
        return copy

    rows = bc_in.shape[1]

    def rows_of(index):
        return bc_send.at[pl.ds(pl.multiple_of(index * rows, 16), rows)]

    bc_send[...] = bc_ref[...].astype(jnp.bfloat16)
    first = [push(rows_of(other), bc_in.at[data], device) for other, device in line]
    small = [push(piece_ref, line_in.at[data], device) for _, device in line]
    late = []
    for chip, device in zip(others, chips):
        late.append(push(bulk.at[chip], back.at[place], device))
    own = pltpu.make_async_copy(bulk.at[place], back.at[place], own_sem)
    own.start()
    bc_in[data] = rows_of(data)[...]
    line_in[data] = piece_ref[...]
    for copy in first:
        copy.wait_recv()
    total = bc_in[0].astype(jnp.float32)
    for index in range(1, count):
        total = total + bc_in[index].astype(jnp.float32)
    bc_line[data] = total.astype(jnp.bfloat16)
    second = [push(bc_line.at[data], bc_line.at[data], device) for _, device in line]
    for copy in small:
        copy.wait_recv()
    total = line_in[0]
    for index in range(1, count):
        total = total + line_in[index]
    small_all[mine] = total
    late += [push(small_all.at[mine], small_all.at[mine], device) for device in plane]
    for copy in second:
        copy.wait_recv()
    half = count // 2

    def half_of(chip, at):
        return bc_all.at[2 * chip + core, pl.ds(at * half, half)]

    def send_half(chip, at, device):
        held = half_of(chip, at)
        return push(held, held, device)

    to_x, to_y = (data, along_x, core), (data, along_y, core)
    bc_all[mine] = bc_line[...]
    x_first = send_half(place, 0, to_x)
    y_second = send_half(place, 1, to_y)
    x_second = send_half(place, 1, to_x)
    y_first = send_half(place, 0, to_y)
    late.append(push(bc_all.at[mine], bc_all.at[mine], partner))
    x_first.wait_recv()
    over_y = send_half(along_x, 0, to_y)
    y_second.wait_recv()
    over_x = send_half(along_y, 1, to_x)
    for copies, chip in (((x_second,), along_x), ((y_first,), along_y), ((over_x, over_y), across)):
        for copy in copies:
            copy.wait_recv()
        held = bc_all.at[2 * chip + core]
        late.append(push(held, held, partner))
    for copy in late:
        copy.wait_recv()
    for copy in started:
        copy.wait_send()
    own.wait()


def finish_all(piece, bc_sum, bulk):
    count = lax.axis_size("dp")
    places = 2 * GROUP
    pushes = 3 * (count - 1) + (places - 1) + (GROUP - 1) + 6 + GROUP
    shaped = jax.ShapeDtypeStruct
    blocks = (count, bc_sum.shape[0] // count, bc_sum.shape[1])
    return pl.pallas_call(
        finish_kernel,
        out_shape=[
            shaped((places,) + piece.shape, jnp.float32),
            shaped((places,) + blocks, jnp.bfloat16),
            shaped(bulk.shape, bulk.dtype),
        ],
        in_specs=vmem_specs(2) + any_specs(1),
        out_specs=vmem_specs(2) + any_specs(1),
        scratch_shapes=[
            pltpu.VMEM(bc_sum.shape, jnp.bfloat16),
            pltpu.VMEM(blocks, jnp.bfloat16),
            pltpu.VMEM(blocks, jnp.bfloat16),
            pltpu.VMEM((count,) + piece.shape, jnp.float32),
            pltpu.SemaphoreType.DMA,
            pltpu.SemaphoreType.DMA((pushes,)),
            pltpu.SemaphoreType.DMA((pushes,)),
        ],
        cost_estimate=lasting(30),
        compiler_params=pltpu.CompilerParams(
            collective_id=6, has_side_effects=True, vmem_limit_bytes=VMEM_BYTES
        ),
    )(piece, bc_sum, bulk)


def unpack_early_kernel(
    gu_ref,
    down_ref,
    out_ref,
    both_ref,
    both_out,
    gate_ref,
    up_ref,
    d_ref,
    mo_ref,
    ao_ref,
    input_ref,
    output_ref,
):
    units, width = down_ref.shape[2], HEADS * HP
    input_ref[...] = both_ref[0]
    output_ref[...] = both_out[0]
    gate_ref[...] = gu_ref[0, :, :units].astype(jnp.float32)
    up_ref[...] = gu_ref[0, :, units:].astype(jnp.float32)
    d_ref[...] = down_ref[0].astype(jnp.float32).T
    turned = out_ref[0].astype(jnp.float32).T
    mo_ref[...] = turned[:width]
    ao_ref[...] = turned[width:]


def unpack_kernel(
    in_ref,
    bc_ref,
    misc_ref,
    pieces_ref,
    z_ref,
    x_ref,
    q_ref,
    grad_bc_ref,
    k_ref,
    v_ref,
    dt_ref,
    conv_ref,
    bias_ref,
    dtb_ref,
    alog_ref,
    skip_ref,
    group_ref,
    one_ref,
    two_ref,
    sums_ref,
):
    width, part = HEADS * HP, HD // 4
    z_ref[...] = in_ref[0, :, :width].astype(jnp.float32)
    q_ref[...] = in_ref[0, :, width : width + HD].astype(jnp.float32)
    x_ref[...] = in_ref[0, :, width + HD : 2 * width + HD].astype(jnp.float32)
    wide = bc_ref.shape[2]
    for core in range(2):
        grad_bc_ref[wide * core : wide * (core + 1)] = bc_ref[core].astype(jnp.float32).T

    @pl.when(pl.program_id(0) == 0)
    def _():
        for index in range(2 * GROUP):
            piece = pieces_ref.shape[2]
            sums_ref[:, piece * index : piece * (index + 1)] = pieces_ref[index]
        held = [misc_ref[chip].astype(jnp.float32) for chip in range(GROUP)]
        k_ref[...] = jnp.concatenate(
            [
                held[0][:, :part],
                held[1][:, :part],
                held[0][:, part : 2 * part],
                held[1][:, part : 2 * part],
            ],
            axis=1,
        )
        v_ref[...] = jnp.concatenate([held[2][:, : 2 * part], held[3][:, : 2 * part]], axis=1)
        dt_ref[...] = jnp.concatenate(
            [values[:, DT_LANE : DT_LANE + HEADS] for values in held], axis=1
        ).T
        taps = bias_ref.shape[1]
        conv_ref[...] = sums_ref[:KC, :taps]
        bias_ref[...] = sums_ref[KC : KC + 1, :taps]
        dtb_ref[...] = sums_ref[0:1, taps : taps + MH]
        alog_ref[...] = sums_ref[1:2, taps : taps + MH]
        skip_ref[...] = sums_ref[2:3, taps : taps + MH]
        start = taps + 128
        mine = GROUP * lax.axis_index("dp") + lax.axis_index("seq")
        slice_rows = one_ref.shape[1]
        each = slice_rows * GROUP * lax.axis_size("dp") // 8
        for ref in (one_ref, two_ref):
            gains = sums_ref[:, start : start + each]
            row = lax.broadcasted_iota(jnp.int32, (8, 1), 0)
            total = jnp.zeros((1, slice_rows), jnp.float32)
            for at in range(each // slice_rows):
                block = gains[:, slice_rows * at : slice_rows * (at + 1)]
                wanted = row * (each // slice_rows) + at == mine
                total = total + jnp.sum(jnp.where(wanted, block, 0.0), axis=0, keepdims=True)
            ref[...] = total
            start += each
        per_row = MH // 8
        for head in range(MH):
            row, lane = head // per_row, start + HP * (head % per_row)
            group_ref[head : head + 1, :] = sums_ref[row : row + 1, lane : lane + HP]


def across_chips(shape):
    return pl.BlockSpec((shape[0], shape[1] // GROUP), lambda chip: (0, chip))


def along_chips(shape):
    return pl.BlockSpec((shape[0] // GROUP, shape[1]), lambda chip: (chip, 0))


def per_chip(array, rows=1):
    return pl.BlockSpec((rows,) + array.shape[1:], lambda chip: (chip, 0, 0))


def unpack_early(gu, down, out, both, shapes):
    rows, width = both[0].shape[1:]
    step = 2 * rows // GROUP
    rows_in = pl.BlockSpec((1, step, width), lambda chip: (chip // 2, lax.rem(chip, 2), 0))
    kinds = [across_chips, across_chips, along_chips, along_chips, along_chips]
    out_shape = [jax.ShapeDtypeStruct(shape, jnp.float32) for shape in shapes]
    out_shape += [jax.ShapeDtypeStruct((2 * rows, width), array.dtype) for array in both]
    return pl.pallas_call(
        unpack_early_kernel,
        grid=(GROUP,),
        in_specs=[per_chip(gu), per_chip(down), per_chip(out), rows_in, rows_in],
        out_specs=[kind(shape) for kind, shape in zip(kinds, shapes)]
        + [along_chips((2 * rows, width))] * 2,
        out_shape=out_shape,
        cost_estimate=lasting(6),
        compiler_params=pltpu.CompilerParams(vmem_limit_bytes=VMEM_BYTES),
    )(gu, down, out, *both)


def unpack_late(in_all, bc_all, sums, shapes):
    def once(shape):
        return pl.BlockSpec(shape, lambda chip: (0,) * len(shape))

    misc_block = (GROUP, in_all.shape[1], HD)
    kinds = [across_chips] * 4
    kinds += [once] * (len(shapes) - len(kinds))
    return pl.pallas_call(
        unpack_kernel,
        grid=(GROUP,),
        in_specs=[
            per_chip(in_all),
            per_chip(bc_all, 2),
            pl.BlockSpec(misc_block, lambda chip: (0, 0, in_all.shape[2] // HD - 1)),
            once(sums.shape),
        ],
        out_specs=[kind(shape) for kind, shape in zip(kinds, shapes)],
        out_shape=[jax.ShapeDtypeStruct(shape, jnp.float32) for shape in shapes],
        scratch_shapes=[pltpu.VMEM((8, 2 * GROUP * sums.shape[2]), jnp.float32)],
        cost_estimate=lasting(6),
        compiler_params=pltpu.CompilerParams(vmem_limit_bytes=VMEM_BYTES),
    )(in_all, bc_all, in_all, sums)


def push_moves(moves, sources, targets, local_sems, send_sems, recv_sems, first=0):
    data, place, core, along_x, along_y, across = plane_place()
    copies = []
    for index, chip in enumerate((across, along_x, along_y)):
        for at, move in enumerate(moves):
            source, target = move(sources, targets, place, chip)
            slot = first + index * len(moves) + at
            copy = remote(
                source, target, send_sems.at[slot], recv_sems.at[slot], (data, chip, core)
            )
            copy.start()
            copies.append(copy)
    for at, move in enumerate(moves):
        source, target = move(sources, targets, place, place)
        copy = pltpu.make_async_copy(source, target, local_sems.at[at])
        copy.start()
        copies.append(copy)
    return copies


def plane_peers():
    data, place, core, along_x, along_y, across = plane_place()
    return [(data, chip, core) for chip in (across, along_x, along_y)]


def exchange_kernel(moves, count_in, *refs):
    sources, targets = refs[:count_in], refs[count_in:-3]
    meet(plane_peers())
    for copy in push_moves(moves, sources, targets, *refs[-3:]):
        copy.wait()


def first_exchange_kernel(
    moves,
    z_ref,
    q_ref,
    x_ref,
    key_ref,
    value_ref,
    dt_ref,
    one_ref,
    two_ref,
    in_ref,
    gains_ref,
    misc,
    gains,
    local_sems,
    send_sems,
    recv_sems,
):
    data, place, core, along_x, along_y, across = plane_place()
    places = GROUP * lax.axis_size("dp")
    mine = GROUP * data + place
    devices = []
    for turn_by in range(1, places):
        other = lax.rem(mine + turn_by, places)
        devices.append((other // GROUP, lax.rem(other, GROUP), core))
    meet(devices)
    half, part = HD // 2, HD // 4
    keys, values = key_ref[...], value_ref[...]
    steps = dt_ref[...].astype(jnp.float32).T.astype(keys.dtype)
    columns = (
        (keys[:, :part], keys[:, half : half + part]),
        (keys[:, part:half], keys[:, half + part :]),
        (values[:, :half],),
        (values[:, half:],),
    )
    for chip in range(GROUP):
        heads = steps[:, HEADS * chip : HEADS * (chip + 1)]
        rest = jnp.zeros((keys.shape[0], half - HEADS), keys.dtype)
        misc[chip] = jnp.concatenate([*columns[chip], heads, rest], axis=1)
    gains[...] = jnp.zeros_like(gains)
    gains[0:1] = one_ref[...].astype(jnp.float32)
    gains[1:2] = two_ref[...].astype(jnp.float32)
    sources = (z_ref, q_ref, x_ref, misc)
    copies = push_moves(moves, sources, (in_ref,), local_sems, send_sems, recv_sems)
    for index, device in enumerate(devices):
        slot = 3 * len(moves) + index
        copy = remote(
            gains, gains_ref.at[mine], send_sems.at[slot], recv_sems.at[slot], device
        )
        copy.start()
        copies.append(copy)
    gains_ref[mine] = gains[...]
    for copy in copies:
        copy.wait()


def first_exchange(moves, arrays, width_in):
    places = GROUP * lax.axis_size("dp")
    slice_rows = arrays[0].shape[0]
    count = 3 * len(moves) + places - 1
    return pl.pallas_call(
        partial(first_exchange_kernel, moves),
        out_shape=[
            jax.ShapeDtypeStruct((GROUP, slice_rows, width_in), jnp.bfloat16),
            jax.ShapeDtypeStruct((places, 8, slice_rows), jnp.float32),
        ],
        in_specs=any_specs(3) + vmem_specs(5),
        out_specs=any_specs(1) + vmem_specs(1),
        scratch_shapes=[
            pltpu.VMEM((GROUP, slice_rows, HD), jnp.bfloat16),
            pltpu.VMEM((8, slice_rows), jnp.float32),
            pltpu.SemaphoreType.DMA((len(moves),)),
            pltpu.SemaphoreType.DMA((count,)),
            pltpu.SemaphoreType.DMA((count,)),
        ],
        cost_estimate=lasting(20),
        compiler_params=pltpu.CompilerParams(collective_id=3, has_side_effects=True),
    )(*arrays)


def exchange_plane(moves, arrays, out_shapes, identity):
    count = 3 * len(moves)
    return pl.pallas_call(
        partial(exchange_kernel, moves, len(arrays)),
        out_shape=[jax.ShapeDtypeStruct(shape, jnp.bfloat16) for shape in out_shapes],
        in_specs=any_specs(len(arrays)),
        out_specs=any_specs(len(out_shapes)),
        scratch_shapes=[
            pltpu.SemaphoreType.DMA((len(moves),)),
            pltpu.SemaphoreType.DMA((count,)),
            pltpu.SemaphoreType.DMA((count,)),
        ],
        cost_estimate=lasting(25),
        compiler_params=pltpu.CompilerParams(collective_id=identity, has_side_effects=True),
    )(*arrays)


def column_move(source, target, start, width):
    def move(sources, targets, place, chip):
        columns = pl.ds(pl.multiple_of(chip * width, 128), width)
        return (
            sources[source].at[:, columns],
            targets[target].at[place, :, pl.ds(start, width)],
        )

    return move


def block_move(source, target):
    def move(sources, targets, place, chip):
        return (sources[source].at[chip], targets[target].at[place])

    return move


def misc_move(source, target, start):
    def move(sources, targets, place, chip):
        return (
            sources[source].at[chip],
            targets[target].at[place, :, pl.ds(start, 128)],
        )

    return move


def lane_masks():
    lane = lax.broadcasted_iota(jnp.int32, (1, 2 * HP), 1)
    return (lane < HP, lane >= HP)


DT_LANE = HP


def at_lane(lane, values):
    row = lax.broadcasted_iota(jnp.int32, (1, 2 * HP), 1)
    return jnp.where(row == lane, values, 0.0)


def dot_beside(exact, values, left_dim):
    width = values.shape[1]
    both = dot_f32(exact, jnp.concatenate(halves(values), axis=1), left_dim, 0)
    return both[:, :width] + both[:, width:]


def dot_along(left, right):
    left_high, left_low = halves(left)
    right_high, right_low = halves(right)
    return dot_f32(
        jnp.concatenate([left_high, left_high, left_low], axis=1),
        jnp.concatenate([right_high, right_low, right_high], axis=1),
        1,
        1,
    )


def spread_heads(*columns):
    width = HEADS * HP
    row = lax.rem(lax.broadcasted_iota(jnp.int32, (4 * HP, width), 0), 2 * HP)
    head = lax.broadcasted_iota(jnp.int32, (4 * HP, width), 1) // HP
    pick = jnp.where(row == DT_LANE + head, 1.0, 0.0).astype(jnp.bfloat16)
    parts = [jnp.concatenate(halves(values), axis=1) for values in columns]
    wide = dot_f32(jnp.concatenate(parts, axis=0), pick, 1, 0)
    size = columns[0].shape[0]
    return [wide[size * at : size * (at + 1)] for at in range(len(columns))]


def wide_keeps(keeps_ref):
    size = keeps_ref.shape[0]
    return [None] + [
        jnp.broadcast_to(keeps_ref[:, 1 + back : 2 + back], (size, 2 * HP))
        for back in range(1, KC)
    ]


def head_sums(values):
    low, high = lane_masks()
    first = jnp.sum(jnp.where(low, values, 0.0), axis=1, keepdims=True)
    second = jnp.sum(jnp.where(high, values, 0.0), axis=1, keepdims=True)
    return (first, second)


def head_means(values):
    low, high = lane_masks()
    first, second = head_sums(values)
    return jnp.where(low, first, second) * (1.0 / HP)


def stack_heads(values):
    low, high = lane_masks()
    zero = jnp.zeros_like(values)
    return jnp.concatenate([jnp.where(low, values, zero), jnp.where(high, values, zero)], axis=0)


def order_in(size):
    row = lax.broadcasted_iota(jnp.int32, (size, size), 0)
    column = lax.broadcasted_iota(jnp.int32, (size, size), 1)
    return (row, column)


def exact_sum(ones, values):
    high = values.astype(jnp.bfloat16)
    rest = values - high.astype(jnp.float32)
    middle = rest.astype(jnp.bfloat16)
    low = (rest - middle.astype(jnp.float32)).astype(jnp.bfloat16)
    return dot_f32(ones, high, 1, 0) + (dot_f32(ones, middle, 1, 0) + dot_f32(ones, low, 1, 0))


def chunk_decays(proj_ref, heads_ref, keeps_ref):
    size, width = proj_ref.shape
    raw = proj_ref[:, width - 2 * HP :] + heads_ref[0:1]
    dt_rows = jnp.maximum(raw, 0.0) + jnp.log1p(jnp.exp(-jnp.abs(raw)))
    row, column = order_in(size)
    lower = jnp.where(row >= column, 1.0, 0.0).astype(jnp.bfloat16)
    cumul = exact_sum(lower, -heads_ref[1:2] * dt_rows)
    enter = jnp.exp(cumul) * keeps_ref[:, 0:1]
    leave_bare = jnp.exp(cumul[size - 1 :] - cumul) * keeps_ref[:, 1:2]
    return (raw, dt_rows, cumul, enter, leave_bare)


def conv_windows(block, proj_ref, before_ref, bc_ref, bc_before_ref):
    if block < HEADS // 2:
        start = proj_ref.shape[1] - 2 * HP * (1 + HEADS // 2 - block)
        lanes = slice(start, start + 2 * HP)
        now, before = proj_ref[:, lanes], before_ref[:, lanes]
        now, before = now.astype(jnp.bfloat16), before.astype(jnp.bfloat16)
    else:
        start = 2 * HP * (block - HEADS // 2)
        lanes = slice(start, start + 2 * HP)
        now, before = bc_ref[:, lanes], bc_before_ref[8:, lanes]
    now, before = now.astype(jnp.float32), before.astype(jnp.float32)
    size = now.shape[0]
    extended = jnp.concatenate([before, now], axis=0)
    return [now] + [extended[8 - back : 8 - back + size] for back in range(1, KC)]


def conv_sum(windows, taps_ref, lanes, keeps):
    total = taps_ref[KC : KC + 1, lanes] + taps_ref[KC - 1 : KC, lanes] * windows[0]
    for back in range(1, KC):
        total = total + taps_ref[KC - 1 - back : KC - back, lanes] * (
            windows[back] * keeps[back]
        )
    return total


def head_decay(allowed, cumul, cumul_t, head):
    lane = DT_LANE + head
    differ = cumul[:, lane : lane + 1] - cumul_t[lane : lane + 1, :]
    return jnp.exp(jnp.where(allowed, differ, -jnp.inf))


def ssd_forward_kernel(
    proj_ref,
    before_ref,
    bc_ref,
    bc_before_ref,
    taps_ref,
    heads_ref,
    keeps_ref,
    segc_ref,
    segr_ref,
    skip_ref,
    gain_ref,
    cos_ref,
    sin_ref,
    gated_ref,
    ssm_ref,
    states_ref,
    mixed_ref,
    slope_ref,
    kv_ref,
    state,
):
    @pl.when(pl.program_id(0) == 0)
    def _():
        state[...] = jnp.zeros_like(state)

    size = proj_ref.shape[0]
    width = HEADS * HP
    keeps = wide_keeps(keeps_ref)
    for block in range(mixed_ref.shape[1] // (2 * HP)):
        lanes = slice(2 * HP * block, 2 * HP * (block + 1))
        windows = conv_windows(block, proj_ref, before_ref, bc_ref, bc_before_ref)
        summed = conv_sum(windows, taps_ref, lanes, keeps)
        sigmoid = jax.nn.sigmoid(summed)
        mixed_ref[:, lanes] = (summed * sigmoid).astype(jnp.bfloat16)
        slope_ref[:, lanes] = sigmoid * (1.0 + summed * (1.0 - sigmoid))
    raw, dt_rows, cumul, enter_all, leave_bare = chunk_decays(proj_ref, heads_ref, keeps_ref)
    enter_all, leave_all = spread_heads(enter_all, leave_bare * dt_rows)
    cumul_t, dt_t = cumul.T, dt_rows.T
    entry = state[...]
    states_ref[0] = entry
    b_rows, c_rows = mixed_ref[:, width : width + NS], mixed_ref[:, width + NS :]
    gram = dot_f32(c_rows, b_rows, 1, 1)
    row, column = order_in(size)
    allowed = (segc_ref[...] == segr_ref[0]) & (row >= column)
    entered = dot_beside(c_rows, entry, 1)
    weighted = []
    for pair in range(HEADS // 2):
        lanes = slice(2 * HP * pair, 2 * HP * (pair + 1))
        heads_x = mixed_ref[:, lanes]
        mixing = []
        for head in (2 * pair, 2 * pair + 1):
            lane = DT_LANE + head
            decay = head_decay(allowed, cumul, cumul_t, head)
            mixing.append(gram * decay * dt_t[lane : lane + 1, :])
        stacked = stack_heads(heads_x)
        out = dot_f32(
            jnp.concatenate(halves(jnp.concatenate(mixing, axis=1)), axis=1),
            jnp.concatenate([stacked, stacked], axis=0),
            1,
            0,
        )
        wide_x = heads_x.astype(jnp.float32)
        enter = enter_all[:, lanes]
        out = out + enter * entered[:, lanes] + skip_ref[:, lanes] * wide_x
        ssm_ref[:, lanes] = out
        gate = proj_ref[:, lanes]
        value = out * (gate * jax.nn.sigmoid(gate))
        scale = lax.rsqrt(head_means(value * value) + GROUP_EPSILON)
        gated_ref[:, lanes] = (value * scale * gain_ref[:, lanes]).astype(jnp.bfloat16)
        weighted.append(leave_all[:, lanes] * wide_x)
        state[:, lanes] = enter[size - 1 :, :] * entry[:, lanes]
    state[...] += dot_beside(b_rows, jnp.concatenate(weighted, axis=1), 0)
    kv = proj_ref[:, proj_ref.shape[1] - 2 * HP :][:, :HP]
    kv = jnp.concatenate([kv[: size // 2], kv[size // 2 :]], axis=1)
    kv_ref[...] = turn_folded(kv, cos_ref[...], sin_ref[...]).astype(jnp.bfloat16)


def ssd_backward_kernel(
    moves,
    proj_ref,
    slope_ref,
    bc_ref,
    taps_ref,
    heads_ref,
    keeps_ref,
    segc_ref,
    segr_ref,
    skip_ref,
    gain_ref,
    mixed_ref,
    ssm_ref,
    states_ref,
    dgated_ref,
    dq_ref,
    kv_own_ref,
    kv_x_ref,
    kv_y_ref,
    kv_a_ref,
    cos_ref,
    sin_ref,
    gu_ref,
    down_ref,
    dproj_ref,
    dtaps_ref,
    dheads_ref,
    dskip_ref,
    dgain_ref,
    gu_back,
    down_back,
    state,
    d_mixed,
    next_rows,
    *sems,
):
    def transfers(act):
        data, place, core, along_x, along_y, across = plane_place()
        sources, targets = (gu_ref, down_ref), (gu_back, down_back)
        local_sems, send_sems, recv_sems = sems
        for index, chip in enumerate((across, along_x, along_y)):
            for at, move in enumerate(moves):
                source, target = move(sources, targets, place, chip)
                slot = index * len(moves) + at
                act(
                    remote(
                        source, target, send_sems.at[slot], recv_sems.at[slot], (data, chip, core)
                    )
                )
        for at, move in enumerate(moves):
            source, target = move(sources, targets, place, place)
            act(pltpu.make_async_copy(source, target, local_sems.at[at]))

    @pl.when(pl.program_id(0) == 0)
    def _():
        meet(plane_peers())
        transfers(lambda copy: copy.start())
        state[...] = jnp.zeros_like(state)
        next_rows[...] = jnp.zeros_like(next_rows)
        dtaps_ref[...] = jnp.zeros_like(dtaps_ref)
        dheads_ref[...] = jnp.zeros_like(dheads_ref)
        dskip_ref[...] = jnp.zeros_like(dskip_ref)
        dgain_ref[...] = jnp.zeros_like(dgain_ref)

    size = proj_ref.shape[0]
    width = HEADS * HP
    raw, dt_rows, cumul, enter_all, leave_bare = chunk_decays(proj_ref, heads_ref, keeps_ref)
    cumul_t, dt_t = cumul.T, dt_rows.T
    later = state[...]
    entry = states_ref[0]
    carried = jnp.sum(later * entry, axis=0, keepdims=True)
    b_rows, c_rows = mixed_ref[:, width : width + NS], mixed_ref[:, width + NS :]
    gram = dot_f32(c_rows, b_rows, 1, 1)
    row, column = order_in(size)
    allowed = (segc_ref[...] == segr_ref[0]) & (row >= column)
    d_weighted = dot_beside(b_rows, later, 1)
    enter_all, bare_all, dt_all = spread_heads(enter_all, leave_bare, dt_rows)
    d_gram = jnp.zeros((size, size), jnp.float32)
    row_sums = jnp.zeros((size, 2 * HP), jnp.float32)
    column_sums = jnp.zeros((size, 2 * HP), jnp.float32)
    at_last = jnp.zeros((1, 2 * HP), jnp.float32)
    d_entered, weighted = [], []
    for pair in range(HEADS // 2):
        lanes = slice(2 * HP * pair, 2 * HP * (pair + 1))
        heads_x = mixed_ref[:, lanes]
        wide_x = heads_x.astype(jnp.float32)
        ssm, gate, gain = ssm_ref[:, lanes], proj_ref[:, lanes], gain_ref[:, lanes]
        d_gated = dgated_ref[:, lanes]
        sigmoid = jax.nn.sigmoid(gate)
        silu = gate * sigmoid
        value = ssm * silu
        scale = lax.rsqrt(head_means(value * value) + GROUP_EPSILON)
        dgain_ref[:, lanes] += jnp.sum(d_gated * value * scale, axis=0, keepdims=True)
        d_scaled = d_gated * gain
        d_value = scale * d_scaled - value * (scale * scale * scale) * head_means(d_scaled * value)
        d_out = d_value * silu
        dproj_ref[:, lanes] = (d_value * ssm * (sigmoid * (1.0 + gate * (1.0 - sigmoid)))).astype(
            jnp.bfloat16
        )
        dskip_ref[:, lanes] += jnp.sum(d_out * wide_x, axis=0, keepdims=True)
        enter, bare, dt_pair = enter_all[:, lanes], bare_all[:, lanes], dt_all[:, lanes]
        high, low = [stack_heads(half) for half in halves(d_out)]
        d_mixing = dot_f32(jnp.concatenate([high, low], axis=0), heads_x, 1, 1)
        grams = []
        for side in range(2):
            head = 2 * pair + side
            lane = DT_LANE + head
            decay = head_decay(allowed, cumul, cumul_t, head)
            grams.append(gram * decay)
            first = size * side
            d_mix = d_mixing[first : first + size] + d_mixing[2 * size + first : 3 * size + first]
            d_gram = d_gram + d_mix * (decay * dt_t[lane : lane + 1, :])
        gram_high, gram_low = halves(jnp.concatenate(grams, axis=0))
        bare_x = dot_f32(
            jnp.concatenate([high, low, high], axis=0),
            jnp.concatenate([gram_high, gram_high, gram_low], axis=0),
            0,
            0,
        ).T
        left = bare * d_weighted[:, lanes]
        d_x = bare_x + left
        first_lane = DT_LANE + 2 * pair
        first, second = head_sums(d_out * (ssm - skip_ref[:, lanes] * wide_x))
        row_sums = row_sums + at_lane(first_lane, first) + at_lane(first_lane + 1, second)
        first, second = head_sums(d_x * wide_x)
        column_sums = column_sums + at_lane(first_lane, first) + at_lane(first_lane + 1, second)
        last = jnp.sum(dt_pair * left * wide_x, axis=0, keepdims=True)
        last = last + carried[:, lanes] * enter[size - 1 :]
        first, second = head_sums(last)
        at_last = at_last + at_lane(first_lane, first) + at_lane(first_lane + 1, second)
        d_mixed[:, lanes] = dt_pair * d_x + skip_ref[:, lanes] * d_out
        d_entered.append(enter * d_out)
        weighted.append(bare * dt_pair * wide_x)
        state[:, lanes] = enter[size - 1 :, :] * later[:, lanes]
    d_entered = jnp.concatenate(d_entered, axis=1)
    state[...] += dot_beside(c_rows, d_entered, 0)
    d_gram_parts = halves(d_gram)
    d_b = dot_along(jnp.concatenate(weighted, axis=1), later)
    d_mixed[:, width : width + NS] = d_b + dot_f32(
        jnp.concatenate(d_gram_parts, axis=0),
        jnp.concatenate([c_rows, c_rows], axis=0),
        0,
        0,
    )
    d_c = dot_along(d_entered, entry)
    d_mixed[:, width + NS :] = d_c + dot_f32(
        jnp.concatenate(d_gram_parts, axis=1),
        jnp.concatenate([b_rows, b_rows], axis=0),
        1,
        0,
    )

    d_cumul = row_sums - column_sums * dt_rows
    last_row = lax.broadcasted_iota(jnp.int32, (size, 1), 0) == size - 1
    d_cumul = d_cumul + jnp.where(last_row, at_last, 0.0)
    upper = jnp.where(row <= column, 1.0, 0.0).astype(jnp.bfloat16)
    d_log = exact_sum(upper, d_cumul)
    rate = heads_ref[1:2]
    d_raw = (column_sums - rate * d_log) * jax.nn.sigmoid(raw)
    lane_row = lax.broadcasted_iota(jnp.int32, (1, 2 * HP), 1)
    d_raw = jnp.where((lane_row >= DT_LANE) & (lane_row < DT_LANE + HEADS), d_raw, 0.0)
    dheads_ref[0:1] += jnp.sum(d_raw, axis=0, keepdims=True)
    dheads_ref[1:2] += -rate * jnp.sum(d_log * dt_rows, axis=0, keepdims=True)
    total = proj_ref.shape[1]
    d_kv = kv_own_ref[...].astype(jnp.float32)
    for ref in (kv_x_ref, kv_y_ref, kv_a_ref):
        d_kv = d_kv + ref[...].astype(jnp.float32)
    d_kv = turn_folded(d_kv, cos_ref[...], -sin_ref[...])
    d_kv = jnp.concatenate([d_kv[:, :DT_LANE], d_kv[:, DT_LANE:]], axis=0)
    dproj_ref[:, total - 2 * HP : total] = jnp.concatenate(
        [d_kv, d_raw[:, DT_LANE:]], axis=1
    ).astype(jnp.bfloat16)
    dproj_ref[:, width : width + HD] = dq_ref[...]

    keeps = wide_keeps(keeps_ref)
    for block in range(mixed_ref.shape[1] // (2 * HP)):
        lanes = slice(2 * HP * block, 2 * HP * (block + 1))
        if block < HEADS // 2:
            start = total - 2 * HP * (1 + HEADS // 2 - block)
            pre = proj_ref[:, start : start + 2 * HP].astype(jnp.bfloat16).astype(jnp.float32)
        else:
            start = 2 * HP * (block - HEADS // 2)
            pre = bc_ref[:, start : start + 2 * HP].astype(jnp.float32)
        d_sum = d_mixed[:, lanes] * slope_ref[:, lanes]
        dtaps_ref[KC : KC + 1, lanes] += jnp.sum(d_sum, axis=0, keepdims=True)
        dtaps_ref[KC - 1 : KC, lanes] += jnp.sum(d_sum * pre, axis=0, keepdims=True)
        d_pre = taps_ref[KC - 1 : KC, lanes] * d_sum
        for back in range(1, KC):
            tap = KC - 1 - back
            kept = d_sum * keeps[back]
            extended = jnp.concatenate([kept, next_rows[back - 1, :, lanes]], axis=0)
            later_rows = extended[back : back + size]
            dtaps_ref[tap : tap + 1, lanes] += jnp.sum(later_rows * pre, axis=0, keepdims=True)
            d_pre = d_pre + taps_ref[tap : tap + 1, lanes] * later_rows
            next_rows[back - 1, :, lanes] = kept[:8]
        if block < HEADS // 2:
            start = total - 2 * HP * (1 + HEADS // 2 - block)
            dproj_ref[:, start : start + 2 * HP] = d_pre.astype(jnp.bfloat16)
        else:
            start = total + 2 * HP * (block - HEADS // 2)
            dproj_ref[:, start : start + 2 * HP] = d_pre.astype(jnp.bfloat16)

    @pl.when(pl.program_id(0) == pl.num_programs(0) - 1)
    def _():
        transfers(lambda copy: copy.wait())


def ssd_specs(length, reverse, width_in, width_all, width):
    laps = length // CHUNK

    def at(lap):
        return laps - 1 - lap if reverse else lap

    def tall(columns):
        return pl.BlockSpec((CHUNK, columns), lambda lap: (at(lap), 0))

    def rim(rows, columns):
        each = CHUNK // rows
        return pl.BlockSpec((rows, columns), lambda lap: (lax.rem(each * (at(lap) + laps) - 1, each * laps), 0))

    def whole(rows, columns):
        return pl.BlockSpec((rows, columns), lambda lap: (0, 0))

    def slab(rows, columns):
        return pl.BlockSpec((1, rows, columns), lambda lap: (at(lap), 0, 0))

    specs = [
        tall(width_in),
        rim(8, width_in),
        tall(2 * NS),
        rim(16, 2 * NS),
        whole(8, width_all),
        whole(8, 2 * HP),
        tall(8),
        tall(1),
        slab(1, CHUNK),
        whole(1, width),
        whole(1, width),
    ]
    return (laps, tall, whole, slab, specs)


def ssd_forward(arrays, cos_part, sin_part):
    length, width_in = arrays[0].shape
    width, width_all = HEADS * HP, HEADS * HP + 2 * NS
    laps, tall, whole, slab, specs = ssd_specs(length, False, width_in, width_all, width)
    shaped = jax.ShapeDtypeStruct
    fold = pl.BlockSpec((CHUNK // 2, 2 * HP), lambda lap: (lap, 0))
    return pl.pallas_call(
        ssd_forward_kernel,
        grid=(laps,),
        in_specs=specs + [fold, fold],
        out_specs=[
            tall(width),
            tall(width),
            slab(NS, width),
            tall(width_all),
            tall(width_all),
            fold,
        ],
        out_shape=[
            shaped((length, width), jnp.bfloat16),
            shaped((length, width), jnp.float32),
            shaped((laps, NS, width), jnp.float32),
            shaped((length, width_all), jnp.bfloat16),
            shaped((length, width_all), jnp.float32),
            shaped((length // 2, 2 * HP), jnp.bfloat16),
        ],
        scratch_shapes=[pltpu.VMEM((NS, width), jnp.float32)],
        cost_estimate=lasting(6),
        compiler_params=pltpu.CompilerParams(vmem_limit_bytes=VMEM_BYTES),
    )(*arrays, cos_part, sin_part)


def ssd_backward(arrays, slope, mixed, ssm, states, d_outs, d_query, d_kv_parts, tables, grads):
    length, width_in = arrays[0].shape
    width, width_all = HEADS * HP, HEADS * HP + 2 * NS
    laps, tall, whole, slab, specs = ssd_specs(length, True, width_in, width_all, width)
    shaped = jax.ShapeDtypeStruct
    moves = (block_move(0, 0), block_move(1, 1))
    fold = pl.BlockSpec((CHUNK // 2, 2 * HP), lambda lap: (laps - 1 - lap, 0))
    return pl.pallas_call(
        partial(ssd_backward_kernel, moves),
        grid=(laps,),
        in_specs=[specs[0], tall(width_all), specs[2], *specs[4:]]
        + [
            tall(width_all),
            tall(width),
            slab(NS, width),
            tall(width),
            tall(HD),
        ]
        + [fold] * 6
        + any_specs(2),
        out_specs=[
            tall(width_in + 2 * NS),
            whole(8, width_all),
            whole(8, 2 * HP),
            whole(1, width),
            whole(1, width),
        ]
        + any_specs(2),
        out_shape=[
            shaped((length, width_in + 2 * NS), jnp.bfloat16),
            shaped((8, width_all), jnp.float32),
            shaped((8, 2 * HP), jnp.float32),
            shaped((1, width), jnp.float32),
            shaped((1, width), jnp.float32),
        ]
        + [shaped(array.shape, array.dtype) for array in grads],
        scratch_shapes=[
            pltpu.VMEM((NS, width), jnp.float32),
            pltpu.VMEM((CHUNK, width_all), jnp.float32),
            pltpu.VMEM((KC - 1, 8, width_all), jnp.float32),
            pltpu.SemaphoreType.DMA((len(moves),)),
            pltpu.SemaphoreType.DMA((3 * len(moves),)),
            pltpu.SemaphoreType.DMA((3 * len(moves),)),
        ],
        cost_estimate=lasting(48),
        compiler_params=pltpu.CompilerParams(
            collective_id=13, has_side_effects=True, vmem_limit_bytes=VMEM_BYTES
        ),
    )(arrays[0], slope, arrays[2], *arrays[4:], mixed, ssm, states, d_outs, d_query, *d_kv_parts, *tables, *grads)


QUERY_ROWS = 256


def masked_scores(q_rows, k_ref, segc_ref, segr_ref, start, reach):
    rows = q_rows.shape[0]
    scores = dot_f32(q_rows, k_ref[:reach], 1, 1) * HD ** (-0.5)
    row = lax.broadcasted_iota(jnp.int32, (rows, reach), 0) + start
    column = lax.broadcasted_iota(jnp.int32, (rows, reach), 1)
    allowed = (segc_ref[start : start + rows] == segr_ref[:, :reach]) & (row >= column)
    return jnp.where(allowed, scores, -jnp.inf)


def rotate_rows(values, cos_ref, sin_ref, sign):
    return values * cos_ref[...] + sign * (pltpu.roll(values, HD // 2, 1) * sin_ref[...])


def swap_middle(values):
    lane = lax.broadcasted_iota(jnp.int32, (1, HD), 1) // (HD // 4)
    up = pltpu.roll(values, HD // 4, 1)
    down = pltpu.roll(values, HD - HD // 4, 1)
    return jnp.where(lane == 1, down, jnp.where(lane == 2, up, values))


def unfold_rows(values, write):
    step, columns = CHUNK // 2, values.shape[1] // 2
    for start in range(0, values.shape[0], step):
        rows = values[start : start + step]
        write(2 * start, rows[:, :columns])
        write(2 * start + step, rows[:, columns:])


def fold_rows(ref, index, values):
    step = CHUNK // 2
    for start in range(0, values.shape[0] // 2, step):
        ref[index, start : start + step] = jnp.concatenate(
            [values[2 * start : 2 * start + step], values[2 * start + step : 2 * start + 2 * step]],
            axis=1,
        ).astype(ref.dtype)


def join_halves(ref, first, target):
    half = HD // 2

    def write_at(lanes):
        def write(start, rows):
            target[start : start + rows.shape[0], lanes] = rows

        return write

    unfold_rows(ref[first], write_at(slice(0, half)))
    unfold_rows(ref[first + 1], write_at(slice(half, HD)))


def attend_forward_kernel(
    raw_ref, cos_ref, sin_ref, kv_ref, segc_ref, segr_ref, out_ref, total_ref, q_ref, k_ref, v_ref
):
    q_ref[...] = swap_middle(rotate_rows(raw_ref[...], cos_ref, sin_ref, 1.0)).astype(jnp.bfloat16)
    join_halves(kv_ref, 0, k_ref)
    join_halves(kv_ref, 2, v_ref)
    for start in range(0, q_ref.shape[0], QUERY_ROWS):
        reach = start + QUERY_ROWS
        rows = slice(start, reach)
        scores = masked_scores(q_ref[rows], k_ref, segc_ref, segr_ref, start, reach)
        top = jnp.max(scores, axis=1, keepdims=True)
        powers = jnp.exp(scores - top)
        total = jnp.sum(powers, axis=1, keepdims=True)
        probs = (powers * (1.0 / total)).astype(jnp.bfloat16)
        out_ref[rows] = dot_f32(probs, v_ref[:reach], 1, 0).astype(jnp.bfloat16)
        total_ref[rows] = top + jnp.log(total)


def attend_backward_kernel(
    q_ref,
    k_ref,
    v_ref,
    cos_ref,
    sin_ref,
    segc_ref,
    segr_ref,
    total_ref,
    dout_ref,
    dq_ref,
    dkv_ref,
    dq_sum,
    dk_sum,
    dv_sum,
):
    dk_sum[...] = jnp.zeros_like(dk_sum)
    dv_sum[...] = jnp.zeros_like(dv_sum)
    for start in range(0, q_ref.shape[0], QUERY_ROWS):
        reach = start + QUERY_ROWS
        rows = slice(start, reach)
        q_rows, d_out = q_ref[rows], dout_ref[rows]
        scores = masked_scores(q_rows, k_ref, segc_ref, segr_ref, start, reach)
        probs = jnp.exp(scores - total_ref[rows])
        d_probs = dot_f32(d_out, v_ref[:reach], 1, 1)
        delta = jnp.sum(probs * d_probs, axis=1, keepdims=True)
        d_scores = (probs * (d_probs - delta)).astype(jnp.bfloat16)
        dq_sum[rows] = dot_f32(d_scores, k_ref[:reach], 1, 0) * HD ** (-0.5)
        dk_sum[:reach] += dot_f32(d_scores, q_rows, 0, 0) * HD ** (-0.5)
        dv_sum[:reach] += dot_f32(probs.astype(jnp.bfloat16), d_out, 0, 0)
    dq_ref[...] = rotate_rows(swap_middle(dq_sum[...]), cos_ref, sin_ref, -1.0).astype(jnp.bfloat16)
    half = HD // 2
    fold_rows(dkv_ref, 0, dk_sum[:, :half])
    fold_rows(dkv_ref, 1, dk_sum[:, half:])
    fold_rows(dkv_ref, 2, dv_sum[:, :half])
    fold_rows(dkv_ref, 3, dv_sum[:, half:])


def rotation_tables(length):
    half, part = HD // 2, HD // 4
    frequency = np.float32(ROPE_BASE) ** (
        np.float32(-2.0) * np.arange(half).astype(np.float32) / np.float32(HD)
    )
    angles = np.arange(length).astype(np.float32)[:, None] * frequency[None, :]
    cosine, sine_part = np.cos(angles), np.sin(angles)

    def folded(values):
        rows = values.reshape(length // CHUNK, 2, CHUNK // 2, half)
        return rows.transpose(0, 2, 1, 3).reshape(length // 2, HD)

    cos_kinds, sin_kinds = [], []
    for start in (0, part):
        columns = slice(start, start + part)
        cos_part, sin_part = cosine[:, columns], sine_part[:, columns]
        cos_kinds.append(folded(np.concatenate([cos_part, cos_part], axis=1)))
        sin_kinds.append(folded(np.concatenate([-sin_part, sin_part], axis=1)))
    cos_kinds.append(np.ones_like(cos_kinds[0]))
    sin_kinds.append(np.zeros_like(sin_kinds[0]))
    tables = (
        np.concatenate([cosine, cosine], axis=1),
        np.concatenate([-sine_part, sine_part], axis=1),
        np.stack(cos_kinds),
        np.stack(sin_kinds),
    )
    return [jnp.asarray(table.astype(np.float32)) for table in tables]


def turn_folded(values, cosine, sine_part):
    lane = lax.rem(lax.broadcasted_iota(jnp.int32, (1, HD), 1), HD // 2)
    quarter = HD // 4
    other = jnp.where(
        lane < quarter, pltpu.roll(values, HD - quarter, 1), pltpu.roll(values, quarter, 1)
    )
    return values * cosine + other * sine_part


def whole_block(shape):
    return pl.BlockSpec(shape, lambda step: (0,) * len(shape))


def attend(kernel, arrays, out_shapes, scratch=(), blocks=None):
    return pl.pallas_call(
        kernel,
        grid=(1,),
        in_specs=[
            whole_block(array.shape) if blocks is None or blocks[at] is None else blocks[at]
            for at, array in enumerate(arrays)
        ],
        out_specs=[whole_block(shape) for shape, _ in out_shapes],
        out_shape=[jax.ShapeDtypeStruct(shape, dtype) for shape, dtype in out_shapes],
        scratch_shapes=[pltpu.VMEM(shape, dtype) for shape, dtype in scratch],
        cost_estimate=lasting(9),
        compiler_params=pltpu.CompilerParams(vmem_limit_bytes=VMEM_BYTES),
    )(*arrays)


def after(value, *earlier):
    return lax.optimization_barrier((value,) + earlier)[0]


def over_chips(block):
    place = lax.axis_index("seq")
    count = lax.axis_size("seq")
    stacked = jnp.zeros((count,) + block.shape, block.dtype)
    stacked = lax.dynamic_update_index_in_dim(stacked, block, place, 0)
    for mask in range(1, count):
        moved = lax.ppermute(block, "seq", [(i, i ^ mask) for i in range(count)])
        stacked = lax.dynamic_update_index_in_dim(stacked, moved, place ^ mask, 0)
    return stacked


def from_chips(blocks):
    place = lax.axis_index("seq")
    count = lax.axis_size("seq")
    moved = [lax.dynamic_index_in_dim(blocks, place, 0, False)]
    for mask in range(1, count):
        block = lax.dynamic_index_in_dim(blocks, place ^ mask, 0, False)
        moved.append(lax.ppermute(block, "seq", [(i, i ^ mask) for i in range(count)]))
    return moved


def heads_local_plan(
    hidden_in,
    teacher,
    segment_ids,
    valid_mask,
    norm1_gain,
    w_z,
    w_x,
    w_bc,
    w_dt,
    conv_weight,
    conv_bias,
    dt_bias,
    a_log,
    d_skip,
    group_gain,
    w_mamba_out,
    w_query,
    w_key,
    w_value,
    w_attn_out,
    norm2_gain,
    w_gate,
    w_up,
    w_down,
):
    place, core, data_rank = (
        lax.axis_index("seq"),
        lax.axis_index("tensor"),
        lax.axis_index("dp"),
    )
    data_count = lax.axis_size("dp")
    chip_rows, width = hidden_in.shape[1:]
    own_rows = chip_rows // 2
    length = segment_ids.shape[1]
    slice_rows = w_z.shape[0]
    width_x = HEADS * HP
    hidden_units = w_gate.shape[1] // GROUP
    segment = segment_ids[0]
    own_start = place * chip_rows + core * own_rows
    token_count = jnp.sum(valid_mask).astype(jnp.float32)
    mask_rows = lax.dynamic_slice(valid_mask, (data_rank, own_start), (1, own_rows))[0]
    total_tokens = float(valid_mask.shape[0] * valid_mask.shape[1])
    bf16 = jnp.bfloat16

    half, part = HD // 2, HD // 4
    width_in = 2 * width_x + 2 * HD
    in_slices, gains_all = first_exchange(
        (
            column_move(0, 0, 0, width_x),
            column_move(1, 0, width_x, HD),
            column_move(2, 0, width_x + HD, width_x),
            misc_move(3, 0, 2 * width_x + HD),
        ),
        (w_z, w_query, w_x, w_key, w_value, w_dt.T, norm1_gain[None], norm2_gain[None]),
        width_in,
    )
    gain_one, gain_two = gains_all[:, 0].reshape(width), gains_all[:, 1].reshape(width)
    full_in = lax.all_gather(in_slices, "dp", axis=0, tiled=True).reshape(width, width_in)
    hidden_own = lax.dynamic_slice(hidden_in[0], (core * own_rows, 0), (own_rows, width))
    hidden_own = after(hidden_own, in_slices)
    hidden_all, normed, pre_bc = gather_plane(
        hidden_own,
        1,
        apply_norm,
        (gain_one[None], w_bc),
        (((length, width), bf16), ((length, 2 * NS), bf16)),
    )
    hidden_low, hidden_own = hidden_own, hidden_own.astype(jnp.float32)
    width_out = width_x + HD
    out_slices, gu_slices, down_slices = exchange_plane(
        (
            column_move(0, 0, 0, width_x),
            column_move(1, 0, width_x, HD),
            column_move(2, 1, 0, hidden_units),
            column_move(3, 1, hidden_units, hidden_units),
            column_move(4, 2, 0, hidden_units),
        ),
        (after(w_mamba_out.T, normed), w_attn_out.T, w_gate, w_up, w_down.T),
        [
            (GROUP, slice_rows, width_out),
            (GROUP, slice_rows, 2 * hidden_units),
            (GROUP, slice_rows, hidden_units),
        ],
        4,
    )
    out_gathered = lax.all_gather(after(out_slices, full_in), "dp", axis=0, tiled=True)
    full_out = out_gathered.reshape(width, width_out)

    segment, conv_weight, conv_bias, dt_bias, a_log, d_skip, group_gain = (
        lax.optimization_barrier(
            (segment, conv_weight, conv_bias, dt_bias, a_log, d_skip, group_gain, out_slices)
        )[:7]
    )
    seg_column, seg_row = segment[:, None], segment[None, :]
    cos_wide, sin_wide, cos_folded, sin_folded = rotation_tables(length)
    kind = jnp.minimum(place, 2)
    cos_folded = lax.dynamic_index_in_dim(cos_folded, kind, 0, False)
    sin_folded = lax.dynamic_index_in_dim(sin_folded, kind, 0, False)
    head_start = core * (MH // 2) + place * HEADS

    def local_rows(values, width_head):
        return jnp.concatenate(
            [
                lax.dynamic_slice_in_dim(values, head_start * width_head, HEADS * width_head, 0),
                values[MH * width_head :],
            ],
            axis=0,
        )

    taps = jnp.concatenate(
        [local_rows(conv_weight, HP).T, local_rows(conv_bias, HP)[None]], axis=0
    )
    taps = jnp.pad(taps, ((0, 8 - KC - 1), (0, 0)))
    rate = jnp.exp(local_rows(a_log, 1))
    head_rows = jnp.stack([local_rows(dt_bias, 1), rate])
    head_rows = jnp.pad(head_rows, ((0, 6), (DT_LANE, HD - DT_LANE - HEADS)))
    skip_row = jnp.repeat(local_rows(d_skip, 1), HP)[None, :]
    gain_row = lax.dynamic_slice_in_dim(group_gain, head_start, HEADS, 0).reshape(1, width_x)
    laps = length // CHUNK
    seg_laps = segment.reshape(laps, CHUNK)
    seg_last = seg_laps[:, -1:]
    seg_before = jnp.concatenate([jnp.full((1, 1), -1, jnp.int32), seg_last[:-1]])
    seg_ext = jnp.concatenate([jnp.full((KC - 1,), -1, jnp.int32), segment])
    keeps = [(seg_laps == seg_before).reshape(length), (seg_laps == seg_last).reshape(length)]
    keeps += [seg_ext[KC - 1 - back : KC - 1 - back + length] == segment for back in range(1, KC)]
    keeps = jnp.stack(keeps + [jnp.zeros((length,), bool)] * 3, axis=1).astype(jnp.float32)

    projected = mat_dot(normed, full_in)

    ssd_arrays = (
        projected,
        projected,
        pre_bc,
        pre_bc,
        taps,
        head_rows,
        keeps,
        seg_column,
        seg_laps[:, None, :],
        skip_row,
        gain_row,
    )
    gated, ssm, states, mixed, slope, kv_own = ssd_forward(ssd_arrays, cos_folded, sin_folded)
    kv_all = over_chips(kv_own)
    gu_gathered = lax.all_gather(after(gu_slices, out_gathered, gated), "dp", axis=0, tiled=True)
    down_gathered = lax.all_gather(after(down_slices, gu_gathered), "dp", axis=0, tiled=True)
    full_gu = gu_gathered.reshape(width, 2 * hidden_units)
    full_down = down_gathered.reshape(width, hidden_units)
    attended, log_total, queries, keys, vals = attend(
        attend_forward_kernel,
        (
            projected,
            cos_wide,
            sin_wide,
            after(kv_all, out_gathered),
            seg_column,
            seg_row,
        ),
        (
            ((length, HD), bf16),
            ((length, 1), jnp.float32),
            ((length, HD), bf16),
            ((length, HD), bf16),
            ((length, HD), bf16),
        ),
        blocks=[pl.BlockSpec((length, HD), lambda step: (0, width_x // HD))] + [None] * 5,
    )
    outs = jnp.concatenate([gated, attended], axis=1)
    middle = hidden_own + scatter_plane(outs, full_out, 2)[0]

    scale_two = lax.rsqrt(jnp.mean(middle * middle, axis=-1, keepdims=True) + EPSILON)
    normed_two, gate_up, activated = gather_plane(
        after((middle * scale_two * gain_two).astype(bf16), gu_gathered),
        9,
        apply_gate_up,
        (full_gu,),
        (((length, 2 * hidden_units), jnp.float32), ((length, hidden_units), bf16)),
    )
    teacher_own = lax.dynamic_slice(teacher[0], (core * own_rows, 0), (own_rows, width))
    factor = 2.0 * total_tokens / token_count * mask_rows.astype(jnp.float32)[:, None]
    block_out, d_out, d_gate_up, grad_down = down_and_back(
        activated, full_down, middle, teacher_own, factor, gate_up
    )

    def sum_rows(grads):
        summed = lax.psum_scatter(grads.astype(bf16), "dp", scatter_dimension=0, tiled=True)
        return summed.reshape(GROUP, slice_rows, grads.shape[1])

    grad_down = sum_rows(grad_down)
    d_normed_two, grad_gate_up = up_back(d_gate_up, full_gu, normed_two)
    grad_gate_up = sum_rows(after(grad_gate_up, grad_down))
    grad_gain_two = jnp.sum(d_normed_two * middle * scale_two, axis=0)
    d_scaled = d_normed_two * gain_two
    d_middle = (
        d_out
        + scale_two * d_scaled
        - middle * scale_two**3 * jnp.mean(d_scaled * middle, axis=-1, keepdims=True)
    )
    d_branch, d_gated, d_attended = gather_plane(
        after(d_middle.astype(bf16), grad_down),
        12,
        apply_out_back,
        (full_out,),
        (((length, width_x), jnp.float32), ((length, HD), bf16)),
    )
    d_query, d_kv = attend(
        attend_backward_kernel,
        (
            queries,
            keys,
            vals,
            cos_wide,
            sin_wide,
            seg_column,
            seg_row,
            log_total,
            d_attended,
        ),
        (((length, HD), bf16), ((GROUP, length // 2, HD), bf16)),
        (((length, HD), jnp.float32),) * 3,
    )
    d_kv_parts = from_chips(d_kv)
    grad_out = sum_rows(
        after(dot_left_t(d_branch, outs).astype(bf16), grad_gate_up, d_query)
    )
    (
        d_projected,
        grad_taps,
        grad_heads,
        d_skip_lanes,
        d_gain_lanes,
        back_gate_up,
        back_down,
    ) = ssd_backward(
        ssd_arrays,
        slope,
        mixed,
        ssm,
        states,
        d_gated,
        d_query,
        d_kv_parts,
        (cos_folded, sin_folded),
        (grad_gate_up, grad_down),
    )
    grad_skip = jnp.sum(d_skip_lanes.reshape(HEADS, HP), axis=-1)
    grad_group = d_gain_lanes.reshape(HEADS, HP)
    grad_in = sum_rows(
        after(dot_left_t(normed, d_projected[:, :width_in]).astype(bf16), grad_out)
    )
    bc_cols = 2 * NS // GROUP
    grad_input, bc_sum, gain_sums = input_back(
        after(d_projected, grad_out),
        full_in,
        normed,
        w_bc,
        hidden_low,
        d_middle,
        gain_one[None],
        bc_cols,
    )
    grad_gain_one = jnp.sum(gain_sums, axis=0)

    taps_all = jnp.concatenate(
        [
            lax.dynamic_update_slice(
                jnp.zeros((8, MH * HP), jnp.float32), grad_taps[:, :width_x], (0, head_start * HP)
            ),
            grad_taps[:, width_x:],
        ],
        axis=1,
    )
    heads_all = lax.dynamic_update_slice(
        jnp.zeros((8, 128), jnp.float32),
        jnp.concatenate([grad_heads[:2, DT_LANE : DT_LANE + HEADS], grad_skip[None]]),
        (0, head_start),
    )
    group_all = lax.dynamic_update_slice(
        jnp.zeros((MH, HP), jnp.float32), grad_group, (head_start, 0)
    )
    small = [taps_all, heads_all]
    small += [
        values.reshape(8, -1) for values in (grad_gain_one, grad_gain_two, group_all)
    ]
    small = jnp.concatenate(small, axis=1)
    small_width = -(-small.shape[1] // (2 * GROUP * 128)) * 2 * GROUP * 128
    small = jnp.pad(small, ((0, 0), (0, small_width - small.shape[1])))
    piece, both_input, both_output, back_out = plane_sum(small, grad_input, block_out, grad_out)
    grad_gate, grad_up, grad_down, grad_mo, grad_ao, grad_input, block_out = unpack_early(
        back_gate_up,
        back_down,
        back_out,
        (both_input, both_output),
        [array.shape for array in (w_gate, w_up, w_down, w_mamba_out, w_attn_out)],
    )
    small_all, bc_all, back_in = finish_all(after(piece, grad_input), bc_sum, grad_in)
    bc_all = bc_all.reshape(2 * GROUP, bc_cols, width // 2)
    shapes = [
        array.shape
        for array in (w_z, w_x, w_query, w_bc, w_key, w_value, w_dt.T, conv_weight.T)
    ]
    shapes += [(1, conv_bias.shape[0])] + [(1, MH)] * 3 + [(MH, HP)] + [(1, slice_rows)] * 2
    (
        grad_z,
        grad_x,
        grad_q,
        grad_bc,
        grad_k,
        grad_v,
        grad_dt,
        grad_conv,
        grad_bias,
        grad_dtb,
        grad_alog,
        grad_skip,
        grad_group,
        grad_one,
        grad_two,
    ) = unpack_late(back_in, bc_all, small_all, shapes)
    return (
        block_out[None],
        grad_input[None],
        grad_one[0],
        grad_z,
        grad_x,
        grad_bc,
        grad_dt.T,
        grad_conv.T,
        grad_bias.reshape(-1),
        grad_dtb[0],
        grad_alog[0],
        grad_skip[0],
        grad_group,
        grad_mo,
        grad_q,
        grad_k,
        grad_v,
        grad_ao,
        grad_two[0],
        grad_gate,
        grad_up,
        grad_down,
    )


def solution(mesh):
    placed = (
        P("dp", "seq", None),
        P("dp", "seq", None),
        P("dp", None),
        P(),
        P(("dp", "seq")),
        P(("dp", "seq"), "tensor"),
        P(("dp", "seq"), "tensor"),
        P(),
        P(("dp", "seq"), "tensor"),
        P(),
        P(),
        P(),
        P(),
        P(),
        P(),
        P("tensor", ("dp", "seq")),
        P(("dp", "seq"), "tensor"),
        P(("dp", "seq"), "tensor"),
        P(("dp", "seq"), "tensor"),
        P("tensor", ("dp", "seq")),
        P(("dp", "seq")),
        P(("dp", "seq"), "tensor"),
        P(("dp", "seq"), "tensor"),
        P("tensor", ("dp", "seq")),
    )
    whole_row = mesh.shape["seq"] == GROUP and mesh.shape["tensor"] == 2
    return jax.shard_map(
        heads_local_plan if whole_row else local,
        mesh=mesh,
        in_specs=placed,
        out_specs=(
            P("dp", "seq", None),
            P("dp", "seq", None),
            P(("dp", "seq")),
            P(("dp", "seq"), "tensor"),
            P(("dp", "seq"), "tensor"),
            P(),
            P(("dp", "seq"), "tensor"),
            P(),
            P(),
            P(),
            P(),
            P(),
            P(),
            P("tensor", ("dp", "seq")),
            P(("dp", "seq"), "tensor"),
            P(("dp", "seq"), "tensor"),
            P(("dp", "seq"), "tensor"),
            P("tensor", ("dp", "seq")),
            P(("dp", "seq")),
            P(("dp", "seq"), "tensor"),
            P(("dp", "seq"), "tensor"),
            P("tensor", ("dp", "seq")),
        ),
        check_vma=False,
    )
```

```python
from functools import partial

import jax
import jax.numpy as jnp
import numpy as np
from jax import lax
from jax.experimental import pallas as pl
from jax.experimental.pallas import tpu as pltpu
from jax.sharding import PartitionSpec as P

MH = 48
HP = 64
NS = 256
KC = 4
HD = 128


EPSILON = 1e-06
GROUP_EPSILON = 1e-05
ROPE_BASE = 10000.0
HIGHEST = lax.Precision.HIGHEST


def shifted(block, axis, distance):
    devices = range(lax.axis_size(axis))
    route = [(i - distance, i) for i in devices if i - distance in devices]
    return lax.ppermute(block, axis, route)


def carried_in(part, axis, combine, identity, reverse):
    count = lax.axis_size(axis)
    place = lax.axis_index(axis)
    ahead = count - 1 - place if reverse else place
    gathered = jax.tree.map(lambda a: lax.all_gather(a, axis), part)
    state = jax.tree.map(lambda a, e: jnp.zeros_like(a) + jnp.asarray(e, a.dtype), part, identity)

    def one(lap, state):
        source = count - 1 - lap if reverse else lap
        return combine(
            state, jax.tree.map(lambda a: lax.dynamic_index_in_dim(a, source, 0, False), gathered)
        )

    return lax.fori_loop(0, ahead, one, state)


def mat_dot(left_side, right_side):
    return jnp.dot(left_side, right_side, preferred_element_type=jnp.float32)


def dot_left_t(left_side, right_side):
    return lax.dot_general(
        left_side, right_side, (((0,), (0,)), ((), ())), preferred_element_type=jnp.float32
    )


def dot_right_t(left_side, right_side):
    return lax.dot_general(
        left_side, right_side, (((1,), (1,)), ((), ())), preferred_element_type=jnp.float32
    )


def rms_norm(values, gain_row):
    scale_row = lax.rsqrt(jnp.mean(values * values, axis=-1, keepdims=True) + EPSILON)
    return values * scale_row * gain_row


def rotate(positions, values):
    half_dim = values.shape[-1] // 2
    frequency = ROPE_BASE ** (-2.0 * jnp.arange(half_dim).astype(jnp.float32) / values.shape[-1])
    angles = positions.astype(jnp.float32)[:, None] * frequency[None, :]
    cosine = jnp.cos(angles)[:, None, :]
    sine_part = jnp.sin(angles)[:, None, :]
    first_half = values[..., :half_dim]
    second = values[..., half_dim:]
    return jnp.concatenate(
        [first_half * cosine - second * sine_part, second * cosine + first_half * sine_part],
        axis=-1,
    )


def conv_silu(seg_ext, seg_rows, extended, weights, bias_row):
    size_rows = seg_rows.shape[0]
    summed = jnp.zeros((size_rows, weights.shape[0]), jnp.float32) + bias_row[None, :]
    for tap_index in range(weights.shape[1]):
        window = lax.slice_in_dim(extended, tap_index, tap_index + size_rows, axis=0)
        keep_mask = (
            lax.slice_in_dim(seg_ext, tap_index, tap_index + size_rows) == seg_rows
        ).astype(jnp.float32)
        summed = summed + window * weights[:, tap_index][None, :] * keep_mask[:, None]
    return jax.nn.silu(summed)


def group_gate(ssm_out, gate_z, group_gain):
    mixed_val = ssm_out * jax.nn.silu(gate_z)
    return (
        mixed_val
        * lax.rsqrt(jnp.mean(mixed_val * mixed_val, axis=-1, keepdims=True) + GROUP_EPSILON)
        * group_gain[None]
    )


def swiglu(gate_pre, up_pre):
    return jax.nn.silu(gate_pre) * up_pre


def split_mixed(mixed_in, heads_local):
    size_rows = mixed_in.shape[0]
    width_x = heads_local * HP
    heads_x = mixed_in[:, :width_x].reshape(size_rows, heads_local, HP)
    return (heads_x, mixed_in[:, width_x : width_x + NS], mixed_in[:, width_x + NS :])


def ssd_main(seg_rows, seg_before, mixed_in, dt_raw, dt_bias_row, a_log_row, d_skip_row):
    size_rows = seg_rows.shape[0]
    heads_x, b_rows, c_rows = split_mixed(mixed_in, dt_raw.shape[1])
    dt_rows = jax.nn.softplus(dt_raw + dt_bias_row[None, :])
    cumul = jnp.cumsum(-jnp.exp(a_log_row)[None, :] * dt_rows, axis=0)
    order_pos = jnp.arange(size_rows)
    allowed = (seg_rows[:, None] == seg_rows[None, :]) & (order_pos[:, None] >= order_pos[None, :])
    differ = cumul[:, None, :] - cumul[None, :, :]
    decay = jnp.exp(jnp.where(allowed[:, :, None], differ, -jnp.inf))
    gram = jnp.dot(c_rows, b_rows.T, precision=HIGHEST, preferred_element_type=jnp.float32)
    mixing = gram[:, :, None] * decay * dt_rows[None, :, :]
    outputs = jnp.einsum("tsh,shp->thp", mixing, heads_x, precision=HIGHEST)
    outputs = outputs + d_skip_row[None, :, None] * heads_x
    tail_keep = (seg_rows == seg_rows[-1]).astype(jnp.float32)
    tail_weight = jnp.exp(cumul[-1][None, :] - cumul) * tail_keep[:, None] * dt_rows
    local_state = jnp.einsum("sh,shp,sn->hpn", tail_weight, heads_x, b_rows, precision=HIGHEST)
    carry_factor = jnp.exp(cumul[-1]) * (seg_rows[-1] == seg_before).astype(jnp.float32)
    return (outputs, carry_factor, local_state)


def ssd_state(seg_rows, seg_before, mixed_in, dt_raw, dt_bias_row, a_log_row, entry_state):
    heads_x, b_rows, c_rows = split_mixed(mixed_in, dt_raw.shape[1])
    dt_rows = jax.nn.softplus(dt_raw + dt_bias_row[None, :])
    cumul = jnp.cumsum(-jnp.exp(a_log_row)[None, :] * dt_rows, axis=0)
    entry_keep = (seg_rows == seg_before).astype(jnp.float32)
    entry_part = jnp.einsum("tn,hpn->thp", c_rows, entry_state, precision=HIGHEST)
    return jnp.exp(cumul)[:, :, None] * entry_keep[:, None, None] * entry_part


def chain_states(earlier, later):
    return (earlier[0] * later[0], later[0][:, None, None] * earlier[1] + later[1])


def block_scores(queries, keys_all, vals_all, seg_full, query_pos, seg_query, block_index, key_len):
    key_blk = keys_all[block_index * key_len : (block_index + 1) * key_len]
    val_blk = vals_all[block_index * key_len : (block_index + 1) * key_len]
    seg_key = seg_full[block_index * key_len : (block_index + 1) * key_len]
    key_pos = block_index * key_len + jnp.arange(key_len)
    scores = jnp.einsum(
        "tkgd,skd->kgts", queries, key_blk, preferred_element_type=jnp.float32
    ) * HD ** (-0.5)
    allowed = (query_pos[:, None] >= key_pos[None, :]) & (seg_query[:, None] == seg_key[None, :])
    return (key_blk, val_blk, jnp.where(allowed[None, None], scores, -jnp.inf))


def attend_forward(queries, keys_all, vals_all, seg_full, query_pos, seg_query, block_count):
    key_len = keys_all.shape[0] // block_count
    stat_shape = (queries.shape[1], queries.shape[2], queries.shape[0])
    running_max = jnp.full(stat_shape, -1e30, jnp.float32)
    running_sum = jnp.zeros(stat_shape, jnp.float32)
    for block_index in range(block_count):
        needed = block_index * key_len <= query_pos[-1]

        def stat_step(stats, block_index=block_index):
            old_max, old_sum = stats
            key_blk, val_blk, scores = block_scores(
                queries, keys_all, vals_all, seg_full, query_pos, seg_query, block_index, key_len
            )
            new_max = jnp.maximum(old_max, jnp.max(scores, axis=-1))
            new_sum = old_sum * jnp.exp(old_max - new_max) + jnp.sum(
                jnp.exp(scores - new_max[..., None]), axis=-1
            )
            return (new_max, new_sum)

        running_max, running_sum = lax.cond(
            needed, stat_step, lambda stats: stats, (running_max, running_sum)
        )
    log_total = running_max + jnp.log(running_sum)
    attended = jnp.zeros(queries.shape, jnp.float32)
    for block_index in range(block_count):
        needed = block_index * key_len <= query_pos[-1]

        def value_step(total, block_index=block_index):
            key_blk, val_blk, scores = block_scores(
                queries, keys_all, vals_all, seg_full, query_pos, seg_query, block_index, key_len
            )
            probs = jnp.exp(scores - log_total[..., None]).astype(jnp.bfloat16)
            return total + jnp.einsum(
                "kgts,skd->tkgd", probs, val_blk, preferred_element_type=jnp.float32
            )

        attended = lax.cond(needed, value_step, lambda total: total, attended)
    return (log_total, attended)


def attend_backward(
    queries, keys_all, vals_all, seg_full, query_pos, seg_query, block_count, grad_out, log_total
):
    key_len = keys_all.shape[0] // block_count
    delta = jnp.zeros(log_total.shape, jnp.float32)
    for block_index in range(block_count):
        needed = block_index * key_len <= query_pos[-1]

        def delta_step(total, block_index=block_index):
            key_blk, val_blk, scores = block_scores(
                queries, keys_all, vals_all, seg_full, query_pos, seg_query, block_index, key_len
            )
            probs = jnp.exp(scores - log_total[..., None])
            grad_probs = jnp.einsum(
                "tkgd,skd->kgts", grad_out, val_blk, preferred_element_type=jnp.float32
            )
            return total + jnp.sum(probs * grad_probs, axis=-1)

        delta = lax.cond(needed, delta_step, lambda total: total, delta)
    grad_query = jnp.zeros(queries.shape, jnp.float32)
    empty_part = jnp.zeros((key_len, keys_all.shape[1], keys_all.shape[2]), jnp.float32)
    key_parts = []
    val_parts = []
    for block_index in range(block_count):
        needed = block_index * key_len <= query_pos[-1]

        def grad_step(total, block_index=block_index):
            key_blk, val_blk, scores = block_scores(
                queries, keys_all, vals_all, seg_full, query_pos, seg_query, block_index, key_len
            )
            probs = jnp.exp(scores - log_total[..., None])
            grad_probs = jnp.einsum(
                "tkgd,skd->kgts", grad_out, val_blk, preferred_element_type=jnp.float32
            )
            grad_scores = (probs * (grad_probs - delta[..., None])).astype(jnp.bfloat16)
            new_total = total + jnp.einsum(
                "kgts,skd->tkgd", grad_scores, key_blk, preferred_element_type=jnp.float32
            ) * HD ** (-0.5)
            key_part = jnp.einsum(
                "kgts,tkgd->skd", grad_scores, queries, preferred_element_type=jnp.float32
            ) * HD ** (-0.5)
            val_part = jnp.einsum(
                "kgts,tkgd->skd",
                probs.astype(jnp.bfloat16),
                grad_out,
                preferred_element_type=jnp.float32,
            )
            return (new_total, key_part, val_part)

        grad_query, key_part, val_part = lax.cond(
            needed, grad_step, lambda total: (total, empty_part, empty_part), grad_query
        )
        key_parts.append(key_part)
        val_parts.append(val_part)
    return (grad_query, jnp.concatenate(key_parts, axis=0), jnp.concatenate(val_parts, axis=0))


def local(
    hidden_in,
    teacher,
    segment_ids,
    valid_mask,
    norm1_gain,
    w_z,
    w_x,
    w_bc,
    w_dt,
    conv_weight,
    conv_bias,
    dt_bias,
    a_log,
    d_skip,
    group_gain,
    w_mamba_out,
    w_query,
    w_key,
    w_value,
    w_attn_out,
    norm2_gain,
    w_gate,
    w_up,
    w_down,
):
    tensor_rank = lax.axis_index("tensor")
    seq_rank = lax.axis_index("seq")
    data_rank = lax.axis_index("dp")
    seq_count = lax.axis_size("seq")
    tensor_count = lax.axis_size("tensor")
    size_rows = hidden_in.shape[1]
    full_length = segment_ids.shape[1]
    row_start = seq_rank * size_rows
    seg_full = segment_ids[0]
    seg_local = lax.dynamic_slice_in_dim(seg_full, row_start, size_rows)
    seg_padded = jnp.concatenate([jnp.full((KC - 1,), -1, jnp.int32), seg_full])
    seg_ext = lax.dynamic_slice_in_dim(seg_padded, row_start, size_rows + KC - 1)
    seg_prev = lax.dynamic_index_in_dim(seg_padded, row_start + KC - 2, keepdims=False)
    token_count = jnp.sum(valid_mask).astype(jnp.float32)
    mask_rows = lax.dynamic_slice(valid_mask, (data_rank, row_start), (1, size_rows))[0].astype(
        jnp.float32
    )
    total_tokens = float(valid_mask.shape[0] * valid_mask.shape[1])
    (
        gain_one,
        full_z,
        full_x,
        full_dt,
        full_mo,
        full_q,
        full_k,
        full_v,
        full_ao,
        gain_two,
        full_gate,
        full_up,
        full_down,
    ) = (
        lax.all_gather(norm1_gain, ("dp", "seq"), axis=0, tiled=True),
        lax.all_gather(w_z, ("dp", "seq"), axis=0, tiled=True),
        lax.all_gather(w_x, ("dp", "seq"), axis=0, tiled=True),
        lax.all_gather(w_dt, ("dp", "seq"), axis=0, tiled=True),
        lax.all_gather(w_mamba_out, ("dp", "seq"), axis=1, tiled=True),
        lax.all_gather(w_query, ("dp", "seq"), axis=0, tiled=True),
        lax.all_gather(w_key, ("dp", "seq"), axis=0, tiled=True),
        lax.all_gather(w_value, ("dp", "seq"), axis=0, tiled=True),
        lax.all_gather(w_attn_out, ("dp", "seq"), axis=1, tiled=True),
        lax.all_gather(norm2_gain, ("dp", "seq"), axis=0, tiled=True),
        lax.all_gather(w_gate, ("dp", "seq"), axis=0, tiled=True),
        lax.all_gather(w_up, ("dp", "seq"), axis=0, tiled=True),
        lax.all_gather(w_down, ("dp", "seq"), axis=1, tiled=True),
    )
    heads_local = MH // tensor_count
    width_x = heads_local * HP
    head_start = tensor_rank * heads_local
    hidden = hidden_in[0].astype(jnp.float32)
    normed_f, norm_one_pull = jax.vjp(rms_norm, hidden, gain_one.astype(jnp.float32))
    normed = normed_f.astype(jnp.bfloat16)
    gate_z = mat_dot(normed, full_z)
    pre_x = mat_dot(normed, full_x).astype(jnp.bfloat16)
    pre_bc = mat_dot(normed, w_bc).astype(jnp.bfloat16)
    dt_raw = mat_dot(normed, full_dt)
    pre_all = jnp.concatenate([pre_x, pre_bc], axis=1)
    rim_rows = shifted(pre_all[size_rows - (KC - 1) :], "seq", 1)
    extended = jnp.concatenate([rim_rows, pre_all], axis=0).astype(jnp.float32)
    conv_local = jnp.concatenate(
        [
            lax.dynamic_slice_in_dim(conv_weight, head_start * HP, width_x, 0),
            conv_weight[MH * HP :],
        ],
        axis=0,
    )
    bias_local = jnp.concatenate(
        [lax.dynamic_slice_in_dim(conv_bias, head_start * HP, width_x, 0), conv_bias[MH * HP :]],
        axis=0,
    )
    mixed_f, conv_pull = jax.vjp(
        partial(conv_silu, seg_ext, seg_local), extended, conv_local, bias_local
    )
    mixed_in = lax.optimization_barrier(mixed_f.astype(jnp.bfloat16)).astype(jnp.float32)
    dt_bias_loc = lax.dynamic_slice_in_dim(dt_bias, head_start, heads_local)
    a_log_loc = lax.dynamic_slice_in_dim(a_log, head_start, heads_local)
    d_skip_loc = lax.dynamic_slice_in_dim(d_skip, head_start, heads_local)
    group_loc = lax.dynamic_slice_in_dim(group_gain, head_start, heads_local, 0)
    (ssm_local, carry_dev, state_dev), main_pull = jax.vjp(
        partial(ssd_main, seg_local, seg_prev), mixed_in, dt_raw, dt_bias_loc, a_log_loc, d_skip_loc
    )
    identity = (jnp.ones_like(carry_dev), jnp.zeros_like(state_dev))
    entry_state = carried_in((carry_dev, state_dev), "seq", chain_states, identity, False)[1]
    ssm_entry, state_pull = jax.vjp(
        partial(ssd_state, seg_local, seg_prev),
        mixed_in,
        dt_raw,
        dt_bias_loc,
        a_log_loc,
        entry_state,
    )
    ssm_out = ssm_local + ssm_entry
    gated_f, gate_pull = jax.vjp(
        group_gate, ssm_out, gate_z.reshape(size_rows, heads_local, HP), group_loc
    )
    gated = gated_f.reshape(size_rows, width_x).astype(jnp.bfloat16)
    mamba_part = mat_dot(gated, full_mo)
    positions = row_start + jnp.arange(size_rows)
    heads_q = full_q.shape[1] // HD
    heads_kv = full_k.shape[1] // HD
    groups = heads_q // heads_kv
    query_rot, query_pull = jax.vjp(
        partial(rotate, positions), mat_dot(normed, full_q).reshape(size_rows, heads_q, HD)
    )
    queries = query_rot.astype(jnp.bfloat16).reshape(size_rows, heads_kv, groups, HD)
    key_rot, key_pull = jax.vjp(
        partial(rotate, positions), mat_dot(normed, full_k).reshape(size_rows, heads_kv, HD)
    )
    keys_local = key_rot.astype(jnp.bfloat16).reshape(size_rows, heads_kv * HD)
    vals_local = mat_dot(normed, full_v).astype(jnp.bfloat16)
    keys_all, vals_all = (
        lax.all_gather(keys_local, "seq", axis=0, tiled=True),
        lax.all_gather(vals_local, "seq", axis=0, tiled=True),
    )
    keys_all = keys_all.reshape(full_length, heads_kv, HD)
    vals_all = vals_all.reshape(full_length, heads_kv, HD)
    block_count = seq_count // 4
    log_total, attended_f = attend_forward(
        queries, keys_all, vals_all, seg_full, positions, seg_local, block_count
    )
    attended = attended_f.reshape(size_rows, heads_q * HD).astype(jnp.bfloat16)
    branch = lax.psum(mamba_part + mat_dot(attended, full_ao), "tensor")
    middle = hidden + branch
    normed_two_f, norm_two_pull = jax.vjp(rms_norm, middle, gain_two.astype(jnp.float32))
    normed_two = normed_two_f.astype(jnp.bfloat16)
    act_f, glu_pull = jax.vjp(swiglu, mat_dot(normed_two, full_gate), mat_dot(normed_two, full_up))
    activated = act_f.astype(jnp.bfloat16)
    block_out = middle + lax.psum(mat_dot(activated, full_down), "tensor")
    (
        back_z,
        back_x,
        back_dt,
        back_mo,
        back_q,
        back_k,
        back_v,
        back_ao,
        back_gate,
        back_up,
        back_down,
    ) = (
        lax.all_gather(w_z, ("dp", "seq"), axis=0, tiled=True),
        lax.all_gather(w_x, ("dp", "seq"), axis=0, tiled=True),
        lax.all_gather(w_dt, ("dp", "seq"), axis=0, tiled=True),
        lax.all_gather(w_mamba_out, ("dp", "seq"), axis=1, tiled=True),
        lax.all_gather(w_query, ("dp", "seq"), axis=0, tiled=True),
        lax.all_gather(w_key, ("dp", "seq"), axis=0, tiled=True),
        lax.all_gather(w_value, ("dp", "seq"), axis=0, tiled=True),
        lax.all_gather(w_attn_out, ("dp", "seq"), axis=1, tiled=True),
        lax.all_gather(w_gate, ("dp", "seq"), axis=0, tiled=True),
        lax.all_gather(w_up, ("dp", "seq"), axis=0, tiled=True),
        lax.all_gather(w_down, ("dp", "seq"), axis=1, tiled=True),
    )
    d_out = (
        2.0
        * total_tokens
        / token_count
        * mask_rows[:, None]
        * (block_out - teacher[0].astype(jnp.float32))
    )
    d_mlp = d_out.astype(jnp.bfloat16)
    grad_down = dot_left_t(activated, d_mlp)
    d_gate_f, d_up_f = glu_pull(dot_right_t(d_mlp, back_down))
    d_gate = d_gate_f.astype(jnp.bfloat16)
    d_up = d_up_f.astype(jnp.bfloat16)
    grad_gate = dot_left_t(normed_two, d_gate)
    grad_up = dot_left_t(normed_two, d_up)
    d_normed_two = lax.psum(dot_right_t(d_gate, back_gate) + dot_right_t(d_up, back_up), "tensor")
    d_middle_n, grad_gain_two = norm_two_pull(d_normed_two)
    d_middle = d_out + d_middle_n
    d_branch = d_middle.astype(jnp.bfloat16)
    grad_ao = dot_left_t(attended, d_branch)
    grad_mo = dot_left_t(gated, d_branch)
    d_attended = (
        dot_right_t(d_branch, back_ao).astype(jnp.bfloat16).reshape(size_rows, heads_kv, groups, HD)
    )
    d_gated = dot_right_t(d_branch, back_mo).reshape(size_rows, heads_local, HP)
    d_ssm, d_gate_z_f, grad_group = gate_pull(d_gated)
    d_gate_z = d_gate_z_f.reshape(size_rows, width_x).astype(jnp.bfloat16)
    d_mixed_s, d_dt_s, d_dtb_s, d_alog_s, d_entry = state_pull(d_ssm)
    state_grad = carried_in((carry_dev, d_entry), "seq", chain_states, identity, True)[1]
    d_carry = jnp.sum(state_grad * entry_state, axis=(1, 2))
    d_mixed_m, d_dt_m, d_dtb_m, d_alog_m, grad_skip = main_pull((d_ssm, d_carry, state_grad))
    d_dt_raw = (d_dt_s + d_dt_m).astype(jnp.bfloat16)
    d_ext, grad_conv_loc, grad_bias_loc = conv_pull(d_mixed_s + d_mixed_m)
    rim_grad = shifted(d_ext[: KC - 1], "seq", -1)
    d_pre = d_ext[KC - 1 :] + jnp.pad(rim_grad, ((size_rows - (KC - 1), 0), (0, 0)))
    d_pre_x = d_pre[:, :width_x].astype(jnp.bfloat16)
    d_pre_bc = d_pre[:, width_x:]
    grad_query_rot, key_grads_all, val_grads_all = attend_backward(
        queries,
        keys_all,
        vals_all,
        seg_full,
        positions,
        seg_local,
        block_count,
        d_attended,
        log_total,
    )
    key_grad, val_grad = (
        lax.psum_scatter(
            key_grads_all.reshape(full_length, heads_kv * HD).astype(jnp.bfloat16),
            "seq",
            scatter_dimension=0,
            tiled=True,
        ).astype(jnp.float32),
        lax.psum_scatter(
            val_grads_all.reshape(full_length, heads_kv * HD).astype(jnp.bfloat16),
            "seq",
            scatter_dimension=0,
            tiled=True,
        ).astype(jnp.float32),
    )
    d_query = (
        query_pull(grad_query_rot.reshape(size_rows, heads_q, HD))[0]
        .reshape(size_rows, heads_q * HD)
        .astype(jnp.bfloat16)
    )
    d_key = (
        key_pull(key_grad.reshape(size_rows, heads_kv, HD))[0]
        .reshape(size_rows, heads_kv * HD)
        .astype(jnp.bfloat16)
    )
    d_value = val_grad.astype(jnp.bfloat16)
    grad_z = dot_left_t(normed, d_gate_z)
    grad_x = dot_left_t(normed, d_pre_x)
    grad_dt = dot_left_t(normed, d_dt_raw)
    grad_q = dot_left_t(normed, d_query)
    grad_k = dot_left_t(normed, d_key)
    grad_v = dot_left_t(normed, d_value)
    normed_wide = normed.astype(jnp.float32)
    bc_weight = w_bc.astype(jnp.float32)
    grad_bc = jnp.dot(
        normed_wide.T, d_pre_bc, precision=HIGHEST, preferred_element_type=jnp.float32
    )
    d_normed_part = (
        dot_right_t(d_gate_z, back_z)
        + dot_right_t(d_pre_x, back_x)
        + dot_right_t(d_dt_raw, back_dt)
        + dot_right_t(d_query, back_q)
        + dot_right_t(d_key, back_k)
        + dot_right_t(d_value, back_v)
        + jnp.dot(d_pre_bc, bc_weight.T, precision=HIGHEST, preferred_element_type=jnp.float32)
    )
    d_normed = lax.psum(d_normed_part.astype(jnp.bfloat16), "tensor").astype(jnp.float32)
    d_hidden_n, grad_gain_one = norm_one_pull(d_normed)
    grad_input = d_middle + d_hidden_n
    conv_x_full = lax.dynamic_update_slice_in_dim(
        jnp.zeros((MH * HP, KC), jnp.float32), grad_conv_loc[:width_x], head_start * HP, 0
    )
    grad_conv_full = jnp.concatenate([conv_x_full, grad_conv_loc[width_x:]], axis=0)
    bias_x_full = lax.dynamic_update_slice_in_dim(
        jnp.zeros((MH * HP,), jnp.float32), grad_bias_loc[:width_x], head_start * HP, 0
    )
    grad_bias_full = jnp.concatenate([bias_x_full, grad_bias_loc[width_x:]], axis=0)
    grad_dtb_full = lax.dynamic_update_slice_in_dim(
        jnp.zeros((MH,), jnp.float32), d_dtb_s + d_dtb_m, head_start, 0
    )
    grad_alog_full = lax.dynamic_update_slice_in_dim(
        jnp.zeros((MH,), jnp.float32), d_alog_s + d_alog_m, head_start, 0
    )
    grad_skip_full = lax.dynamic_update_slice_in_dim(
        jnp.zeros((MH,), jnp.float32), grad_skip, head_start, 0
    )
    grad_group_full = lax.dynamic_update_slice_in_dim(
        jnp.zeros((MH, HP), jnp.float32), grad_group, head_start, 0
    )
    sum_bc, sum_conv, sum_bias, sum_dtb, sum_alog, sum_skip, sum_group = lax.psum(
        (
            grad_bc,
            grad_conv_full,
            grad_bias_full,
            grad_dtb_full,
            grad_alog_full,
            grad_skip_full,
            grad_group_full,
        ),
        ("dp", "seq", "tensor"),
    )
    (
        out_gain_one,
        out_z,
        out_x,
        out_dt,
        out_mo,
        out_q,
        out_k,
        out_v,
        out_ao,
        out_gain_two,
        out_gate,
        out_up,
        out_down,
    ) = (
        lax.psum_scatter(grad_gain_one, ("dp", "seq"), scatter_dimension=0, tiled=True),
        lax.psum_scatter(grad_z, ("dp", "seq"), scatter_dimension=0, tiled=True),
        lax.psum_scatter(grad_x, ("dp", "seq"), scatter_dimension=0, tiled=True),
        lax.psum_scatter(grad_dt, ("dp", "seq"), scatter_dimension=0, tiled=True),
        lax.psum_scatter(grad_mo, ("dp", "seq"), scatter_dimension=1, tiled=True),
        lax.psum_scatter(grad_q, ("dp", "seq"), scatter_dimension=0, tiled=True),
        lax.psum_scatter(grad_k, ("dp", "seq"), scatter_dimension=0, tiled=True),
        lax.psum_scatter(grad_v, ("dp", "seq"), scatter_dimension=0, tiled=True),
        lax.psum_scatter(grad_ao, ("dp", "seq"), scatter_dimension=1, tiled=True),
        lax.psum_scatter(grad_gain_two, ("dp", "seq"), scatter_dimension=0, tiled=True),
        lax.psum_scatter(grad_gate, ("dp", "seq"), scatter_dimension=0, tiled=True),
        lax.psum_scatter(grad_up, ("dp", "seq"), scatter_dimension=0, tiled=True),
        lax.psum_scatter(grad_down, ("dp", "seq"), scatter_dimension=1, tiled=True),
    )
    return (
        block_out.astype(jnp.bfloat16)[None],
        grad_input[None],
        out_gain_one,
        out_z,
        out_x,
        sum_bc,
        out_dt,
        sum_conv,
        sum_bias,
        sum_dtb,
        sum_alog,
        sum_skip,
        sum_group,
        out_mo,
        out_q,
        out_k,
        out_v,
        out_ao,
        out_gain_two,
        out_gate,
        out_up,
        out_down,
    )


GROUP = 4
CHUNK = 128
HEADS = 6
MESH_ID = pl.DeviceIdType.MESH
VMEM_BYTES = 56 * 1024 * 1024


def dot_f32(left_side, right_side, left_dim, right_dim):
    return lax.dot_general(
        left_side,
        right_side,
        (((left_dim,), (right_dim,)), ((), ())),
        preferred_element_type=jnp.float32,
    )


def halves(values):
    high = values.astype(jnp.bfloat16)
    return (high, (values - high.astype(jnp.float32)).astype(jnp.bfloat16))


def plane_place():
    data, place, core = lax.axis_index("dp"), lax.axis_index("seq"), lax.axis_index("tensor")
    along_x = place + 1 - 2 * lax.rem(place, 2)
    along_y = lax.rem(place + 2, GROUP)
    across = GROUP - 1 - place
    return (data, place, core, along_x, along_y, across)


def meet(devices):
    barrier = pltpu.get_barrier_semaphore()
    for device in devices:
        pl.semaphore_signal(barrier, inc=1, device_id=device, device_id_type=MESH_ID)
    pl.semaphore_wait(barrier, len(devices))


def remote(source, target, send_sem, recv_sem, device):
    return pltpu.make_async_remote_copy(
        src_ref=source,
        dst_ref=target,
        send_sem=send_sem,
        recv_sem=recv_sem,
        device_id=device,
        device_id_type=MESH_ID,
    )


def lasting(microseconds):
    return pl.CostEstimate(
        flops=int(microseconds * 9e8),
        bytes_accessed=int(microseconds * 3e6),
        transcendentals=0,
    )


def any_specs(count):
    return [pl.BlockSpec(memory_space=pl.ANY)] * count


def vmem_specs(count):
    return [pl.BlockSpec(memory_space=pltpu.VMEM)] * count


def gather_kernel(apply, count_in, count_out, own_ref, *refs):
    inputs, all_ref = refs[:count_in], refs[count_in]
    outputs = refs[count_in + 1 : count_in + 1 + count_out]
    send_sems, recv_sems = refs[count_in + 1 + count_out :]
    data, place, core, along_x, along_y, across = plane_place()
    to_x, to_y, partner = (data, along_x, core), (data, along_y, core), (data, place, 1 - core)
    meet((to_x, to_y, partner))
    gather_steps(apply, own_ref, inputs, all_ref, outputs, send_sems, recv_sems)


def gather_steps(apply, own_ref, inputs, all_ref, outputs, send_sems, recv_sems, ready=None):
    data, place, core, along_x, along_y, across = plane_place()
    height = own_ref.shape[0]
    half = height // 2
    to_x, to_y, partner = (data, along_x, core), (data, along_y, core), (data, place, 1 - core)

    def block(chip, part):
        return all_ref.at[2 * chip + core, pl.ds(part * half, half)]

    def work(chip, side):
        if apply is not None:
            index = 2 * chip + side
            rows = pl.ds(pl.multiple_of(index * height, 16), height)
            apply(all_ref[index], rows, inputs, outputs)

    def push(index, source, target, device):
        copy = remote(source, target, send_sems.at[index], recv_sems.at[index], device)
        copy.start()
        return copy

    first, second = own_ref.at[pl.ds(0, half)], own_ref.at[pl.ds(half, half)]
    x_first = push(0, first, block(place, 0), to_x)
    y_second = push(1, second, block(place, 1), to_y)
    x_second = push(2, second, block(place, 1), to_x)
    y_first = push(3, first, block(place, 0), to_y)
    pair_own = push(4, own_ref, all_ref.at[2 * place + core], partner)
    all_ref[2 * place + core] = own_ref[...]
    work(place, core)
    pair_own.wait_recv()
    work(place, 1 - core)
    if ready is not None:
        ready(place, 0)
    x_first.wait_recv()
    over_y = push(5, block(along_x, 0), block(along_x, 0), to_y)
    y_second.wait_recv()
    over_x = push(6, block(along_y, 1), block(along_y, 1), to_x)
    x_second.wait_recv()
    mine_x = all_ref.at[2 * along_x + core]
    pair_x = push(7, mine_x, mine_x, partner)
    y_first.wait_recv()
    mine_y = all_ref.at[2 * along_y + core]
    pair_y = push(8, mine_y, mine_y, partner)
    work(along_x, core)
    work(along_y, core)
    pair_x.wait_recv()
    work(along_x, 1 - core)
    if ready is not None:
        ready(along_x, 1)
    pair_y.wait_recv()
    work(along_y, 1 - core)
    if ready is not None:
        ready(along_y, 2)
    over_y.wait_recv()
    pair_a = push(9, block(across, 0), block(across, 0), partner)
    over_x.wait_recv()
    pair_b = push(10, block(across, 1), block(across, 1), partner)
    work(across, core)
    if ready is not None:
        ready(across, 3, core)
    pair_a.wait_recv()
    pair_b.wait_recv()
    work(across, 1 - core)
    if ready is not None:
        ready(across, 4, 1 - core)
    for copy in (
        x_first,
        y_second,
        x_second,
        y_first,
        pair_own,
        over_y,
        over_x,
        pair_x,
        pair_y,
        pair_a,
        pair_b,
    ):
        copy.wait_send()


def gather_plane(own, identity=1, apply=None, inputs=(), outputs=()):
    rows, width = own.shape
    gathered, *results = pl.pallas_call(
        partial(gather_kernel, apply, len(inputs), len(outputs)),
        out_shape=[jax.ShapeDtypeStruct((2 * GROUP, rows, width), own.dtype)]
        + [jax.ShapeDtypeStruct(shape, dtype) for shape, dtype in outputs],
        in_specs=vmem_specs(1 + len(inputs)),
        out_specs=vmem_specs(1 + len(outputs)),
        scratch_shapes=[pltpu.SemaphoreType.DMA((11,)), pltpu.SemaphoreType.DMA((11,))],
        cost_estimate=lasting(35),
        compiler_params=pltpu.CompilerParams(
            collective_id=identity, has_side_effects=True, vmem_limit_bytes=VMEM_BYTES
        ),
    )(own, *inputs)
    gathered = gathered.reshape(2 * GROUP * rows, width)
    return (gathered, *results) if results else gathered


def apply_gate_up(block, rows, inputs, outputs):
    weights, (both_ref, act_ref) = inputs[0], outputs
    units = act_ref.shape[1]
    both = jnp.dot(block, weights[...], preferred_element_type=jnp.float32)
    both_ref[rows] = both
    gate = both[:, :units]
    act_ref[rows] = (gate * jax.nn.sigmoid(gate) * both[:, units:]).astype(jnp.bfloat16)


def apply_down_back(block, rows, inputs, outputs):
    weights, both_ref = inputs
    units = weights.shape[1]
    d_act = jnp.dot(block, weights[...], preferred_element_type=jnp.float32)
    gate, up = both_ref[rows, :units], both_ref[rows, units:]
    sigmoid = jax.nn.sigmoid(gate)
    silu = gate * sigmoid
    d_gate = d_act * up * (sigmoid * (1.0 + gate * (1.0 - sigmoid)))
    outputs[0][rows, :units] = d_gate.astype(jnp.bfloat16)
    outputs[0][rows, units:] = (d_act * silu).astype(jnp.bfloat16)


def apply_out_back(block, rows, inputs, outputs):
    both = jnp.dot(block, inputs[0][...], preferred_element_type=jnp.float32)
    width = outputs[0].shape[1]
    outputs[0][rows] = both[:, :width]
    outputs[1][rows] = both[:, width:].astype(jnp.bfloat16)


def apply_norm(block, rows, inputs, outputs):
    gain_ref, weights = inputs
    values = block.astype(jnp.float32)
    scale = lax.rsqrt(jnp.mean(values * values, axis=-1, keepdims=True) + EPSILON)
    normed = (values * scale * gain_ref[...]).astype(jnp.bfloat16)
    outputs[0][rows] = normed
    outputs[1][rows] = jnp.dot(normed, weights[...], preferred_element_type=jnp.float32).astype(
        jnp.bfloat16
    )


def scatter_kernel(
    count, left_ref, right_ref, *refs, store=None, between=None, preparing=None, finishing=None
):
    data, place, core, along_x, along_y, across = plane_place()
    partner = (data, place, 1 - core)
    to_x, to_y = (data, along_x, core), (data, along_y, core)
    order = (across, along_x, along_y, place)
    count_in = 0 if count == 1 else count
    extra, sums = refs[:count_in], refs[count_in : count_in + count]
    parts, scratch = refs[count_in + count : count_in + 2 * count], refs[count_in + 2 * count :]
    step = 16
    meet((partner, to_x, to_y))

    def multiply(at, chip, side):
        part = parts[at]
        index = 2 * chip + side
        height, columns = part.shape[1:]
        if at == 0:
            rows = pl.ds(pl.multiple_of(index * height, 16), height)
            depth = right_ref.shape[1]
            block = dot_f32(left_ref[rows, :depth], right_ref[...], 1, 1)
            if count > 1:
                block = block + dot_f32(left_ref[rows, depth:], extra[-1][...], 1, 1)
        else:
            start = left_ref.shape[1] - GROUP * height
            turned = pl.ds(pl.multiple_of(start + chip * height, 128), height)
            along = pl.ds(pl.multiple_of(side * columns, 128), columns)
            block = dot_f32(left_ref[:, turned], extra[at - 1][:, along], 0, 0)
        part[index] = block.astype(jnp.bfloat16)

    def one_array(at, part_ref, sum_ref, own_refs):
        pair_in, send_a, send_x, send_y, got_x, got_y, pair_s, pair_r, send_s, recv_s = own_refs
        half = part_ref.shape[1] // 2
        pair = []

        def send_pair(index):
            chip = order[index]
            multiply(at, chip, 1 - core)
            copy = remote(
                part_ref.at[2 * chip + 1 - core],
                pair_in.at[index],
                pair_s.at[index],
                pair_r.at[index],
                partner,
            )
            copy.start()
            pair.append(copy)
            multiply(at, chip, core)

        def own_rows(index, rows):
            return part_ref[2 * order[index] + core, rows].astype(jnp.float32) + pair_in[
                index, rows
            ].astype(jnp.float32)

        def fill(target, index, first, extra=None):
            def one(lap, carry):
                rows = pl.ds(pl.multiple_of(lap * step, step), step)
                total = own_rows(index, pl.ds(pl.multiple_of(first + lap * step, step), step))
                if extra is not None:
                    total = total + extra[rows].astype(jnp.float32)
                target[rows] = total.astype(jnp.bfloat16)
                return carry

            lax.fori_loop(0, half // step, one, 0)

        def push(index, source, target, device):
            copy = remote(source, target, send_s.at[index], recv_s.at[index], device)
            copy.start()
            return copy

        send_pair(0)
        pair[0].wait_recv()
        fill(send_a.at[0], 0, 0)
        far_x = push(0, send_a.at[0], got_x.at[0], to_x)
        fill(send_a.at[1], 0, half)
        far_y = push(1, send_a.at[1], got_y.at[0], to_y)
        send_pair(1)
        pair[1].wait_recv()
        fill(send_x.at[0], 1, 0)
        near_x = push(2, send_x.at[0], got_x.at[1], to_x)
        send_pair(2)
        pair[2].wait_recv()
        fill(send_y.at[0], 2, half)
        near_y = push(3, send_y.at[0], got_y.at[1], to_y)
        send_pair(3)
        yield
        far_x.wait_recv()
        fill(send_y.at[1], 2, 0, got_x.at[0])
        last_y = push(4, send_y.at[1], got_y.at[2], to_y)
        far_y.wait_recv()
        fill(send_x.at[1], 1, half, got_y.at[0])
        last_x = push(5, send_x.at[1], got_x.at[2], to_x)
        yield
        pair[3].wait_recv()
        near_x.wait_recv()
        near_y.wait_recv()
        last_y.wait_recv()
        last_x.wait_recv()

        def finish(first, near, last):
            def one(lap, carry):
                rows = pl.ds(pl.multiple_of(lap * step, step), step)
                place_rows = pl.ds(pl.multiple_of(first + lap * step, step), step)
                total = (
                    own_rows(3, place_rows)
                    + near[rows].astype(jnp.float32)
                    + last[rows].astype(jnp.float32)
                )
                if store is None:
                    sum_ref[place_rows] = total
                else:
                    store(at, sum_ref, place_rows, total)
                return carry

            lax.fori_loop(0, half // step, one, 0)

        finish(0, got_x.at[1], got_y.at[2])
        finish(half, got_y.at[1], got_x.at[2])
        for copy in pair + [far_x, far_y, near_x, near_y, last_x, last_y]:
            copy.wait_send()

    each = len(scratch) // count
    runs = [
        one_array(at, parts[at], sums[at], scratch[each * at : each * (at + 1)]) for at in range(count)
    ]
    for stage in range(2):
        for at, run in enumerate(runs):
            if at > 0 and stage == 0 and preparing is not None:
                preparing()
            next(run)
        if between is not None:
            between(stage)
    if finishing is not None:
        finishing()
    for run in runs:
        for _ in run:
            pass


def down_and_back_kernel(
    act_ref,
    weights_ref,
    factor_ref,
    middle_hbm,
    teacher_hbm,
    both_hbm,
    out_hbm,
    d_out_hbm,
    d_both_hbm,
    grad_ref,
    out_ref,
    d_out_ref,
    d_both_ref,
    store_sems,
    own_ref,
    grad_sum,
    d_mlp_ref,
    middle_ref,
    teacher_ref,
    both_ref,
    load_sems,
    gather_send,
    gather_recv,
    *scratch,
):
    loads = []
    for source, target in (
        (middle_hbm, middle_ref),
        (teacher_hbm, teacher_ref),
        (both_hbm, both_ref),
    ):
        copy = pltpu.make_async_copy(source, target, load_sems.at[len(loads)])
        copy.start()
        loads.append(copy)

    def loaded():
        for copy in loads:
            copy.wait()

    def store(at, target, rows, total):
        out = middle_ref[rows] + total
        out_ref[rows] = out.astype(jnp.bfloat16)
        d_out = factor_ref[rows] * (out - teacher_ref[rows].astype(jnp.float32))
        d_out_ref[rows] = d_out
        own_ref[rows] = d_out.astype(jnp.bfloat16)

    stores = []

    def leave(source, target):
        copy = pltpu.make_async_copy(source, target, store_sems.at[len(stores)])
        copy.start()
        stores.append(copy)

    def ready(chip, turn_at, side=None):
        if side is None:
            blocks = d_mlp_ref[pl.ds(2 * chip, 2)]
            first = 2 * chip
        else:
            blocks = d_mlp_ref[pl.ds(2 * chip + side, 1)]
            first = 2 * chip + side
        height = blocks.shape[0] * blocks.shape[1]
        rows = pl.ds(pl.multiple_of(first * blocks.shape[1], 16), height)
        leave(d_both_ref.at[rows], d_both_hbm.at[rows])
        part = dot_f32(blocks.reshape(height, blocks.shape[2]), act_ref[rows], 0, 0)
        if turn_at == 0:
            grad_sum[...] = part
        elif turn_at < GROUP:
            grad_sum[...] += part
        else:
            grad_ref[...] = (grad_sum[...] + part).astype(jnp.bfloat16)

    scatter_kernel(1, act_ref, weights_ref, None, *scratch, store=store, finishing=loaded)
    leave(out_ref, out_hbm)
    leave(d_out_ref, d_out_hbm)
    gather_steps(
        apply_down_back,
        own_ref,
        (weights_ref, both_ref),
        d_mlp_ref,
        (d_both_ref,),
        gather_send,
        gather_recv,
        ready,
    )
    for copy in stores:
        copy.wait()


def down_and_back(activated, full_down, middle, teacher_own, factor, gate_up):
    rows, width = middle.shape
    shaped = jax.ShapeDtypeStruct
    return pl.pallas_call(
        down_and_back_kernel,
        out_shape=[
            shaped((rows, width), jnp.bfloat16),
            shaped((rows, width), jnp.float32),
            shaped(gate_up.shape, jnp.bfloat16),
            shaped(full_down.shape, jnp.bfloat16),
        ],
        in_specs=vmem_specs(3) + any_specs(3),
        out_specs=any_specs(3) + vmem_specs(1),
        scratch_shapes=[
            pltpu.VMEM((rows, width), jnp.bfloat16),
            pltpu.VMEM((rows, width), jnp.float32),
            pltpu.VMEM(gate_up.shape, jnp.bfloat16),
            pltpu.SemaphoreType.DMA((GROUP + 3,)),
            pltpu.VMEM((rows, width), jnp.bfloat16),
            pltpu.VMEM(full_down.shape, jnp.float32),
            pltpu.VMEM((2 * GROUP, rows, width), jnp.bfloat16),
            pltpu.VMEM(middle.shape, middle.dtype),
            pltpu.VMEM(teacher_own.shape, teacher_own.dtype),
            pltpu.VMEM(gate_up.shape, gate_up.dtype),
            pltpu.SemaphoreType.DMA((3,)),
            pltpu.SemaphoreType.DMA((11,)),
            pltpu.SemaphoreType.DMA((11,)),
        ]
        + scatter_scratch([(rows, width)]),
        cost_estimate=lasting(70),
        compiler_params=pltpu.CompilerParams(
            collective_id=10, has_side_effects=True, vmem_limit_bytes=VMEM_BYTES + 3 * 1024 * 1024
        ),
    )(activated, full_down, factor, middle, teacher_own, gate_up)


def up_back_kernel(d_both_ref, weights_ref, normed_ref, sum_ref, grad_ref, *scratch):
    tiles = 4
    width = normed_ref.shape[1] // tiles

    def between(stage):
        for tile in range(2 * stage, 2 * stage + 2):
            columns = slice(width * tile, width * (tile + 1))
            grad_ref[columns] = dot_f32(
                normed_ref[:, columns], d_both_ref[...], 0, 0
            ).astype(jnp.bfloat16)

    scatter_kernel(1, d_both_ref, weights_ref, sum_ref, *scratch, between=between)


def up_back(d_gate_up, full_gu, normed_two):
    rows, width = d_gate_up.shape[0] // (2 * GROUP), full_gu.shape[0]
    return pl.pallas_call(
        up_back_kernel,
        out_shape=[
            jax.ShapeDtypeStruct((rows, width), jnp.float32),
            jax.ShapeDtypeStruct(full_gu.shape, jnp.bfloat16),
        ],
        in_specs=vmem_specs(3),
        out_specs=vmem_specs(2),
        scratch_shapes=scatter_scratch([(rows, width)]),
        cost_estimate=lasting(38),
        compiler_params=pltpu.CompilerParams(
            collective_id=11, has_side_effects=True, vmem_limit_bytes=VMEM_BYTES
        ),
    )(d_gate_up, full_gu, normed_two)


def input_back_kernel(
    left_ref,
    weights_ref,
    bc_weights_ref,
    gain_ref,
    normed_hbm,
    hidden_hbm,
    d_middle_hbm,
    grad_ref,
    bc_ref,
    gain_sum_ref,
    normed_ref,
    hidden_ref,
    d_middle_ref,
    load_sems,
    *scratch,
):
    loads = []
    for source, target in (
        (normed_hbm, normed_ref),
        (hidden_hbm, hidden_ref),
        (d_middle_hbm, d_middle_ref),
    ):
        copy = pltpu.make_async_copy(source, target, load_sems.at[len(loads)])
        copy.start()
        loads.append(copy)
    gain_sum_ref[...] = jnp.zeros_like(gain_sum_ref)

    def loaded():
        for copy in loads[1:]:
            copy.wait()


    def store(at, target, rows, total):
        if at > 0:
            target[rows] = total
            return
        hidden = hidden_ref[rows].astype(jnp.float32)
        scale = lax.rsqrt(jnp.mean(hidden * hidden, axis=-1, keepdims=True) + EPSILON)
        scaled = total * gain_ref[...]
        inner = jnp.mean(scaled * hidden, axis=-1, keepdims=True)
        grad_ref[rows] = d_middle_ref[rows] + scale * scaled - hidden * (scale**3 * inner)
        product = total * hidden * scale
        gain_sum_ref[...] += product[:8] + product[8:]

    scatter_kernel(
        2,
        left_ref,
        weights_ref,
        normed_ref,
        bc_weights_ref,
        None,
        bc_ref,
        *scratch,
        store=store,
        preparing=loads[0].wait,
        finishing=loaded,
    )


def input_back(d_projected, full_in, normed, w_bc, hidden_own, d_middle, gain, bc_cols):
    rows, width = d_middle.shape
    sizes = [(rows, width), (bc_cols, width // 2)]
    shaped = jax.ShapeDtypeStruct
    return pl.pallas_call(
        input_back_kernel,
        out_shape=[
            shaped((rows, width), jnp.float32),
            shaped(sizes[1], jnp.float32),
            shaped((8, width), jnp.float32),
        ],
        in_specs=vmem_specs(4) + any_specs(3),
        out_specs=vmem_specs(3),
        scratch_shapes=[
            pltpu.VMEM(normed.shape, normed.dtype),
            pltpu.VMEM(hidden_own.shape, hidden_own.dtype),
            pltpu.VMEM(d_middle.shape, d_middle.dtype),
            pltpu.SemaphoreType.DMA((3,)),
        ]
        + scatter_scratch(sizes),
        cost_estimate=lasting(50),
        compiler_params=pltpu.CompilerParams(
            collective_id=8, has_side_effects=True, vmem_limit_bytes=VMEM_BYTES
        ),
    )(d_projected, full_in, w_bc, gain, normed, hidden_own, d_middle)


def scatter_scratch(sizes):
    scratch = [pltpu.VMEM((2 * GROUP, *size), jnp.bfloat16) for size in sizes]
    for rows, columns in sizes:
        half = (rows // 2, columns)
        scratch += [
            pltpu.VMEM((4, rows, columns), jnp.bfloat16),
            pltpu.VMEM((2,) + half, jnp.bfloat16),
            pltpu.VMEM((2,) + half, jnp.bfloat16),
            pltpu.VMEM((2,) + half, jnp.bfloat16),
            pltpu.VMEM((3,) + half, jnp.bfloat16),
            pltpu.VMEM((3,) + half, jnp.bfloat16),
            pltpu.SemaphoreType.DMA((4,)),
            pltpu.SemaphoreType.DMA((4,)),
            pltpu.SemaphoreType.DMA((6,)),
            pltpu.SemaphoreType.DMA((6,)),
        ]
    return scratch


def scatter_plane(left, right, identity, extra=(), beside=()):
    height, width = left.shape[0] // (2 * GROUP), right.shape[0]
    sizes = [(height, width)] + [tuple(size) for _, *size in extra]
    shapes = [jax.ShapeDtypeStruct(size, jnp.float32) for size in sizes]
    count = 1 + len(extra)
    return pl.pallas_call(
        partial(scatter_kernel, count),
        out_shape=shapes,
        in_specs=vmem_specs(2 if count == 1 else 2 + count),
        out_specs=vmem_specs(count),
        scratch_shapes=scatter_scratch(sizes),
        cost_estimate=lasting(35),
        compiler_params=pltpu.CompilerParams(
            collective_id=identity, has_side_effects=True, vmem_limit_bytes=VMEM_BYTES
        ),
    )(left, right, *[array for array, *_ in extra], *beside)


def plane_sum_kernel(
    small_ref, own_ref, out_ref, bulk, sum_ref, both_ref, both_out, back, small_in, own_sem, send_s, recv_s
):
    data, place, core, along_x, along_y, across = plane_place()
    mine = 2 * place + core
    partner = (data, place, 1 - core)
    plane = []
    for turn_by in range(1, 2 * GROUP):
        other = lax.rem(mine + turn_by, 2 * GROUP)
        plane.append((other, (data, other // 2, lax.rem(other, 2))))
    meet([device for _, device in plane])
    started = []

    def push(source, target, device):
        slot = len(started)
        copy = remote(source, target, send_s.at[slot], recv_s.at[slot], device)
        copy.start()
        started.append(copy)

    piece = small_in.shape[2]

    def piece_of(index):
        return small_ref.at[:, pl.ds(pl.multiple_of(index * piece, 128), piece)]

    for other, device in plane:
        push(piece_of(other), small_in.at[mine], device)
    for source, target in ((own_ref, both_ref), (out_ref, both_out)):
        push(source, target.at[core], partner)
    for chip in (across, along_x, along_y):
        push(bulk.at[chip], back.at[place], (data, chip, core))
    own = pltpu.make_async_copy(bulk.at[place], back.at[place], own_sem)
    own.start()
    small_in[mine] = piece_of(mine)[...]
    both_ref[core] = own_ref[...]
    both_out[core] = out_ref[...]
    for copy in started:
        copy.wait()
    own.wait()
    total = small_in[0]
    for index in range(1, 2 * GROUP):
        total = total + small_in[index]
    sum_ref[...] = total


def plane_sum(small, own_rows, out_rows, bulk):
    places = 2 * GROUP
    pushes = places - 1 + 2 + 3
    shaped = jax.ShapeDtypeStruct
    piece = small.shape[1] // places
    return pl.pallas_call(
        plane_sum_kernel,
        out_shape=[
            shaped((8, piece), jnp.float32),
            shaped((2,) + own_rows.shape, own_rows.dtype),
            shaped((2,) + out_rows.shape, out_rows.dtype),
            shaped(bulk.shape, bulk.dtype),
        ],
        in_specs=vmem_specs(3) + any_specs(1),
        out_specs=vmem_specs(3) + any_specs(1),
        scratch_shapes=[
            pltpu.VMEM((places, 8, piece), jnp.float32),
            pltpu.SemaphoreType.DMA,
            pltpu.SemaphoreType.DMA((pushes,)),
            pltpu.SemaphoreType.DMA((pushes,)),
        ],
        cost_estimate=lasting(20),
        compiler_params=pltpu.CompilerParams(
            collective_id=7, has_side_effects=True, vmem_limit_bytes=VMEM_BYTES
        ),
    )(small, own_rows, out_rows, bulk)


def finish_kernel(
    piece_ref,
    bc_ref,
    bulk,
    small_all,
    bc_all,
    back,
    bc_send,
    bc_in,
    bc_line,
    line_in,
    own_sem,
    send_s,
    recv_s,
):
    data, place, core, along_x, along_y, across = plane_place()
    count = lax.axis_size("dp")
    mine = 2 * place + core
    partner = (data, place, 1 - core)
    others = (across, along_x, along_y)
    chips = [(data, chip, core) for chip in others]
    plane = []
    for turn_by in range(1, 2 * GROUP):
        other = lax.rem(mine + turn_by, 2 * GROUP)
        plane.append((data, other // 2, lax.rem(other, 2)))
    line = []
    for turn_by in range(1, count):
        other = lax.rem(data + turn_by, count)
        line.append((other, (other, place, core)))
    meet(plane + [device for _, device in line])
    started = []

    def push(source, target, device):
        slot = len(started)
        copy = remote(source, target, send_s.at[slot], recv_s.at[slot], device)
        copy.start()
        started.append(copy)
        return copy

    rows = bc_in.shape[1]

    def rows_of(index):
        return bc_send.at[pl.ds(pl.multiple_of(index * rows, 16), rows)]

    bc_send[...] = bc_ref[...].astype(jnp.bfloat16)
    first = [push(rows_of(other), bc_in.at[data], device) for other, device in line]
    small = [push(piece_ref, line_in.at[data], device) for _, device in line]
    late = []
    for chip, device in zip(others, chips):
        late.append(push(bulk.at[chip], back.at[place], device))
    own = pltpu.make_async_copy(bulk.at[place], back.at[place], own_sem)
    own.start()
    bc_in[data] = rows_of(data)[...]
    line_in[data] = piece_ref[...]
    for copy in first:
        copy.wait_recv()
    total = bc_in[0].astype(jnp.float32)
    for index in range(1, count):
        total = total + bc_in[index].astype(jnp.float32)
    bc_line[data] = total.astype(jnp.bfloat16)
    second = [push(bc_line.at[data], bc_line.at[data], device) for _, device in line]
    for copy in small:
        copy.wait_recv()
    total = line_in[0]
    for index in range(1, count):
        total = total + line_in[index]
    small_all[mine] = total
    late += [push(small_all.at[mine], small_all.at[mine], device) for device in plane]
    for copy in second:
        copy.wait_recv()
    half = count // 2

    def half_of(chip, at):
        return bc_all.at[2 * chip + core, pl.ds(at * half, half)]

    def send_half(chip, at, device):
        held = half_of(chip, at)
        return push(held, held, device)

    to_x, to_y = (data, along_x, core), (data, along_y, core)
    bc_all[mine] = bc_line[...]
    x_first = send_half(place, 0, to_x)
    y_second = send_half(place, 1, to_y)
    x_second = send_half(place, 1, to_x)
    y_first = send_half(place, 0, to_y)
    late.append(push(bc_all.at[mine], bc_all.at[mine], partner))
    x_first.wait_recv()
    over_y = send_half(along_x, 0, to_y)
    y_second.wait_recv()
    over_x = send_half(along_y, 1, to_x)
    for copies, chip in (((x_second,), along_x), ((y_first,), along_y), ((over_x, over_y), across)):
        for copy in copies:
            copy.wait_recv()
        held = bc_all.at[2 * chip + core]
        late.append(push(held, held, partner))
    for copy in late:
        copy.wait_recv()
    for copy in started:
        copy.wait_send()
    own.wait()


def finish_all(piece, bc_sum, bulk):
    count = lax.axis_size("dp")
    places = 2 * GROUP
    pushes = 3 * (count - 1) + (places - 1) + (GROUP - 1) + 6 + GROUP
    shaped = jax.ShapeDtypeStruct
    blocks = (count, bc_sum.shape[0] // count, bc_sum.shape[1])
    return pl.pallas_call(
        finish_kernel,
        out_shape=[
            shaped((places,) + piece.shape, jnp.float32),
            shaped((places,) + blocks, jnp.bfloat16),
            shaped(bulk.shape, bulk.dtype),
        ],
        in_specs=vmem_specs(2) + any_specs(1),
        out_specs=vmem_specs(2) + any_specs(1),
        scratch_shapes=[
            pltpu.VMEM(bc_sum.shape, jnp.bfloat16),
            pltpu.VMEM(blocks, jnp.bfloat16),
            pltpu.VMEM(blocks, jnp.bfloat16),
            pltpu.VMEM((count,) + piece.shape, jnp.float32),
            pltpu.SemaphoreType.DMA,
            pltpu.SemaphoreType.DMA((pushes,)),
            pltpu.SemaphoreType.DMA((pushes,)),
        ],
        cost_estimate=lasting(30),
        compiler_params=pltpu.CompilerParams(
            collective_id=6, has_side_effects=True, vmem_limit_bytes=VMEM_BYTES
        ),
    )(piece, bc_sum, bulk)


def unpack_early_kernel(
    gu_ref,
    down_ref,
    out_ref,
    both_ref,
    both_out,
    gate_ref,
    up_ref,
    d_ref,
    mo_ref,
    ao_ref,
    input_ref,
    output_ref,
):
    units, width = down_ref.shape[2], HEADS * HP
    input_ref[...] = both_ref[0]
    output_ref[...] = both_out[0]
    gate_ref[...] = gu_ref[0, :, :units].astype(jnp.float32)
    up_ref[...] = gu_ref[0, :, units:].astype(jnp.float32)
    d_ref[...] = down_ref[0].astype(jnp.float32).T
    turned = out_ref[0].astype(jnp.float32).T
    mo_ref[...] = turned[:width]
    ao_ref[...] = turned[width:]


def unpack_kernel(
    in_ref,
    bc_ref,
    misc_ref,
    pieces_ref,
    z_ref,
    x_ref,
    q_ref,
    grad_bc_ref,
    k_ref,
    v_ref,
    dt_ref,
    conv_ref,
    bias_ref,
    dtb_ref,
    alog_ref,
    skip_ref,
    group_ref,
    one_ref,
    two_ref,
    sums_ref,
):
    width, part = HEADS * HP, HD // 4
    z_ref[...] = in_ref[0, :, :width].astype(jnp.float32)
    q_ref[...] = in_ref[0, :, width : width + HD].astype(jnp.float32)
    x_ref[...] = in_ref[0, :, width + HD : 2 * width + HD].astype(jnp.float32)
    wide = bc_ref.shape[2]
    for core in range(2):
        grad_bc_ref[wide * core : wide * (core + 1)] = bc_ref[core].astype(jnp.float32).T

    @pl.when(pl.program_id(0) == 0)
    def _():
        for index in range(2 * GROUP):
            piece = pieces_ref.shape[2]
            sums_ref[:, piece * index : piece * (index + 1)] = pieces_ref[index]
        held = [misc_ref[chip].astype(jnp.float32) for chip in range(GROUP)]
        k_ref[...] = jnp.concatenate(
            [
                held[0][:, :part],
                held[1][:, :part],
                held[0][:, part : 2 * part],
                held[1][:, part : 2 * part],
            ],
            axis=1,
        )
        v_ref[...] = jnp.concatenate([held[2][:, : 2 * part], held[3][:, : 2 * part]], axis=1)
        dt_ref[...] = jnp.concatenate(
            [values[:, DT_LANE : DT_LANE + HEADS] for values in held], axis=1
        ).T
        taps = conv_ref.shape[1]
        conv_ref[...] = sums_ref[:KC, :taps]
        for row in range(bias_ref.shape[0]):
            bias_ref[row : row + 1] = sums_ref[KC : KC + 1, 128 * row : 128 * (row + 1)]
        dtb_ref[...] = sums_ref[0:1, taps : taps + MH]
        alog_ref[...] = sums_ref[1:2, taps : taps + MH]
        skip_ref[...] = sums_ref[2:3, taps : taps + MH]
        start = taps + 128
        mine = GROUP * lax.axis_index("dp") + lax.axis_index("seq")
        slice_rows = one_ref.shape[1]
        each = slice_rows * GROUP * lax.axis_size("dp") // 8
        for ref in (one_ref, two_ref):
            gains = sums_ref[:, start : start + each]
            row = lax.broadcasted_iota(jnp.int32, (8, 1), 0)
            total = jnp.zeros((1, slice_rows), jnp.float32)
            for at in range(each // slice_rows):
                block = gains[:, slice_rows * at : slice_rows * (at + 1)]
                wanted = row * (each // slice_rows) + at == mine
                total = total + jnp.sum(jnp.where(wanted, block, 0.0), axis=0, keepdims=True)
            ref[...] = total
            start += each
        per_row = MH // 8
        for head in range(MH):
            row, lane = head // per_row, start + HP * (head % per_row)
            group_ref[head : head + 1, :] = sums_ref[row : row + 1, lane : lane + HP]


def across_chips(shape):
    return pl.BlockSpec((shape[0], shape[1] // GROUP), lambda chip: (0, chip))


def along_chips(shape):
    return pl.BlockSpec((shape[0] // GROUP, shape[1]), lambda chip: (chip, 0))


def per_chip(array, rows=1):
    return pl.BlockSpec((rows,) + array.shape[1:], lambda chip: (chip, 0, 0))


def unpack_early(gu, down, out, both, shapes):
    rows, width = both[0].shape[1:]
    step = 2 * rows // GROUP
    rows_in = pl.BlockSpec((1, step, width), lambda chip: (chip // 2, lax.rem(chip, 2), 0))
    kinds = [across_chips, across_chips, along_chips, along_chips, along_chips]
    out_shape = [jax.ShapeDtypeStruct(shape, jnp.float32) for shape in shapes]
    out_shape += [jax.ShapeDtypeStruct((2 * rows, width), array.dtype) for array in both]
    return pl.pallas_call(
        unpack_early_kernel,
        grid=(GROUP,),
        in_specs=[per_chip(gu), per_chip(down), per_chip(out), rows_in, rows_in],
        out_specs=[kind(shape) for kind, shape in zip(kinds, shapes)]
        + [along_chips((2 * rows, width))] * 2,
        out_shape=out_shape,
        cost_estimate=lasting(6),
        compiler_params=pltpu.CompilerParams(vmem_limit_bytes=VMEM_BYTES),
    )(gu, down, out, *both)


def unpack_late(in_all, bc_all, sums, shapes):
    def once(shape):
        return pl.BlockSpec(shape, lambda chip: (0,) * len(shape))

    misc_block = (GROUP, in_all.shape[1], HD)
    kinds = [across_chips] * 4
    kinds += [once] * (len(shapes) - len(kinds))
    return pl.pallas_call(
        unpack_kernel,
        grid=(GROUP,),
        in_specs=[
            per_chip(in_all),
            per_chip(bc_all, 2),
            pl.BlockSpec(misc_block, lambda chip: (0, 0, in_all.shape[2] // HD - 1)),
            once(sums.shape),
        ],
        out_specs=[kind(shape) for kind, shape in zip(kinds, shapes)],
        out_shape=[jax.ShapeDtypeStruct(shape, jnp.float32) for shape in shapes],
        scratch_shapes=[pltpu.VMEM((8, 2 * GROUP * sums.shape[2]), jnp.float32)],
        cost_estimate=lasting(6),
        compiler_params=pltpu.CompilerParams(vmem_limit_bytes=VMEM_BYTES),
    )(in_all, bc_all, in_all, sums)


def push_moves(moves, sources, targets, local_sems, send_sems, recv_sems, first=0):
    data, place, core, along_x, along_y, across = plane_place()
    copies = []
    for index, chip in enumerate((across, along_x, along_y)):
        for at, move in enumerate(moves):
            source, target = move(sources, targets, place, chip)
            slot = first + index * len(moves) + at
            copy = remote(
                source, target, send_sems.at[slot], recv_sems.at[slot], (data, chip, core)
            )
            copy.start()
            copies.append(copy)
    for at, move in enumerate(moves):
        source, target = move(sources, targets, place, place)
        copy = pltpu.make_async_copy(source, target, local_sems.at[at])
        copy.start()
        copies.append(copy)
    return copies


def plane_peers():
    data, place, core, along_x, along_y, across = plane_place()
    return [(data, chip, core) for chip in (across, along_x, along_y)]


def exchange_kernel(moves, count_in, *refs):
    sources, targets = refs[:count_in], refs[count_in:-3]
    meet(plane_peers())
    for copy in push_moves(moves, sources, targets, *refs[-3:]):
        copy.wait()


def first_exchange_kernel(
    moves,
    z_ref,
    q_ref,
    x_ref,
    key_ref,
    value_ref,
    dt_ref,
    one_ref,
    two_ref,
    in_ref,
    gains_ref,
    misc,
    gains,
    local_sems,
    send_sems,
    recv_sems,
):
    data, place, core, along_x, along_y, across = plane_place()
    places = GROUP * lax.axis_size("dp")
    mine = GROUP * data + place
    devices = []
    for turn_by in range(1, places):
        other = lax.rem(mine + turn_by, places)
        devices.append((other // GROUP, lax.rem(other, GROUP), core))
    half, part = HD // 2, HD // 4
    keys, values = key_ref[...], value_ref[...]
    steps = dt_ref[...].astype(jnp.float32).T.astype(keys.dtype)
    columns = (
        (keys[:, :part], keys[:, half : half + part]),
        (keys[:, part:half], keys[:, half + part :]),
        (values[:, :half],),
        (values[:, half:],),
    )
    for chip in range(GROUP):
        heads = steps[:, HEADS * chip : HEADS * (chip + 1)]
        rest = jnp.zeros((keys.shape[0], half - HEADS), keys.dtype)
        misc[chip] = jnp.concatenate([*columns[chip], heads, rest], axis=1)
    gains[...] = jnp.zeros_like(gains)
    gains[0:1] = one_ref[...].astype(jnp.float32)
    gains[1:2] = two_ref[...].astype(jnp.float32)
    meet(devices)
    sources = (z_ref, q_ref, x_ref, misc)
    copies = push_moves(moves, sources, (in_ref,), local_sems, send_sems, recv_sems)
    for index, device in enumerate(devices):
        slot = 3 * len(moves) + index
        copy = remote(
            gains, gains_ref.at[mine], send_sems.at[slot], recv_sems.at[slot], device
        )
        copy.start()
        copies.append(copy)
    gains_ref[mine] = gains[...]
    for copy in copies:
        copy.wait()


def first_exchange(moves, arrays, width_in):
    places = GROUP * lax.axis_size("dp")
    slice_rows = arrays[0].shape[0]
    count = 3 * len(moves) + places - 1
    return pl.pallas_call(
        partial(first_exchange_kernel, moves),
        out_shape=[
            jax.ShapeDtypeStruct((GROUP, slice_rows, width_in), jnp.bfloat16),
            jax.ShapeDtypeStruct((places, 8, slice_rows), jnp.float32),
        ],
        in_specs=any_specs(3) + vmem_specs(5),
        out_specs=any_specs(1) + vmem_specs(1),
        scratch_shapes=[
            pltpu.VMEM((GROUP, slice_rows, HD), jnp.bfloat16),
            pltpu.VMEM((8, slice_rows), jnp.float32),
            pltpu.SemaphoreType.DMA((len(moves),)),
            pltpu.SemaphoreType.DMA((count,)),
            pltpu.SemaphoreType.DMA((count,)),
        ],
        cost_estimate=lasting(20),
        compiler_params=pltpu.CompilerParams(collective_id=3, has_side_effects=True),
    )(*arrays)


def exchange_plane(moves, arrays, out_shapes, identity):
    count = 3 * len(moves)
    return pl.pallas_call(
        partial(exchange_kernel, moves, len(arrays)),
        out_shape=[jax.ShapeDtypeStruct(shape, jnp.bfloat16) for shape in out_shapes],
        in_specs=any_specs(len(arrays)),
        out_specs=any_specs(len(out_shapes)),
        scratch_shapes=[
            pltpu.SemaphoreType.DMA((len(moves),)),
            pltpu.SemaphoreType.DMA((count,)),
            pltpu.SemaphoreType.DMA((count,)),
        ],
        cost_estimate=lasting(25),
        compiler_params=pltpu.CompilerParams(collective_id=identity, has_side_effects=True),
    )(*arrays)


def column_move(source, target, start, width):
    def move(sources, targets, place, chip):
        columns = pl.ds(pl.multiple_of(chip * width, 128), width)
        return (
            sources[source].at[:, columns],
            targets[target].at[place, :, pl.ds(start, width)],
        )

    return move


def block_move(source, target):
    def move(sources, targets, place, chip):
        return (sources[source].at[chip], targets[target].at[place])

    return move


def misc_move(source, target, start):
    def move(sources, targets, place, chip):
        return (
            sources[source].at[chip],
            targets[target].at[place, :, pl.ds(start, 128)],
        )

    return move


def lane_masks():
    lane = lax.broadcasted_iota(jnp.int32, (1, 2 * HP), 1)
    return (lane < HP, lane >= HP)


DT_LANE = HP


def at_lane(lane, values):
    row = lax.broadcasted_iota(jnp.int32, (1, 2 * HP), 1)
    return jnp.where(row == lane, values, 0.0)


def dot_beside(exact, values, left_dim):
    width = values.shape[1]
    both = dot_f32(exact, jnp.concatenate(halves(values), axis=1), left_dim, 0)
    return both[:, :width] + both[:, width:]


def dot_along(left, right):
    left_high, left_low = halves(left)
    right_high, right_low = halves(right)
    return dot_f32(
        jnp.concatenate([left_high, left_high, left_low], axis=1),
        jnp.concatenate([right_high, right_low, right_high], axis=1),
        1,
        1,
    )


def spread_heads(*columns):
    width = HEADS * HP
    row = lax.rem(lax.broadcasted_iota(jnp.int32, (4 * HP, width), 0), 2 * HP)
    head = lax.broadcasted_iota(jnp.int32, (4 * HP, width), 1) // HP
    pick = jnp.where(row == DT_LANE + head, 1.0, 0.0).astype(jnp.bfloat16)
    parts = [jnp.concatenate(halves(values), axis=1) for values in columns]
    wide = dot_f32(jnp.concatenate(parts, axis=0), pick, 1, 0)
    size = columns[0].shape[0]
    return [wide[size * at : size * (at + 1)] for at in range(len(columns))]


def wide_keeps(keeps_ref):
    size = keeps_ref.shape[0]
    return [None] + [
        jnp.broadcast_to(keeps_ref[:, 1 + back : 2 + back], (size, 2 * HP))
        for back in range(1, KC)
    ]


def head_sums(values):
    low, high = lane_masks()
    first = jnp.sum(jnp.where(low, values, 0.0), axis=1, keepdims=True)
    second = jnp.sum(jnp.where(high, values, 0.0), axis=1, keepdims=True)
    return (first, second)


def head_means(values):
    low, high = lane_masks()
    first, second = head_sums(values)
    return jnp.where(low, first, second) * (1.0 / HP)


def stack_heads(values):
    low, high = lane_masks()
    zero = jnp.zeros_like(values)
    return jnp.concatenate([jnp.where(low, values, zero), jnp.where(high, values, zero)], axis=0)


def order_in(size):
    row = lax.broadcasted_iota(jnp.int32, (size, size), 0)
    column = lax.broadcasted_iota(jnp.int32, (size, size), 1)
    return (row, column)


def exact_sum(ones, values):
    high = values.astype(jnp.bfloat16)
    rest = values - high.astype(jnp.float32)
    middle = rest.astype(jnp.bfloat16)
    low = (rest - middle.astype(jnp.float32)).astype(jnp.bfloat16)
    return dot_f32(ones, high, 1, 0) + (dot_f32(ones, middle, 1, 0) + dot_f32(ones, low, 1, 0))


def chunk_decays(proj_ref, heads_ref, keeps_ref):
    size, width = proj_ref.shape
    raw = proj_ref[:, width - 2 * HP :] + heads_ref[0:1]
    dt_rows = jnp.maximum(raw, 0.0) + jnp.log1p(jnp.exp(-jnp.abs(raw)))
    row, column = order_in(size)
    lower = jnp.where(row >= column, 1.0, 0.0).astype(jnp.bfloat16)
    cumul = exact_sum(lower, -heads_ref[1:2] * dt_rows)
    enter = jnp.exp(cumul) * keeps_ref[:, 0:1]
    leave_bare = jnp.exp(cumul[size - 1 :] - cumul) * keeps_ref[:, 1:2]
    return (raw, dt_rows, cumul, enter, leave_bare)


def conv_windows(block, proj_ref, before_ref, bc_ref, bc_before_ref):
    if block < HEADS // 2:
        start = proj_ref.shape[1] - 2 * HP * (1 + HEADS // 2 - block)
        lanes = slice(start, start + 2 * HP)
        now, before = proj_ref[:, lanes], before_ref[:, lanes]
        now, before = now.astype(jnp.bfloat16), before.astype(jnp.bfloat16)
    else:
        start = 2 * HP * (block - HEADS // 2)
        lanes = slice(start, start + 2 * HP)
        now, before = bc_ref[:, lanes], bc_before_ref[8:, lanes]
    now, before = now.astype(jnp.float32), before.astype(jnp.float32)
    size = now.shape[0]
    extended = jnp.concatenate([before, now], axis=0)
    return [now] + [extended[8 - back : 8 - back + size] for back in range(1, KC)]


def conv_sum(windows, taps_ref, lanes, keeps):
    total = taps_ref[KC : KC + 1, lanes] + taps_ref[KC - 1 : KC, lanes] * windows[0]
    for back in range(1, KC):
        total = total + taps_ref[KC - 1 - back : KC - back, lanes] * (
            windows[back] * keeps[back]
        )
    return total


def head_decay(allowed, cumul, cumul_t, head):
    lane = DT_LANE + head
    differ = cumul[:, lane : lane + 1] - cumul_t[lane : lane + 1, :]
    return jnp.exp(jnp.where(allowed, differ, -jnp.inf))


def ssd_forward_kernel(
    proj_ref,
    before_ref,
    bc_ref,
    bc_before_ref,
    taps_ref,
    heads_ref,
    keeps_ref,
    segc_ref,
    segr_ref,
    skip_ref,
    gain_ref,
    cos_ref,
    sin_ref,
    gated_ref,
    ssm_ref,
    states_ref,
    mixed_ref,
    slope_ref,
    kv_ref,
    state,
):
    @pl.when(pl.program_id(0) == 0)
    def _():
        state[...] = jnp.zeros_like(state)

    size = proj_ref.shape[0]
    width = HEADS * HP
    keeps = wide_keeps(keeps_ref)
    for block in range(mixed_ref.shape[1] // (2 * HP)):
        lanes = slice(2 * HP * block, 2 * HP * (block + 1))
        windows = conv_windows(block, proj_ref, before_ref, bc_ref, bc_before_ref)
        summed = conv_sum(windows, taps_ref, lanes, keeps)
        sigmoid = jax.nn.sigmoid(summed)
        mixed_ref[:, lanes] = (summed * sigmoid).astype(jnp.bfloat16)
        slope_ref[:, lanes] = sigmoid * (1.0 + summed * (1.0 - sigmoid))
    raw, dt_rows, cumul, enter_all, leave_bare = chunk_decays(proj_ref, heads_ref, keeps_ref)
    enter_all, leave_all = spread_heads(enter_all, leave_bare * dt_rows)
    cumul_t, dt_t = cumul.T, dt_rows.T
    entry = state[...]
    states_ref[0] = entry
    b_rows, c_rows = mixed_ref[:, width : width + NS], mixed_ref[:, width + NS :]
    gram = dot_f32(c_rows, b_rows, 1, 1)
    row, column = order_in(size)
    allowed = (segc_ref[...] == segr_ref[0]) & (row >= column)
    entered = dot_beside(c_rows, entry, 1)
    weighted = []
    for pair in range(HEADS // 2):
        lanes = slice(2 * HP * pair, 2 * HP * (pair + 1))
        heads_x = mixed_ref[:, lanes]
        mixing = []
        for head in (2 * pair, 2 * pair + 1):
            lane = DT_LANE + head
            decay = head_decay(allowed, cumul, cumul_t, head)
            mixing.append(gram * decay * dt_t[lane : lane + 1, :])
        stacked = stack_heads(heads_x)
        out = dot_f32(
            jnp.concatenate(halves(jnp.concatenate(mixing, axis=1)), axis=1),
            jnp.concatenate([stacked, stacked], axis=0),
            1,
            0,
        )
        wide_x = heads_x.astype(jnp.float32)
        enter = enter_all[:, lanes]
        out = out + enter * entered[:, lanes] + skip_ref[:, lanes] * wide_x
        ssm_ref[:, lanes] = out
        gate = proj_ref[:, lanes]
        value = out * (gate * jax.nn.sigmoid(gate))
        scale = lax.rsqrt(head_means(value * value) + GROUP_EPSILON)
        gated_ref[:, lanes] = (value * scale * gain_ref[:, lanes]).astype(jnp.bfloat16)
        weighted.append(leave_all[:, lanes] * wide_x)
        state[:, lanes] = enter[size - 1 :, :] * entry[:, lanes]
    state[...] += dot_beside(b_rows, jnp.concatenate(weighted, axis=1), 0)
    kv = proj_ref[:, proj_ref.shape[1] - 2 * HP :][:, :HP]
    kv = jnp.concatenate([kv[: size // 2], kv[size // 2 :]], axis=1)
    kv_ref[...] = turn_folded(kv, cos_ref[...], sin_ref[...]).astype(jnp.bfloat16)


def ssd_backward_kernel(
    moves,
    proj_ref,
    slope_ref,
    bc_ref,
    taps_ref,
    heads_ref,
    keeps_ref,
    segc_ref,
    segr_ref,
    skip_ref,
    gain_ref,
    mixed_ref,
    ssm_ref,
    states_ref,
    dgated_ref,
    dq_ref,
    kv_own_ref,
    kv_x_ref,
    kv_y_ref,
    kv_a_ref,
    cos_ref,
    sin_ref,
    gu_ref,
    down_ref,
    dproj_ref,
    dtaps_ref,
    dheads_ref,
    dskip_ref,
    dgain_ref,
    gu_back,
    down_back,
    state,
    d_mixed,
    next_rows,
    *sems,
):
    def transfers(act):
        data, place, core, along_x, along_y, across = plane_place()
        sources, targets = (gu_ref, down_ref), (gu_back, down_back)
        local_sems, send_sems, recv_sems = sems
        for index, chip in enumerate((across, along_x, along_y)):
            for at, move in enumerate(moves):
                source, target = move(sources, targets, place, chip)
                slot = index * len(moves) + at
                act(
                    remote(
                        source, target, send_sems.at[slot], recv_sems.at[slot], (data, chip, core)
                    )
                )
        for at, move in enumerate(moves):
            source, target = move(sources, targets, place, place)
            act(pltpu.make_async_copy(source, target, local_sems.at[at]))

    @pl.when(pl.program_id(0) == 0)
    def _():
        meet(plane_peers())
        transfers(lambda copy: copy.start())
        state[...] = jnp.zeros_like(state)
        next_rows[...] = jnp.zeros_like(next_rows)
        dtaps_ref[...] = jnp.zeros_like(dtaps_ref)
        dheads_ref[...] = jnp.zeros_like(dheads_ref)
        dskip_ref[...] = jnp.zeros_like(dskip_ref)
        dgain_ref[...] = jnp.zeros_like(dgain_ref)

    size = proj_ref.shape[0]
    width = HEADS * HP
    raw, dt_rows, cumul, enter_all, leave_bare = chunk_decays(proj_ref, heads_ref, keeps_ref)
    cumul_t, dt_t = cumul.T, dt_rows.T
    later = state[...]
    entry = states_ref[0]
    carried = jnp.sum(later * entry, axis=0, keepdims=True)
    b_rows, c_rows = mixed_ref[:, width : width + NS], mixed_ref[:, width + NS :]
    gram = dot_f32(c_rows, b_rows, 1, 1)
    row, column = order_in(size)
    allowed = (segc_ref[...] == segr_ref[0]) & (row >= column)
    d_weighted = dot_beside(b_rows, later, 1)
    enter_all, bare_all, dt_all = spread_heads(enter_all, leave_bare, dt_rows)
    d_gram = jnp.zeros((size, size), jnp.float32)
    row_sums = jnp.zeros((size, 2 * HP), jnp.float32)
    column_sums = jnp.zeros((size, 2 * HP), jnp.float32)
    at_last = jnp.zeros((1, 2 * HP), jnp.float32)
    d_entered, weighted = [], []
    for pair in range(HEADS // 2):
        lanes = slice(2 * HP * pair, 2 * HP * (pair + 1))
        heads_x = mixed_ref[:, lanes]
        wide_x = heads_x.astype(jnp.float32)
        ssm, gate, gain = ssm_ref[:, lanes], proj_ref[:, lanes], gain_ref[:, lanes]
        d_gated = dgated_ref[:, lanes]
        sigmoid = jax.nn.sigmoid(gate)
        silu = gate * sigmoid
        value = ssm * silu
        scale = lax.rsqrt(head_means(value * value) + GROUP_EPSILON)
        dgain_ref[:, lanes] += jnp.sum(d_gated * value * scale, axis=0, keepdims=True)
        d_scaled = d_gated * gain
        d_value = scale * d_scaled - value * (scale * scale * scale) * head_means(d_scaled * value)
        d_out = d_value * silu
        dproj_ref[:, lanes] = (d_value * ssm * (sigmoid * (1.0 + gate * (1.0 - sigmoid)))).astype(
            jnp.bfloat16
        )
        dskip_ref[:, lanes] += jnp.sum(d_out * wide_x, axis=0, keepdims=True)
        enter, bare, dt_pair = enter_all[:, lanes], bare_all[:, lanes], dt_all[:, lanes]
        high, low = [stack_heads(half) for half in halves(d_out)]
        d_mixing = dot_f32(jnp.concatenate([high, low], axis=0), heads_x, 1, 1)
        grams = []
        for side in range(2):
            head = 2 * pair + side
            lane = DT_LANE + head
            decay = head_decay(allowed, cumul, cumul_t, head)
            grams.append(gram * decay)
            first = size * side
            d_mix = d_mixing[first : first + size] + d_mixing[2 * size + first : 3 * size + first]
            d_gram = d_gram + d_mix * (decay * dt_t[lane : lane + 1, :])
        gram_high, gram_low = halves(jnp.concatenate(grams, axis=0))
        bare_x = dot_f32(
            jnp.concatenate([high, low, high], axis=0),
            jnp.concatenate([gram_high, gram_high, gram_low], axis=0),
            0,
            0,
        ).T
        left = bare * d_weighted[:, lanes]
        d_x = bare_x + left
        first_lane = DT_LANE + 2 * pair
        first, second = head_sums(d_out * (ssm - skip_ref[:, lanes] * wide_x))
        row_sums = row_sums + at_lane(first_lane, first) + at_lane(first_lane + 1, second)
        first, second = head_sums(d_x * wide_x)
        column_sums = column_sums + at_lane(first_lane, first) + at_lane(first_lane + 1, second)
        last = jnp.sum(dt_pair * left * wide_x, axis=0, keepdims=True)
        last = last + carried[:, lanes] * enter[size - 1 :]
        first, second = head_sums(last)
        at_last = at_last + at_lane(first_lane, first) + at_lane(first_lane + 1, second)
        d_mixed[:, lanes] = dt_pair * d_x + skip_ref[:, lanes] * d_out
        d_entered.append(enter * d_out)
        weighted.append(bare * dt_pair * wide_x)
        state[:, lanes] = enter[size - 1 :, :] * later[:, lanes]
    d_entered = jnp.concatenate(d_entered, axis=1)
    state[...] += dot_beside(c_rows, d_entered, 0)
    d_gram_parts = halves(d_gram)
    d_b = dot_along(jnp.concatenate(weighted, axis=1), later)
    d_mixed[:, width : width + NS] = d_b + dot_f32(
        jnp.concatenate(d_gram_parts, axis=0),
        jnp.concatenate([c_rows, c_rows], axis=0),
        0,
        0,
    )
    d_c = dot_along(d_entered, entry)
    d_mixed[:, width + NS :] = d_c + dot_f32(
        jnp.concatenate(d_gram_parts, axis=1),
        jnp.concatenate([b_rows, b_rows], axis=0),
        1,
        0,
    )

    d_cumul = row_sums - column_sums * dt_rows
    last_row = lax.broadcasted_iota(jnp.int32, (size, 1), 0) == size - 1
    d_cumul = d_cumul + jnp.where(last_row, at_last, 0.0)
    upper = jnp.where(row <= column, 1.0, 0.0).astype(jnp.bfloat16)
    d_log = exact_sum(upper, d_cumul)
    rate = heads_ref[1:2]
    d_raw = (column_sums - rate * d_log) * jax.nn.sigmoid(raw)
    lane_row = lax.broadcasted_iota(jnp.int32, (1, 2 * HP), 1)
    d_raw = jnp.where((lane_row >= DT_LANE) & (lane_row < DT_LANE + HEADS), d_raw, 0.0)
    dheads_ref[0:1] += jnp.sum(d_raw, axis=0, keepdims=True)
    dheads_ref[1:2] += -rate * jnp.sum(d_log * dt_rows, axis=0, keepdims=True)
    total = proj_ref.shape[1]
    d_kv = kv_own_ref[...].astype(jnp.float32)
    for ref in (kv_x_ref, kv_y_ref, kv_a_ref):
        d_kv = d_kv + ref[...].astype(jnp.float32)
    d_kv = turn_folded(d_kv, cos_ref[...], -sin_ref[...])
    d_kv = jnp.concatenate([d_kv[:, :DT_LANE], d_kv[:, DT_LANE:]], axis=0)
    dproj_ref[:, total - 2 * HP : total] = jnp.concatenate(
        [d_kv, d_raw[:, DT_LANE:]], axis=1
    ).astype(jnp.bfloat16)
    dproj_ref[:, width : width + HD] = dq_ref[...]

    keeps = wide_keeps(keeps_ref)
    for block in range(mixed_ref.shape[1] // (2 * HP)):
        lanes = slice(2 * HP * block, 2 * HP * (block + 1))
        if block < HEADS // 2:
            start = total - 2 * HP * (1 + HEADS // 2 - block)
            pre = proj_ref[:, start : start + 2 * HP].astype(jnp.bfloat16).astype(jnp.float32)
        else:
            start = 2 * HP * (block - HEADS // 2)
            pre = bc_ref[:, start : start + 2 * HP].astype(jnp.float32)
        d_sum = d_mixed[:, lanes] * slope_ref[:, lanes]
        dtaps_ref[KC : KC + 1, lanes] += jnp.sum(d_sum, axis=0, keepdims=True)
        dtaps_ref[KC - 1 : KC, lanes] += jnp.sum(d_sum * pre, axis=0, keepdims=True)
        d_pre = taps_ref[KC - 1 : KC, lanes] * d_sum
        for back in range(1, KC):
            tap = KC - 1 - back
            kept = d_sum * keeps[back]
            extended = jnp.concatenate([kept, next_rows[back - 1, :, lanes]], axis=0)
            later_rows = extended[back : back + size]
            dtaps_ref[tap : tap + 1, lanes] += jnp.sum(later_rows * pre, axis=0, keepdims=True)
            d_pre = d_pre + taps_ref[tap : tap + 1, lanes] * later_rows
            next_rows[back - 1, :, lanes] = kept[:8]
        if block < HEADS // 2:
            start = total - 2 * HP * (1 + HEADS // 2 - block)
            dproj_ref[:, start : start + 2 * HP] = d_pre.astype(jnp.bfloat16)
        else:
            start = total + 2 * HP * (block - HEADS // 2)
            dproj_ref[:, start : start + 2 * HP] = d_pre.astype(jnp.bfloat16)

    @pl.when(pl.program_id(0) == pl.num_programs(0) - 1)
    def _():
        transfers(lambda copy: copy.wait())


def ssd_specs(length, reverse, width_in, width_all, width):
    laps = length // CHUNK

    def at(lap):
        return laps - 1 - lap if reverse else lap

    def tall(columns):
        return pl.BlockSpec((CHUNK, columns), lambda lap: (at(lap), 0))

    def rim(rows, columns):
        each = CHUNK // rows
        return pl.BlockSpec((rows, columns), lambda lap: (lax.rem(each * (at(lap) + laps) - 1, each * laps), 0))

    def whole(rows, columns):
        return pl.BlockSpec((rows, columns), lambda lap: (0, 0))

    def slab(rows, columns):
        return pl.BlockSpec((1, rows, columns), lambda lap: (at(lap), 0, 0))

    specs = [
        tall(width_in),
        rim(8, width_in),
        tall(2 * NS),
        rim(16, 2 * NS),
        whole(8, width_all),
        whole(8, 2 * HP),
        tall(8),
        tall(1),
        slab(1, CHUNK),
        whole(1, width),
        whole(1, width),
    ]
    return (laps, tall, whole, slab, specs)


def ssd_forward(arrays, cos_part, sin_part):
    length, width_in = arrays[0].shape
    width, width_all = HEADS * HP, HEADS * HP + 2 * NS
    laps, tall, whole, slab, specs = ssd_specs(length, False, width_in, width_all, width)
    shaped = jax.ShapeDtypeStruct
    fold = pl.BlockSpec((CHUNK // 2, 2 * HP), lambda lap: (lap, 0))
    return pl.pallas_call(
        ssd_forward_kernel,
        grid=(laps,),
        in_specs=specs + [fold, fold],
        out_specs=[
            tall(width),
            tall(width),
            slab(NS, width),
            tall(width_all),
            tall(width_all),
            fold,
        ],
        out_shape=[
            shaped((length, width), jnp.bfloat16),
            shaped((length, width), jnp.float32),
            shaped((laps, NS, width), jnp.float32),
            shaped((length, width_all), jnp.bfloat16),
            shaped((length, width_all), jnp.float32),
            shaped((length // 2, 2 * HP), jnp.bfloat16),
        ],
        scratch_shapes=[pltpu.VMEM((NS, width), jnp.float32)],
        cost_estimate=lasting(6),
        compiler_params=pltpu.CompilerParams(vmem_limit_bytes=VMEM_BYTES),
    )(*arrays, cos_part, sin_part)


def ssd_backward(arrays, slope, mixed, ssm, states, d_outs, d_query, d_kv_parts, tables, grads):
    length, width_in = arrays[0].shape
    width, width_all = HEADS * HP, HEADS * HP + 2 * NS
    laps, tall, whole, slab, specs = ssd_specs(length, True, width_in, width_all, width)
    shaped = jax.ShapeDtypeStruct
    moves = (block_move(0, 0), block_move(1, 1))
    fold = pl.BlockSpec((CHUNK // 2, 2 * HP), lambda lap: (laps - 1 - lap, 0))
    return pl.pallas_call(
        partial(ssd_backward_kernel, moves),
        grid=(laps,),
        in_specs=[specs[0], tall(width_all), specs[2], *specs[4:]]
        + [
            tall(width_all),
            tall(width),
            slab(NS, width),
            tall(width),
            tall(HD),
        ]
        + [fold] * 6
        + any_specs(2),
        out_specs=[
            tall(width_in + 2 * NS),
            whole(8, width_all),
            whole(8, 2 * HP),
            whole(1, width),
            whole(1, width),
        ]
        + any_specs(2),
        out_shape=[
            shaped((length, width_in + 2 * NS), jnp.bfloat16),
            shaped((8, width_all), jnp.float32),
            shaped((8, 2 * HP), jnp.float32),
            shaped((1, width), jnp.float32),
            shaped((1, width), jnp.float32),
        ]
        + [shaped(array.shape, array.dtype) for array in grads],
        scratch_shapes=[
            pltpu.VMEM((NS, width), jnp.float32),
            pltpu.VMEM((CHUNK, width_all), jnp.float32),
            pltpu.VMEM((KC - 1, 8, width_all), jnp.float32),
            pltpu.SemaphoreType.DMA((len(moves),)),
            pltpu.SemaphoreType.DMA((3 * len(moves),)),
            pltpu.SemaphoreType.DMA((3 * len(moves),)),
        ],
        cost_estimate=lasting(48),
        compiler_params=pltpu.CompilerParams(
            collective_id=13, has_side_effects=True, vmem_limit_bytes=VMEM_BYTES
        ),
    )(arrays[0], slope, arrays[2], *arrays[4:], mixed, ssm, states, d_outs, d_query, *d_kv_parts, *tables, *grads)


QUERY_ROWS = 256


def masked_scores(q_rows, k_ref, segc_ref, segr_ref, start, reach):
    rows = q_rows.shape[0]
    scores = dot_f32(q_rows, k_ref[:reach], 1, 1) * HD ** (-0.5)
    row = lax.broadcasted_iota(jnp.int32, (rows, reach), 0) + start
    column = lax.broadcasted_iota(jnp.int32, (rows, reach), 1)
    allowed = (segc_ref[start : start + rows] == segr_ref[:, :reach]) & (row >= column)
    return jnp.where(allowed, scores, -jnp.inf)


def rotate_rows(values, cos_ref, sin_ref, sign):
    return values * cos_ref[...] + sign * (pltpu.roll(values, HD // 2, 1) * sin_ref[...])


def swap_middle(values):
    lane = lax.broadcasted_iota(jnp.int32, (1, HD), 1) // (HD // 4)
    up = pltpu.roll(values, HD // 4, 1)
    down = pltpu.roll(values, HD - HD // 4, 1)
    return jnp.where(lane == 1, down, jnp.where(lane == 2, up, values))


def unfold_rows(values, write):
    step, columns = CHUNK // 2, values.shape[1] // 2
    for start in range(0, values.shape[0], step):
        rows = values[start : start + step]
        write(2 * start, rows[:, :columns])
        write(2 * start + step, rows[:, columns:])


def fold_rows(ref, index, values):
    step = CHUNK // 2
    for start in range(0, values.shape[0] // 2, step):
        ref[index, start : start + step] = jnp.concatenate(
            [values[2 * start : 2 * start + step], values[2 * start + step : 2 * start + 2 * step]],
            axis=1,
        ).astype(ref.dtype)


def join_halves(ref, first, target):
    half = HD // 2

    def write_at(lanes):
        def write(start, rows):
            target[start : start + rows.shape[0], lanes] = rows

        return write

    unfold_rows(ref[first], write_at(slice(0, half)))
    unfold_rows(ref[first + 1], write_at(slice(half, HD)))


def attend_forward_kernel(
    raw_ref, cos_ref, sin_ref, kv_ref, segc_ref, segr_ref, out_ref, total_ref, q_ref, k_ref, v_ref
):
    q_ref[...] = swap_middle(rotate_rows(raw_ref[...], cos_ref, sin_ref, 1.0)).astype(jnp.bfloat16)
    join_halves(kv_ref, 0, k_ref)
    join_halves(kv_ref, 2, v_ref)
    for start in range(0, q_ref.shape[0], QUERY_ROWS):
        reach = start + QUERY_ROWS
        rows = slice(start, reach)
        scores = masked_scores(q_ref[rows], k_ref, segc_ref, segr_ref, start, reach)
        top = jnp.max(scores, axis=1, keepdims=True)
        powers = jnp.exp(scores - top)
        total = jnp.sum(powers, axis=1, keepdims=True)
        probs = (powers * (1.0 / total)).astype(jnp.bfloat16)
        out_ref[rows] = dot_f32(probs, v_ref[:reach], 1, 0).astype(jnp.bfloat16)
        total_ref[rows] = top + jnp.log(total)


def attend_backward_kernel(
    q_ref,
    k_ref,
    v_ref,
    cos_ref,
    sin_ref,
    segc_ref,
    segr_ref,
    total_ref,
    dout_ref,
    dq_ref,
    dkv_ref,
    dq_sum,
    dk_sum,
    dv_sum,
):
    dk_sum[...] = jnp.zeros_like(dk_sum)
    dv_sum[...] = jnp.zeros_like(dv_sum)
    for start in range(0, q_ref.shape[0], QUERY_ROWS):
        reach = start + QUERY_ROWS
        rows = slice(start, reach)
        q_rows, d_out = q_ref[rows], dout_ref[rows]
        scores = masked_scores(q_rows, k_ref, segc_ref, segr_ref, start, reach)
        probs = jnp.exp(scores - total_ref[rows])
        d_probs = dot_f32(d_out, v_ref[:reach], 1, 1)
        delta = jnp.sum(probs * d_probs, axis=1, keepdims=True)
        d_scores = (probs * (d_probs - delta)).astype(jnp.bfloat16)
        dq_sum[rows] = dot_f32(d_scores, k_ref[:reach], 1, 0) * HD ** (-0.5)
        dk_sum[:reach] += dot_f32(d_scores, q_rows, 0, 0) * HD ** (-0.5)
        dv_sum[:reach] += dot_f32(probs.astype(jnp.bfloat16), d_out, 0, 0)
    dq_ref[...] = rotate_rows(swap_middle(dq_sum[...]), cos_ref, sin_ref, -1.0).astype(jnp.bfloat16)
    half = HD // 2
    fold_rows(dkv_ref, 0, dk_sum[:, :half])
    fold_rows(dkv_ref, 1, dk_sum[:, half:])
    fold_rows(dkv_ref, 2, dv_sum[:, :half])
    fold_rows(dkv_ref, 3, dv_sum[:, half:])


def rotation_tables(length):
    half, part = HD // 2, HD // 4
    frequency = np.float32(ROPE_BASE) ** (
        np.float32(-2.0) * np.arange(half).astype(np.float32) / np.float32(HD)
    )
    angles = np.arange(length).astype(np.float32)[:, None] * frequency[None, :]
    cosine, sine_part = np.cos(angles), np.sin(angles)

    def folded(values):
        rows = values.reshape(length // CHUNK, 2, CHUNK // 2, half)
        return rows.transpose(0, 2, 1, 3).reshape(length // 2, HD)

    cos_kinds, sin_kinds = [], []
    for start in (0, part):
        columns = slice(start, start + part)
        cos_part, sin_part = cosine[:, columns], sine_part[:, columns]
        cos_kinds.append(folded(np.concatenate([cos_part, cos_part], axis=1)))
        sin_kinds.append(folded(np.concatenate([-sin_part, sin_part], axis=1)))
    cos_kinds.append(np.ones_like(cos_kinds[0]))
    sin_kinds.append(np.zeros_like(sin_kinds[0]))
    tables = (
        np.concatenate([cosine, cosine], axis=1),
        np.concatenate([-sine_part, sine_part], axis=1),
        np.stack(cos_kinds),
        np.stack(sin_kinds),
    )
    return [jnp.asarray(table.astype(np.float32)) for table in tables]


def turn_folded(values, cosine, sine_part):
    lane = lax.rem(lax.broadcasted_iota(jnp.int32, (1, HD), 1), HD // 2)
    quarter = HD // 4
    other = jnp.where(
        lane < quarter, pltpu.roll(values, HD - quarter, 1), pltpu.roll(values, quarter, 1)
    )
    return values * cosine + other * sine_part


def whole_block(shape):
    return pl.BlockSpec(shape, lambda step: (0,) * len(shape))


def attend(kernel, arrays, out_shapes, scratch=(), blocks=None):
    return pl.pallas_call(
        kernel,
        grid=(1,),
        in_specs=[
            whole_block(array.shape) if blocks is None or blocks[at] is None else blocks[at]
            for at, array in enumerate(arrays)
        ],
        out_specs=[whole_block(shape) for shape, _ in out_shapes],
        out_shape=[jax.ShapeDtypeStruct(shape, dtype) for shape, dtype in out_shapes],
        scratch_shapes=[pltpu.VMEM(shape, dtype) for shape, dtype in scratch],
        cost_estimate=lasting(9),
        compiler_params=pltpu.CompilerParams(vmem_limit_bytes=VMEM_BYTES),
    )(*arrays)


def after(value, *earlier):
    return lax.optimization_barrier((value,) + earlier)[0]


def over_chips(block):
    place = lax.axis_index("seq")
    count = lax.axis_size("seq")
    stacked = jnp.zeros((count,) + block.shape, block.dtype)
    stacked = lax.dynamic_update_index_in_dim(stacked, block, place, 0)
    for mask in range(1, count):
        moved = lax.ppermute(block, "seq", [(i, i ^ mask) for i in range(count)])
        stacked = lax.dynamic_update_index_in_dim(stacked, moved, place ^ mask, 0)
    return stacked


def from_chips(blocks):
    place = lax.axis_index("seq")
    count = lax.axis_size("seq")
    moved = [lax.dynamic_index_in_dim(blocks, place, 0, False)]
    for mask in range(1, count):
        block = lax.dynamic_index_in_dim(blocks, place ^ mask, 0, False)
        moved.append(lax.ppermute(block, "seq", [(i, i ^ mask) for i in range(count)]))
    return moved


def heads_local_plan(
    hidden_in,
    teacher,
    segment_ids,
    valid_mask,
    norm1_gain,
    w_z,
    w_x,
    w_bc,
    w_dt,
    conv_weight,
    conv_bias,
    dt_bias,
    a_log,
    d_skip,
    group_gain,
    w_mamba_out,
    w_query,
    w_key,
    w_value,
    w_attn_out,
    norm2_gain,
    w_gate,
    w_up,
    w_down,
):
    place, core, data_rank = (
        lax.axis_index("seq"),
        lax.axis_index("tensor"),
        lax.axis_index("dp"),
    )
    data_count = lax.axis_size("dp")
    chip_rows, width = hidden_in.shape[1:]
    own_rows = chip_rows // 2
    length = segment_ids.shape[1]
    slice_rows = w_z.shape[0]
    width_x = HEADS * HP
    hidden_units = w_gate.shape[1] // GROUP
    segment = segment_ids[0]
    own_start = place * chip_rows + core * own_rows
    token_count = jnp.sum(valid_mask).astype(jnp.float32)
    mask_rows = lax.dynamic_slice(valid_mask, (data_rank, own_start), (1, own_rows))[0]
    total_tokens = float(valid_mask.shape[0] * valid_mask.shape[1])
    bf16 = jnp.bfloat16

    half, part = HD // 2, HD // 4
    width_in = 2 * width_x + 2 * HD
    in_slices, gains_all = first_exchange(
        (
            column_move(0, 0, 0, width_x),
            column_move(1, 0, width_x, HD),
            column_move(2, 0, width_x + HD, width_x),
            misc_move(3, 0, 2 * width_x + HD),
        ),
        (w_z, w_query, w_x, w_key, w_value, w_dt.T, norm1_gain[None], norm2_gain[None]),
        width_in,
    )
    gain_one, gain_two = gains_all[:, 0].reshape(width), gains_all[:, 1].reshape(width)
    full_in = lax.all_gather(in_slices, "dp", axis=0, tiled=True).reshape(width, width_in)
    hidden_own = lax.dynamic_slice(hidden_in[0], (core * own_rows, 0), (own_rows, width))
    hidden_own = after(hidden_own, in_slices)
    hidden_all, normed, pre_bc = gather_plane(
        hidden_own,
        1,
        apply_norm,
        (gain_one[None], w_bc),
        (((length, width), bf16), ((length, 2 * NS), bf16)),
    )
    hidden_low, hidden_own = hidden_own, hidden_own.astype(jnp.float32)
    width_out = width_x + HD
    out_slices, gu_slices, down_slices = exchange_plane(
        (
            column_move(0, 0, 0, width_x),
            column_move(1, 0, width_x, HD),
            column_move(2, 1, 0, hidden_units),
            column_move(3, 1, hidden_units, hidden_units),
            column_move(4, 2, 0, hidden_units),
        ),
        (after(w_mamba_out.T, normed), w_attn_out.T, w_gate, w_up, w_down.T),
        [
            (GROUP, slice_rows, width_out),
            (GROUP, slice_rows, 2 * hidden_units),
            (GROUP, slice_rows, hidden_units),
        ],
        4,
    )
    out_gathered = lax.all_gather(after(out_slices, full_in), "dp", axis=0, tiled=True)
    full_out = out_gathered.reshape(width, width_out)

    segment, conv_weight, conv_bias, dt_bias, a_log, d_skip, group_gain = (
        lax.optimization_barrier(
            (segment, conv_weight, conv_bias, dt_bias, a_log, d_skip, group_gain, out_slices)
        )[:7]
    )
    seg_column, seg_row = segment[:, None], segment[None, :]
    cos_wide, sin_wide, cos_folded, sin_folded = rotation_tables(length)
    kind = jnp.minimum(place, 2)
    cos_folded = lax.dynamic_index_in_dim(cos_folded, kind, 0, False)
    sin_folded = lax.dynamic_index_in_dim(sin_folded, kind, 0, False)
    head_start = core * (MH // 2) + place * HEADS

    def local_rows(values, width_head):
        return jnp.concatenate(
            [
                lax.dynamic_slice_in_dim(values, head_start * width_head, HEADS * width_head, 0),
                values[MH * width_head :],
            ],
            axis=0,
        )

    taps = jnp.concatenate(
        [local_rows(conv_weight, HP).T, local_rows(conv_bias, HP)[None]], axis=0
    )
    taps = jnp.pad(taps, ((0, 8 - KC - 1), (0, 0)))
    rate = jnp.exp(local_rows(a_log, 1))
    head_rows = jnp.stack([local_rows(dt_bias, 1), rate])
    head_rows = jnp.pad(head_rows, ((0, 6), (DT_LANE, HD - DT_LANE - HEADS)))
    skip_row = jnp.repeat(local_rows(d_skip, 1), HP)[None, :]
    gain_row = lax.dynamic_slice_in_dim(group_gain, head_start, HEADS, 0).reshape(1, width_x)
    laps = length // CHUNK
    seg_laps = segment.reshape(laps, CHUNK)
    seg_last = seg_laps[:, -1:]
    seg_before = jnp.concatenate([jnp.full((1, 1), -1, jnp.int32), seg_last[:-1]])
    seg_ext = jnp.concatenate([jnp.full((KC - 1,), -1, jnp.int32), segment])
    keeps = [(seg_laps == seg_before).reshape(length), (seg_laps == seg_last).reshape(length)]
    keeps += [seg_ext[KC - 1 - back : KC - 1 - back + length] == segment for back in range(1, KC)]
    keeps = jnp.stack(keeps + [jnp.zeros((length,), bool)] * 3, axis=1).astype(jnp.float32)

    projected = mat_dot(normed, full_in)

    ssd_arrays = (
        projected,
        projected,
        pre_bc,
        pre_bc,
        taps,
        head_rows,
        keeps,
        seg_column,
        seg_laps[:, None, :],
        skip_row,
        gain_row,
    )
    gated, ssm, states, mixed, slope, kv_own = ssd_forward(ssd_arrays, cos_folded, sin_folded)
    kv_all = over_chips(kv_own)
    gu_gathered = lax.all_gather(after(gu_slices, out_gathered, gated), "dp", axis=0, tiled=True)
    down_gathered = lax.all_gather(after(down_slices, gu_gathered), "dp", axis=0, tiled=True)
    full_gu = gu_gathered.reshape(width, 2 * hidden_units)
    full_down = down_gathered.reshape(width, hidden_units)
    attended, log_total, queries, keys, vals = attend(
        attend_forward_kernel,
        (
            projected,
            cos_wide,
            sin_wide,
            after(kv_all, out_gathered),
            seg_column,
            seg_row,
        ),
        (
            ((length, HD), bf16),
            ((length, 1), jnp.float32),
            ((length, HD), bf16),
            ((length, HD), bf16),
            ((length, HD), bf16),
        ),
        blocks=[pl.BlockSpec((length, HD), lambda step: (0, width_x // HD))] + [None] * 5,
    )
    outs = jnp.concatenate([gated, attended], axis=1)
    middle = hidden_own + scatter_plane(outs, full_out, 2)[0]

    scale_two = lax.rsqrt(jnp.mean(middle * middle, axis=-1, keepdims=True) + EPSILON)
    normed_two, gate_up, activated = gather_plane(
        after((middle * scale_two * gain_two).astype(bf16), gu_gathered),
        9,
        apply_gate_up,
        (full_gu,),
        (((length, 2 * hidden_units), jnp.float32), ((length, hidden_units), bf16)),
    )
    teacher_own = lax.dynamic_slice(teacher[0], (core * own_rows, 0), (own_rows, width))
    factor = 2.0 * total_tokens / token_count * mask_rows.astype(jnp.float32)[:, None]
    block_out, d_out, d_gate_up, grad_down = down_and_back(
        activated, full_down, middle, teacher_own, factor, gate_up
    )

    def sum_rows(grads):
        summed = lax.psum_scatter(grads.astype(bf16), "dp", scatter_dimension=0, tiled=True)
        return summed.reshape(GROUP, slice_rows, grads.shape[1])

    grad_down = sum_rows(grad_down)
    d_normed_two, grad_gate_up = up_back(d_gate_up, full_gu, normed_two)
    grad_gate_up = sum_rows(after(grad_gate_up, grad_down))
    grad_gain_two = jnp.sum(d_normed_two * middle * scale_two, axis=0)
    d_scaled = d_normed_two * gain_two
    d_middle = (
        d_out
        + scale_two * d_scaled
        - middle * scale_two**3 * jnp.mean(d_scaled * middle, axis=-1, keepdims=True)
    )
    d_branch, d_gated, d_attended = gather_plane(
        after(d_middle.astype(bf16), grad_down),
        12,
        apply_out_back,
        (full_out,),
        (((length, width_x), jnp.float32), ((length, HD), bf16)),
    )
    d_query, d_kv = attend(
        attend_backward_kernel,
        (
            queries,
            keys,
            vals,
            cos_wide,
            sin_wide,
            seg_column,
            seg_row,
            log_total,
            d_attended,
        ),
        (((length, HD), bf16), ((GROUP, length // 2, HD), bf16)),
        (((length, HD), jnp.float32),) * 3,
    )
    d_kv_parts = from_chips(d_kv)
    grad_out = sum_rows(
        after(dot_left_t(d_branch, outs).astype(bf16), grad_gate_up, d_query)
    )
    (
        d_projected,
        grad_taps,
        grad_heads,
        d_skip_lanes,
        d_gain_lanes,
        back_gate_up,
        back_down,
    ) = ssd_backward(
        ssd_arrays,
        slope,
        mixed,
        ssm,
        states,
        d_gated,
        d_query,
        d_kv_parts,
        (cos_folded, sin_folded),
        (grad_gate_up, grad_down),
    )
    grad_skip = jnp.sum(d_skip_lanes.reshape(HEADS, HP), axis=-1)
    grad_group = d_gain_lanes.reshape(HEADS, HP)
    grad_in = sum_rows(
        after(dot_left_t(normed, d_projected[:, :width_in]).astype(bf16), grad_out)
    )
    bc_cols = 2 * NS // GROUP
    grad_input, bc_sum, gain_sums = input_back(
        after(d_projected, grad_out),
        full_in,
        normed,
        w_bc,
        hidden_low,
        d_middle,
        gain_one[None],
        bc_cols,
    )
    grad_gain_one = jnp.sum(gain_sums, axis=0)

    taps_all = jnp.concatenate(
        [
            lax.dynamic_update_slice(
                jnp.zeros((8, MH * HP), jnp.float32), grad_taps[:, :width_x], (0, head_start * HP)
            ),
            grad_taps[:, width_x:],
        ],
        axis=1,
    )
    heads_all = lax.dynamic_update_slice(
        jnp.zeros((8, 128), jnp.float32),
        jnp.concatenate([grad_heads[:2, DT_LANE : DT_LANE + HEADS], grad_skip[None]]),
        (0, head_start),
    )
    group_all = lax.dynamic_update_slice(
        jnp.zeros((MH, HP), jnp.float32), grad_group, (head_start, 0)
    )
    small = [taps_all, heads_all]
    small += [
        values.reshape(8, -1) for values in (grad_gain_one, grad_gain_two, group_all)
    ]
    small = jnp.concatenate(small, axis=1)
    small_width = -(-small.shape[1] // (2 * GROUP * 128)) * 2 * GROUP * 128
    small = jnp.pad(small, ((0, 0), (0, small_width - small.shape[1])))
    piece, both_input, both_output, back_out = plane_sum(small, grad_input, block_out, grad_out)
    grad_gate, grad_up, grad_down, grad_mo, grad_ao, grad_input, block_out = unpack_early(
        back_gate_up,
        back_down,
        back_out,
        (both_input, both_output),
        [array.shape for array in (w_gate, w_up, w_down, w_mamba_out, w_attn_out)],
    )
    small_all, bc_all, back_in = finish_all(after(piece, grad_input), bc_sum, grad_in)
    bc_all = bc_all.reshape(2 * GROUP, bc_cols, width // 2)
    shapes = [
        array.shape
        for array in (w_z, w_x, w_query, w_bc, w_key, w_value, w_dt.T, conv_weight.T)
    ]
    shapes += [(conv_bias.shape[0] // 128, 128)] + [(1, MH)] * 3 + [(MH, HP)] + [(1, slice_rows)] * 2
    (
        grad_z,
        grad_x,
        grad_q,
        grad_bc,
        grad_k,
        grad_v,
        grad_dt,
        grad_conv,
        grad_bias,
        grad_dtb,
        grad_alog,
        grad_skip,
        grad_group,
        grad_one,
        grad_two,
    ) = unpack_late(back_in, bc_all, small_all, shapes)
    return (
        block_out[None],
        grad_input[None],
        grad_one[0],
        grad_z,
        grad_x,
        grad_bc,
        grad_dt.T,
        grad_conv.T,
        grad_bias.reshape(-1),
        grad_dtb[0],
        grad_alog[0],
        grad_skip[0],
        grad_group,
        grad_mo,
        grad_q,
        grad_k,
        grad_v,
        grad_ao,
        grad_two[0],
        grad_gate,
        grad_up,
        grad_down,
    )


def solution(mesh):
    placed = (
        P("dp", "seq", None),
        P("dp", "seq", None),
        P("dp", None),
        P(),
        P(("dp", "seq")),
        P(("dp", "seq"), "tensor"),
        P(("dp", "seq"), "tensor"),
        P(),
        P(("dp", "seq"), "tensor"),
        P(),
        P(),
        P(),
        P(),
        P(),
        P(),
        P("tensor", ("dp", "seq")),
        P(("dp", "seq"), "tensor"),
        P(("dp", "seq"), "tensor"),
        P(("dp", "seq"), "tensor"),
        P("tensor", ("dp", "seq")),
        P(("dp", "seq")),
        P(("dp", "seq"), "tensor"),
        P(("dp", "seq"), "tensor"),
        P("tensor", ("dp", "seq")),
    )
    whole_row = mesh.shape["seq"] == GROUP and mesh.shape["tensor"] == 2
    return jax.shard_map(
        heads_local_plan if whole_row else local,
        mesh=mesh,
        in_specs=placed,
        out_specs=(
            P("dp", "seq", None),
            P("dp", "seq", None),
            P(("dp", "seq")),
            P(("dp", "seq"), "tensor"),
            P(("dp", "seq"), "tensor"),
            P(),
            P(("dp", "seq"), "tensor"),
            P(),
            P(),
            P(),
            P(),
            P(),
            P(),
            P("tensor", ("dp", "seq")),
            P(("dp", "seq"), "tensor"),
            P(("dp", "seq"), "tensor"),
            P(("dp", "seq"), "tensor"),
            P("tensor", ("dp", "seq")),
            P(("dp", "seq")),
            P(("dp", "seq"), "tensor"),
            P(("dp", "seq"), "tensor"),
            P("tensor", ("dp", "seq")),
        ),
        check_vma=False,
    )
```

```python
from functools import partial

import jax
import jax.numpy as jnp
import numpy as np
from jax import lax
from jax.experimental import pallas as pl
from jax.experimental.pallas import tpu as pltpu
from jax.sharding import PartitionSpec as P

MH = 48
HP = 64
NS = 256
KC = 4
HD = 128


EPSILON = 1e-06
GROUP_EPSILON = 1e-05
ROPE_BASE = 10000.0
HIGHEST = lax.Precision.HIGHEST


def shifted(block, axis, distance):
    devices = range(lax.axis_size(axis))
    route = [(i - distance, i) for i in devices if i - distance in devices]
    return lax.ppermute(block, axis, route)


def carried_in(part, axis, combine, identity, reverse):
    count = lax.axis_size(axis)
    place = lax.axis_index(axis)
    ahead = count - 1 - place if reverse else place
    gathered = jax.tree.map(lambda a: lax.all_gather(a, axis), part)
    state = jax.tree.map(lambda a, e: jnp.zeros_like(a) + jnp.asarray(e, a.dtype), part, identity)

    def one(lap, state):
        source = count - 1 - lap if reverse else lap
        return combine(
            state, jax.tree.map(lambda a: lax.dynamic_index_in_dim(a, source, 0, False), gathered)
        )

    return lax.fori_loop(0, ahead, one, state)


def mat_dot(left_side, right_side):
    return jnp.dot(left_side, right_side, preferred_element_type=jnp.float32)


def dot_left_t(left_side, right_side):
    return lax.dot_general(
        left_side, right_side, (((0,), (0,)), ((), ())), preferred_element_type=jnp.float32
    )


def dot_right_t(left_side, right_side):
    return lax.dot_general(
        left_side, right_side, (((1,), (1,)), ((), ())), preferred_element_type=jnp.float32
    )


def rms_norm(values, gain_row):
    scale_row = lax.rsqrt(jnp.mean(values * values, axis=-1, keepdims=True) + EPSILON)
    return values * scale_row * gain_row


def rotate(positions, values):
    half_dim = values.shape[-1] // 2
    frequency = ROPE_BASE ** (-2.0 * jnp.arange(half_dim).astype(jnp.float32) / values.shape[-1])
    angles = positions.astype(jnp.float32)[:, None] * frequency[None, :]
    cosine = jnp.cos(angles)[:, None, :]
    sine_part = jnp.sin(angles)[:, None, :]
    first_half = values[..., :half_dim]
    second = values[..., half_dim:]
    return jnp.concatenate(
        [first_half * cosine - second * sine_part, second * cosine + first_half * sine_part],
        axis=-1,
    )


def conv_silu(seg_ext, seg_rows, extended, weights, bias_row):
    size_rows = seg_rows.shape[0]
    summed = jnp.zeros((size_rows, weights.shape[0]), jnp.float32) + bias_row[None, :]
    for tap_index in range(weights.shape[1]):
        window = lax.slice_in_dim(extended, tap_index, tap_index + size_rows, axis=0)
        keep_mask = (
            lax.slice_in_dim(seg_ext, tap_index, tap_index + size_rows) == seg_rows
        ).astype(jnp.float32)
        summed = summed + window * weights[:, tap_index][None, :] * keep_mask[:, None]
    return jax.nn.silu(summed)


def group_gate(ssm_out, gate_z, group_gain):
    mixed_val = ssm_out * jax.nn.silu(gate_z)
    return (
        mixed_val
        * lax.rsqrt(jnp.mean(mixed_val * mixed_val, axis=-1, keepdims=True) + GROUP_EPSILON)
        * group_gain[None]
    )


def swiglu(gate_pre, up_pre):
    return jax.nn.silu(gate_pre) * up_pre


def split_mixed(mixed_in, heads_local):
    size_rows = mixed_in.shape[0]
    width_x = heads_local * HP
    heads_x = mixed_in[:, :width_x].reshape(size_rows, heads_local, HP)
    return (heads_x, mixed_in[:, width_x : width_x + NS], mixed_in[:, width_x + NS :])


def ssd_main(seg_rows, seg_before, mixed_in, dt_raw, dt_bias_row, a_log_row, d_skip_row):
    size_rows = seg_rows.shape[0]
    heads_x, b_rows, c_rows = split_mixed(mixed_in, dt_raw.shape[1])
    dt_rows = jax.nn.softplus(dt_raw + dt_bias_row[None, :])
    cumul = jnp.cumsum(-jnp.exp(a_log_row)[None, :] * dt_rows, axis=0)
    order_pos = jnp.arange(size_rows)
    allowed = (seg_rows[:, None] == seg_rows[None, :]) & (order_pos[:, None] >= order_pos[None, :])
    differ = cumul[:, None, :] - cumul[None, :, :]
    decay = jnp.exp(jnp.where(allowed[:, :, None], differ, -jnp.inf))
    gram = jnp.dot(c_rows, b_rows.T, precision=HIGHEST, preferred_element_type=jnp.float32)
    mixing = gram[:, :, None] * decay * dt_rows[None, :, :]
    outputs = jnp.einsum("tsh,shp->thp", mixing, heads_x, precision=HIGHEST)
    outputs = outputs + d_skip_row[None, :, None] * heads_x
    tail_keep = (seg_rows == seg_rows[-1]).astype(jnp.float32)
    tail_weight = jnp.exp(cumul[-1][None, :] - cumul) * tail_keep[:, None] * dt_rows
    local_state = jnp.einsum("sh,shp,sn->hpn", tail_weight, heads_x, b_rows, precision=HIGHEST)
    carry_factor = jnp.exp(cumul[-1]) * (seg_rows[-1] == seg_before).astype(jnp.float32)
    return (outputs, carry_factor, local_state)


def ssd_state(seg_rows, seg_before, mixed_in, dt_raw, dt_bias_row, a_log_row, entry_state):
    heads_x, b_rows, c_rows = split_mixed(mixed_in, dt_raw.shape[1])
    dt_rows = jax.nn.softplus(dt_raw + dt_bias_row[None, :])
    cumul = jnp.cumsum(-jnp.exp(a_log_row)[None, :] * dt_rows, axis=0)
    entry_keep = (seg_rows == seg_before).astype(jnp.float32)
    entry_part = jnp.einsum("tn,hpn->thp", c_rows, entry_state, precision=HIGHEST)
    return jnp.exp(cumul)[:, :, None] * entry_keep[:, None, None] * entry_part


def chain_states(earlier, later):
    return (earlier[0] * later[0], later[0][:, None, None] * earlier[1] + later[1])


def block_scores(queries, keys_all, vals_all, seg_full, query_pos, seg_query, block_index, key_len):
    key_blk = keys_all[block_index * key_len : (block_index + 1) * key_len]
    val_blk = vals_all[block_index * key_len : (block_index + 1) * key_len]
    seg_key = seg_full[block_index * key_len : (block_index + 1) * key_len]
    key_pos = block_index * key_len + jnp.arange(key_len)
    scores = jnp.einsum(
        "tkgd,skd->kgts", queries, key_blk, preferred_element_type=jnp.float32
    ) * HD ** (-0.5)
    allowed = (query_pos[:, None] >= key_pos[None, :]) & (seg_query[:, None] == seg_key[None, :])
    return (key_blk, val_blk, jnp.where(allowed[None, None], scores, -jnp.inf))


def attend_forward(queries, keys_all, vals_all, seg_full, query_pos, seg_query, block_count):
    key_len = keys_all.shape[0] // block_count
    stat_shape = (queries.shape[1], queries.shape[2], queries.shape[0])
    running_max = jnp.full(stat_shape, -1e30, jnp.float32)
    running_sum = jnp.zeros(stat_shape, jnp.float32)
    for block_index in range(block_count):
        needed = block_index * key_len <= query_pos[-1]

        def stat_step(stats, block_index=block_index):
            old_max, old_sum = stats
            key_blk, val_blk, scores = block_scores(
                queries, keys_all, vals_all, seg_full, query_pos, seg_query, block_index, key_len
            )
            new_max = jnp.maximum(old_max, jnp.max(scores, axis=-1))
            new_sum = old_sum * jnp.exp(old_max - new_max) + jnp.sum(
                jnp.exp(scores - new_max[..., None]), axis=-1
            )
            return (new_max, new_sum)

        running_max, running_sum = lax.cond(
            needed, stat_step, lambda stats: stats, (running_max, running_sum)
        )
    log_total = running_max + jnp.log(running_sum)
    attended = jnp.zeros(queries.shape, jnp.float32)
    for block_index in range(block_count):
        needed = block_index * key_len <= query_pos[-1]

        def value_step(total, block_index=block_index):
            key_blk, val_blk, scores = block_scores(
                queries, keys_all, vals_all, seg_full, query_pos, seg_query, block_index, key_len
            )
            probs = jnp.exp(scores - log_total[..., None]).astype(jnp.bfloat16)
            return total + jnp.einsum(
                "kgts,skd->tkgd", probs, val_blk, preferred_element_type=jnp.float32
            )

        attended = lax.cond(needed, value_step, lambda total: total, attended)
    return (log_total, attended)


def attend_backward(
    queries, keys_all, vals_all, seg_full, query_pos, seg_query, block_count, grad_out, log_total
):
    key_len = keys_all.shape[0] // block_count
    delta = jnp.zeros(log_total.shape, jnp.float32)
    for block_index in range(block_count):
        needed = block_index * key_len <= query_pos[-1]

        def delta_step(total, block_index=block_index):
            key_blk, val_blk, scores = block_scores(
                queries, keys_all, vals_all, seg_full, query_pos, seg_query, block_index, key_len
            )
            probs = jnp.exp(scores - log_total[..., None])
            grad_probs = jnp.einsum(
                "tkgd,skd->kgts", grad_out, val_blk, preferred_element_type=jnp.float32
            )
            return total + jnp.sum(probs * grad_probs, axis=-1)

        delta = lax.cond(needed, delta_step, lambda total: total, delta)
    grad_query = jnp.zeros(queries.shape, jnp.float32)
    empty_part = jnp.zeros((key_len, keys_all.shape[1], keys_all.shape[2]), jnp.float32)
    key_parts = []
    val_parts = []
    for block_index in range(block_count):
        needed = block_index * key_len <= query_pos[-1]

        def grad_step(total, block_index=block_index):
            key_blk, val_blk, scores = block_scores(
                queries, keys_all, vals_all, seg_full, query_pos, seg_query, block_index, key_len
            )
            probs = jnp.exp(scores - log_total[..., None])
            grad_probs = jnp.einsum(
                "tkgd,skd->kgts", grad_out, val_blk, preferred_element_type=jnp.float32
            )
            grad_scores = (probs * (grad_probs - delta[..., None])).astype(jnp.bfloat16)
            new_total = total + jnp.einsum(
                "kgts,skd->tkgd", grad_scores, key_blk, preferred_element_type=jnp.float32
            ) * HD ** (-0.5)
            key_part = jnp.einsum(
                "kgts,tkgd->skd", grad_scores, queries, preferred_element_type=jnp.float32
            ) * HD ** (-0.5)
            val_part = jnp.einsum(
                "kgts,tkgd->skd",
                probs.astype(jnp.bfloat16),
                grad_out,
                preferred_element_type=jnp.float32,
            )
            return (new_total, key_part, val_part)

        grad_query, key_part, val_part = lax.cond(
            needed, grad_step, lambda total: (total, empty_part, empty_part), grad_query
        )
        key_parts.append(key_part)
        val_parts.append(val_part)
    return (grad_query, jnp.concatenate(key_parts, axis=0), jnp.concatenate(val_parts, axis=0))


def local(
    hidden_in,
    teacher,
    segment_ids,
    valid_mask,
    norm1_gain,
    w_z,
    w_x,
    w_bc,
    w_dt,
    conv_weight,
    conv_bias,
    dt_bias,
    a_log,
    d_skip,
    group_gain,
    w_mamba_out,
    w_query,
    w_key,
    w_value,
    w_attn_out,
    norm2_gain,
    w_gate,
    w_up,
    w_down,
):
    tensor_rank = lax.axis_index("tensor")
    seq_rank = lax.axis_index("seq")
    data_rank = lax.axis_index("dp")
    seq_count = lax.axis_size("seq")
    tensor_count = lax.axis_size("tensor")
    size_rows = hidden_in.shape[1]
    full_length = segment_ids.shape[1]
    row_start = seq_rank * size_rows
    seg_full = segment_ids[0]
    seg_local = lax.dynamic_slice_in_dim(seg_full, row_start, size_rows)
    seg_padded = jnp.concatenate([jnp.full((KC - 1,), -1, jnp.int32), seg_full])
    seg_ext = lax.dynamic_slice_in_dim(seg_padded, row_start, size_rows + KC - 1)
    seg_prev = lax.dynamic_index_in_dim(seg_padded, row_start + KC - 2, keepdims=False)
    token_count = jnp.sum(valid_mask).astype(jnp.float32)
    mask_rows = lax.dynamic_slice(valid_mask, (data_rank, row_start), (1, size_rows))[0].astype(
        jnp.float32
    )
    total_tokens = float(valid_mask.shape[0] * valid_mask.shape[1])
    (
        gain_one,
        full_z,
        full_x,
        full_dt,
        full_mo,
        full_q,
        full_k,
        full_v,
        full_ao,
        gain_two,
        full_gate,
        full_up,
        full_down,
    ) = (
        lax.all_gather(norm1_gain, ("dp", "seq"), axis=0, tiled=True),
        lax.all_gather(w_z, ("dp", "seq"), axis=0, tiled=True),
        lax.all_gather(w_x, ("dp", "seq"), axis=0, tiled=True),
        lax.all_gather(w_dt, ("dp", "seq"), axis=0, tiled=True),
        lax.all_gather(w_mamba_out, ("dp", "seq"), axis=1, tiled=True),
        lax.all_gather(w_query, ("dp", "seq"), axis=0, tiled=True),
        lax.all_gather(w_key, ("dp", "seq"), axis=0, tiled=True),
        lax.all_gather(w_value, ("dp", "seq"), axis=0, tiled=True),
        lax.all_gather(w_attn_out, ("dp", "seq"), axis=1, tiled=True),
        lax.all_gather(norm2_gain, ("dp", "seq"), axis=0, tiled=True),
        lax.all_gather(w_gate, ("dp", "seq"), axis=0, tiled=True),
        lax.all_gather(w_up, ("dp", "seq"), axis=0, tiled=True),
        lax.all_gather(w_down, ("dp", "seq"), axis=1, tiled=True),
    )
    heads_local = MH // tensor_count
    width_x = heads_local * HP
    head_start = tensor_rank * heads_local
    hidden = hidden_in[0].astype(jnp.float32)
    normed_f, norm_one_pull = jax.vjp(rms_norm, hidden, gain_one.astype(jnp.float32))
    normed = normed_f.astype(jnp.bfloat16)
    gate_z = mat_dot(normed, full_z)
    pre_x = mat_dot(normed, full_x).astype(jnp.bfloat16)
    pre_bc = mat_dot(normed, w_bc).astype(jnp.bfloat16)
    dt_raw = mat_dot(normed, full_dt)
    pre_all = jnp.concatenate([pre_x, pre_bc], axis=1)
    rim_rows = shifted(pre_all[size_rows - (KC - 1) :], "seq", 1)
    extended = jnp.concatenate([rim_rows, pre_all], axis=0).astype(jnp.float32)
    conv_local = jnp.concatenate(
        [
            lax.dynamic_slice_in_dim(conv_weight, head_start * HP, width_x, 0),
            conv_weight[MH * HP :],
        ],
        axis=0,
    )
    bias_local = jnp.concatenate(
        [lax.dynamic_slice_in_dim(conv_bias, head_start * HP, width_x, 0), conv_bias[MH * HP :]],
        axis=0,
    )
    mixed_f, conv_pull = jax.vjp(
        partial(conv_silu, seg_ext, seg_local), extended, conv_local, bias_local
    )
    mixed_in = lax.optimization_barrier(mixed_f.astype(jnp.bfloat16)).astype(jnp.float32)
    dt_bias_loc = lax.dynamic_slice_in_dim(dt_bias, head_start, heads_local)
    a_log_loc = lax.dynamic_slice_in_dim(a_log, head_start, heads_local)
    d_skip_loc = lax.dynamic_slice_in_dim(d_skip, head_start, heads_local)
    group_loc = lax.dynamic_slice_in_dim(group_gain, head_start, heads_local, 0)
    (ssm_local, carry_dev, state_dev), main_pull = jax.vjp(
        partial(ssd_main, seg_local, seg_prev), mixed_in, dt_raw, dt_bias_loc, a_log_loc, d_skip_loc
    )
    identity = (jnp.ones_like(carry_dev), jnp.zeros_like(state_dev))
    entry_state = carried_in((carry_dev, state_dev), "seq", chain_states, identity, False)[1]
    ssm_entry, state_pull = jax.vjp(
        partial(ssd_state, seg_local, seg_prev),
        mixed_in,
        dt_raw,
        dt_bias_loc,
        a_log_loc,
        entry_state,
    )
    ssm_out = ssm_local + ssm_entry
    gated_f, gate_pull = jax.vjp(
        group_gate, ssm_out, gate_z.reshape(size_rows, heads_local, HP), group_loc
    )
    gated = gated_f.reshape(size_rows, width_x).astype(jnp.bfloat16)
    mamba_part = mat_dot(gated, full_mo)
    positions = row_start + jnp.arange(size_rows)
    heads_q = full_q.shape[1] // HD
    heads_kv = full_k.shape[1] // HD
    groups = heads_q // heads_kv
    query_rot, query_pull = jax.vjp(
        partial(rotate, positions), mat_dot(normed, full_q).reshape(size_rows, heads_q, HD)
    )
    queries = query_rot.astype(jnp.bfloat16).reshape(size_rows, heads_kv, groups, HD)
    key_rot, key_pull = jax.vjp(
        partial(rotate, positions), mat_dot(normed, full_k).reshape(size_rows, heads_kv, HD)
    )
    keys_local = key_rot.astype(jnp.bfloat16).reshape(size_rows, heads_kv * HD)
    vals_local = mat_dot(normed, full_v).astype(jnp.bfloat16)
    keys_all, vals_all = (
        lax.all_gather(keys_local, "seq", axis=0, tiled=True),
        lax.all_gather(vals_local, "seq", axis=0, tiled=True),
    )
    keys_all = keys_all.reshape(full_length, heads_kv, HD)
    vals_all = vals_all.reshape(full_length, heads_kv, HD)
    block_count = seq_count // 4
    log_total, attended_f = attend_forward(
        queries, keys_all, vals_all, seg_full, positions, seg_local, block_count
    )
    attended = attended_f.reshape(size_rows, heads_q * HD).astype(jnp.bfloat16)
    branch = lax.psum(mamba_part + mat_dot(attended, full_ao), "tensor")
    middle = hidden + branch
    normed_two_f, norm_two_pull = jax.vjp(rms_norm, middle, gain_two.astype(jnp.float32))
    normed_two = normed_two_f.astype(jnp.bfloat16)
    act_f, glu_pull = jax.vjp(swiglu, mat_dot(normed_two, full_gate), mat_dot(normed_two, full_up))
    activated = act_f.astype(jnp.bfloat16)
    block_out = middle + lax.psum(mat_dot(activated, full_down), "tensor")
    (
        back_z,
        back_x,
        back_dt,
        back_mo,
        back_q,
        back_k,
        back_v,
        back_ao,
        back_gate,
        back_up,
        back_down,
    ) = (
        lax.all_gather(w_z, ("dp", "seq"), axis=0, tiled=True),
        lax.all_gather(w_x, ("dp", "seq"), axis=0, tiled=True),
        lax.all_gather(w_dt, ("dp", "seq"), axis=0, tiled=True),
        lax.all_gather(w_mamba_out, ("dp", "seq"), axis=1, tiled=True),
        lax.all_gather(w_query, ("dp", "seq"), axis=0, tiled=True),
        lax.all_gather(w_key, ("dp", "seq"), axis=0, tiled=True),
        lax.all_gather(w_value, ("dp", "seq"), axis=0, tiled=True),
        lax.all_gather(w_attn_out, ("dp", "seq"), axis=1, tiled=True),
        lax.all_gather(w_gate, ("dp", "seq"), axis=0, tiled=True),
        lax.all_gather(w_up, ("dp", "seq"), axis=0, tiled=True),
        lax.all_gather(w_down, ("dp", "seq"), axis=1, tiled=True),
    )
    d_out = (
        2.0
        * total_tokens
        / token_count
        * mask_rows[:, None]
        * (block_out - teacher[0].astype(jnp.float32))
    )
    d_mlp = d_out.astype(jnp.bfloat16)
    grad_down = dot_left_t(activated, d_mlp)
    d_gate_f, d_up_f = glu_pull(dot_right_t(d_mlp, back_down))
    d_gate = d_gate_f.astype(jnp.bfloat16)
    d_up = d_up_f.astype(jnp.bfloat16)
    grad_gate = dot_left_t(normed_two, d_gate)
    grad_up = dot_left_t(normed_two, d_up)
    d_normed_two = lax.psum(dot_right_t(d_gate, back_gate) + dot_right_t(d_up, back_up), "tensor")
    d_middle_n, grad_gain_two = norm_two_pull(d_normed_two)
    d_middle = d_out + d_middle_n
    d_branch = d_middle.astype(jnp.bfloat16)
    grad_ao = dot_left_t(attended, d_branch)
    grad_mo = dot_left_t(gated, d_branch)
    d_attended = (
        dot_right_t(d_branch, back_ao).astype(jnp.bfloat16).reshape(size_rows, heads_kv, groups, HD)
    )
    d_gated = dot_right_t(d_branch, back_mo).reshape(size_rows, heads_local, HP)
    d_ssm, d_gate_z_f, grad_group = gate_pull(d_gated)
    d_gate_z = d_gate_z_f.reshape(size_rows, width_x).astype(jnp.bfloat16)
    d_mixed_s, d_dt_s, d_dtb_s, d_alog_s, d_entry = state_pull(d_ssm)
    state_grad = carried_in((carry_dev, d_entry), "seq", chain_states, identity, True)[1]
    d_carry = jnp.sum(state_grad * entry_state, axis=(1, 2))
    d_mixed_m, d_dt_m, d_dtb_m, d_alog_m, grad_skip = main_pull((d_ssm, d_carry, state_grad))
    d_dt_raw = (d_dt_s + d_dt_m).astype(jnp.bfloat16)
    d_ext, grad_conv_loc, grad_bias_loc = conv_pull(d_mixed_s + d_mixed_m)
    rim_grad = shifted(d_ext[: KC - 1], "seq", -1)
    d_pre = d_ext[KC - 1 :] + jnp.pad(rim_grad, ((size_rows - (KC - 1), 0), (0, 0)))
    d_pre_x = d_pre[:, :width_x].astype(jnp.bfloat16)
    d_pre_bc = d_pre[:, width_x:]
    grad_query_rot, key_grads_all, val_grads_all = attend_backward(
        queries,
        keys_all,
        vals_all,
        seg_full,
        positions,
        seg_local,
        block_count,
        d_attended,
        log_total,
    )
    key_grad, val_grad = (
        lax.psum_scatter(
            key_grads_all.reshape(full_length, heads_kv * HD).astype(jnp.bfloat16),
            "seq",
            scatter_dimension=0,
            tiled=True,
        ).astype(jnp.float32),
        lax.psum_scatter(
            val_grads_all.reshape(full_length, heads_kv * HD).astype(jnp.bfloat16),
            "seq",
            scatter_dimension=0,
            tiled=True,
        ).astype(jnp.float32),
    )
    d_query = (
        query_pull(grad_query_rot.reshape(size_rows, heads_q, HD))[0]
        .reshape(size_rows, heads_q * HD)
        .astype(jnp.bfloat16)
    )
    d_key = (
        key_pull(key_grad.reshape(size_rows, heads_kv, HD))[0]
        .reshape(size_rows, heads_kv * HD)
        .astype(jnp.bfloat16)
    )
    d_value = val_grad.astype(jnp.bfloat16)
    grad_z = dot_left_t(normed, d_gate_z)
    grad_x = dot_left_t(normed, d_pre_x)
    grad_dt = dot_left_t(normed, d_dt_raw)
    grad_q = dot_left_t(normed, d_query)
    grad_k = dot_left_t(normed, d_key)
    grad_v = dot_left_t(normed, d_value)
    normed_wide = normed.astype(jnp.float32)
    bc_weight = w_bc.astype(jnp.float32)
    grad_bc = jnp.dot(
        normed_wide.T, d_pre_bc, precision=HIGHEST, preferred_element_type=jnp.float32
    )
    d_normed_part = (
        dot_right_t(d_gate_z, back_z)
        + dot_right_t(d_pre_x, back_x)
        + dot_right_t(d_dt_raw, back_dt)
        + dot_right_t(d_query, back_q)
        + dot_right_t(d_key, back_k)
        + dot_right_t(d_value, back_v)
        + jnp.dot(d_pre_bc, bc_weight.T, precision=HIGHEST, preferred_element_type=jnp.float32)
    )
    d_normed = lax.psum(d_normed_part.astype(jnp.bfloat16), "tensor").astype(jnp.float32)
    d_hidden_n, grad_gain_one = norm_one_pull(d_normed)
    grad_input = d_middle + d_hidden_n
    conv_x_full = lax.dynamic_update_slice_in_dim(
        jnp.zeros((MH * HP, KC), jnp.float32), grad_conv_loc[:width_x], head_start * HP, 0
    )
    grad_conv_full = jnp.concatenate([conv_x_full, grad_conv_loc[width_x:]], axis=0)
    bias_x_full = lax.dynamic_update_slice_in_dim(
        jnp.zeros((MH * HP,), jnp.float32), grad_bias_loc[:width_x], head_start * HP, 0
    )
    grad_bias_full = jnp.concatenate([bias_x_full, grad_bias_loc[width_x:]], axis=0)
    grad_dtb_full = lax.dynamic_update_slice_in_dim(
        jnp.zeros((MH,), jnp.float32), d_dtb_s + d_dtb_m, head_start, 0
    )
    grad_alog_full = lax.dynamic_update_slice_in_dim(
        jnp.zeros((MH,), jnp.float32), d_alog_s + d_alog_m, head_start, 0
    )
    grad_skip_full = lax.dynamic_update_slice_in_dim(
        jnp.zeros((MH,), jnp.float32), grad_skip, head_start, 0
    )
    grad_group_full = lax.dynamic_update_slice_in_dim(
        jnp.zeros((MH, HP), jnp.float32), grad_group, head_start, 0
    )
    sum_bc, sum_conv, sum_bias, sum_dtb, sum_alog, sum_skip, sum_group = lax.psum(
        (
            grad_bc,
            grad_conv_full,
            grad_bias_full,
            grad_dtb_full,
            grad_alog_full,
            grad_skip_full,
            grad_group_full,
        ),
        ("dp", "seq", "tensor"),
    )
    (
        out_gain_one,
        out_z,
        out_x,
        out_dt,
        out_mo,
        out_q,
        out_k,
        out_v,
        out_ao,
        out_gain_two,
        out_gate,
        out_up,
        out_down,
    ) = (
        lax.psum_scatter(grad_gain_one, ("dp", "seq"), scatter_dimension=0, tiled=True),
        lax.psum_scatter(grad_z, ("dp", "seq"), scatter_dimension=0, tiled=True),
        lax.psum_scatter(grad_x, ("dp", "seq"), scatter_dimension=0, tiled=True),
        lax.psum_scatter(grad_dt, ("dp", "seq"), scatter_dimension=0, tiled=True),
        lax.psum_scatter(grad_mo, ("dp", "seq"), scatter_dimension=1, tiled=True),
        lax.psum_scatter(grad_q, ("dp", "seq"), scatter_dimension=0, tiled=True),
        lax.psum_scatter(grad_k, ("dp", "seq"), scatter_dimension=0, tiled=True),
        lax.psum_scatter(grad_v, ("dp", "seq"), scatter_dimension=0, tiled=True),
        lax.psum_scatter(grad_ao, ("dp", "seq"), scatter_dimension=1, tiled=True),
        lax.psum_scatter(grad_gain_two, ("dp", "seq"), scatter_dimension=0, tiled=True),
        lax.psum_scatter(grad_gate, ("dp", "seq"), scatter_dimension=0, tiled=True),
        lax.psum_scatter(grad_up, ("dp", "seq"), scatter_dimension=0, tiled=True),
        lax.psum_scatter(grad_down, ("dp", "seq"), scatter_dimension=1, tiled=True),
    )
    return (
        block_out.astype(jnp.bfloat16)[None],
        grad_input[None],
        out_gain_one,
        out_z,
        out_x,
        sum_bc,
        out_dt,
        sum_conv,
        sum_bias,
        sum_dtb,
        sum_alog,
        sum_skip,
        sum_group,
        out_mo,
        out_q,
        out_k,
        out_v,
        out_ao,
        out_gain_two,
        out_gate,
        out_up,
        out_down,
    )


GROUP = 4
CHUNK = 128
HEADS = 6
MESH_ID = pl.DeviceIdType.MESH
VMEM_BYTES = 56 * 1024 * 1024


def dot_f32(left_side, right_side, left_dim, right_dim):
    return lax.dot_general(
        left_side,
        right_side,
        (((left_dim,), (right_dim,)), ((), ())),
        preferred_element_type=jnp.float32,
    )


def halves(values):
    high = values.astype(jnp.bfloat16)
    return (high, (values - high.astype(jnp.float32)).astype(jnp.bfloat16))


def plane_place():
    data, place, core = lax.axis_index("dp"), lax.axis_index("seq"), lax.axis_index("tensor")
    along_x = place + 1 - 2 * lax.rem(place, 2)
    along_y = lax.rem(place + 2, GROUP)
    across = GROUP - 1 - place
    return (data, place, core, along_x, along_y, across)


def meet(devices):
    barrier = pltpu.get_barrier_semaphore()
    for device in devices:
        pl.semaphore_signal(barrier, inc=1, device_id=device, device_id_type=MESH_ID)
    pl.semaphore_wait(barrier, len(devices))


def remote(source, target, send_sem, recv_sem, device):
    return pltpu.make_async_remote_copy(
        src_ref=source,
        dst_ref=target,
        send_sem=send_sem,
        recv_sem=recv_sem,
        device_id=device,
        device_id_type=MESH_ID,
    )


def lasting(microseconds):
    return pl.CostEstimate(
        flops=int(microseconds * 9e8),
        bytes_accessed=int(microseconds * 3e6),
        transcendentals=0,
    )


def any_specs(count):
    return [pl.BlockSpec(memory_space=pl.ANY)] * count


def vmem_specs(count):
    return [pl.BlockSpec(memory_space=pltpu.VMEM)] * count


def gather_kernel(apply, count_in, count_out, own_ref, *refs):
    inputs, all_ref = refs[:count_in], refs[count_in]
    outputs = refs[count_in + 1 : count_in + 1 + count_out]
    send_sems, recv_sems = refs[count_in + 1 + count_out :]
    data, place, core, along_x, along_y, across = plane_place()
    to_x, to_y, partner = (data, along_x, core), (data, along_y, core), (data, place, 1 - core)
    meet((to_x, to_y, partner))
    gather_steps(apply, own_ref, inputs, all_ref, outputs, send_sems, recv_sems)


def gather_steps(apply, own_ref, inputs, all_ref, outputs, send_sems, recv_sems, ready=None):
    data, place, core, along_x, along_y, across = plane_place()
    height = own_ref.shape[0]
    half = height // 2
    to_x, to_y, partner = (data, along_x, core), (data, along_y, core), (data, place, 1 - core)

    def block(chip, part):
        return all_ref.at[2 * chip + core, pl.ds(part * half, half)]

    def work(chip, side):
        if apply is not None:
            index = 2 * chip + side
            rows = pl.ds(pl.multiple_of(index * height, 16), height)
            apply(all_ref[index], rows, inputs, outputs)

    def push(index, source, target, device):
        copy = remote(source, target, send_sems.at[index], recv_sems.at[index], device)
        copy.start()
        return copy

    first, second = own_ref.at[pl.ds(0, half)], own_ref.at[pl.ds(half, half)]
    x_first = push(0, first, block(place, 0), to_x)
    y_second = push(1, second, block(place, 1), to_y)
    x_second = push(2, second, block(place, 1), to_x)
    y_first = push(3, first, block(place, 0), to_y)
    pair_own = push(4, own_ref, all_ref.at[2 * place + core], partner)
    all_ref[2 * place + core] = own_ref[...]
    work(place, core)
    pair_own.wait_recv()
    work(place, 1 - core)
    if ready is not None:
        ready(place, 0)
    x_first.wait_recv()
    over_y = push(5, block(along_x, 0), block(along_x, 0), to_y)
    y_second.wait_recv()
    over_x = push(6, block(along_y, 1), block(along_y, 1), to_x)
    x_second.wait_recv()
    mine_x = all_ref.at[2 * along_x + core]
    pair_x = push(7, mine_x, mine_x, partner)
    y_first.wait_recv()
    mine_y = all_ref.at[2 * along_y + core]
    pair_y = push(8, mine_y, mine_y, partner)
    work(along_x, core)
    work(along_y, core)
    pair_x.wait_recv()
    work(along_x, 1 - core)
    if ready is not None:
        ready(along_x, 1)
    pair_y.wait_recv()
    work(along_y, 1 - core)
    if ready is not None:
        ready(along_y, 2)
    over_y.wait_recv()
    pair_a = push(9, block(across, 0), block(across, 0), partner)
    over_x.wait_recv()
    pair_b = push(10, block(across, 1), block(across, 1), partner)
    work(across, core)
    if ready is not None:
        ready(across, 3, core)
    pair_a.wait_recv()
    pair_b.wait_recv()
    work(across, 1 - core)
    if ready is not None:
        ready(across, 4, 1 - core)
    for copy in (
        x_first,
        y_second,
        x_second,
        y_first,
        pair_own,
        over_y,
        over_x,
        pair_x,
        pair_y,
        pair_a,
        pair_b,
    ):
        copy.wait_send()


def gather_plane(own, identity=1, apply=None, inputs=(), outputs=()):
    rows, width = own.shape
    gathered, *results = pl.pallas_call(
        partial(gather_kernel, apply, len(inputs), len(outputs)),
        out_shape=[jax.ShapeDtypeStruct((2 * GROUP, rows, width), own.dtype)]
        + [jax.ShapeDtypeStruct(shape, dtype) for shape, dtype in outputs],
        in_specs=vmem_specs(1 + len(inputs)),
        out_specs=vmem_specs(1 + len(outputs)),
        scratch_shapes=[pltpu.SemaphoreType.DMA((11,)), pltpu.SemaphoreType.DMA((11,))],
        cost_estimate=lasting(35),
        compiler_params=pltpu.CompilerParams(
            collective_id=identity, has_side_effects=True, vmem_limit_bytes=VMEM_BYTES
        ),
    )(own, *inputs)
    gathered = gathered.reshape(2 * GROUP * rows, width)
    return (gathered, *results) if results else gathered


def apply_gate_up(block, rows, inputs, outputs):
    weights, (both_ref, act_ref) = inputs[0], outputs
    units = act_ref.shape[1]
    both = jnp.dot(block, weights[...], preferred_element_type=jnp.float32)
    both_ref[rows] = both
    gate = both[:, :units]
    act_ref[rows] = (gate * jax.nn.sigmoid(gate) * both[:, units:]).astype(jnp.bfloat16)


def apply_down_back(block, rows, inputs, outputs):
    weights, both_ref = inputs
    units = weights.shape[1]
    d_act = jnp.dot(block, weights[...], preferred_element_type=jnp.float32)
    gate, up = both_ref[rows, :units], both_ref[rows, units:]
    sigmoid = jax.nn.sigmoid(gate)
    silu = gate * sigmoid
    d_gate = d_act * up * (sigmoid * (1.0 + gate * (1.0 - sigmoid)))
    outputs[0][rows, :units] = d_gate.astype(jnp.bfloat16)
    outputs[0][rows, units:] = (d_act * silu).astype(jnp.bfloat16)


def apply_out_back(block, rows, inputs, outputs):
    both = jnp.dot(block, inputs[0][...], preferred_element_type=jnp.float32)
    width = outputs[0].shape[1]
    outputs[0][rows] = both[:, :width]
    outputs[1][rows] = both[:, width:].astype(jnp.bfloat16)


def apply_norm(block, rows, inputs, outputs):
    gain_ref, weights = inputs
    values = block.astype(jnp.float32)
    scale = lax.rsqrt(jnp.mean(values * values, axis=-1, keepdims=True) + EPSILON)
    normed = (values * scale * gain_ref[...]).astype(jnp.bfloat16)
    outputs[0][rows] = normed
    outputs[1][rows] = jnp.dot(normed, weights[...], preferred_element_type=jnp.float32).astype(
        jnp.bfloat16
    )


def scatter_kernel(
    count, left_ref, right_ref, *refs, store=None, between=None, preparing=None, finishing=None
):
    data, place, core, along_x, along_y, across = plane_place()
    partner = (data, place, 1 - core)
    to_x, to_y = (data, along_x, core), (data, along_y, core)
    order = (across, along_x, along_y, place)
    count_in = 0 if count == 1 else count
    extra, sums = refs[:count_in], refs[count_in : count_in + count]
    parts, scratch = refs[count_in + count : count_in + 2 * count], refs[count_in + 2 * count :]
    step = 16
    meet((partner, to_x, to_y))

    def multiply(at, chip, side):
        part = parts[at]
        index = 2 * chip + side
        height, columns = part.shape[1:]
        if at == 0:
            rows = pl.ds(pl.multiple_of(index * height, 16), height)
            depth = right_ref.shape[1]
            block = dot_f32(left_ref[rows, :depth], right_ref[...], 1, 1)
            if count > 1:
                block = block + dot_f32(left_ref[rows, depth:], extra[-1][...], 1, 1)
        else:
            start = left_ref.shape[1] - GROUP * height
            turned = pl.ds(pl.multiple_of(start + chip * height, 128), height)
            along = pl.ds(pl.multiple_of(side * columns, 128), columns)
            block = dot_f32(left_ref[:, turned], extra[at - 1][:, along], 0, 0)
        part[index] = block.astype(jnp.bfloat16)

    def one_array(at, part_ref, sum_ref, own_refs):
        pair_in, send_a, send_x, send_y, got_x, got_y, pair_s, pair_r, send_s, recv_s = own_refs
        half = part_ref.shape[1] // 2
        pair = []

        def send_pair(index):
            chip = order[index]
            multiply(at, chip, 1 - core)
            copy = remote(
                part_ref.at[2 * chip + 1 - core],
                pair_in.at[index],
                pair_s.at[index],
                pair_r.at[index],
                partner,
            )
            copy.start()
            pair.append(copy)
            multiply(at, chip, core)

        def own_rows(index, rows):
            return part_ref[2 * order[index] + core, rows].astype(jnp.float32) + pair_in[
                index, rows
            ].astype(jnp.float32)

        def fill(target, index, first, extra=None):
            def one(lap, carry):
                rows = pl.ds(pl.multiple_of(lap * step, step), step)
                total = own_rows(index, pl.ds(pl.multiple_of(first + lap * step, step), step))
                if extra is not None:
                    total = total + extra[rows].astype(jnp.float32)
                target[rows] = total.astype(jnp.bfloat16)
                return carry

            lax.fori_loop(0, half // step, one, 0)

        def push(index, source, target, device):
            copy = remote(source, target, send_s.at[index], recv_s.at[index], device)
            copy.start()
            return copy

        send_pair(0)
        pair[0].wait_recv()
        fill(send_a.at[0], 0, 0)
        far_x = push(0, send_a.at[0], got_x.at[0], to_x)
        fill(send_a.at[1], 0, half)
        far_y = push(1, send_a.at[1], got_y.at[0], to_y)
        send_pair(1)
        pair[1].wait_recv()
        fill(send_x.at[0], 1, 0)
        near_x = push(2, send_x.at[0], got_x.at[1], to_x)
        send_pair(2)
        pair[2].wait_recv()
        fill(send_y.at[0], 2, half)
        near_y = push(3, send_y.at[0], got_y.at[1], to_y)
        send_pair(3)
        yield
        far_x.wait_recv()
        fill(send_y.at[1], 2, 0, got_x.at[0])
        last_y = push(4, send_y.at[1], got_y.at[2], to_y)
        far_y.wait_recv()
        fill(send_x.at[1], 1, half, got_y.at[0])
        last_x = push(5, send_x.at[1], got_x.at[2], to_x)
        yield
        pair[3].wait_recv()
        near_x.wait_recv()
        near_y.wait_recv()
        last_y.wait_recv()
        last_x.wait_recv()

        def finish(first, near, last):
            def one(lap, carry):
                rows = pl.ds(pl.multiple_of(lap * step, step), step)
                place_rows = pl.ds(pl.multiple_of(first + lap * step, step), step)
                total = (
                    own_rows(3, place_rows)
                    + near[rows].astype(jnp.float32)
                    + last[rows].astype(jnp.float32)
                )
                if store is None:
                    sum_ref[place_rows] = total
                else:
                    store(at, sum_ref, place_rows, total)
                return carry

            lax.fori_loop(0, half // step, one, 0)

        finish(0, got_x.at[1], got_y.at[2])
        finish(half, got_y.at[1], got_x.at[2])
        for copy in pair + [far_x, far_y, near_x, near_y, last_x, last_y]:
            copy.wait_send()

    each = len(scratch) // count
    runs = [
        one_array(at, parts[at], sums[at], scratch[each * at : each * (at + 1)]) for at in range(count)
    ]
    for stage in range(2):
        for at, run in enumerate(runs):
            if at > 0 and stage == 0 and preparing is not None:
                preparing()
            next(run)
        if between is not None:
            between(stage)
    if finishing is not None:
        finishing()
    for run in runs:
        for _ in run:
            pass


def down_and_back_kernel(
    act_ref,
    weights_ref,
    factor_ref,
    middle_hbm,
    teacher_hbm,
    both_hbm,
    out_hbm,
    d_out_hbm,
    d_both_hbm,
    grad_ref,
    out_ref,
    d_out_ref,
    d_both_ref,
    store_sems,
    own_ref,
    grad_sum,
    d_mlp_ref,
    middle_ref,
    teacher_ref,
    both_ref,
    load_sems,
    gather_send,
    gather_recv,
    *scratch,
):
    loads = []
    for source, target in (
        (middle_hbm, middle_ref),
        (teacher_hbm, teacher_ref),
        (both_hbm, both_ref),
    ):
        copy = pltpu.make_async_copy(source, target, load_sems.at[len(loads)])
        copy.start()
        loads.append(copy)

    def loaded():
        for copy in loads:
            copy.wait()

    def store(at, target, rows, total):
        out = middle_ref[rows] + total
        out_ref[rows] = out.astype(jnp.bfloat16)
        d_out = factor_ref[rows] * (out - teacher_ref[rows].astype(jnp.float32))
        d_out_ref[rows] = d_out
        own_ref[rows] = d_out.astype(jnp.bfloat16)

    stores = []

    def leave(source, target):
        copy = pltpu.make_async_copy(source, target, store_sems.at[len(stores)])
        copy.start()
        stores.append(copy)

    def ready(chip, turn_at, side=None):
        if side is None:
            blocks = d_mlp_ref[pl.ds(2 * chip, 2)]
            first = 2 * chip
        else:
            blocks = d_mlp_ref[pl.ds(2 * chip + side, 1)]
            first = 2 * chip + side
        height = blocks.shape[0] * blocks.shape[1]
        rows = pl.ds(pl.multiple_of(first * blocks.shape[1], 16), height)
        leave(d_both_ref.at[rows], d_both_hbm.at[rows])
        part = dot_f32(blocks.reshape(height, blocks.shape[2]), act_ref[rows], 0, 0)
        if turn_at == 0:
            grad_sum[...] = part
        elif turn_at < GROUP:
            grad_sum[...] += part
        else:
            grad_ref[...] = (grad_sum[...] + part).astype(jnp.bfloat16)

    scatter_kernel(1, act_ref, weights_ref, None, *scratch, store=store, finishing=loaded)
    leave(out_ref, out_hbm)
    leave(d_out_ref, d_out_hbm)
    gather_steps(
        apply_down_back,
        own_ref,
        (weights_ref, both_ref),
        d_mlp_ref,
        (d_both_ref,),
        gather_send,
        gather_recv,
        ready,
    )
    for copy in stores:
        copy.wait()


def down_and_back(activated, full_down, middle, teacher_own, factor, gate_up):
    rows, width = middle.shape
    shaped = jax.ShapeDtypeStruct
    return pl.pallas_call(
        down_and_back_kernel,
        out_shape=[
            shaped((rows, width), jnp.bfloat16),
            shaped((rows, width), jnp.float32),
            shaped(gate_up.shape, jnp.bfloat16),
            shaped(full_down.shape, jnp.bfloat16),
        ],
        in_specs=vmem_specs(3) + any_specs(3),
        out_specs=any_specs(3) + vmem_specs(1),
        scratch_shapes=[
            pltpu.VMEM((rows, width), jnp.bfloat16),
            pltpu.VMEM((rows, width), jnp.float32),
            pltpu.VMEM(gate_up.shape, jnp.bfloat16),
            pltpu.SemaphoreType.DMA((GROUP + 3,)),
            pltpu.VMEM((rows, width), jnp.bfloat16),
            pltpu.VMEM(full_down.shape, jnp.float32),
            pltpu.VMEM((2 * GROUP, rows, width), jnp.bfloat16),
            pltpu.VMEM(middle.shape, middle.dtype),
            pltpu.VMEM(teacher_own.shape, teacher_own.dtype),
            pltpu.VMEM(gate_up.shape, gate_up.dtype),
            pltpu.SemaphoreType.DMA((3,)),
            pltpu.SemaphoreType.DMA((11,)),
            pltpu.SemaphoreType.DMA((11,)),
        ]
        + scatter_scratch([(rows, width)]),
        cost_estimate=lasting(70),
        compiler_params=pltpu.CompilerParams(
            collective_id=10, has_side_effects=True, vmem_limit_bytes=VMEM_BYTES + 3 * 1024 * 1024
        ),
    )(activated, full_down, factor, middle, teacher_own, gate_up)


def up_back_kernel(d_both_ref, weights_ref, normed_ref, sum_ref, grad_ref, *scratch):
    tiles = 4
    width = normed_ref.shape[1] // tiles

    def between(stage):
        for tile in range(2 * stage, 2 * stage + 2):
            columns = slice(width * tile, width * (tile + 1))
            grad_ref[columns] = dot_f32(
                normed_ref[:, columns], d_both_ref[...], 0, 0
            ).astype(jnp.bfloat16)

    scatter_kernel(1, d_both_ref, weights_ref, sum_ref, *scratch, between=between)


def up_back(d_gate_up, full_gu, normed_two):
    rows, width = d_gate_up.shape[0] // (2 * GROUP), full_gu.shape[0]
    return pl.pallas_call(
        up_back_kernel,
        out_shape=[
            jax.ShapeDtypeStruct((rows, width), jnp.float32),
            jax.ShapeDtypeStruct(full_gu.shape, jnp.bfloat16),
        ],
        in_specs=vmem_specs(3),
        out_specs=vmem_specs(2),
        scratch_shapes=scatter_scratch([(rows, width)]),
        cost_estimate=lasting(38),
        compiler_params=pltpu.CompilerParams(
            collective_id=11, has_side_effects=True, vmem_limit_bytes=VMEM_BYTES
        ),
    )(d_gate_up, full_gu, normed_two)


def input_back_kernel(
    left_ref,
    weights_ref,
    bc_weights_ref,
    gain_ref,
    normed_hbm,
    hidden_hbm,
    d_middle_hbm,
    grad_ref,
    bc_ref,
    gain_sum_ref,
    normed_ref,
    hidden_ref,
    d_middle_ref,
    load_sems,
    *scratch,
):
    loads = []
    for source, target in (
        (normed_hbm, normed_ref),
        (hidden_hbm, hidden_ref),
        (d_middle_hbm, d_middle_ref),
    ):
        copy = pltpu.make_async_copy(source, target, load_sems.at[len(loads)])
        copy.start()
        loads.append(copy)
    gain_sum_ref[...] = jnp.zeros_like(gain_sum_ref)

    def loaded():
        for copy in loads[1:]:
            copy.wait()


    def store(at, target, rows, total):
        if at > 0:
            target[rows] = total
            return
        hidden = hidden_ref[rows].astype(jnp.float32)
        scale = lax.rsqrt(jnp.mean(hidden * hidden, axis=-1, keepdims=True) + EPSILON)
        scaled = total * gain_ref[...]
        inner = jnp.mean(scaled * hidden, axis=-1, keepdims=True)
        grad_ref[rows] = d_middle_ref[rows] + scale * scaled - hidden * (scale**3 * inner)
        product = total * hidden * scale
        gain_sum_ref[...] += product[:8] + product[8:]

    scatter_kernel(
        2,
        left_ref,
        weights_ref,
        normed_ref,
        bc_weights_ref,
        None,
        bc_ref,
        *scratch,
        store=store,
        preparing=loads[0].wait,
        finishing=loaded,
    )


def input_back(d_projected, full_in, normed, w_bc, hidden_own, d_middle, gain, bc_cols):
    rows, width = d_middle.shape
    sizes = [(rows, width), (bc_cols, width // 2)]
    shaped = jax.ShapeDtypeStruct
    return pl.pallas_call(
        input_back_kernel,
        out_shape=[
            shaped((rows, width), jnp.float32),
            shaped(sizes[1], jnp.float32),
            shaped((8, width), jnp.float32),
        ],
        in_specs=vmem_specs(4) + any_specs(3),
        out_specs=vmem_specs(3),
        scratch_shapes=[
            pltpu.VMEM(normed.shape, normed.dtype),
            pltpu.VMEM(hidden_own.shape, hidden_own.dtype),
            pltpu.VMEM(d_middle.shape, d_middle.dtype),
            pltpu.SemaphoreType.DMA((3,)),
        ]
        + scatter_scratch(sizes),
        cost_estimate=lasting(50),
        compiler_params=pltpu.CompilerParams(
            collective_id=8, has_side_effects=True, vmem_limit_bytes=VMEM_BYTES
        ),
    )(d_projected, full_in, w_bc, gain, normed, hidden_own, d_middle)


def scatter_scratch(sizes):
    scratch = [pltpu.VMEM((2 * GROUP, *size), jnp.bfloat16) for size in sizes]
    for rows, columns in sizes:
        half = (rows // 2, columns)
        scratch += [
            pltpu.VMEM((4, rows, columns), jnp.bfloat16),
            pltpu.VMEM((2,) + half, jnp.bfloat16),
            pltpu.VMEM((2,) + half, jnp.bfloat16),
            pltpu.VMEM((2,) + half, jnp.bfloat16),
            pltpu.VMEM((3,) + half, jnp.bfloat16),
            pltpu.VMEM((3,) + half, jnp.bfloat16),
            pltpu.SemaphoreType.DMA((4,)),
            pltpu.SemaphoreType.DMA((4,)),
            pltpu.SemaphoreType.DMA((6,)),
            pltpu.SemaphoreType.DMA((6,)),
        ]
    return scratch


def scatter_plane(left, right, identity, extra=(), beside=()):
    height, width = left.shape[0] // (2 * GROUP), right.shape[0]
    sizes = [(height, width)] + [tuple(size) for _, *size in extra]
    shapes = [jax.ShapeDtypeStruct(size, jnp.float32) for size in sizes]
    count = 1 + len(extra)
    return pl.pallas_call(
        partial(scatter_kernel, count),
        out_shape=shapes,
        in_specs=vmem_specs(2 if count == 1 else 2 + count),
        out_specs=vmem_specs(count),
        scratch_shapes=scatter_scratch(sizes),
        cost_estimate=lasting(35),
        compiler_params=pltpu.CompilerParams(
            collective_id=identity, has_side_effects=True, vmem_limit_bytes=VMEM_BYTES
        ),
    )(left, right, *[array for array, *_ in extra], *beside)


def plane_sum_kernel(
    small_ref, own_ref, out_ref, bulk, sum_ref, both_ref, both_out, back, small_in, own_sem, send_s, recv_s
):
    data, place, core, along_x, along_y, across = plane_place()
    mine = 2 * place + core
    partner = (data, place, 1 - core)
    plane = []
    for turn_by in range(1, 2 * GROUP):
        other = lax.rem(mine + turn_by, 2 * GROUP)
        plane.append((other, (data, other // 2, lax.rem(other, 2))))
    meet([device for _, device in plane])
    started = []

    def push(source, target, device):
        slot = len(started)
        copy = remote(source, target, send_s.at[slot], recv_s.at[slot], device)
        copy.start()
        started.append(copy)

    piece = small_in.shape[2]

    def piece_of(index):
        return small_ref.at[:, pl.ds(pl.multiple_of(index * piece, 128), piece)]

    for other, device in plane:
        push(piece_of(other), small_in.at[mine], device)
    for source, target in ((own_ref, both_ref), (out_ref, both_out)):
        push(source, target.at[core], partner)
    for chip in (across, along_x, along_y):
        push(bulk.at[chip], back.at[place], (data, chip, core))
    own = pltpu.make_async_copy(bulk.at[place], back.at[place], own_sem)
    own.start()
    small_in[mine] = piece_of(mine)[...]
    both_ref[core] = own_ref[...]
    both_out[core] = out_ref[...]
    for copy in started:
        copy.wait()
    own.wait()
    total = small_in[0]
    for index in range(1, 2 * GROUP):
        total = total + small_in[index]
    sum_ref[...] = total


def plane_sum(small, own_rows, out_rows, bulk):
    places = 2 * GROUP
    pushes = places - 1 + 2 + 3
    shaped = jax.ShapeDtypeStruct
    piece = small.shape[1] // places
    return pl.pallas_call(
        plane_sum_kernel,
        out_shape=[
            shaped((8, piece), jnp.float32),
            shaped((2,) + own_rows.shape, own_rows.dtype),
            shaped((2,) + out_rows.shape, out_rows.dtype),
            shaped(bulk.shape, bulk.dtype),
        ],
        in_specs=vmem_specs(3) + any_specs(1),
        out_specs=vmem_specs(3) + any_specs(1),
        scratch_shapes=[
            pltpu.VMEM((places, 8, piece), jnp.float32),
            pltpu.SemaphoreType.DMA,
            pltpu.SemaphoreType.DMA((pushes,)),
            pltpu.SemaphoreType.DMA((pushes,)),
        ],
        cost_estimate=lasting(20),
        compiler_params=pltpu.CompilerParams(
            collective_id=7, has_side_effects=True, vmem_limit_bytes=VMEM_BYTES
        ),
    )(small, own_rows, out_rows, bulk)


def finish_kernel(
    piece_ref,
    bc_ref,
    bulk,
    small_all,
    bc_all,
    back,
    bc_send,
    bc_in,
    bc_line,
    line_in,
    own_sem,
    send_s,
    recv_s,
):
    data, place, core, along_x, along_y, across = plane_place()
    count = lax.axis_size("dp")
    mine = 2 * place + core
    partner = (data, place, 1 - core)
    others = (across, along_x, along_y)
    chips = [(data, chip, core) for chip in others]
    plane = []
    for turn_by in range(1, 2 * GROUP):
        other = lax.rem(mine + turn_by, 2 * GROUP)
        plane.append((data, other // 2, lax.rem(other, 2)))
    line = []
    for turn_by in range(1, count):
        other = lax.rem(data + turn_by, count)
        line.append((other, (other, place, core)))
    meet(plane + [device for _, device in line])
    started = []

    def push(source, target, device):
        slot = len(started)
        copy = remote(source, target, send_s.at[slot], recv_s.at[slot], device)
        copy.start()
        started.append(copy)
        return copy

    rows = bc_in.shape[1]

    def rows_of(index):
        return bc_send.at[pl.ds(pl.multiple_of(index * rows, 16), rows)]

    bc_send[...] = bc_ref[...].astype(jnp.bfloat16)
    first = [push(rows_of(other), bc_in.at[data], device) for other, device in line]
    small = [push(piece_ref, line_in.at[data], device) for _, device in line]
    late = []
    for chip, device in zip(others, chips):
        late.append(push(bulk.at[chip], back.at[place], device))
    own = pltpu.make_async_copy(bulk.at[place], back.at[place], own_sem)
    own.start()
    bc_in[data] = rows_of(data)[...]
    line_in[data] = piece_ref[...]
    for copy in first:
        copy.wait_recv()
    total = bc_in[0].astype(jnp.float32)
    for index in range(1, count):
        total = total + bc_in[index].astype(jnp.float32)
    bc_line[data] = total.astype(jnp.bfloat16)
    second = [push(bc_line.at[data], bc_line.at[data], device) for _, device in line]
    for copy in small:
        copy.wait_recv()
    total = line_in[0]
    for index in range(1, count):
        total = total + line_in[index]
    small_all[mine] = total
    late += [push(small_all.at[mine], small_all.at[mine], device) for device in plane]
    for copy in second:
        copy.wait_recv()
    half = count // 2

    def half_of(chip, at):
        return bc_all.at[2 * chip + core, pl.ds(at * half, half)]

    def send_half(chip, at, device):
        held = half_of(chip, at)
        return push(held, held, device)

    to_x, to_y = (data, along_x, core), (data, along_y, core)
    bc_all[mine] = bc_line[...]
    x_first = send_half(place, 0, to_x)
    y_second = send_half(place, 1, to_y)
    x_second = send_half(place, 1, to_x)
    y_first = send_half(place, 0, to_y)
    late.append(push(bc_all.at[mine], bc_all.at[mine], partner))
    x_first.wait_recv()
    over_y = send_half(along_x, 0, to_y)
    y_second.wait_recv()
    over_x = send_half(along_y, 1, to_x)
    for copies, chip in (((x_second,), along_x), ((y_first,), along_y), ((over_x, over_y), across)):
        for copy in copies:
            copy.wait_recv()
        held = bc_all.at[2 * chip + core]
        late.append(push(held, held, partner))
    for copy in late:
        copy.wait_recv()
    for copy in started:
        copy.wait_send()
    own.wait()


def finish_all(piece, bc_sum, bulk):
    count = lax.axis_size("dp")
    places = 2 * GROUP
    pushes = 3 * (count - 1) + (places - 1) + (GROUP - 1) + 6 + GROUP
    shaped = jax.ShapeDtypeStruct
    blocks = (count, bc_sum.shape[0] // count, bc_sum.shape[1])
    return pl.pallas_call(
        finish_kernel,
        out_shape=[
            shaped((places,) + piece.shape, jnp.float32),
            shaped((places,) + blocks, jnp.bfloat16),
            shaped(bulk.shape, bulk.dtype),
        ],
        in_specs=vmem_specs(2) + any_specs(1),
        out_specs=vmem_specs(2) + any_specs(1),
        scratch_shapes=[
            pltpu.VMEM(bc_sum.shape, jnp.bfloat16),
            pltpu.VMEM(blocks, jnp.bfloat16),
            pltpu.VMEM(blocks, jnp.bfloat16),
            pltpu.VMEM((count,) + piece.shape, jnp.float32),
            pltpu.SemaphoreType.DMA,
            pltpu.SemaphoreType.DMA((pushes,)),
            pltpu.SemaphoreType.DMA((pushes,)),
        ],
        cost_estimate=lasting(30),
        compiler_params=pltpu.CompilerParams(
            collective_id=6, has_side_effects=True, vmem_limit_bytes=VMEM_BYTES
        ),
    )(piece, bc_sum, bulk)


def unpack_early_kernel(
    gu_ref,
    down_ref,
    out_ref,
    both_ref,
    both_out,
    gate_ref,
    up_ref,
    d_ref,
    mo_ref,
    ao_ref,
    input_ref,
    output_ref,
):
    units, width = down_ref.shape[2], HEADS * HP
    input_ref[...] = both_ref[0]
    output_ref[...] = both_out[0]
    gate_ref[...] = gu_ref[0, :, :units].astype(jnp.float32)
    up_ref[...] = gu_ref[0, :, units:].astype(jnp.float32)
    d_ref[...] = down_ref[0].T.astype(jnp.float32)
    turned = out_ref[0].T.astype(jnp.float32)
    mo_ref[...] = turned[:width]
    ao_ref[...] = turned[width:]


def unpack_kernel(
    in_ref,
    bc_ref,
    misc_ref,
    pieces_ref,
    z_ref,
    x_ref,
    q_ref,
    grad_bc_ref,
    k_ref,
    v_ref,
    dt_ref,
    conv_ref,
    bias_ref,
    dtb_ref,
    alog_ref,
    skip_ref,
    group_ref,
    one_ref,
    two_ref,
    sums_ref,
):
    width, part = HEADS * HP, HD // 4
    z_ref[...] = in_ref[0, :, :width].astype(jnp.float32)
    q_ref[...] = in_ref[0, :, width : width + HD].astype(jnp.float32)
    x_ref[...] = in_ref[0, :, width + HD : 2 * width + HD].astype(jnp.float32)
    wide = bc_ref.shape[2]
    for core in range(2):
        grad_bc_ref[wide * core : wide * (core + 1)] = bc_ref[core].T.astype(jnp.float32)

    @pl.when(pl.program_id(0) == 0)
    def _():
        for index in range(2 * GROUP):
            piece = pieces_ref.shape[2]
            sums_ref[:, piece * index : piece * (index + 1)] = pieces_ref[index]
        held = [misc_ref[chip].astype(jnp.float32) for chip in range(GROUP)]
        k_ref[...] = jnp.concatenate(
            [
                held[0][:, :part],
                held[1][:, :part],
                held[0][:, part : 2 * part],
                held[1][:, part : 2 * part],
            ],
            axis=1,
        )
        v_ref[...] = jnp.concatenate([held[2][:, : 2 * part], held[3][:, : 2 * part]], axis=1)
        dt_ref[...] = jnp.concatenate(
            [values[:, DT_LANE : DT_LANE + HEADS] for values in held], axis=1
        ).T
        taps = conv_ref.shape[1]
        conv_ref[...] = sums_ref[:KC, :taps]
        for row in range(bias_ref.shape[0]):
            bias_ref[row : row + 1] = sums_ref[KC : KC + 1, 128 * row : 128 * (row + 1)]
        dtb_ref[...] = sums_ref[0:1, taps : taps + MH]
        alog_ref[...] = sums_ref[1:2, taps : taps + MH]
        skip_ref[...] = sums_ref[2:3, taps : taps + MH]
        start = taps + 128
        mine = GROUP * lax.axis_index("dp") + lax.axis_index("seq")
        slice_rows = one_ref.shape[1]
        each = slice_rows * GROUP * lax.axis_size("dp") // 8
        for ref in (one_ref, two_ref):
            gains = sums_ref[:, start : start + each]
            row = lax.broadcasted_iota(jnp.int32, (8, 1), 0)
            total = jnp.zeros((1, slice_rows), jnp.float32)
            for at in range(each // slice_rows):
                block = gains[:, slice_rows * at : slice_rows * (at + 1)]
                wanted = row * (each // slice_rows) + at == mine
                total = total + jnp.sum(jnp.where(wanted, block, 0.0), axis=0, keepdims=True)
            ref[...] = total
            start += each
        per_row = MH // 8
        for head in range(MH):
            row, lane = head // per_row, start + HP * (head % per_row)
            group_ref[head : head + 1, :] = sums_ref[row : row + 1, lane : lane + HP]


def across_chips(shape):
    return pl.BlockSpec((shape[0], shape[1] // GROUP), lambda chip: (0, chip))


def along_chips(shape):
    return pl.BlockSpec((shape[0] // GROUP, shape[1]), lambda chip: (chip, 0))


def per_chip(array, rows=1):
    return pl.BlockSpec((rows,) + array.shape[1:], lambda chip: (chip, 0, 0))


def unpack_early(gu, down, out, both, shapes):
    rows, width = both[0].shape[1:]
    step = 2 * rows // GROUP
    rows_in = pl.BlockSpec((1, step, width), lambda chip: (chip // 2, lax.rem(chip, 2), 0))
    kinds = [across_chips, across_chips, along_chips, along_chips, along_chips]
    out_shape = [jax.ShapeDtypeStruct(shape, jnp.float32) for shape in shapes]
    out_shape += [jax.ShapeDtypeStruct((2 * rows, width), array.dtype) for array in both]
    return pl.pallas_call(
        unpack_early_kernel,
        grid=(GROUP,),
        in_specs=[per_chip(gu), per_chip(down), per_chip(out), rows_in, rows_in],
        out_specs=[kind(shape) for kind, shape in zip(kinds, shapes)]
        + [along_chips((2 * rows, width))] * 2,
        out_shape=out_shape,
        cost_estimate=lasting(6),
        compiler_params=pltpu.CompilerParams(vmem_limit_bytes=VMEM_BYTES),
    )(gu, down, out, *both)


def unpack_late(in_all, bc_all, sums, shapes):
    def once(shape):
        return pl.BlockSpec(shape, lambda chip: (0,) * len(shape))

    misc_block = (GROUP, in_all.shape[1], HD)
    kinds = [across_chips] * 4
    kinds += [once] * (len(shapes) - len(kinds))
    return pl.pallas_call(
        unpack_kernel,
        grid=(GROUP,),
        in_specs=[
            per_chip(in_all),
            per_chip(bc_all, 2),
            pl.BlockSpec(misc_block, lambda chip: (0, 0, in_all.shape[2] // HD - 1)),
            once(sums.shape),
        ],
        out_specs=[kind(shape) for kind, shape in zip(kinds, shapes)],
        out_shape=[jax.ShapeDtypeStruct(shape, jnp.float32) for shape in shapes],
        scratch_shapes=[pltpu.VMEM((8, 2 * GROUP * sums.shape[2]), jnp.float32)],
        cost_estimate=lasting(6),
        compiler_params=pltpu.CompilerParams(vmem_limit_bytes=VMEM_BYTES),
    )(in_all, bc_all, in_all, sums)


def push_moves(moves, sources, targets, local_sems, send_sems, recv_sems, first=0):
    data, place, core, along_x, along_y, across = plane_place()
    copies = []
    for index, chip in enumerate((across, along_x, along_y)):
        for at, move in enumerate(moves):
            source, target = move(sources, targets, place, chip)
            slot = first + index * len(moves) + at
            copy = remote(
                source, target, send_sems.at[slot], recv_sems.at[slot], (data, chip, core)
            )
            copy.start()
            copies.append(copy)
    for at, move in enumerate(moves):
        source, target = move(sources, targets, place, place)
        copy = pltpu.make_async_copy(source, target, local_sems.at[at])
        copy.start()
        copies.append(copy)
    return copies


def plane_peers():
    data, place, core, along_x, along_y, across = plane_place()
    return [(data, chip, core) for chip in (across, along_x, along_y)]


def exchange_kernel(moves, count_in, *refs):
    sources, targets = refs[:count_in], refs[count_in:-3]
    meet(plane_peers())
    for copy in push_moves(moves, sources, targets, *refs[-3:]):
        copy.wait()


def first_exchange_kernel(
    moves,
    z_ref,
    q_ref,
    x_ref,
    key_ref,
    value_ref,
    dt_ref,
    one_ref,
    two_ref,
    in_ref,
    gains_ref,
    misc,
    gains,
    local_sems,
    send_sems,
    recv_sems,
):
    data, place, core, along_x, along_y, across = plane_place()
    places = GROUP * lax.axis_size("dp")
    mine = GROUP * data + place
    devices = []
    for turn_by in range(1, places):
        other = lax.rem(mine + turn_by, places)
        devices.append((other // GROUP, lax.rem(other, GROUP), core))
    half, part = HD // 2, HD // 4
    keys, values = key_ref[...], value_ref[...]
    steps = dt_ref[...].astype(jnp.float32).T.astype(keys.dtype)
    columns = (
        (keys[:, :part], keys[:, half : half + part]),
        (keys[:, part:half], keys[:, half + part :]),
        (values[:, :half],),
        (values[:, half:],),
    )
    for chip in range(GROUP):
        heads = steps[:, HEADS * chip : HEADS * (chip + 1)]
        rest = jnp.zeros((keys.shape[0], half - HEADS), keys.dtype)
        misc[chip] = jnp.concatenate([*columns[chip], heads, rest], axis=1)
    gains[...] = jnp.zeros_like(gains)
    gains[0:1] = one_ref[...].astype(jnp.float32)
    gains[1:2] = two_ref[...].astype(jnp.float32)
    meet(devices)
    sources = (z_ref, q_ref, x_ref, misc)
    copies = push_moves(moves, sources, (in_ref,), local_sems, send_sems, recv_sems)
    for index, device in enumerate(devices):
        slot = 3 * len(moves) + index
        copy = remote(
            gains, gains_ref.at[mine], send_sems.at[slot], recv_sems.at[slot], device
        )
        copy.start()
        copies.append(copy)
    gains_ref[mine] = gains[...]
    for copy in copies:
        copy.wait()


def first_exchange(moves, arrays, width_in):
    places = GROUP * lax.axis_size("dp")
    slice_rows = arrays[0].shape[0]
    count = 3 * len(moves) + places - 1
    return pl.pallas_call(
        partial(first_exchange_kernel, moves),
        out_shape=[
            jax.ShapeDtypeStruct((GROUP, slice_rows, width_in), jnp.bfloat16),
            jax.ShapeDtypeStruct((places, 8, slice_rows), jnp.float32),
        ],
        in_specs=any_specs(3) + vmem_specs(5),
        out_specs=any_specs(1) + vmem_specs(1),
        scratch_shapes=[
            pltpu.VMEM((GROUP, slice_rows, HD), jnp.bfloat16),
            pltpu.VMEM((8, slice_rows), jnp.float32),
            pltpu.SemaphoreType.DMA((len(moves),)),
            pltpu.SemaphoreType.DMA((count,)),
            pltpu.SemaphoreType.DMA((count,)),
        ],
        cost_estimate=lasting(20),
        compiler_params=pltpu.CompilerParams(collective_id=3, has_side_effects=True),
    )(*arrays)


def exchange_plane(moves, arrays, out_shapes, identity):
    count = 3 * len(moves)
    return pl.pallas_call(
        partial(exchange_kernel, moves, len(arrays)),
        out_shape=[jax.ShapeDtypeStruct(shape, jnp.bfloat16) for shape in out_shapes],
        in_specs=any_specs(len(arrays)),
        out_specs=any_specs(len(out_shapes)),
        scratch_shapes=[
            pltpu.SemaphoreType.DMA((len(moves),)),
            pltpu.SemaphoreType.DMA((count,)),
            pltpu.SemaphoreType.DMA((count,)),
        ],
        cost_estimate=lasting(25),
        compiler_params=pltpu.CompilerParams(collective_id=identity, has_side_effects=True),
    )(*arrays)


def column_move(source, target, start, width):
    def move(sources, targets, place, chip):
        columns = pl.ds(pl.multiple_of(chip * width, 128), width)
        return (
            sources[source].at[:, columns],
            targets[target].at[place, :, pl.ds(start, width)],
        )

    return move


def block_move(source, target):
    def move(sources, targets, place, chip):
        return (sources[source].at[chip], targets[target].at[place])

    return move


def misc_move(source, target, start):
    def move(sources, targets, place, chip):
        return (
            sources[source].at[chip],
            targets[target].at[place, :, pl.ds(start, 128)],
        )

    return move


def lane_masks():
    lane = lax.broadcasted_iota(jnp.int32, (1, 2 * HP), 1)
    return (lane < HP, lane >= HP)


DT_LANE = HP


def at_lane(lane, values):
    row = lax.broadcasted_iota(jnp.int32, (1, 2 * HP), 1)
    return jnp.where(row == lane, values, 0.0)


def dot_beside(exact, values, left_dim):
    width = values.shape[1]
    both = dot_f32(exact, jnp.concatenate(halves(values), axis=1), left_dim, 0)
    return both[:, :width] + both[:, width:]


def dot_along(left, right):
    left_high, left_low = halves(left)
    right_high, right_low = halves(right)
    return dot_f32(
        jnp.concatenate([left_high, left_high, left_low], axis=1),
        jnp.concatenate([right_high, right_low, right_high], axis=1),
        1,
        1,
    )


def spread_heads(*columns):
    width = HEADS * HP
    row = lax.rem(lax.broadcasted_iota(jnp.int32, (4 * HP, width), 0), 2 * HP)
    head = lax.broadcasted_iota(jnp.int32, (4 * HP, width), 1) // HP
    pick = jnp.where(row == DT_LANE + head, 1.0, 0.0).astype(jnp.bfloat16)
    parts = [jnp.concatenate(halves(values), axis=1) for values in columns]
    wide = dot_f32(jnp.concatenate(parts, axis=0), pick, 1, 0)
    size = columns[0].shape[0]
    return [wide[size * at : size * (at + 1)] for at in range(len(columns))]


def wide_keeps(keeps_ref):
    size = keeps_ref.shape[0]
    return [None] + [
        jnp.broadcast_to(keeps_ref[:, 1 + back : 2 + back], (size, 2 * HP))
        for back in range(1, KC)
    ]


def head_sums(values):
    low, high = lane_masks()
    first = jnp.sum(jnp.where(low, values, 0.0), axis=1, keepdims=True)
    second = jnp.sum(jnp.where(high, values, 0.0), axis=1, keepdims=True)
    return (first, second)


def head_means(values):
    low, high = lane_masks()
    first, second = head_sums(values)
    return jnp.where(low, first, second) * (1.0 / HP)


def stack_heads(values):
    low, high = lane_masks()
    zero = jnp.zeros_like(values)
    return jnp.concatenate([jnp.where(low, values, zero), jnp.where(high, values, zero)], axis=0)


def order_in(size):
    row = lax.broadcasted_iota(jnp.int32, (size, size), 0)
    column = lax.broadcasted_iota(jnp.int32, (size, size), 1)
    return (row, column)


def exact_sum(ones, values):
    high = values.astype(jnp.bfloat16)
    rest = values - high.astype(jnp.float32)
    middle = rest.astype(jnp.bfloat16)
    low = (rest - middle.astype(jnp.float32)).astype(jnp.bfloat16)
    return dot_f32(ones, high, 1, 0) + (dot_f32(ones, middle, 1, 0) + dot_f32(ones, low, 1, 0))


def chunk_decays(proj_ref, heads_ref, keeps_ref):
    size, width = proj_ref.shape
    raw = proj_ref[:, width - 2 * HP :] + heads_ref[0:1]
    dt_rows = jnp.maximum(raw, 0.0) + jnp.log1p(jnp.exp(-jnp.abs(raw)))
    row, column = order_in(size)
    lower = jnp.where(row >= column, 1.0, 0.0).astype(jnp.bfloat16)
    cumul = exact_sum(lower, -heads_ref[1:2] * dt_rows)
    enter = jnp.exp(cumul) * keeps_ref[:, 0:1]
    leave_bare = jnp.exp(cumul[size - 1 :] - cumul) * keeps_ref[:, 1:2]
    return (raw, dt_rows, cumul, enter, leave_bare)


def conv_windows(block, proj_ref, before_ref, bc_ref, bc_before_ref):
    if block < HEADS // 2:
        start = proj_ref.shape[1] - 2 * HP * (1 + HEADS // 2 - block)
        lanes = slice(start, start + 2 * HP)
        now, before = proj_ref[:, lanes], before_ref[:, lanes]
        now, before = now.astype(jnp.bfloat16), before.astype(jnp.bfloat16)
    else:
        start = 2 * HP * (block - HEADS // 2)
        lanes = slice(start, start + 2 * HP)
        now, before = bc_ref[:, lanes], bc_before_ref[8:, lanes]
    now, before = now.astype(jnp.float32), before.astype(jnp.float32)
    size = now.shape[0]
    extended = jnp.concatenate([before, now], axis=0)
    return [now] + [extended[8 - back : 8 - back + size] for back in range(1, KC)]


def conv_sum(windows, taps_ref, lanes, keeps):
    total = taps_ref[KC : KC + 1, lanes] + taps_ref[KC - 1 : KC, lanes] * windows[0]
    for back in range(1, KC):
        total = total + taps_ref[KC - 1 - back : KC - back, lanes] * (
            windows[back] * keeps[back]
        )
    return total


def head_decay(allowed, cumul, cumul_t, head):
    lane = DT_LANE + head
    differ = cumul[:, lane : lane + 1] - cumul_t[lane : lane + 1, :]
    return jnp.exp(jnp.where(allowed, differ, -jnp.inf))


def ssd_forward_kernel(
    proj_ref,
    before_ref,
    bc_ref,
    bc_before_ref,
    taps_ref,
    heads_ref,
    keeps_ref,
    segc_ref,
    segr_ref,
    skip_ref,
    gain_ref,
    cos_ref,
    sin_ref,
    gated_ref,
    ssm_ref,
    states_ref,
    mixed_ref,
    slope_ref,
    kv_ref,
    state,
):
    @pl.when(pl.program_id(0) == 0)
    def _():
        state[...] = jnp.zeros_like(state)

    size = proj_ref.shape[0]
    width = HEADS * HP
    keeps = wide_keeps(keeps_ref)
    for block in range(mixed_ref.shape[1] // (2 * HP)):
        lanes = slice(2 * HP * block, 2 * HP * (block + 1))
        windows = conv_windows(block, proj_ref, before_ref, bc_ref, bc_before_ref)
        summed = conv_sum(windows, taps_ref, lanes, keeps)
        sigmoid = jax.nn.sigmoid(summed)
        mixed_ref[:, lanes] = (summed * sigmoid).astype(jnp.bfloat16)
        slope_ref[:, lanes] = sigmoid * (1.0 + summed * (1.0 - sigmoid))
    raw, dt_rows, cumul, enter_all, leave_bare = chunk_decays(proj_ref, heads_ref, keeps_ref)
    enter_all, leave_all = spread_heads(enter_all, leave_bare * dt_rows)
    cumul_t, dt_t = cumul.T, dt_rows.T
    entry = state[...]
    states_ref[0] = entry
    b_rows, c_rows = mixed_ref[:, width : width + NS], mixed_ref[:, width + NS :]
    gram = dot_f32(c_rows, b_rows, 1, 1)
    row, column = order_in(size)
    allowed = (segc_ref[...] == segr_ref[0]) & (row >= column)
    entered = dot_beside(c_rows, entry, 1)
    weighted = []
    for pair in range(HEADS // 2):
        lanes = slice(2 * HP * pair, 2 * HP * (pair + 1))
        heads_x = mixed_ref[:, lanes]
        mixing = []
        for head in (2 * pair, 2 * pair + 1):
            lane = DT_LANE + head
            decay = head_decay(allowed, cumul, cumul_t, head)
            mixing.append(gram * decay * dt_t[lane : lane + 1, :])
        stacked = stack_heads(heads_x)
        out = dot_f32(
            jnp.concatenate(halves(jnp.concatenate(mixing, axis=1)), axis=1),
            jnp.concatenate([stacked, stacked], axis=0),
            1,
            0,
        )
        wide_x = heads_x.astype(jnp.float32)
        enter = enter_all[:, lanes]
        out = out + enter * entered[:, lanes] + skip_ref[:, lanes] * wide_x
        ssm_ref[:, lanes] = out
        gate = proj_ref[:, lanes]
        value = out * (gate * jax.nn.sigmoid(gate))
        scale = lax.rsqrt(head_means(value * value) + GROUP_EPSILON)
        gated_ref[:, lanes] = (value * scale * gain_ref[:, lanes]).astype(jnp.bfloat16)
        weighted.append(leave_all[:, lanes] * wide_x)
        state[:, lanes] = enter[size - 1 :, :] * entry[:, lanes]
    state[...] += dot_beside(b_rows, jnp.concatenate(weighted, axis=1), 0)
    kv = proj_ref[:, proj_ref.shape[1] - 2 * HP :][:, :HP]
    kv = jnp.concatenate([kv[: size // 2], kv[size // 2 :]], axis=1)
    kv_ref[...] = turn_folded(kv, cos_ref[...], sin_ref[...]).astype(jnp.bfloat16)


def ssd_backward_kernel(
    moves,
    proj_ref,
    slope_ref,
    bc_ref,
    taps_ref,
    heads_ref,
    keeps_ref,
    segc_ref,
    segr_ref,
    skip_ref,
    gain_ref,
    mixed_ref,
    ssm_ref,
    states_ref,
    dgated_ref,
    dq_ref,
    kv_own_ref,
    kv_x_ref,
    kv_y_ref,
    kv_a_ref,
    cos_ref,
    sin_ref,
    gu_ref,
    down_ref,
    dproj_ref,
    dtaps_ref,
    dheads_ref,
    dskip_ref,
    dgain_ref,
    gu_back,
    down_back,
    state,
    d_mixed,
    next_rows,
    *sems,
):
    def transfers(act):
        data, place, core, along_x, along_y, across = plane_place()
        sources, targets = (gu_ref, down_ref), (gu_back, down_back)
        local_sems, send_sems, recv_sems = sems
        for index, chip in enumerate((across, along_x, along_y)):
            for at, move in enumerate(moves):
                source, target = move(sources, targets, place, chip)
                slot = index * len(moves) + at
                act(
                    remote(
                        source, target, send_sems.at[slot], recv_sems.at[slot], (data, chip, core)
                    )
                )
        for at, move in enumerate(moves):
            source, target = move(sources, targets, place, place)
            act(pltpu.make_async_copy(source, target, local_sems.at[at]))

    @pl.when(pl.program_id(0) == 0)
    def _():
        meet(plane_peers())
        transfers(lambda copy: copy.start())
        state[...] = jnp.zeros_like(state)
        next_rows[...] = jnp.zeros_like(next_rows)
        dtaps_ref[...] = jnp.zeros_like(dtaps_ref)
        dheads_ref[...] = jnp.zeros_like(dheads_ref)
        dskip_ref[...] = jnp.zeros_like(dskip_ref)
        dgain_ref[...] = jnp.zeros_like(dgain_ref)

    size = proj_ref.shape[0]
    width = HEADS * HP
    raw, dt_rows, cumul, enter_all, leave_bare = chunk_decays(proj_ref, heads_ref, keeps_ref)
    cumul_t, dt_t = cumul.T, dt_rows.T
    later = state[...]
    entry = states_ref[0]
    carried = jnp.sum(later * entry, axis=0, keepdims=True)
    b_rows, c_rows = mixed_ref[:, width : width + NS], mixed_ref[:, width + NS :]
    gram = dot_f32(c_rows, b_rows, 1, 1)
    row, column = order_in(size)
    allowed = (segc_ref[...] == segr_ref[0]) & (row >= column)
    d_weighted = dot_beside(b_rows, later, 1)
    enter_all, bare_all, dt_all = spread_heads(enter_all, leave_bare, dt_rows)
    d_gram = jnp.zeros((size, size), jnp.float32)
    row_sums = jnp.zeros((size, 2 * HP), jnp.float32)
    column_sums = jnp.zeros((size, 2 * HP), jnp.float32)
    at_last = jnp.zeros((1, 2 * HP), jnp.float32)
    d_entered, weighted = [], []
    for pair in range(HEADS // 2):
        lanes = slice(2 * HP * pair, 2 * HP * (pair + 1))
        heads_x = mixed_ref[:, lanes]
        wide_x = heads_x.astype(jnp.float32)
        ssm, gate, gain = ssm_ref[:, lanes], proj_ref[:, lanes], gain_ref[:, lanes]
        d_gated = dgated_ref[:, lanes]
        sigmoid = jax.nn.sigmoid(gate)
        silu = gate * sigmoid
        value = ssm * silu
        scale = lax.rsqrt(head_means(value * value) + GROUP_EPSILON)
        dgain_ref[:, lanes] += jnp.sum(d_gated * value * scale, axis=0, keepdims=True)
        d_scaled = d_gated * gain
        d_value = scale * d_scaled - value * (scale * scale * scale) * head_means(d_scaled * value)
        d_out = d_value * silu
        dproj_ref[:, lanes] = (d_value * ssm * (sigmoid * (1.0 + gate * (1.0 - sigmoid)))).astype(
            jnp.bfloat16
        )
        dskip_ref[:, lanes] += jnp.sum(d_out * wide_x, axis=0, keepdims=True)
        enter, bare, dt_pair = enter_all[:, lanes], bare_all[:, lanes], dt_all[:, lanes]
        high, low = [stack_heads(half) for half in halves(d_out)]
        d_mixing = dot_f32(jnp.concatenate([high, low], axis=0), heads_x, 1, 1)
        grams = []
        for side in range(2):
            head = 2 * pair + side
            lane = DT_LANE + head
            decay = head_decay(allowed, cumul, cumul_t, head)
            grams.append(gram * decay)
            first = size * side
            d_mix = d_mixing[first : first + size] + d_mixing[2 * size + first : 3 * size + first]
            d_gram = d_gram + d_mix * (decay * dt_t[lane : lane + 1, :])
        gram_high, gram_low = halves(jnp.concatenate(grams, axis=0))
        bare_x = dot_f32(
            jnp.concatenate([high, low, high], axis=0),
            jnp.concatenate([gram_high, gram_high, gram_low], axis=0),
            0,
            0,
        ).T
        left = bare * d_weighted[:, lanes]
        d_x = bare_x + left
        first_lane = DT_LANE + 2 * pair
        first, second = head_sums(d_out * (ssm - skip_ref[:, lanes] * wide_x))
        row_sums = row_sums + at_lane(first_lane, first) + at_lane(first_lane + 1, second)
        first, second = head_sums(d_x * wide_x)
        column_sums = column_sums + at_lane(first_lane, first) + at_lane(first_lane + 1, second)
        last = jnp.sum(dt_pair * left * wide_x, axis=0, keepdims=True)
        last = last + carried[:, lanes] * enter[size - 1 :]
        first, second = head_sums(last)
        at_last = at_last + at_lane(first_lane, first) + at_lane(first_lane + 1, second)
        d_mixed[:, lanes] = dt_pair * d_x + skip_ref[:, lanes] * d_out
        d_entered.append(enter * d_out)
        weighted.append(bare * dt_pair * wide_x)
        state[:, lanes] = enter[size - 1 :, :] * later[:, lanes]
    d_entered = jnp.concatenate(d_entered, axis=1)
    state[...] += dot_beside(c_rows, d_entered, 0)
    d_gram_parts = halves(d_gram)
    d_b = dot_along(jnp.concatenate(weighted, axis=1), later)
    d_mixed[:, width : width + NS] = d_b + dot_f32(
        jnp.concatenate(d_gram_parts, axis=0),
        jnp.concatenate([c_rows, c_rows], axis=0),
        0,
        0,
    )
    d_c = dot_along(d_entered, entry)
    d_mixed[:, width + NS :] = d_c + dot_f32(
        jnp.concatenate(d_gram_parts, axis=1),
        jnp.concatenate([b_rows, b_rows], axis=0),
        1,
        0,
    )

    d_cumul = row_sums - column_sums * dt_rows
    last_row = lax.broadcasted_iota(jnp.int32, (size, 1), 0) == size - 1
    d_cumul = d_cumul + jnp.where(last_row, at_last, 0.0)
    upper = jnp.where(row <= column, 1.0, 0.0).astype(jnp.bfloat16)
    d_log = exact_sum(upper, d_cumul)
    rate = heads_ref[1:2]
    d_raw = (column_sums - rate * d_log) * jax.nn.sigmoid(raw)
    lane_row = lax.broadcasted_iota(jnp.int32, (1, 2 * HP), 1)
    d_raw = jnp.where((lane_row >= DT_LANE) & (lane_row < DT_LANE + HEADS), d_raw, 0.0)
    dheads_ref[0:1] += jnp.sum(d_raw, axis=0, keepdims=True)
    dheads_ref[1:2] += -rate * jnp.sum(d_log * dt_rows, axis=0, keepdims=True)
    total = proj_ref.shape[1]
    d_kv = kv_own_ref[...].astype(jnp.float32)
    for ref in (kv_x_ref, kv_y_ref, kv_a_ref):
        d_kv = d_kv + ref[...].astype(jnp.float32)
    d_kv = turn_folded(d_kv, cos_ref[...], -sin_ref[...])
    d_kv = jnp.concatenate([d_kv[:, :DT_LANE], d_kv[:, DT_LANE:]], axis=0)
    dproj_ref[:, total - 2 * HP : total] = jnp.concatenate(
        [d_kv, d_raw[:, DT_LANE:]], axis=1
    ).astype(jnp.bfloat16)
    dproj_ref[:, width : width + HD] = dq_ref[...]

    keeps = wide_keeps(keeps_ref)
    for block in range(mixed_ref.shape[1] // (2 * HP)):
        lanes = slice(2 * HP * block, 2 * HP * (block + 1))
        if block < HEADS // 2:
            start = total - 2 * HP * (1 + HEADS // 2 - block)
            pre = proj_ref[:, start : start + 2 * HP].astype(jnp.bfloat16).astype(jnp.float32)
        else:
            start = 2 * HP * (block - HEADS // 2)
            pre = bc_ref[:, start : start + 2 * HP].astype(jnp.float32)
        d_sum = d_mixed[:, lanes] * slope_ref[:, lanes]
        dtaps_ref[KC : KC + 1, lanes] += jnp.sum(d_sum, axis=0, keepdims=True)
        dtaps_ref[KC - 1 : KC, lanes] += jnp.sum(d_sum * pre, axis=0, keepdims=True)
        d_pre = taps_ref[KC - 1 : KC, lanes] * d_sum
        for back in range(1, KC):
            tap = KC - 1 - back
            kept = d_sum * keeps[back]
            extended = jnp.concatenate([kept, next_rows[back - 1, :, lanes]], axis=0)
            later_rows = extended[back : back + size]
            dtaps_ref[tap : tap + 1, lanes] += jnp.sum(later_rows * pre, axis=0, keepdims=True)
            d_pre = d_pre + taps_ref[tap : tap + 1, lanes] * later_rows
            next_rows[back - 1, :, lanes] = kept[:8]
        if block < HEADS // 2:
            start = total - 2 * HP * (1 + HEADS // 2 - block)
            dproj_ref[:, start : start + 2 * HP] = d_pre.astype(jnp.bfloat16)
        else:
            start = total + 2 * HP * (block - HEADS // 2)
            dproj_ref[:, start : start + 2 * HP] = d_pre.astype(jnp.bfloat16)

    @pl.when(pl.program_id(0) == pl.num_programs(0) - 1)
    def _():
        transfers(lambda copy: copy.wait())


def ssd_specs(length, reverse, width_in, width_all, width):
    laps = length // CHUNK

    def at(lap):
        return laps - 1 - lap if reverse else lap

    def tall(columns):
        return pl.BlockSpec((CHUNK, columns), lambda lap: (at(lap), 0))

    def rim(rows, columns):
        each = CHUNK // rows
        return pl.BlockSpec((rows, columns), lambda lap: (lax.rem(each * (at(lap) + laps) - 1, each * laps), 0))

    def whole(rows, columns):
        return pl.BlockSpec((rows, columns), lambda lap: (0, 0))

    def slab(rows, columns):
        return pl.BlockSpec((1, rows, columns), lambda lap: (at(lap), 0, 0))

    specs = [
        tall(width_in),
        rim(8, width_in),
        tall(2 * NS),
        rim(16, 2 * NS),
        whole(8, width_all),
        whole(8, 2 * HP),
        tall(8),
        tall(1),
        slab(1, CHUNK),
        whole(1, width),
        whole(1, width),
    ]
    return (laps, tall, whole, slab, specs)


def ssd_forward(arrays, cos_part, sin_part):
    length, width_in = arrays[0].shape
    width, width_all = HEADS * HP, HEADS * HP + 2 * NS
    laps, tall, whole, slab, specs = ssd_specs(length, False, width_in, width_all, width)
    shaped = jax.ShapeDtypeStruct
    fold = pl.BlockSpec((CHUNK // 2, 2 * HP), lambda lap: (lap, 0))
    return pl.pallas_call(
        ssd_forward_kernel,
        grid=(laps,),
        in_specs=specs + [fold, fold],
        out_specs=[
            tall(width),
            tall(width),
            slab(NS, width),
            tall(width_all),
            tall(width_all),
            fold,
        ],
        out_shape=[
            shaped((length, width), jnp.bfloat16),
            shaped((length, width), jnp.float32),
            shaped((laps, NS, width), jnp.float32),
            shaped((length, width_all), jnp.bfloat16),
            shaped((length, width_all), jnp.float32),
            shaped((length // 2, 2 * HP), jnp.bfloat16),
        ],
        scratch_shapes=[pltpu.VMEM((NS, width), jnp.float32)],
        cost_estimate=lasting(6),
        compiler_params=pltpu.CompilerParams(vmem_limit_bytes=VMEM_BYTES),
    )(*arrays, cos_part, sin_part)


def ssd_backward(arrays, slope, mixed, ssm, states, d_outs, d_query, d_kv_parts, tables, grads):
    length, width_in = arrays[0].shape
    width, width_all = HEADS * HP, HEADS * HP + 2 * NS
    laps, tall, whole, slab, specs = ssd_specs(length, True, width_in, width_all, width)
    shaped = jax.ShapeDtypeStruct
    moves = (block_move(0, 0), block_move(1, 1))
    fold = pl.BlockSpec((CHUNK // 2, 2 * HP), lambda lap: (laps - 1 - lap, 0))
    return pl.pallas_call(
        partial(ssd_backward_kernel, moves),
        grid=(laps,),
        in_specs=[specs[0], tall(width_all), specs[2], *specs[4:]]
        + [
            tall(width_all),
            tall(width),
            slab(NS, width),
            tall(width),
            tall(HD),
        ]
        + [fold] * 6
        + any_specs(2),
        out_specs=[
            tall(width_in + 2 * NS),
            whole(8, width_all),
            whole(8, 2 * HP),
            whole(1, width),
            whole(1, width),
        ]
        + any_specs(2),
        out_shape=[
            shaped((length, width_in + 2 * NS), jnp.bfloat16),
            shaped((8, width_all), jnp.float32),
            shaped((8, 2 * HP), jnp.float32),
            shaped((1, width), jnp.float32),
            shaped((1, width), jnp.float32),
        ]
        + [shaped(array.shape, array.dtype) for array in grads],
        scratch_shapes=[
            pltpu.VMEM((NS, width), jnp.float32),
            pltpu.VMEM((CHUNK, width_all), jnp.float32),
            pltpu.VMEM((KC - 1, 8, width_all), jnp.float32),
            pltpu.SemaphoreType.DMA((len(moves),)),
            pltpu.SemaphoreType.DMA((3 * len(moves),)),
            pltpu.SemaphoreType.DMA((3 * len(moves),)),
        ],
        cost_estimate=lasting(48),
        compiler_params=pltpu.CompilerParams(
            collective_id=13, has_side_effects=True, vmem_limit_bytes=VMEM_BYTES
        ),
    )(arrays[0], slope, arrays[2], *arrays[4:], mixed, ssm, states, d_outs, d_query, *d_kv_parts, *tables, *grads)


QUERY_ROWS = 256


def masked_scores(q_rows, k_ref, segc_ref, segr_ref, start, reach):
    rows = q_rows.shape[0]
    scores = dot_f32(q_rows, k_ref[:reach], 1, 1) * HD ** (-0.5)
    row = lax.broadcasted_iota(jnp.int32, (rows, reach), 0) + start
    column = lax.broadcasted_iota(jnp.int32, (rows, reach), 1)
    allowed = (segc_ref[start : start + rows] == segr_ref[:, :reach]) & (row >= column)
    return jnp.where(allowed, scores, -jnp.inf)


def rotate_rows(values, cos_ref, sin_ref, sign):
    return values * cos_ref[...] + sign * (pltpu.roll(values, HD // 2, 1) * sin_ref[...])


def swap_middle(values):
    lane = lax.broadcasted_iota(jnp.int32, (1, HD), 1) // (HD // 4)
    up = pltpu.roll(values, HD // 4, 1)
    down = pltpu.roll(values, HD - HD // 4, 1)
    return jnp.where(lane == 1, down, jnp.where(lane == 2, up, values))


def unfold_rows(values, write):
    step, columns = CHUNK // 2, values.shape[1] // 2
    for start in range(0, values.shape[0], step):
        rows = values[start : start + step]
        write(2 * start, rows[:, :columns])
        write(2 * start + step, rows[:, columns:])


def fold_rows(ref, index, values):
    step = CHUNK // 2
    for start in range(0, values.shape[0] // 2, step):
        ref[index, start : start + step] = jnp.concatenate(
            [values[2 * start : 2 * start + step], values[2 * start + step : 2 * start + 2 * step]],
            axis=1,
        ).astype(ref.dtype)


def join_halves(ref, first, target):
    half = HD // 2

    def write_at(lanes):
        def write(start, rows):
            target[start : start + rows.shape[0], lanes] = rows

        return write

    unfold_rows(ref[first], write_at(slice(0, half)))
    unfold_rows(ref[first + 1], write_at(slice(half, HD)))


def attend_forward_kernel(
    raw_ref, cos_ref, sin_ref, kv_ref, segc_ref, segr_ref, out_ref, total_ref, q_ref, k_ref, v_ref
):
    q_ref[...] = swap_middle(rotate_rows(raw_ref[...], cos_ref, sin_ref, 1.0)).astype(jnp.bfloat16)
    join_halves(kv_ref, 0, k_ref)
    join_halves(kv_ref, 2, v_ref)
    for start in range(0, q_ref.shape[0], QUERY_ROWS):
        reach = start + QUERY_ROWS
        rows = slice(start, reach)
        scores = masked_scores(q_ref[rows], k_ref, segc_ref, segr_ref, start, reach)
        top = jnp.max(scores, axis=1, keepdims=True)
        powers = jnp.exp(scores - top)
        total = jnp.sum(powers, axis=1, keepdims=True)
        probs = (powers * (1.0 / total)).astype(jnp.bfloat16)
        out_ref[rows] = dot_f32(probs, v_ref[:reach], 1, 0).astype(jnp.bfloat16)
        total_ref[rows] = top + jnp.log(total)


def attend_backward_kernel(
    q_ref,
    k_ref,
    v_ref,
    cos_ref,
    sin_ref,
    segc_ref,
    segr_ref,
    total_ref,
    dout_ref,
    dq_ref,
    dkv_ref,
    dq_sum,
    dk_sum,
    dv_sum,
):
    dk_sum[...] = jnp.zeros_like(dk_sum)
    dv_sum[...] = jnp.zeros_like(dv_sum)
    for start in range(0, q_ref.shape[0], QUERY_ROWS):
        reach = start + QUERY_ROWS
        rows = slice(start, reach)
        q_rows, d_out = q_ref[rows], dout_ref[rows]
        scores = masked_scores(q_rows, k_ref, segc_ref, segr_ref, start, reach)
        probs = jnp.exp(scores - total_ref[rows])
        d_probs = dot_f32(d_out, v_ref[:reach], 1, 1)
        delta = jnp.sum(probs * d_probs, axis=1, keepdims=True)
        d_scores = (probs * (d_probs - delta)).astype(jnp.bfloat16)
        dq_sum[rows] = dot_f32(d_scores, k_ref[:reach], 1, 0) * HD ** (-0.5)
        dk_sum[:reach] += dot_f32(d_scores, q_rows, 0, 0) * HD ** (-0.5)
        dv_sum[:reach] += dot_f32(probs.astype(jnp.bfloat16), d_out, 0, 0)
    dq_ref[...] = rotate_rows(swap_middle(dq_sum[...]), cos_ref, sin_ref, -1.0).astype(jnp.bfloat16)
    half = HD // 2
    fold_rows(dkv_ref, 0, dk_sum[:, :half])
    fold_rows(dkv_ref, 1, dk_sum[:, half:])
    fold_rows(dkv_ref, 2, dv_sum[:, :half])
    fold_rows(dkv_ref, 3, dv_sum[:, half:])


def rotation_tables(length):
    half, part = HD // 2, HD // 4
    frequency = np.float32(ROPE_BASE) ** (
        np.float32(-2.0) * np.arange(half).astype(np.float32) / np.float32(HD)
    )
    angles = np.arange(length).astype(np.float32)[:, None] * frequency[None, :]
    cosine, sine_part = np.cos(angles), np.sin(angles)

    def folded(values):
        rows = values.reshape(length // CHUNK, 2, CHUNK // 2, half)
        return rows.transpose(0, 2, 1, 3).reshape(length // 2, HD)

    cos_kinds, sin_kinds = [], []
    for start in (0, part):
        columns = slice(start, start + part)
        cos_part, sin_part = cosine[:, columns], sine_part[:, columns]
        cos_kinds.append(folded(np.concatenate([cos_part, cos_part], axis=1)))
        sin_kinds.append(folded(np.concatenate([-sin_part, sin_part], axis=1)))
    cos_kinds.append(np.ones_like(cos_kinds[0]))
    sin_kinds.append(np.zeros_like(sin_kinds[0]))
    tables = (
        np.concatenate([cosine, cosine], axis=1),
        np.concatenate([-sine_part, sine_part], axis=1),
        np.stack(cos_kinds),
        np.stack(sin_kinds),
    )
    return [jnp.asarray(table.astype(np.float32)) for table in tables]


def turn_folded(values, cosine, sine_part):
    lane = lax.rem(lax.broadcasted_iota(jnp.int32, (1, HD), 1), HD // 2)
    quarter = HD // 4
    other = jnp.where(
        lane < quarter, pltpu.roll(values, HD - quarter, 1), pltpu.roll(values, quarter, 1)
    )
    return values * cosine + other * sine_part


def whole_block(shape):
    return pl.BlockSpec(shape, lambda step: (0,) * len(shape))


def attend(kernel, arrays, out_shapes, scratch=(), blocks=None):
    return pl.pallas_call(
        kernel,
        grid=(1,),
        in_specs=[
            whole_block(array.shape) if blocks is None or blocks[at] is None else blocks[at]
            for at, array in enumerate(arrays)
        ],
        out_specs=[whole_block(shape) for shape, _ in out_shapes],
        out_shape=[jax.ShapeDtypeStruct(shape, dtype) for shape, dtype in out_shapes],
        scratch_shapes=[pltpu.VMEM(shape, dtype) for shape, dtype in scratch],
        cost_estimate=lasting(9),
        compiler_params=pltpu.CompilerParams(vmem_limit_bytes=VMEM_BYTES),
    )(*arrays)


def after(value, *earlier):
    return lax.optimization_barrier((value,) + earlier)[0]


def over_chips(block):
    place = lax.axis_index("seq")
    count = lax.axis_size("seq")
    stacked = jnp.zeros((count,) + block.shape, block.dtype)
    stacked = lax.dynamic_update_index_in_dim(stacked, block, place, 0)
    for mask in range(1, count):
        moved = lax.ppermute(block, "seq", [(i, i ^ mask) for i in range(count)])
        stacked = lax.dynamic_update_index_in_dim(stacked, moved, place ^ mask, 0)
    return stacked


def from_chips(blocks):
    place = lax.axis_index("seq")
    count = lax.axis_size("seq")
    moved = [lax.dynamic_index_in_dim(blocks, place, 0, False)]
    for mask in range(1, count):
        block = lax.dynamic_index_in_dim(blocks, place ^ mask, 0, False)
        moved.append(lax.ppermute(block, "seq", [(i, i ^ mask) for i in range(count)]))
    return moved


def heads_local_plan(
    hidden_in,
    teacher,
    segment_ids,
    valid_mask,
    norm1_gain,
    w_z,
    w_x,
    w_bc,
    w_dt,
    conv_weight,
    conv_bias,
    dt_bias,
    a_log,
    d_skip,
    group_gain,
    w_mamba_out,
    w_query,
    w_key,
    w_value,
    w_attn_out,
    norm2_gain,
    w_gate,
    w_up,
    w_down,
):
    place, core, data_rank = (
        lax.axis_index("seq"),
        lax.axis_index("tensor"),
        lax.axis_index("dp"),
    )
    data_count = lax.axis_size("dp")
    chip_rows, width = hidden_in.shape[1:]
    own_rows = chip_rows // 2
    length = segment_ids.shape[1]
    slice_rows = w_z.shape[0]
    width_x = HEADS * HP
    hidden_units = w_gate.shape[1] // GROUP
    segment = segment_ids[0]
    own_start = place * chip_rows + core * own_rows
    token_count = jnp.sum(valid_mask).astype(jnp.float32)
    mask_rows = lax.dynamic_slice(valid_mask, (data_rank, own_start), (1, own_rows))[0]
    total_tokens = float(valid_mask.shape[0] * valid_mask.shape[1])
    bf16 = jnp.bfloat16

    half, part = HD // 2, HD // 4
    width_in = 2 * width_x + 2 * HD
    in_slices, gains_all = first_exchange(
        (
            column_move(0, 0, 0, width_x),
            column_move(1, 0, width_x, HD),
            column_move(2, 0, width_x + HD, width_x),
            misc_move(3, 0, 2 * width_x + HD),
        ),
        (w_z, w_query, w_x, w_key, w_value, w_dt.T, norm1_gain[None], norm2_gain[None]),
        width_in,
    )
    gain_one, gain_two = gains_all[:, 0].reshape(width), gains_all[:, 1].reshape(width)
    full_in = lax.all_gather(in_slices, "dp", axis=0, tiled=True).reshape(width, width_in)
    hidden_own = lax.dynamic_slice(hidden_in[0], (core * own_rows, 0), (own_rows, width))
    hidden_own = after(hidden_own, in_slices)
    hidden_all, normed, pre_bc = gather_plane(
        hidden_own,
        1,
        apply_norm,
        (gain_one[None], w_bc),
        (((length, width), bf16), ((length, 2 * NS), bf16)),
    )
    hidden_low, hidden_own = hidden_own, hidden_own.astype(jnp.float32)
    width_out = width_x + HD
    out_slices, gu_slices, down_slices = exchange_plane(
        (
            column_move(0, 0, 0, width_x),
            column_move(1, 0, width_x, HD),
            column_move(2, 1, 0, hidden_units),
            column_move(3, 1, hidden_units, hidden_units),
            column_move(4, 2, 0, hidden_units),
        ),
        (after(w_mamba_out.T, normed), w_attn_out.T, w_gate, w_up, w_down.T),
        [
            (GROUP, slice_rows, width_out),
            (GROUP, slice_rows, 2 * hidden_units),
            (GROUP, slice_rows, hidden_units),
        ],
        4,
    )
    out_gathered = lax.all_gather(after(out_slices, full_in), "dp", axis=0, tiled=True)
    full_out = out_gathered.reshape(width, width_out)

    segment, conv_weight, conv_bias, dt_bias, a_log, d_skip, group_gain = (
        lax.optimization_barrier(
            (segment, conv_weight, conv_bias, dt_bias, a_log, d_skip, group_gain, out_slices)
        )[:7]
    )
    seg_column, seg_row = segment[:, None], segment[None, :]
    cos_wide, sin_wide, cos_folded, sin_folded = rotation_tables(length)
    kind = jnp.minimum(place, 2)
    cos_folded = lax.dynamic_index_in_dim(cos_folded, kind, 0, False)
    sin_folded = lax.dynamic_index_in_dim(sin_folded, kind, 0, False)
    head_start = core * (MH // 2) + place * HEADS

    def local_rows(values, width_head):
        return jnp.concatenate(
            [
                lax.dynamic_slice_in_dim(values, head_start * width_head, HEADS * width_head, 0),
                values[MH * width_head :],
            ],
            axis=0,
        )

    taps = jnp.concatenate(
        [local_rows(conv_weight, HP).T, local_rows(conv_bias, HP)[None]], axis=0
    )
    taps = jnp.pad(taps, ((0, 8 - KC - 1), (0, 0)))
    rate = jnp.exp(local_rows(a_log, 1))
    head_rows = jnp.stack([local_rows(dt_bias, 1), rate])
    head_rows = jnp.pad(head_rows, ((0, 6), (DT_LANE, HD - DT_LANE - HEADS)))
    skip_row = jnp.repeat(local_rows(d_skip, 1), HP)[None, :]
    gain_row = lax.dynamic_slice_in_dim(group_gain, head_start, HEADS, 0).reshape(1, width_x)
    laps = length // CHUNK
    seg_laps = segment.reshape(laps, CHUNK)
    seg_last = seg_laps[:, -1:]
    seg_before = jnp.concatenate([jnp.full((1, 1), -1, jnp.int32), seg_last[:-1]])
    seg_ext = jnp.concatenate([jnp.full((KC - 1,), -1, jnp.int32), segment])
    keeps = [(seg_laps == seg_before).reshape(length), (seg_laps == seg_last).reshape(length)]
    keeps += [seg_ext[KC - 1 - back : KC - 1 - back + length] == segment for back in range(1, KC)]
    keeps = jnp.stack(keeps + [jnp.zeros((length,), bool)] * 3, axis=1).astype(jnp.float32)

    projected = mat_dot(normed, full_in)

    ssd_arrays = (
        projected,
        projected,
        pre_bc,
        pre_bc,
        taps,
        head_rows,
        keeps,
        seg_column,
        seg_laps[:, None, :],
        skip_row,
        gain_row,
    )
    gated, ssm, states, mixed, slope, kv_own = ssd_forward(ssd_arrays, cos_folded, sin_folded)
    kv_all = over_chips(kv_own)
    gu_gathered = lax.all_gather(after(gu_slices, out_gathered, gated), "dp", axis=0, tiled=True)
    down_gathered = lax.all_gather(after(down_slices, gu_gathered), "dp", axis=0, tiled=True)
    full_gu = gu_gathered.reshape(width, 2 * hidden_units)
    full_down = down_gathered.reshape(width, hidden_units)
    attended, log_total, queries, keys, vals = attend(
        attend_forward_kernel,
        (
            projected,
            cos_wide,
            sin_wide,
            after(kv_all, out_gathered),
            seg_column,
            seg_row,
        ),
        (
            ((length, HD), bf16),
            ((length, 1), jnp.float32),
            ((length, HD), bf16),
            ((length, HD), bf16),
            ((length, HD), bf16),
        ),
        blocks=[pl.BlockSpec((length, HD), lambda step: (0, width_x // HD))] + [None] * 5,
    )
    outs = jnp.concatenate([gated, attended], axis=1)
    middle = hidden_own + scatter_plane(outs, full_out, 2)[0]

    scale_two = lax.rsqrt(jnp.mean(middle * middle, axis=-1, keepdims=True) + EPSILON)
    normed_two, gate_up, activated = gather_plane(
        after((middle * scale_two * gain_two).astype(bf16), gu_gathered),
        9,
        apply_gate_up,
        (full_gu,),
        (((length, 2 * hidden_units), jnp.float32), ((length, hidden_units), bf16)),
    )
    teacher_own = lax.dynamic_slice(teacher[0], (core * own_rows, 0), (own_rows, width))
    factor = 2.0 * total_tokens / token_count * mask_rows.astype(jnp.float32)[:, None]
    block_out, d_out, d_gate_up, grad_down = down_and_back(
        activated, full_down, middle, teacher_own, factor, gate_up
    )

    def sum_rows(grads):
        summed = lax.psum_scatter(grads.astype(bf16), "dp", scatter_dimension=0, tiled=True)
        return summed.reshape(GROUP, slice_rows, grads.shape[1])

    grad_down = sum_rows(grad_down)
    d_normed_two, grad_gate_up = up_back(d_gate_up, full_gu, normed_two)
    grad_gate_up = sum_rows(after(grad_gate_up, grad_down))
    grad_gain_two = jnp.sum(d_normed_two * middle * scale_two, axis=0)
    d_scaled = d_normed_two * gain_two
    d_middle = (
        d_out
        + scale_two * d_scaled
        - middle * scale_two**3 * jnp.mean(d_scaled * middle, axis=-1, keepdims=True)
    )
    d_branch, d_gated, d_attended = gather_plane(
        after(d_middle.astype(bf16), grad_down),
        12,
        apply_out_back,
        (full_out,),
        (((length, width_x), jnp.float32), ((length, HD), bf16)),
    )
    d_query, d_kv = attend(
        attend_backward_kernel,
        (
            queries,
            keys,
            vals,
            cos_wide,
            sin_wide,
            seg_column,
            seg_row,
            log_total,
            d_attended,
        ),
        (((length, HD), bf16), ((GROUP, length // 2, HD), bf16)),
        (((length, HD), jnp.float32),) * 3,
    )
    d_kv_parts = from_chips(d_kv)
    grad_out = sum_rows(
        after(dot_left_t(d_branch, outs).astype(bf16), grad_gate_up, d_query)
    )
    (
        d_projected,
        grad_taps,
        grad_heads,
        d_skip_lanes,
        d_gain_lanes,
        back_gate_up,
        back_down,
    ) = ssd_backward(
        ssd_arrays,
        slope,
        mixed,
        ssm,
        states,
        d_gated,
        d_query,
        d_kv_parts,
        (cos_folded, sin_folded),
        (grad_gate_up, grad_down),
    )
    grad_skip = jnp.sum(d_skip_lanes.reshape(HEADS, HP), axis=-1)
    grad_group = d_gain_lanes.reshape(HEADS, HP)
    grad_in = sum_rows(
        after(dot_left_t(normed, d_projected[:, :width_in]).astype(bf16), grad_out)
    )
    bc_cols = 2 * NS // GROUP
    grad_input, bc_sum, gain_sums = input_back(
        after(d_projected, grad_out),
        full_in,
        normed,
        w_bc,
        hidden_low,
        d_middle,
        gain_one[None],
        bc_cols,
    )
    grad_gain_one = jnp.sum(gain_sums, axis=0)

    taps_all = jnp.concatenate(
        [
            lax.dynamic_update_slice(
                jnp.zeros((8, MH * HP), jnp.float32), grad_taps[:, :width_x], (0, head_start * HP)
            ),
            grad_taps[:, width_x:],
        ],
        axis=1,
    )
    heads_all = lax.dynamic_update_slice(
        jnp.zeros((8, 128), jnp.float32),
        jnp.concatenate([grad_heads[:2, DT_LANE : DT_LANE + HEADS], grad_skip[None]]),
        (0, head_start),
    )
    group_all = lax.dynamic_update_slice(
        jnp.zeros((MH, HP), jnp.float32), grad_group, (head_start, 0)
    )
    small = [taps_all, heads_all]
    small += [
        values.reshape(8, -1) for values in (grad_gain_one, grad_gain_two, group_all)
    ]
    small = jnp.concatenate(small, axis=1)
    small_width = -(-small.shape[1] // (2 * GROUP * 128)) * 2 * GROUP * 128
    small = jnp.pad(small, ((0, 0), (0, small_width - small.shape[1])))
    piece, both_input, both_output, back_out = plane_sum(small, grad_input, block_out, grad_out)
    grad_gate, grad_up, grad_down, grad_mo, grad_ao, grad_input, block_out = unpack_early(
        back_gate_up,
        back_down,
        back_out,
        (both_input, both_output),
        [array.shape for array in (w_gate, w_up, w_down, w_mamba_out, w_attn_out)],
    )
    small_all, bc_all, back_in = finish_all(after(piece, grad_input), bc_sum, grad_in)
    bc_all = bc_all.reshape(2 * GROUP, bc_cols, width // 2)
    shapes = [
        array.shape
        for array in (w_z, w_x, w_query, w_bc, w_key, w_value, w_dt.T, conv_weight.T)
    ]
    shapes += [(conv_bias.shape[0] // 128, 128)] + [(1, MH)] * 3 + [(MH, HP)] + [(1, slice_rows)] * 2
    (
        grad_z,
        grad_x,
        grad_q,
        grad_bc,
        grad_k,
        grad_v,
        grad_dt,
        grad_conv,
        grad_bias,
        grad_dtb,
        grad_alog,
        grad_skip,
        grad_group,
        grad_one,
        grad_two,
    ) = unpack_late(back_in, bc_all, small_all, shapes)
    return (
        block_out[None],
        grad_input[None],
        grad_one[0],
        grad_z,
        grad_x,
        grad_bc,
        grad_dt.T,
        grad_conv.T,
        grad_bias.reshape(-1),
        grad_dtb[0],
        grad_alog[0],
        grad_skip[0],
        grad_group,
        grad_mo,
        grad_q,
        grad_k,
        grad_v,
        grad_ao,
        grad_two[0],
        grad_gate,
        grad_up,
        grad_down,
    )


def solution(mesh):
    placed = (
        P("dp", "seq", None),
        P("dp", "seq", None),
        P("dp", None),
        P(),
        P(("dp", "seq")),
        P(("dp", "seq"), "tensor"),
        P(("dp", "seq"), "tensor"),
        P(),
        P(("dp", "seq"), "tensor"),
        P(),
        P(),
        P(),
        P(),
        P(),
        P(),
        P("tensor", ("dp", "seq")),
        P(("dp", "seq"), "tensor"),
        P(("dp", "seq"), "tensor"),
        P(("dp", "seq"), "tensor"),
        P("tensor", ("dp", "seq")),
        P(("dp", "seq")),
        P(("dp", "seq"), "tensor"),
        P(("dp", "seq"), "tensor"),
        P("tensor", ("dp", "seq")),
    )
    whole_row = mesh.shape["seq"] == GROUP and mesh.shape["tensor"] == 2
    return jax.shard_map(
        heads_local_plan if whole_row else local,
        mesh=mesh,
        in_specs=placed,
        out_specs=(
            P("dp", "seq", None),
            P("dp", "seq", None),
            P(("dp", "seq")),
            P(("dp", "seq"), "tensor"),
            P(("dp", "seq"), "tensor"),
            P(),
            P(("dp", "seq"), "tensor"),
            P(),
            P(),
            P(),
            P(),
            P(),
            P(),
            P("tensor", ("dp", "seq")),
            P(("dp", "seq"), "tensor"),
            P(("dp", "seq"), "tensor"),
            P(("dp", "seq"), "tensor"),
            P("tensor", ("dp", "seq")),
            P(("dp", "seq")),
            P(("dp", "seq"), "tensor"),
            P(("dp", "seq"), "tensor"),
            P("tensor", ("dp", "seq")),
        ),
        check_vma=False,
    )
```
